32 devices in a mesh: groups: 2 (over x), op: 16 (over z, y, core).
Axes of the slice: x: 2, y: 2, z: 4, core: 2. Of those that a mesh axis runs over, the one named last changes fastest.
Arguments:
- trial: bfloat16 [32, 2, 128, 128], P(('groups', 'op')), parts along dimension 0, may hold values from -8 to 8
- left_ops: bfloat16 [8192, 128, 128], P(('groups', 'op')), parts along dimension 0, may hold values from -0.03125 to 0.03125
- right_ops: bfloat16 [128, 128, 128], P(('groups', 'op')), parts along dimension 0, may hold values from -0.5 to 0.5
- task_list: int32 [8192, 4], P(('groups', 'op')), parts along dimension 0, may hold values from 0 to 63, as said below
Outputs:
- product: float32 [32, 2, 128, 128], P(('groups', 'op')), parts along dimension 0
- correlation: float32 [4, 2], P('groups'), parts along dimension 0
- projected: float32 [4, 2], P('groups'), parts along dimension 0
The draws below stay inside these ranges and needn't reach their ends.
There are 2 independent parts, one for each index of `groups`. The reference program is written for one: setup_inputs(seed, part) draws one part's arguments, and reference() takes and returns one part's arrays. A program takes and returns all parts, laid end to end along the dimension named above; each array names one. Nothing has to cross between parts.
Inputs may be any that keep to these rules, and one draw needn't show every extreme that they name: `task_list`: column 0 and 1 are sectors below 16, column 2 a term below 64, column 3 is 0 or 1; the live slots of one device's 256 rows come first, and some device has all 256 slots live.
All inputs are finite; a program needn't handle non-finite values.
Results may differ from the reference program's by a relative error of at most 0.005.
Values may be sent and summed in bfloat16 or wider, within the bound.
No kernel may reach another device: no remote copies, remote signals or barrier semaphores. Data moves between devices by JAX's collectives and lax.ppermute only.
A program may use at most 128 MiB of HBM per device.

```python
import jax
import jax.numpy as jnp
from jax import lax

B = 128
TASK_DEV = 256
SECTORS = 16
TASKS = 4096
KTERMS = 64


def draw_trial(key, part):
    key = jax.random.fold_in(key, 7)
    keys = jax.random.split(key, 2)
    shape = (SECTORS, B, B)
    first = jnp.clip(jax.random.normal(keys[0], shape, jnp.float32), -5.0, 5.0)
    noise = jnp.clip(jax.random.normal(keys[1], shape, jnp.float32), -5.0, 5.0)
    share = 0.6
    second = share * first + jnp.sqrt(1.0 - share * share) * noise
    return jnp.stack([first, second], axis=1).astype(jnp.bfloat16)


def draw_task_list(key, part):
    key = jax.random.fold_in(key, 11)
    devices = TASKS // TASK_DEV
    keys = jax.random.split(key, 5)
    counts = jax.random.randint(keys[0], (devices,), TASK_DEV // 2, TASK_DEV + 1)
    full = jax.random.randint(keys[1], (), 0, devices)
    counts = jnp.where(jnp.arange(devices) == full, TASK_DEV, counts)
    slots = jnp.arange(TASK_DEV)
    live = (slots[None, :] < counts[:, None]).astype(jnp.int32)
    source = jax.random.randint(keys[2], (devices, TASK_DEV), 0, SECTORS)
    target = jax.random.randint(keys[3], (devices, TASK_DEV), 0, SECTORS)
    terms = jax.random.randint(keys[4], (devices, TASK_DEV), 0, KTERMS)
    table = jnp.stack([source, target, terms, live], axis=-1)
    return table.reshape(TASKS, 4).astype(jnp.int32)


def steps_of(key, extent, shards, least, largest):
    factor_of, own = 1.0, jax.random.fold_in(key, 6)
    for axis_at, shards_of in shards:
        heights = jnp.exp(jax.random.uniform(jax.random.fold_in(own, axis_at), (shards_of,), jnp.float32, least / len(shards), largest / len(shards)))
        factor_of = factor_of * jnp.repeat(heights, extent[axis_at] // shards_of).reshape([-1 if axis == axis_at else 1 for axis in range(len(extent))])
    return factor_of


def scatter_about(rng, shape, width, bound, shards=(), dtype=jnp.bfloat16):
    result = width * jax.random.normal(rng, shape, jnp.float32)
    if shards:
        result = result * steps_of(rng, shape, shards, -0.22, 0.18)
    return jnp.clip(result, -bound, bound).astype(dtype)


def setup_inputs(seed: int = 0, part: int = 0) -> dict:
    key_list = jax.random.split(jax.random.key(seed), 5)
    own_keys = jax.random.split(jax.random.fold_in(key_list[4], part), 5)
    return {
        "trial": draw_trial(jax.random.fold_in(jax.random.fold_in(key_list[4], part), 71), part),
        "left_ops": scatter_about(own_keys[1], (TASKS, B, B), (B * TASK_DEV) ** -0.5, 0.03125, ((0, 16),)),
        "right_ops": scatter_about(own_keys[2], (KTERMS, B, B), B ** -0.5, 0.5, ((0, 16),)),
        "task_list": draw_task_list(jax.random.fold_in(jax.random.fold_in(key_list[4], part), 71), part),
    }


def reference(trial, left_ops, right_ops, task_list):
    start = jnp.zeros(trial.shape, jnp.float32)

    def step(acc, item):
        left, row = item

        def work(acc):
            source = lax.dynamic_index_in_dim(trial, row[0], 0, keepdims=False).astype(jnp.float32)
            right = lax.dynamic_index_in_dim(right_ops, row[2], 0, keepdims=False).astype(jnp.float32)
            half = jnp.einsum("ab,vbc->vac", left.astype(jnp.float32), source).astype(jnp.bfloat16)
            term = jnp.einsum("vac,dc->vad", half.astype(jnp.float32), right)
            old = lax.dynamic_index_in_dim(acc, row[1], 0, keepdims=False)
            return lax.dynamic_update_index_in_dim(acc, old + term, row[1], 0)

        return lax.cond(row[3] > 0, work, lambda a: a, acc), None

    product, unused = lax.scan(step, start, (left_ops, task_list))
    vectors = trial.astype(jnp.float32)
    correlation = jnp.einsum("sibc,sjbc->ij", vectors, vectors)
    projected = jnp.einsum("sibc,sjbc->ij", vectors, product)
    return product, correlation, projected
```

```python
import functools

import jax
import jax.numpy as jnp
from jax import lax
from jax.experimental import pallas as pl
from jax.experimental.pallas import tpu as pltpu
from jax.sharding import PartitionSpec as P

VMEM_LIMIT = 56 * 1024 * 1024
TAIL = 32
LEFT_CHUNK = 16
UNROLL = 4


def exchange(value, n, mask):
    return lax.ppermute(value, "op", [(i, i ^ mask) for i in range(n)])


def gather(block, n):
    have = {0: block}
    for r in range(4, n, 4):
        have[r] = exchange(block, n, r)
    for r in sorted(have):
        have[r ^ 2] = exchange(have[r], n, 2)
    for r in sorted(have):
        have[r ^ 1] = exchange(have[r], n, 1)
    return [have[r] for r in range(n)]


def split3(value):
    high = value.astype(jnp.bfloat16)
    rest = value - high.astype(jnp.float32)
    middle = rest.astype(jnp.bfloat16)
    low = (rest - middle.astype(jnp.float32)).astype(jnp.bfloat16)
    zero = jnp.zeros_like(value)
    return jnp.concatenate(
        [high.astype(jnp.float32), middle.astype(jnp.float32), low.astype(jnp.float32), zero], axis=0
    ).astype(jnp.bfloat16)


def join3(tail):
    wide = tail.astype(jnp.float32)
    return wide[0:8] + wide[8:16] + wide[16:24]


def matrix_of(values):
    rows = lax.broadcasted_iota(jnp.int32, (8, 128), 0)
    lanes = lax.broadcasted_iota(jnp.int32, (8, 128), 1)
    total = jnp.zeros((8, 128), jnp.float32)
    for (i, j), value in values.items():
        total = total + jnp.where((rows == i) & (lanes == j), value, 0.0)
    return total


def fold(value):
    return value.reshape(16, 8, 128).sum(axis=0)


def tasks_kernel(n, terms_per, tasks_ref, left_ref, *refs):
    blocks = refs[:n]
    send_ref, keep_ref, own_ref, corr_ref = refs[n : n + 4]
    trial, right, left, acc, block_sem, left_sem = refs[n + 4 :]
    slots = left_ref.shape[0]
    me = lax.axis_index("op")
    chunks = slots // LEFT_CHUNK

    def left_copy(chunk):
        rows = pl.ds(chunk * LEFT_CHUNK, LEFT_CHUNK)
        return pltpu.make_async_copy(left_ref.at[rows], left.at[rows], left_sem.at[chunk])

    def block_copies(r):
        owner = jnp.bitwise_xor(me, r)
        return (
            pltpu.make_async_copy(blocks[r].at[pl.ds(0, 2)], trial.at[owner], block_sem.at[r, 0]),
            pltpu.make_async_copy(
                blocks[r].at[pl.ds(2, terms_per)],
                right.at[pl.ds(owner * terms_per, terms_per)],
                block_sem.at[r, 1],
            ),
        )

    for r in range(n):
        for copy in block_copies(r):
            copy.start()
    for chunk in range(chunks):
        left_copy(chunk).start()

    def clear(s, carry):
        acc[s] = jnp.zeros((256, 128), jnp.float32)
        return carry

    lax.fori_loop(0, n + 1, clear, 0)
    for r in range(n):
        for copy in block_copies(r):
            copy.wait()

    def group(first):
        halves = []
        for u in range(UNROLL):
            slot = first + u
            source = tasks_ref[0, slot]
            vectors = jnp.concatenate([trial[source, 0], trial[source, 1]], axis=1)
            half = jnp.dot(left[slot], vectors, preferred_element_type=jnp.float32)
            halves.append(half.astype(jnp.bfloat16))
        for u in range(UNROLL):
            slot = first + u
            half = jnp.concatenate([halves[u][:, :128], halves[u][:, 128:]], axis=0)
            term = lax.dot_general(
                half, right[tasks_ref[2, slot]], (((1,), (1,)), ((), ())), preferred_element_type=jnp.float32
            )
            target = jnp.where(tasks_ref[3, slot] > 0, tasks_ref[1, slot], n)
            acc[target] = acc[target] + term

    def chunk_step(chunk, carry):
        left_copy(chunk).wait()
        for part in range(LEFT_CHUNK // UNROLL):
            first = chunk * LEFT_CHUNK + part * UNROLL

            @pl.when(tasks_ref[3, first] > 0)
            def _():
                group(first)

        return carry

    lax.fori_loop(0, chunks, chunk_step, 0)

    def dots(s, carry):
        c00, c01, c11, p00, p01, p10, p11 = carry
        t0 = trial[s, 0].astype(jnp.float32)
        t1 = trial[s, 1].astype(jnp.float32)
        a0 = acc[s, 0:128, :]
        a1 = acc[s, 128:256, :]
        return (
            c00 + fold(t0 * t0),
            c01 + fold(t0 * t1),
            c11 + fold(t1 * t1),
            p00 + fold(t0 * a0),
            p01 + fold(t0 * a1),
            p10 + fold(t1 * a0),
            p11 + fold(t1 * a1),
        )

    zero = jnp.zeros((8, 128), jnp.float32)
    c00, c01, c11, p00, p01, p10, p11 = [jnp.sum(x) for x in lax.fori_loop(0, n, dots, (zero,) * 7)]
    corr_ref[...] = matrix_of({(0, 0): c00, (0, 1): c01, (1, 0): c01, (1, 1): c11})[0:2, 0:2]
    own = matrix_of({(0, 0): p00, (0, 1): p01, (1, 0): p10, (1, 1): p11})
    own_ref[...] = own

    def pack(j, carry):
        mine = jnp.bitwise_xor(me, 2 * j)
        keep_ref[j] = acc[mine]
        send_ref[pl.ds(pl.multiple_of(j * 256, 256), 256), :] = acc[jnp.bitwise_xor(mine, 1)].astype(jnp.bfloat16)
        return carry

    lax.fori_loop(0, n // 2, pack, 0)
    send_ref[n // 2 * 256 :, :] = split3(own)


def run_tasks(tasks, left_ops, blocks):
    n = len(blocks)
    terms_per = blocks[0].shape[0] - 2
    slots = left_ops.shape[0]
    return pl.pallas_call(
        functools.partial(tasks_kernel, n, terms_per),
        out_shape=(
            jax.ShapeDtypeStruct((n // 2 * 256 + TAIL, 128), jnp.bfloat16),
            jax.ShapeDtypeStruct((n // 2, 256, 128), jnp.float32),
            jax.ShapeDtypeStruct((8, 128), jnp.float32),
            jax.ShapeDtypeStruct((2, 2), jnp.float32),
        ),
        in_specs=[pl.BlockSpec(memory_space=pltpu.SMEM)] + [pl.BlockSpec(memory_space=pl.ANY)] * (1 + n),
        scratch_shapes=[
            pltpu.VMEM((n, 2, 128, 128), jnp.bfloat16),
            pltpu.VMEM((n * terms_per, 128, 128), jnp.bfloat16),
            pltpu.VMEM((slots, 128, 128), jnp.bfloat16),
            pltpu.VMEM((n + 1, 256, 128), jnp.float32),
            pltpu.SemaphoreType.DMA((n, 2)),
            pltpu.SemaphoreType.DMA((slots // LEFT_CHUNK,)),
        ],
        compiler_params=pltpu.CompilerParams(vmem_limit_bytes=VMEM_LIMIT),
        cost_estimate=pl.CostEstimate(
            flops=slots * 8 * 128**3, bytes_accessed=slots * 32768 + n * 200000, transcendentals=0
        ),
    )(tasks, left_ops, *blocks)


def chip_kernel(chips, keep_ref, own_ref, received_ref, mine_ref, total_ref, *sends):
    total = own_ref[...] + join3(received_ref[chips * 256 :, :])
    total_ref[...] = total
    tail = split3(total)
    for j in range(chips):
        value = keep_ref[j] + received_ref[j * 256 : (j + 1) * 256, :].astype(jnp.float32)
        if j == 0:
            mine_ref[...] = value
        else:
            sends[j - 1][0:256, :] = value.astype(jnp.bfloat16)
            sends[j - 1][256:, :] = tail


def add_chip(keep, own, received):
    chips = keep.shape[0]
    return pl.pallas_call(
        functools.partial(chip_kernel, chips),
        out_shape=(jax.ShapeDtypeStruct((256, 128), jnp.float32), jax.ShapeDtypeStruct((8, 128), jnp.float32))
        + (jax.ShapeDtypeStruct((256 + TAIL, 128), jnp.bfloat16),) * (chips - 1),
        compiler_params=pltpu.CompilerParams(vmem_limit_bytes=VMEM_LIMIT),
    )(keep, own, received)


def last_kernel(mine_ref, total_ref, *refs):
    received, (product_ref, projected_ref) = refs[:-2], refs[-2:]
    value, total = mine_ref[...], total_ref[...]
    for ref in received:
        value = value + ref[0:256, :].astype(jnp.float32)
        total = total + join3(ref[256:, :])
    product_ref[0, 0] = value[0:128]
    product_ref[0, 1] = value[128:256]
    projected_ref[...] = total[0:2, 0:2]


def add_all(mine, total, received):
    return pl.pallas_call(
        last_kernel,
        out_shape=(
            jax.ShapeDtypeStruct((1, 2, 128, 128), jnp.float32),
            jax.ShapeDtypeStruct((2, 2), jnp.float32),
        ),
        compiler_params=pltpu.CompilerParams(vmem_limit_bytes=VMEM_LIMIT),
    )(mine, total, *received)


def body(n, trial, left_ops, right_ops, task_list):
    blocks = gather(jnp.concatenate([trial[0], right_ops], axis=0), n)
    send, keep, own, correlation = run_tasks(task_list.T, left_ops, blocks)
    mine, total, *sends = add_chip(keep, own, exchange(send, n, 1))
    received = [exchange(value, n, 2 * (j + 1)) for j, value in enumerate(sends)]
    product, projected = add_all(mine, total, received)
    return product, correlation, projected


def solution(mesh):
    return jax.shard_map(
        functools.partial(body, mesh.shape["op"]),
        mesh=mesh,
        in_specs=(
            P(("groups", "op"), None, None, None),
            P(("groups", "op"), None, None),
            P(("groups", "op"), None, None),
            P(("groups", "op"), None),
        ),
        out_specs=(P(("groups", "op"), None, None, None), P("groups", None), P("groups", None)),
        check_vma=False,
    )
```

```python
import functools

import jax
import jax.numpy as jnp
from jax import lax
from jax.experimental import pallas as pl
from jax.experimental.pallas import tpu as pltpu
from jax.sharding import PartitionSpec as P

VMEM_LIMIT = 56 * 1024 * 1024
TAIL = 32
CHUNK = 32
UNROLL = 16
PAIRS = 8


def exchange(value, n, mask):
    return lax.ppermute(value, "op", [(i, i ^ mask) for i in range(n)])


def ring_step(value, n):
    return lax.ppermute(value, "op", [(i, (i + 4) % n) for i in range(n)])


def gather(block, n):
    blocks = []
    for step in range(n // 4):
        if step:
            block = ring_step(block, n)
        across = exchange(block, n, 2)
        blocks += [block, exchange(block, n, 1), across, exchange(across, n, 1)]
    return blocks


def owner_of(place, n):
    me = lax.axis_index("op")
    step, mask = divmod(place, 4)
    return lax.rem(me // 4 - step + n // 4, n // 4) * 4 + jnp.bitwise_xor(lax.rem(me, 4), mask)


def split3(value):
    high = value.astype(jnp.bfloat16)
    rest = value - high.astype(jnp.float32)
    middle = rest.astype(jnp.bfloat16)
    low = (rest - middle.astype(jnp.float32)).astype(jnp.bfloat16)
    zero = jnp.zeros_like(value)
    return jnp.concatenate(
        [high.astype(jnp.float32), middle.astype(jnp.float32), low.astype(jnp.float32), zero], axis=0
    ).astype(jnp.bfloat16)


def join3(tail):
    wide = tail.astype(jnp.float32)
    return wide[0:8] + wide[8:16] + wide[16:24]


def matrix_of(values):
    rows = lax.broadcasted_iota(jnp.int32, (8, 128), 0)
    lanes = lax.broadcasted_iota(jnp.int32, (8, 128), 1)
    total = jnp.zeros((8, 128), jnp.float32)
    for (i, j), value in values.items():
        total = total + jnp.where((rows == i) & (lanes == j), value, 0.0)
    return total


def fold(value):
    return value.reshape(16, 8, 128).sum(axis=0)


def plan_kernel(sectors, terms, tasks_ref, plan_ref):
    slots = tasks_ref.shape[1]
    places = plan_ref.shape[1]
    rows = tasks_ref[...].astype(jnp.float32)
    source, target, term, live = rows[0:1], rows[1:2], rows[2:3], rows[3:4]
    key = jnp.where(live > 0, target, float(sectors))
    lane = lax.broadcasted_iota(jnp.int32, (1, slots), 1).astype(jnp.float32)

    def column(*values):
        pad = [jnp.zeros((8 - len(values), slots), jnp.float32)]
        return jnp.transpose(jnp.concatenate(list(values) + pad, axis=0))

    columns = column(key, lane, source, term)
    key_column, lane_column = columns[:, 0:1], columns[:, 1:2]
    earlier = jnp.where((key_column == key) & (lane_column < lane), 1.0, 0.0)
    within = jnp.sum(earlier, axis=0, keepdims=True)
    sector = lax.broadcasted_iota(jnp.int32, (sectors, slots), 0).astype(jnp.float32)
    count = jnp.sum(jnp.where(sector == key, 1.0, 0.0), axis=1, keepdims=True)
    padded = 2.0 * jnp.floor((count + 1.0) * 0.5)
    start = jnp.sum(jnp.where(sector < key, padded, 0.0), axis=0, keepdims=True)
    place = jnp.where(live > 0, start + within, -1.0)
    place_column = column(place)[:, 0:1]
    at = lax.broadcasted_iota(jnp.int32, (slots, places), 1).astype(jnp.float32)
    hit = place_column == at

    def pick(values, other):
        found = jnp.sum(jnp.where(hit, values - other, 0.0), axis=0, keepdims=True)
        return (found + other).astype(jnp.int32)

    plan_ref[0:1] = pick(lane_column, 0.0)
    plan_ref[1:2] = pick(columns[:, 2:3], 0.0)
    plan_ref[2:3] = pick(columns[:, 3:4], float(terms))
    plan_ref[3:4] = pick(key_column, float(sectors))
    plan_ref[4:8] = jnp.zeros((4, places), jnp.int32)


def make_plan(tasks, sectors, terms):
    places = -(-(tasks.shape[1] + sectors) // CHUNK) * CHUNK
    return pl.pallas_call(
        functools.partial(plan_kernel, sectors, terms),
        out_shape=jax.ShapeDtypeStruct((8, places), jnp.int32),
        compiler_params=pltpu.CompilerParams(vmem_limit_bytes=VMEM_LIMIT),
    )(tasks)


def half_kernel(n, plan_ref, left_ref, *refs):
    blocks = refs[:n]
    half_ref, corr_ref, trial, left, trial_sem, left_sem = refs[n:]
    step, steps = pl.program_id(0), pl.num_programs(0)

    def fetch(chunk):
        def one(u, carry):
            slot = plan_ref[0, chunk * CHUNK + u]
            pltpu.make_async_copy(
                left_ref.at[slot], left.at[lax.rem(chunk, 2), u], left_sem.at[lax.rem(chunk, 2)]
            ).start()
            return carry

        lax.fori_loop(0, CHUNK, one, 0)

    def trial_copy(place):
        return pltpu.make_async_copy(
            blocks[place].at[pl.ds(0, 2)], trial.at[owner_of(place, n)], trial_sem.at[place]
        )

    @pl.when(step == 0)
    def _():
        for place in range(n):
            trial_copy(place).start()
        fetch(0)

    @pl.when(step + 1 < steps)
    def _():
        fetch(step + 1)

    @pl.when(step == 0)
    def _():
        for place in range(n):
            trial_copy(place).wait()

        def dots(s, carry):
            t0 = trial[s, 0].astype(jnp.float32)
            t1 = trial[s, 1].astype(jnp.float32)
            return carry[0] + fold(t0 * t0), carry[1] + fold(t0 * t1), carry[2] + fold(t1 * t1)

        zero = jnp.zeros((8, 128), jnp.float32)
        c00, c01, c11 = [jnp.sum(x) for x in lax.fori_loop(0, n, dots, (zero,) * 3)]
        corr_ref[...] = matrix_of({(0, 0): c00, (0, 1): c01, (1, 0): c01, (1, 1): c11})[0:2, 0:2]

    now = lax.rem(step, 2)
    pltpu.make_async_copy(left_ref.at[pl.ds(0, CHUNK)], left.at[now], left_sem.at[now]).wait()

    def some(part, carry):
        for u in range(UNROLL):
            at = part * UNROLL + u
            source = plan_ref[1, step * CHUNK + at]
            vectors = jnp.concatenate([trial[source, 0], trial[source, 1]], axis=1)
            half = jnp.dot(left[now, at], vectors, preferred_element_type=jnp.float32).astype(jnp.bfloat16)
            half_ref[at, 0:128, :] = half[:, :128]
            half_ref[at, 128:256, :] = half[:, 128:]
        return carry

    lax.fori_loop(0, CHUNK // UNROLL, some, 0)


def make_halves(plan, left_ops, blocks):
    n = len(blocks)
    places = plan.shape[1]
    return pl.pallas_call(
        functools.partial(half_kernel, n),
        grid=(places // CHUNK,),
        out_shape=(
            jax.ShapeDtypeStruct((places, 256, 128), jnp.bfloat16),
            jax.ShapeDtypeStruct((2, 2), jnp.float32),
        ),
        in_specs=[pl.BlockSpec(memory_space=pltpu.SMEM)] + [pl.BlockSpec(memory_space=pl.ANY)] * (1 + n),
        out_specs=(
            pl.BlockSpec((CHUNK, 256, 128), lambda i: (i, 0, 0)),
            pl.BlockSpec((2, 2), lambda i: (0, 0)),
        ),
        scratch_shapes=[
            pltpu.VMEM((n, 2, 128, 128), jnp.bfloat16),
            pltpu.VMEM((2, CHUNK, 128, 128), jnp.bfloat16),
            pltpu.SemaphoreType.DMA((n,)),
            pltpu.SemaphoreType.DMA((2,)),
        ],
        compiler_params=pltpu.CompilerParams(vmem_limit_bytes=VMEM_LIMIT),
        cost_estimate=pl.CostEstimate(
            flops=places * 4 * 128**3, bytes_accessed=places * 98304 + n * 65536, transcendentals=0
        ),
    )(plan, left_ops, *blocks)


def term_kernel(n, terms_per, plan_ref, half_ref, *refs):
    blocks = refs[:n]
    send_ref, keep_ref, own_ref, trial, right, acc, block_sem = refs[n:]
    step, steps = pl.program_id(0), pl.num_programs(0)

    def block_copies(place):
        owner = owner_of(place, n)
        return (
            pltpu.make_async_copy(blocks[place].at[pl.ds(0, 2)], trial.at[owner], block_sem.at[place, 0]),
            pltpu.make_async_copy(
                blocks[place].at[pl.ds(2, terms_per)],
                right.at[pl.ds(owner * terms_per, terms_per)],
                block_sem.at[place, 1],
            ),
        )

    @pl.when(step == 0)
    def _():
        for place in range(n):
            for copy in block_copies(place):
                copy.start()
        right[n * terms_per] = jnp.zeros((128, 128), jnp.bfloat16)

        def clear(s, carry):
            acc[s] = jnp.zeros((256, 128), jnp.float32)
            return carry

        lax.fori_loop(0, n + 1, clear, 0)
        for place in range(n):
            for copy in block_copies(place):
                copy.wait()

    for part in range(CHUNK // 2 // PAIRS):
        first = step * CHUNK + part * 2 * PAIRS

        @pl.when(plan_ref[3, first] < n)
        def _():
            for u in range(PAIRS):
                at = part * 2 * PAIRS + 2 * u
                place = first + 2 * u
                halves = jnp.concatenate([half_ref[at], half_ref[at + 1]], axis=1)
                rights = jnp.concatenate([right[plan_ref[2, place]], right[plan_ref[2, place + 1]]], axis=1)
                term = lax.dot_general(
                    halves, rights, (((1,), (1,)), ((), ())), preferred_element_type=jnp.float32
                )
                target = plan_ref[3, place]
                acc[target] = acc[target] + term

    @pl.when(step == steps - 1)
    def _():
        def dots(s, carry):
            t0 = trial[s, 0].astype(jnp.float32)
            t1 = trial[s, 1].astype(jnp.float32)
            a0 = acc[s, 0:128, :]
            a1 = acc[s, 128:256, :]
            p00, p01, p10, p11 = carry
            return p00 + fold(t0 * a0), p01 + fold(t0 * a1), p10 + fold(t1 * a0), p11 + fold(t1 * a1)

        zero = jnp.zeros((8, 128), jnp.float32)
        p00, p01, p10, p11 = [jnp.sum(x) for x in lax.fori_loop(0, n, dots, (zero,) * 4)]
        own = matrix_of({(0, 0): p00, (0, 1): p01, (1, 0): p10, (1, 1): p11})
        own_ref[...] = own
        core = lax.rem(lax.axis_index("op"), 2)

        def pack(j, carry):
            keep_ref[j] = acc[2 * j + core]
            send_ref[pl.ds(pl.multiple_of(j * 256, 256), 256), :] = acc[2 * j + 1 - core].astype(jnp.bfloat16)
            return carry

        lax.fori_loop(0, n // 2, pack, 0)
        send_ref[n // 2 * 256 :, :] = split3(own)


def add_terms(plan, halves, blocks):
    n = len(blocks)
    terms_per = blocks[0].shape[0] - 2
    places = plan.shape[1]
    return pl.pallas_call(
        functools.partial(term_kernel, n, terms_per),
        grid=(places // CHUNK,),
        out_shape=(
            jax.ShapeDtypeStruct((n // 2 * 256 + TAIL, 128), jnp.bfloat16),
            jax.ShapeDtypeStruct((n // 2, 256, 128), jnp.float32),
            jax.ShapeDtypeStruct((8, 128), jnp.float32),
        ),
        in_specs=[
            pl.BlockSpec(memory_space=pltpu.SMEM),
            pl.BlockSpec((CHUNK, 256, 128), lambda i: (i, 0, 0)),
        ]
        + [pl.BlockSpec(memory_space=pl.ANY)] * n,
        out_specs=(
            pl.BlockSpec((n // 2 * 256 + TAIL, 128), lambda i: (0, 0)),
            pl.BlockSpec((n // 2, 256, 128), lambda i: (0, 0, 0)),
            pl.BlockSpec((8, 128), lambda i: (0, 0)),
        ),
        scratch_shapes=[
            pltpu.VMEM((n, 2, 128, 128), jnp.bfloat16),
            pltpu.VMEM((n * terms_per + 1, 128, 128), jnp.bfloat16),
            pltpu.VMEM((n + 1, 256, 128), jnp.float32),
            pltpu.SemaphoreType.DMA((n, 2)),
        ],
        compiler_params=pltpu.CompilerParams(vmem_limit_bytes=VMEM_LIMIT),
        cost_estimate=pl.CostEstimate(
            flops=places * 4 * 128**3, bytes_accessed=places * 65536 + n * 200000, transcendentals=0
        ),
    )(plan, halves, *blocks)


def chip_kernel(chips, keep_ref, own_ref, received_ref, mine_ref, total_ref, send_ref):
    total = own_ref[...] + join3(received_ref[chips * 256 :, :])
    total_ref[...] = total
    tail = split3(total)
    here = lax.axis_index("op") // 2
    for j in range(chips):
        value = keep_ref[j] + received_ref[j * 256 : (j + 1) * 256, :].astype(jnp.float32)
        send_ref[j, 0:256, :] = value.astype(jnp.bfloat16)
        send_ref[j, 256:, :] = tail

    mine_ref[...] = keep_ref[here] + received_ref[
        pl.ds(pl.multiple_of(here * 256, 256), 256), :
    ].astype(jnp.float32)
    send_ref[here] = jnp.zeros((256 + TAIL, 128), jnp.bfloat16)


def add_chip(keep, own, received):
    chips = keep.shape[0]
    return pl.pallas_call(
        functools.partial(chip_kernel, chips),
        out_shape=(
            jax.ShapeDtypeStruct((256, 128), jnp.float32),
            jax.ShapeDtypeStruct((8, 128), jnp.float32),
            jax.ShapeDtypeStruct((chips, 256 + TAIL, 128), jnp.bfloat16),
        ),
        compiler_params=pltpu.CompilerParams(vmem_limit_bytes=VMEM_LIMIT),
    )(keep, own, received)


def last_kernel(mine_ref, total_ref, received_ref, product_ref, projected_ref):
    value, total = mine_ref[...], total_ref[...]
    for j in range(received_ref.shape[0]):
        value = value + received_ref[j, 0:256, :].astype(jnp.float32)
        total = total + join3(received_ref[j, 256:, :])
    product_ref[0, 0] = value[0:128]
    product_ref[0, 1] = value[128:256]
    projected_ref[...] = total[0:2, 0:2]


def add_all(mine, total, received):
    return pl.pallas_call(
        last_kernel,
        out_shape=(
            jax.ShapeDtypeStruct((1, 2, 128, 128), jnp.float32),
            jax.ShapeDtypeStruct((2, 2), jnp.float32),
        ),
        compiler_params=pltpu.CompilerParams(vmem_limit_bytes=VMEM_LIMIT),
    )(mine, total, received)


def body(n, trial, left_ops, right_ops, task_list):
    blocks = gather(jnp.concatenate([trial[0], right_ops], axis=0), n)
    plan = make_plan(task_list.T, n, n * right_ops.shape[0])
    halves, correlation = make_halves(plan, left_ops, blocks)
    send, keep, own = add_terms(plan, halves, blocks)
    mine, total, send = add_chip(keep, own, exchange(send, n, 1))
    same_core = [list(range(core, n, 2)) for core in range(2)]
    received = lax.all_to_all(send, "op", 0, 0, axis_index_groups=same_core, tiled=True)
    product, projected = add_all(mine, total, received)
    return product, correlation, projected


def solution(mesh):
    return jax.shard_map(
        functools.partial(body, mesh.shape["op"]),
        mesh=mesh,
        in_specs=(
            P(("groups", "op"), None, None, None),
            P(("groups", "op"), None, None),
            P(("groups", "op"), None, None),
            P(("groups", "op"), None),
        ),
        out_specs=(P(("groups", "op"), None, None, None), P("groups", None), P("groups", None)),
        check_vma=False,
    )
```

```python
import functools

import jax
import jax.numpy as jnp
from jax import lax
from jax.experimental import pallas as pl
from jax.experimental.pallas import tpu as pltpu
from jax.sharding import PartitionSpec as P

TAIL = 32
PAIRS = 4
GROUP = 2 * PAIRS
SLOTS_AHEAD = 4
TRIALS = 2


def exchange(value, n, mask):
    return lax.ppermute(value, "op", [(i, i ^ mask) for i in range(n)])


def chip_at(place, chips):
    return 2 * place if place < chips // 2 else 2 * (chips - place) - 1


def ring_step(value, n):
    chips = n // 2
    order = [chip_at(place, chips) for place in range(chips)]
    pairs = []
    for place, chip in enumerate(order):
        pairs.append((2 * chip, 2 * order[(place + 1) % chips]))
        pairs.append((2 * chip + 1, 2 * order[(place - 1) % chips] + 1))
    return lax.ppermute(value, "op", pairs)


def place_of(chip, chips):
    half = jnp.floor(chip * 0.5)
    return jnp.where(chip == 2.0 * half, half, chips - 1.0 - half)


def owner_of(step, swapped, half, n):
    chips = n // 2
    me = lax.axis_index("op")
    chip, core = me // 2, lax.rem(me, 2)
    odd = lax.rem(chip, 2)
    mine = jnp.where(odd == 0, chip // 2, chips - 1 - chip // 2)
    line = 1 - core if swapped else core
    place = lax.rem(mine + (2 * line - 1) * step + 2 * chips, chips)
    there = jnp.where(place < chips // 2, 2 * place, 2 * (chips - place) - 1)
    return 2 * there + (line if half == 0 else 1 - line)


def split3(value):
    high = value.astype(jnp.bfloat16)
    rest = value - high.astype(jnp.float32)
    middle = rest.astype(jnp.bfloat16)
    low = (rest - middle.astype(jnp.float32)).astype(jnp.bfloat16)
    zero = jnp.zeros_like(value)
    return jnp.concatenate(
        [high.astype(jnp.float32), middle.astype(jnp.float32), low.astype(jnp.float32), zero], axis=0
    ).astype(jnp.bfloat16)


def join3(tail):
    wide = tail.astype(jnp.float32)
    return wide[0:8] + wide[8:16] + wide[16:24]


def matrix_of(values):
    rows = lax.broadcasted_iota(jnp.int32, (8, 128), 0)
    lanes = lax.broadcasted_iota(jnp.int32, (8, 128), 1)
    total = jnp.zeros((8, 128), jnp.float32)
    for (i, j), value in values.items():
        total = total + jnp.where((rows == i) & (lanes == j), value, 0.0)
    return total


def fold(value):
    return value.reshape(16, 8, 128).sum(axis=0)


def phases_of(n):
    return min(4, n // 4)


def plan_kernel(n, terms, tasks_ref, plan_ref):
    slots = tasks_ref.shape[1]
    places = plan_ref.shape[1]
    chips = n // 2
    phases = phases_of(n)
    steps = chips // 2
    rows = tasks_ref[...].astype(jnp.float32)
    source, target, term, live = rows[0:1], rows[1:2], rows[2:3], rows[3:4]
    me = lax.axis_index("op")
    mine = place_of((jnp.zeros((1, slots), jnp.int32) + me // 2).astype(jnp.float32), float(chips))

    def distance(owner):
        gap = place_of(jnp.floor(owner * 0.5), float(chips)) - mine
        up = jnp.where(gap < 0, gap + chips, gap)
        return jnp.minimum(up, chips - up)

    far = jnp.maximum(distance(source), distance(jnp.floor(term * (n / terms))))
    phase = jnp.maximum(jnp.ceil(far * (phases / steps)), 1.0) - 1.0
    keys = phases * n
    key = jnp.where(live > 0, phase * n + target, float(keys))
    lane = lax.broadcasted_iota(jnp.int32, (1, slots), 1).astype(jnp.float32)

    def column(*values):
        pad = [jnp.zeros((8 - len(values), slots), jnp.float32)]
        return jnp.transpose(jnp.concatenate(list(values) + pad, axis=0))

    columns = column(key, lane, source, term, target)
    key_column, lane_column = columns[:, 0:1], columns[:, 1:2]
    earlier = jnp.where((key_column == key) & (lane_column < lane), 1.0, 0.0)
    place = jnp.sum(earlier, axis=0, keepdims=True)
    index = lax.broadcasted_iota(jnp.int32, (keys, slots), 0).astype(jnp.float32)
    count = jnp.sum(jnp.where(index == key, 1.0, 0.0), axis=1, keepdims=True)
    padded = 2.0 * jnp.floor((count + 1.0) * 0.5)
    number = lax.broadcasted_iota(jnp.int32, (1, places), 1).astype(jnp.float32)
    starts = jnp.zeros((1, places), jnp.float32)
    start = jnp.zeros((1, 1), jnp.float32)
    for p in range(phases):
        part = padded[p * n : (p + 1) * n]
        before = jnp.sum(jnp.where(index[p * n : (p + 1) * n] < key, part, 0.0), axis=0, keepdims=True)
        place = place + jnp.where(phase == p, start + before, 0.0)
        groups = jnp.ceil(jnp.sum(part, axis=0, keepdims=True) / GROUP)
        start = start + groups * GROUP
        starts = starts + jnp.where(number > p, groups, 0.0)
    place = jnp.where(live > 0, place, -1.0)
    place_column = column(place)[:, 0:1]
    at = lax.broadcasted_iota(jnp.int32, (slots, places), 1).astype(jnp.float32)
    hit = place_column == at

    def pick(values, other):
        found = jnp.sum(jnp.where(hit, values - other, 0.0), axis=0, keepdims=True)
        return (found + other).astype(jnp.int32)

    own = (jnp.zeros((1, 1), jnp.int32) + me).astype(jnp.float32)
    plan_ref[0:1] = pick(lane_column, 0.0)
    plan_ref[1:2] = pick(columns[:, 2:3], own)
    plan_ref[2:3] = pick(columns[:, 3:4], float(terms))
    plan_ref[3:4] = pick(columns[:, 4:5], float(n))
    plan_ref[4:5] = starts.astype(jnp.int32)
    plan_ref[5:8] = jnp.zeros((3, places), jnp.int32)


def make_plan(tasks, n, terms):
    slots = tasks.shape[1]
    phases = phases_of(n)
    most = slots + min(slots, phases * n) + phases * GROUP
    return pl.pallas_call(
        functools.partial(plan_kernel, n, terms),
        out_shape=jax.ShapeDtypeStruct((8, -(-most // 128) * 128), jnp.int32),
    )(tasks)


def tasks_kernel(n, terms_per, phase, last, kinds, plan_ref, left_ref, *refs):
    if phase:
        acc_in, corr_in, *refs = refs
    blocks, refs = refs[: len(kinds)], refs[len(kinds) :]
    if last:
        send_ref, keep_ref, own_ref, corr_ref, *refs = refs
    else:
        acc_out, corr_out, *refs = refs
    trial, right, acc, left, block_sem, left_sem, acc_sem = refs
    first, count = plan_ref[4, phase], plan_ref[4, phase + 1] - plan_ref[4, phase]
    per = TRIALS + terms_per

    def block_copies(b):
        step, swapped, unused = kinds[b]
        copies = []
        for half in range(2):
            owner = owner_of(step, swapped, half, n)
            copies.append(
                pltpu.make_async_copy(
                    blocks[b].at[pl.ds(half * per, TRIALS)], trial.at[owner], block_sem.at[b, 2 * half]
                )
            )
            copies.append(
                pltpu.make_async_copy(
                    blocks[b].at[pl.ds(half * per + TRIALS, terms_per)],
                    right.at[pl.ds(owner * terms_per, terms_per)],
                    block_sem.at[b, 2 * half + 1],
                )
            )
        return copies

    def fetch(group):
        at = lax.rem(group, SLOTS_AHEAD)
        for u in range(GROUP):
            slot = plan_ref[0, (first + group) * GROUP + u]
            pltpu.make_async_copy(left_ref.at[slot], left.at[at, u], left_sem.at[at]).start()

    for b in range(len(kinds)):
        for copy in block_copies(b):
            copy.start()
    for group in range(SLOTS_AHEAD - 1):

        @pl.when(group < count)
        def _():
            fetch(group)

    if phase:
        acc_copy = pltpu.make_async_copy(acc_in, acc.at[pl.ds(0, n)], acc_sem)
        acc_copy.start()
    else:

        def clear(s, carry):
            acc[s] = jnp.zeros((256, 128), jnp.float32)
            return carry

        lax.fori_loop(0, n, clear, 0)
    right[n * terms_per] = jnp.zeros((128, 128), jnp.bfloat16)
    for b in range(len(kinds)):
        for copy in block_copies(b):
            copy.wait()
    if phase:
        acc_copy.wait()

    corr = [corr_in[8 * i : 8 * i + 8, :] if phase else jnp.zeros((8, 128), jnp.float32) for i in range(3)]
    for step, swapped, new in kinds:
        for half in range(2) if new else ():
            owner = owner_of(step, swapped, half, n)
            t0, t1 = trial[owner, 0].astype(jnp.float32), trial[owner, 1].astype(jnp.float32)
            corr = [corr[0] + fold(t0 * t0), corr[1] + fold(t0 * t1), corr[2] + fold(t1 * t1)]

    def turn(group, carry):
        @pl.when(group + SLOTS_AHEAD - 1 < count)
        def _():
            fetch(group + SLOTS_AHEAD - 1)

        at = lax.rem(group, SLOTS_AHEAD)
        pltpu.make_async_copy(left_ref.at[pl.ds(0, GROUP)], left.at[at], left_sem.at[at]).wait()
        place = (first + group) * GROUP
        halves = []
        for u in range(GROUP):
            source = plan_ref[1, place + u]
            vectors = jnp.concatenate([trial[source, 0], trial[source, 1]], axis=1)
            half = jnp.dot(left[at, u], vectors, preferred_element_type=jnp.float32)
            halves.append(half.astype(jnp.bfloat16))
        for u in range(0, GROUP, 2):
            one, two = halves[u], halves[u + 1]
            pair = jnp.concatenate(
                [
                    jnp.concatenate([one[:, :128], two[:, :128]], axis=1),
                    jnp.concatenate([one[:, 128:], two[:, 128:]], axis=1),
                ],
                axis=0,
            )
            rights = jnp.concatenate(
                [right[plan_ref[2, place + u]], right[plan_ref[2, place + u + 1]]], axis=1
            )
            term = lax.dot_general(
                pair, rights, (((1,), (1,)), ((), ())), preferred_element_type=jnp.float32
            )
            target = plan_ref[3, place + u]
            acc[target] = acc[target] + term
        return carry

    lax.fori_loop(0, count, turn, 0)
    if not last:
        for i in range(3):
            corr_out[8 * i : 8 * i + 8, :] = corr[i]
        acc_copy = pltpu.make_async_copy(acc.at[pl.ds(0, n)], acc_out, acc_sem)
        acc_copy.start()
        acc_copy.wait()
        return
    c00, c01, c11 = [jnp.sum(x) for x in corr]
    corr_ref[...] = matrix_of({(0, 0): c00, (0, 1): c01, (1, 0): c01, (1, 1): c11})[0:2, 0:2]

    def dots(s, carry):
        t0 = trial[s, 0].astype(jnp.float32)
        t1 = trial[s, 1].astype(jnp.float32)
        a0 = acc[s, 0:128, :]
        a1 = acc[s, 128:256, :]
        p00, p01, p10, p11 = carry
        return p00 + fold(t0 * a0), p01 + fold(t0 * a1), p10 + fold(t1 * a0), p11 + fold(t1 * a1)

    zero = jnp.zeros((8, 128), jnp.float32)
    p00, p01, p10, p11 = [jnp.sum(x) for x in lax.fori_loop(0, n, dots, (zero,) * 4)]
    own = matrix_of({(0, 0): p00, (0, 1): p01, (1, 0): p10, (1, 1): p11})
    own_ref[...] = own
    core = lax.rem(lax.axis_index("op"), 2)

    def pack(j, carry):
        keep_ref[j] = acc[2 * j + core]
        send_ref[pl.ds(pl.multiple_of(j * 256, 256), 256), :] = acc[2 * j + 1 - core].astype(jnp.bfloat16)
        return carry

    lax.fori_loop(0, n // 2, pack, 0)
    send_ref[n // 2 * 256 :, :] = split3(own)


def run_phase(n, phase, plan, left_ops, state, blocks):
    last = phase == phases_of(n) - 1
    slots = left_ops.shape[0]
    terms_per = blocks[0][0].shape[0] // 2 - TRIALS
    kinds = tuple(block[1:] for block in blocks)
    hbm = pl.BlockSpec(memory_space=pltpu.HBM)
    vmem = pl.BlockSpec(memory_space=pltpu.VMEM)
    if last:
        out_shape = (
            jax.ShapeDtypeStruct((n // 2 * 256 + TAIL, 128), jnp.bfloat16),
            jax.ShapeDtypeStruct((n // 2, 256, 128), jnp.float32),
            jax.ShapeDtypeStruct((8, 128), jnp.float32),
            jax.ShapeDtypeStruct((2, 2), jnp.float32),
        )
        out_specs = (vmem,) * 4
    else:
        out_shape = (
            jax.ShapeDtypeStruct((n, 256, 128), jnp.float32),
            jax.ShapeDtypeStruct((24, 128), jnp.float32),
        )
        out_specs = (hbm, vmem)
    share = 4 * slots // (4 * phases_of(n))
    return pl.pallas_call(
        functools.partial(tasks_kernel, n, terms_per, phase, last, kinds),
        out_shape=out_shape,
        in_specs=[pl.BlockSpec(memory_space=pltpu.SMEM), hbm]
        + ([hbm, vmem] if phase else [])
        + [hbm] * len(blocks),
        out_specs=out_specs,
        scratch_shapes=[
            pltpu.VMEM((n, TRIALS, 128, 128), jnp.bfloat16),
            pltpu.VMEM((n * terms_per + 1, 128, 128), jnp.bfloat16),
            pltpu.VMEM((n + 1, 256, 128), jnp.float32),
            pltpu.VMEM((SLOTS_AHEAD, GROUP, 128, 128), jnp.bfloat16),
            pltpu.SemaphoreType.DMA((len(blocks), 4)),
            pltpu.SemaphoreType.DMA((SLOTS_AHEAD,)),
            pltpu.SemaphoreType.DMA,
        ],
        compiler_params=pltpu.CompilerParams(vmem_limit_bytes=n * 640 * 1024 + 10 * 1024 * 1024),
        cost_estimate=pl.CostEstimate(
            flops=share * 8 * 128**3, bytes_accessed=share * 32768 + n * 450000, transcendentals=0
        ),
    )(plan, left_ops, *state, *[block[0] for block in blocks])


def add_kernel(keep_ref, total_ref, received_ref, *outs):
    levels = keep_ref.shape[0] // 2
    send_ref, rest_ref, sum_ref = outs
    total = total_ref[...] + join3(received_ref[2 * levels * 256 :, :])
    sum_ref[...] = total
    y = lax.rem(lax.axis_index("op") // 2, 2)

    def level(z, carry):
        def at(chip):
            rows = pl.ds(pl.multiple_of(chip * 256, 256), 256)
            return keep_ref[chip] + received_ref[rows, :].astype(jnp.float32)

        rest_ref[z] = at(2 * z + y)
        send_ref[pl.ds(pl.multiple_of(z * 256, 256), 256), :] = at(2 * z + 1 - y).astype(jnp.bfloat16)
        return carry

    lax.fori_loop(0, levels, level, 0)
    send_ref[levels * 256 :, :] = split3(total)


def add_core(keep, total, received):
    levels = keep.shape[0] // 2
    return pl.pallas_call(
        add_kernel,
        out_shape=(
            jax.ShapeDtypeStruct((levels * 256 + TAIL, 128), jnp.bfloat16),
            jax.ShapeDtypeStruct((levels, 256, 128), jnp.float32),
            jax.ShapeDtypeStruct((8, 128), jnp.float32),
        ),
    )(keep, total, received)


def level_kernel(rest_ref, total_ref, received_ref, mine_ref, sum_ref, *sends):
    levels = rest_ref.shape[0]
    total = total_ref[...] + join3(received_ref[levels * 256 :, :])
    sum_ref[...] = total
    tail = split3(total)
    here = lax.axis_index("op") // 4
    for r in range(levels):
        z = jnp.bitwise_xor(here, r)
        rows = pl.ds(pl.multiple_of(z * 256, 256), 256)
        value = rest_ref[z] + received_ref[rows, :].astype(jnp.float32)
        if r == 0:
            mine_ref[...] = value
        else:
            sends[r - 1][0:256, :] = value.astype(jnp.bfloat16)
            sends[r - 1][256:, :] = tail


def add_level(rest, total, received):
    levels = rest.shape[0]
    return pl.pallas_call(
        level_kernel,
        out_shape=(jax.ShapeDtypeStruct((256, 128), jnp.float32), jax.ShapeDtypeStruct((8, 128), jnp.float32))
        + (jax.ShapeDtypeStruct((256 + TAIL, 128), jnp.bfloat16),) * (levels - 1),
    )(rest, total, received)


def last_kernel(mine_ref, total_ref, *refs):
    received, (product_ref, projected_ref) = refs[:-2], refs[-2:]
    value, total = mine_ref[...], total_ref[...]
    for ref in received:
        value = value + ref[0:256, :].astype(jnp.float32)
        total = total + join3(ref[256:, :])
    product_ref[0, 0] = value[0:128]
    product_ref[0, 1] = value[128:256]
    projected_ref[...] = total[0:2, 0:2]


def add_all(mine, total, received):
    return pl.pallas_call(
        last_kernel,
        out_shape=(
            jax.ShapeDtypeStruct((1, 2, 128, 128), jnp.float32),
            jax.ShapeDtypeStruct((2, 2), jnp.float32),
        ),
    )(mine, total, *received)


def body(n, trial, left_ops, right_ops, task_list):
    steps = n // 4
    phases = phases_of(n)
    own = (trial[0], right_ops)
    other = [exchange(value, n, 1) for value in own]
    block = jnp.concatenate([*own, *other], axis=0)
    plan = make_plan(task_list.T, n, n * right_ops.shape[0])
    blocks = [(block, 0, False)]
    seen = 0
    state = ()
    phase = 0
    for step in range(1, steps + 1):
        block = ring_step(block, n)
        blocks.append((block, step, False))
        if step < steps:
            blocks.append((exchange(block, n, 1), step, True))
        if step * phases // steps > phase:
            these = [(*entry, b >= seen) for b, entry in enumerate(blocks)]
            state = run_phase(n, phase, plan, left_ops, state, these)
            seen = len(blocks)
            phase += 1
    send, keep, total, correlation = state
    send, rest, total = add_core(keep, total, exchange(send, n, 1))
    mine, total, *sends = add_level(rest, total, exchange(send, n, 2))
    received = [exchange(value, n, 4 * (r + 1)) for r, value in enumerate(sends)]
    product, projected = add_all(mine, total, received)
    return product, correlation, projected


def solution(mesh):
    return jax.shard_map(
        functools.partial(body, mesh.shape["op"]),
        mesh=mesh,
        in_specs=(
            P(("groups", "op"), None, None, None),
            P(("groups", "op"), None, None),
            P(("groups", "op"), None, None),
            P(("groups", "op"), None),
        ),
        out_specs=(P(("groups", "op"), None, None, None), P("groups", None), P("groups", None)),
        check_vma=False,
    )
```

```python
import functools

import jax
import jax.numpy as jnp
from jax import lax
from jax.experimental import pallas as pl
from jax.experimental.pallas import tpu as pltpu
from jax.sharding import PartitionSpec as P

VMEM_LIMIT = 56 * 1024 * 1024
TAIL = 32
TRIALS = 2
CHUNK = 16
PAIRS = 8
AHEAD = 3


def exchange(value, n, mask):
    return lax.ppermute(value, "op", [(i, i ^ mask) for i in range(n)])


def chip_at(place, chips):
    return 2 * place if place < chips // 2 else 2 * (chips - place) - 1


def ring_step(value, n):
    chips = n // 2
    order = [chip_at(place, chips) for place in range(chips)]
    pairs = []
    for place, chip in enumerate(order):
        pairs.append((2 * chip, 2 * order[(place + 1) % chips]))
        pairs.append((2 * chip + 1, 2 * order[(place - 1) % chips] + 1))
    return lax.ppermute(value, "op", pairs)


def owner_of(step, swapped, half, n):
    chips = n // 2
    me = lax.axis_index("op")
    chip, core = me // 2, lax.rem(me, 2)
    odd = lax.rem(chip, 2)
    mine = jnp.where(odd == 0, chip // 2, chips - 1 - chip // 2)
    line = 1 - core if swapped else core
    place = lax.rem(mine + (2 * line - 1) * step + 2 * chips, chips)
    there = jnp.where(place < chips // 2, 2 * place, 2 * (chips - place) - 1)
    return 2 * there + (line if half == 0 else 1 - line)


def split3(value):
    high = value.astype(jnp.bfloat16)
    rest = value - high.astype(jnp.float32)
    middle = rest.astype(jnp.bfloat16)
    low = (rest - middle.astype(jnp.float32)).astype(jnp.bfloat16)
    zero = jnp.zeros_like(value)
    return jnp.concatenate(
        [high.astype(jnp.float32), middle.astype(jnp.float32), low.astype(jnp.float32), zero], axis=0
    ).astype(jnp.bfloat16)


def join3(tail):
    wide = tail.astype(jnp.float32)
    return wide[0:8] + wide[8:16] + wide[16:24]


def matrix_of(values):
    rows = lax.broadcasted_iota(jnp.int32, (8, 128), 0)
    lanes = lax.broadcasted_iota(jnp.int32, (8, 128), 1)
    total = jnp.zeros((8, 128), jnp.float32)
    for (i, j), value in values.items():
        total = total + jnp.where((rows == i) & (lanes == j), value, 0.0)
    return total


def fold(value):
    return value.reshape(16, 8, 128).sum(axis=0)


def run_of(slots, n):
    return 4 if slots >= 8 * n else 2


def plan_kernel(n, terms, tasks_ref, plan_ref):
    slots = tasks_ref.shape[1]
    places = plan_ref.shape[1]
    rows = tasks_ref[...].astype(jnp.float32)
    source, target, term, live = rows[0:1], rows[1:2], rows[2:3], rows[3:4]
    lane = lax.broadcasted_iota(jnp.int32, (1, slots), 1).astype(jnp.float32)
    number = lax.broadcasted_iota(jnp.int32, (1, places), 1).astype(jnp.float32)
    at = lax.broadcasted_iota(jnp.int32, (slots, places), 1).astype(jnp.float32)
    index = lax.broadcasted_iota(jnp.int32, (n, slots), 0).astype(jnp.float32)

    def column(*values):
        pad = [jnp.zeros((8 - len(values), slots), jnp.float32)]
        return jnp.transpose(jnp.concatenate(list(values) + pad, axis=0))

    def sort(sector, unit):
        key = jnp.where(live > 0, sector, float(n))
        columns = column(key, lane)
        earlier = jnp.where((columns[:, 0:1] == key) & (columns[:, 1:2] < lane), 1.0, 0.0)
        count = jnp.sum(jnp.where(index == key, 1.0, 0.0), axis=1, keepdims=True)
        padded = jnp.ceil(count / unit) * unit
        before = jnp.sum(jnp.where(index < key, padded, 0.0), axis=0, keepdims=True)
        place = before + jnp.sum(earlier, axis=0, keepdims=True)
        return jnp.where(live > 0, place, -1.0), jnp.sum(padded, axis=0, keepdims=True)

    by_source, source_places = sort(source, float(run_of(slots, n)))
    by_target, target_places = sort(target, 2.0)
    columns = column(by_source, by_target, lane, source, term, target)

    def picker(places_column):
        hit = places_column == at

        def pick(values, other):
            found = jnp.sum(jnp.where(hit, values - other, 0.0), axis=0, keepdims=True)
            return (found + other).astype(jnp.int32)

        return pick

    pick = picker(columns[:, 0:1])
    plan_ref[0:1] = pick(columns[:, 2:3], 0.0)
    plan_ref[1:2] = pick(columns[:, 3:4], 0.0)
    pick = picker(columns[:, 1:2])
    plan_ref[2:3] = pick(columns[:, 0:1], 0.0)
    plan_ref[3:4] = pick(columns[:, 4:5], float(terms))
    plan_ref[4:5] = pick(columns[:, 5:6], float(n))
    turns = jnp.where(
        number == 0, jnp.ceil(source_places / CHUNK), jnp.ceil(target_places / (2 * PAIRS))
    )
    plan_ref[5:6] = turns.astype(jnp.int32)
    plan_ref[6:8] = jnp.zeros((2, places), jnp.int32)


def make_plan(tasks, n, terms):
    slots = tasks.shape[1]
    most = slots + min(slots, n) * (run_of(slots, n) - 1) + CHUNK
    return pl.pallas_call(
        functools.partial(plan_kernel, n, terms),
        out_shape=jax.ShapeDtypeStruct((8, -(-most // 128) * 128), jnp.int32),
    )(tasks)


def tasks_kernel(n, terms_per, kinds, plan_ref, left_ref, *refs):
    blocks, refs = refs[: len(kinds)], refs[len(kinds) :]
    send_ref, keep_ref, own_ref, trial, right, acc, left, halves, block_sem, left_sem = refs
    per = TRIALS + terms_per
    run = run_of(left_ref.shape[0], n)
    source_turns, target_turns = plan_ref[5, 0], plan_ref[5, 1]

    def block_copies(b, which):
        step, swapped = kinds[b]
        copies = []
        for half in range(2):
            owner = owner_of(step, swapped, half, n)
            if which == 0:
                source, to = blocks[b].at[pl.ds(half * per, TRIALS)], trial.at[owner]
            else:
                source = blocks[b].at[pl.ds(half * per + TRIALS, terms_per)]
                to = right.at[pl.ds(owner * terms_per, terms_per)]
            copies.append(pltpu.make_async_copy(source, to, block_sem.at[b, 2 * half + which]))
        return copies

    def fetch(turn):
        at = lax.rem(turn, AHEAD)
        for u in range(CHUNK):
            slot = plan_ref[0, turn * CHUNK + u]
            pltpu.make_async_copy(left_ref.at[slot], left.at[at, u], left_sem.at[at]).start()

    for b in range(len(kinds)):
        for copy in block_copies(b, 0):
            copy.start()
    for turn in range(AHEAD - 1):

        @pl.when(turn < source_turns)
        def _():
            fetch(turn)

    for b in range(len(kinds)):
        for copy in block_copies(b, 1):
            copy.start()
    right[n * terms_per] = jnp.zeros((128, 128), jnp.bfloat16)

    def clear(s, carry):
        acc[s] = jnp.zeros((256, 128), jnp.float32)
        return carry

    lax.fori_loop(0, n, clear, 0)
    for b in range(len(kinds)):
        for copy in block_copies(b, 0):
            copy.wait()

    def source_turn(turn, carry):
        @pl.when(turn + AHEAD - 1 < source_turns)
        def _():
            fetch(turn + AHEAD - 1)

        at = lax.rem(turn, AHEAD)
        pltpu.make_async_copy(left_ref.at[pl.ds(0, CHUNK)], left.at[at], left_sem.at[at]).wait()
        first = turn * CHUNK
        for r in range(CHUNK // run):
            source = plan_ref[1, first + r * run]
            vectors = jnp.concatenate([trial[source, 0], trial[source, 1]], axis=1)
            rows = left[at, r * run : (r + 1) * run].reshape(run * 128, 128)
            half = jnp.dot(rows, vectors, preferred_element_type=jnp.float32).astype(jnp.bfloat16)
            for u in range(run):
                halves[first + r * run + u, 0] = half[u * 128 : (u + 1) * 128, :128]
                halves[first + r * run + u, 1] = half[u * 128 : (u + 1) * 128, 128:]
        return carry

    lax.fori_loop(0, source_turns, source_turn, 0)
    for b in range(len(kinds)):
        for copy in block_copies(b, 1):
            copy.wait()

    def target_turn(turn, carry):
        first = turn * 2 * PAIRS
        for u in range(0, 2 * PAIRS, 2):
            place = first + u
            one, two = plan_ref[2, place], plan_ref[2, place + 1]
            pair = jnp.concatenate(
                [
                    jnp.concatenate([halves[one, 0], halves[two, 0]], axis=1),
                    jnp.concatenate([halves[one, 1], halves[two, 1]], axis=1),
                ],
                axis=0,
            )
            rights = jnp.concatenate([right[plan_ref[3, place]], right[plan_ref[3, place + 1]]], axis=1)
            term = lax.dot_general(
                pair, rights, (((1,), (1,)), ((), ())), preferred_element_type=jnp.float32
            )
            target = plan_ref[4, place]
            acc[target] = acc[target] + term
        return carry

    lax.fori_loop(0, target_turns, target_turn, 0)

    def dots(s, carry):
        t0 = trial[s, 0].astype(jnp.float32)
        t1 = trial[s, 1].astype(jnp.float32)
        a0 = acc[s, 0:128, :]
        a1 = acc[s, 128:256, :]
        p00, p01, p10, p11 = carry
        return p00 + fold(t0 * a0), p01 + fold(t0 * a1), p10 + fold(t1 * a0), p11 + fold(t1 * a1)

    zero = jnp.zeros((8, 128), jnp.float32)
    p00, p01, p10, p11 = [jnp.sum(x) for x in lax.fori_loop(0, n, dots, (zero,) * 4)]
    own = matrix_of({(0, 0): p00, (0, 1): p01, (1, 0): p10, (1, 1): p11})
    own_ref[...] = own
    me = lax.axis_index("op")

    def pack(j, carry):
        mine = jnp.bitwise_xor(me, 2 * j)
        keep_ref[j] = acc[mine]
        send_ref[pl.ds(pl.multiple_of(j * 256, 256), 256), :] = acc[jnp.bitwise_xor(mine, 1)].astype(jnp.bfloat16)
        return carry

    lax.fori_loop(0, n // 2, pack, 0)
    send_ref[n // 2 * 256 :, :] = split3(own)


def run_tasks(n, plan, left_ops, blocks):
    slots = left_ops.shape[0]
    places = plan.shape[1]
    terms_per = blocks[0][0].shape[0] // 2 - TRIALS
    kinds = tuple(block[1:] for block in blocks)
    hbm = pl.BlockSpec(memory_space=pltpu.HBM)
    return pl.pallas_call(
        functools.partial(tasks_kernel, n, terms_per, kinds),
        out_shape=(
            jax.ShapeDtypeStruct((n // 2 * 256 + TAIL, 128), jnp.bfloat16),
            jax.ShapeDtypeStruct((n // 2, 256, 128), jnp.float32),
            jax.ShapeDtypeStruct((8, 128), jnp.float32),
        ),
        in_specs=[pl.BlockSpec(memory_space=pltpu.SMEM), hbm] + [hbm] * len(blocks),
        scratch_shapes=[
            pltpu.VMEM((n, TRIALS, 128, 128), jnp.bfloat16),
            pltpu.VMEM((n * terms_per + 1, 128, 128), jnp.bfloat16),
            pltpu.VMEM((n + 1, 256, 128), jnp.float32),
            pltpu.VMEM((AHEAD, CHUNK, 128, 128), jnp.bfloat16),
            pltpu.VMEM((places, 2, 128, 128), jnp.bfloat16),
            pltpu.SemaphoreType.DMA((len(blocks), 4)),
            pltpu.SemaphoreType.DMA((AHEAD,)),
        ],
        compiler_params=pltpu.CompilerParams(vmem_limit_bytes=VMEM_LIMIT),
        cost_estimate=pl.CostEstimate(
            flops=slots * 8 * 128**3, bytes_accessed=slots * 32768 + n * 450000, transcendentals=0
        ),
    )(plan, left_ops, *[block[0] for block in blocks])


def corr_kernel(spans, *refs):
    blocks, corr_ref = refs[:-1], refs[-1]
    total = [jnp.zeros((8, 128), jnp.float32)] * 3
    for ref, span in zip(blocks, spans):
        for start in (0, span):
            t0, t1 = ref[start].astype(jnp.float32), ref[start + 1].astype(jnp.float32)
            total = [total[0] + fold(t0 * t0), total[1] + fold(t0 * t1), total[2] + fold(t1 * t1)]
    c00, c01, c11 = [jnp.sum(x) for x in total]
    corr_ref[...] = matrix_of({(0, 0): c00, (0, 1): c01, (1, 0): c01, (1, 1): c11})[0:2, 0:2]


def correlate(blocks):
    return pl.pallas_call(
        functools.partial(corr_kernel, [block.shape[0] // 2 for block in blocks]),
        out_shape=jax.ShapeDtypeStruct((2, 2), jnp.float32),
        compiler_params=pltpu.CompilerParams(vmem_limit_bytes=VMEM_LIMIT),
    )(*blocks)


def chip_kernel(chips, keep_ref, own_ref, received_ref, mine_ref, total_ref, *sends):
    total = own_ref[...] + join3(received_ref[chips * 256 :, :])
    total_ref[...] = total
    tail = split3(total)
    for j in range(chips):
        value = keep_ref[j] + received_ref[j * 256 : (j + 1) * 256, :].astype(jnp.float32)
        if j == 0:
            mine_ref[...] = value
        else:
            sends[j - 1][0:256, :] = value.astype(jnp.bfloat16)
            sends[j - 1][256:, :] = tail


def add_chip(keep, own, received):
    chips = keep.shape[0]
    return pl.pallas_call(
        functools.partial(chip_kernel, chips),
        out_shape=(jax.ShapeDtypeStruct((256, 128), jnp.float32), jax.ShapeDtypeStruct((8, 128), jnp.float32))
        + (jax.ShapeDtypeStruct((256 + TAIL, 128), jnp.bfloat16),) * (chips - 1),
        compiler_params=pltpu.CompilerParams(vmem_limit_bytes=VMEM_LIMIT),
    )(keep, own, received)


def last_kernel(mine_ref, total_ref, *refs):
    received, (product_ref, projected_ref) = refs[:-2], refs[-2:]
    value, total = mine_ref[...], total_ref[...]
    for ref in received:
        value = value + ref[0:256, :].astype(jnp.float32)
        total = total + join3(ref[256:, :])
    product_ref[0, 0] = value[0:128]
    product_ref[0, 1] = value[128:256]
    projected_ref[...] = total[0:2, 0:2]


def add_all(mine, total, received):
    return pl.pallas_call(
        last_kernel,
        out_shape=(
            jax.ShapeDtypeStruct((1, 2, 128, 128), jnp.float32),
            jax.ShapeDtypeStruct((2, 2), jnp.float32),
        ),
        compiler_params=pltpu.CompilerParams(vmem_limit_bytes=VMEM_LIMIT),
    )(mine, total, *received)


def body(n, trial, left_ops, right_ops, task_list):
    steps = n // 4
    own = (trial[0], right_ops)
    other = [exchange(value, n, 1) for value in own]
    block = jnp.concatenate([*own, *other], axis=0)
    plan = make_plan(task_list.T, n, n * right_ops.shape[0])
    blocks = [(block, 0, False)]
    for step in range(1, steps + 1):
        block = ring_step(block, n)
        blocks.append((block, step, False))
        if step < steps:
            blocks.append((exchange(block, n, 1), step, True))
    send, keep, own = run_tasks(n, plan, left_ops, blocks)
    send, arrays = lax.optimization_barrier((send, [block[0] for block in blocks]))
    correlation = correlate(arrays)
    mine, total, *sends = add_chip(keep, own, exchange(send, n, 1))
    received = [exchange(value, n, 2 * (j + 1)) for j, value in enumerate(sends)]
    product, projected = add_all(mine, total, received)
    return product, correlation, projected


def solution(mesh):
    return jax.shard_map(
        functools.partial(body, mesh.shape["op"]),
        mesh=mesh,
        in_specs=(
            P(("groups", "op"), None, None, None),
            P(("groups", "op"), None, None),
            P(("groups", "op"), None, None),
            P(("groups", "op"), None),
        ),
        out_specs=(P(("groups", "op"), None, None, None), P("groups", None), P("groups", None)),
        check_vma=False,
    )
```

```python
import functools

import jax
import jax.numpy as jnp
from jax import lax
from jax.experimental import pallas as pl
from jax.experimental.pallas import tpu as pltpu
from jax.sharding import PartitionSpec as P

MIB = 1024 * 1024
TAIL = 32
TRIALS = 2
CHUNK = 32
PAIRS = 16
AHEAD = 3


def exchange(value, n, mask):
    return lax.ppermute(value, "op", [(i, i ^ mask) for i in range(n)])


def chip_at(place, chips):
    return 2 * place if place < chips // 2 else 2 * (chips - place) - 1


def ring_step(value, n):
    chips = n // 2
    order = [chip_at(place, chips) for place in range(chips)]
    pairs = []
    for place, chip in enumerate(order):
        pairs.append((2 * chip, 2 * order[(place + 1) % chips]))
        pairs.append((2 * chip + 1, 2 * order[(place - 1) % chips] + 1))
    return lax.ppermute(value, "op", pairs)


def owner_of(step, swapped, half, n):
    chips = n // 2
    me = lax.axis_index("op")
    chip, core = me // 2, lax.rem(me, 2)
    odd = lax.rem(chip, 2)
    mine = jnp.where(odd == 0, chip // 2, chips - 1 - chip // 2)
    line = 1 - core if swapped else core
    place = lax.rem(mine + (2 * line - 1) * step + 2 * chips, chips)
    there = jnp.where(place < chips // 2, 2 * place, 2 * (chips - place) - 1)
    return 2 * there + (line if half == 0 else 1 - line)


def split3(value):
    high = value.astype(jnp.bfloat16)
    rest = value - high.astype(jnp.float32)
    middle = rest.astype(jnp.bfloat16)
    low = (rest - middle.astype(jnp.float32)).astype(jnp.bfloat16)
    zero = jnp.zeros_like(value)
    return jnp.concatenate(
        [high.astype(jnp.float32), middle.astype(jnp.float32), low.astype(jnp.float32), zero], axis=0
    ).astype(jnp.bfloat16)


def join3(tail):
    wide = tail.astype(jnp.float32)
    return wide[0:8] + wide[8:16] + wide[16:24]


def matrix_of(values):
    rows = lax.broadcasted_iota(jnp.int32, (8, 128), 0)
    lanes = lax.broadcasted_iota(jnp.int32, (8, 128), 1)
    total = jnp.zeros((8, 128), jnp.float32)
    for (i, j), value in values.items():
        total = total + jnp.where((rows == i) & (lanes == j), value, 0.0)
    return total


def fold(value):
    return value.reshape(16, 8, 128).sum(axis=0)


def run_of(slots, n):
    return 4 if slots >= 8 * n else 2


def plan_kernel(n, terms, tasks_ref, plan_ref):
    slots = tasks_ref.shape[1]
    places = plan_ref.shape[1]
    rows = tasks_ref[...].astype(jnp.float32)
    source, target, term, live = rows[0:1], rows[1:2], rows[2:3], rows[3:4]
    lane = lax.broadcasted_iota(jnp.int32, (1, slots), 1).astype(jnp.float32)
    number = lax.broadcasted_iota(jnp.int32, (1, places), 1).astype(jnp.float32)
    at = lax.broadcasted_iota(jnp.int32, (slots, places), 1).astype(jnp.float32)
    index = lax.broadcasted_iota(jnp.int32, (n, slots), 0).astype(jnp.float32)

    def column(*values):
        pad = [jnp.zeros((8 - len(values), slots), jnp.float32)]
        return jnp.transpose(jnp.concatenate(list(values) + pad, axis=0))

    def sort(sector, unit):
        key = jnp.where(live > 0, sector, float(n))
        columns = column(key, lane)
        earlier = jnp.where((columns[:, 0:1] == key) & (columns[:, 1:2] < lane), 1.0, 0.0)
        count = jnp.sum(jnp.where(index == key, 1.0, 0.0), axis=1, keepdims=True)
        padded = jnp.ceil(count / unit) * unit
        before = jnp.sum(jnp.where(index < key, padded, 0.0), axis=0, keepdims=True)
        place = before + jnp.sum(earlier, axis=0, keepdims=True)
        return jnp.where(live > 0, place, -1.0), jnp.sum(padded, axis=0, keepdims=True)

    by_source, source_places = sort(source, float(run_of(slots, n)))
    by_target, target_places = sort(target, 2.0)
    columns = column(by_source, by_target, lane, source, term, target)

    def picker(places_column):
        hit = places_column == at

        def pick(values, other):
            found = jnp.sum(jnp.where(hit, values - other, 0.0), axis=0, keepdims=True)
            return (found + other).astype(jnp.int32)

        return pick

    pick = picker(columns[:, 0:1])
    plan_ref[0:1] = pick(columns[:, 2:3], 0.0)
    plan_ref[1:2] = pick(columns[:, 3:4], 0.0)
    pick = picker(columns[:, 1:2])
    plan_ref[2:3] = pick(columns[:, 0:1], 0.0)
    plan_ref[3:4] = pick(columns[:, 4:5], float(terms))
    plan_ref[4:5] = pick(columns[:, 5:6], float(n))
    turns = jnp.where(
        number == 0, jnp.ceil(source_places / CHUNK), jnp.ceil(target_places / (2 * PAIRS))
    )
    plan_ref[5:6] = turns.astype(jnp.int32)
    plan_ref[6:8] = jnp.zeros((2, places), jnp.int32)


def make_plan(tasks, n, terms):
    slots = tasks.shape[1]
    most = slots + min(slots, n) * (run_of(slots, n) - 1) + CHUNK
    return pl.pallas_call(
        functools.partial(plan_kernel, n, terms),
        out_shape=jax.ShapeDtypeStruct((8, -(-most // 128) * 128), jnp.int32),
    )(tasks)


def tasks_kernel(n, terms_per, kinds, plan_ref, left_ref, *refs):
    blocks, refs = refs[: len(kinds)], refs[len(kinds) :]
    send_ref, keep_ref, own_ref, trial, right, acc, left, halves, block_sem, left_sem = refs
    per = TRIALS + terms_per
    run = run_of(left_ref.shape[0], n)
    source_turns, target_turns = plan_ref[5, 0], plan_ref[5, 1]

    def block_copies(b, which):
        step, swapped = kinds[b]
        copies = []
        for half in range(2):
            owner = owner_of(step, swapped, half, n)
            if which == 0:
                source, to = blocks[b].at[pl.ds(half * per, TRIALS)], trial.at[owner]
            else:
                source = blocks[b].at[pl.ds(half * per + TRIALS, terms_per)]
                to = right.at[pl.ds(owner * terms_per, terms_per)]
            copies.append(pltpu.make_async_copy(source, to, block_sem.at[b, 2 * half + which]))
        return copies

    def fetch(turn):
        at = lax.rem(turn, AHEAD)
        for u in range(CHUNK):
            slot = plan_ref[0, turn * CHUNK + u]
            pltpu.make_async_copy(left_ref.at[slot], left.at[at, u], left_sem.at[at]).start()

    for b in range(len(kinds)):
        for copy in block_copies(b, 0):
            copy.start()
    for turn in range(AHEAD - 1):

        @pl.when(turn < source_turns)
        def _():
            fetch(turn)

    for b in range(len(kinds)):
        for copy in block_copies(b, 1):
            copy.start()
    right[n * terms_per] = jnp.zeros((128, 128), jnp.bfloat16)

    def clear(s, carry):
        acc[s] = jnp.zeros((256, 128), jnp.float32)
        return carry

    lax.fori_loop(0, n, clear, 0)
    for b in range(len(kinds)):
        for copy in block_copies(b, 0):
            copy.wait()

    def source_turn(turn, carry):
        @pl.when(turn + AHEAD - 1 < source_turns)
        def _():
            fetch(turn + AHEAD - 1)

        at = lax.rem(turn, AHEAD)
        pltpu.make_async_copy(left_ref.at[pl.ds(0, CHUNK)], left.at[at], left_sem.at[at]).wait()
        first = turn * CHUNK
        for r in range(CHUNK // run):
            source = plan_ref[1, first + r * run]
            vectors = jnp.concatenate([trial[source, 0], trial[source, 1]], axis=1)
            rows = left[at, r * run : (r + 1) * run].reshape(run * 128, 128)
            half = jnp.dot(rows, vectors, preferred_element_type=jnp.float32).astype(jnp.bfloat16)
            for u in range(run):
                halves[first + r * run + u, 0] = half[u * 128 : (u + 1) * 128, :128]
                halves[first + r * run + u, 1] = half[u * 128 : (u + 1) * 128, 128:]
        return carry

    lax.fori_loop(0, source_turns, source_turn, 0)
    for b in range(len(kinds)):
        for copy in block_copies(b, 1):
            copy.wait()

    def target_turn(turn, carry):
        first = turn * 2 * PAIRS
        for u in range(0, 2 * PAIRS, 2):
            place = first + u
            one, two = plan_ref[2, place], plan_ref[2, place + 1]
            pair = jnp.concatenate(
                [
                    jnp.concatenate([halves[one, 0], halves[two, 0]], axis=1),
                    jnp.concatenate([halves[one, 1], halves[two, 1]], axis=1),
                ],
                axis=0,
            )
            rights = jnp.concatenate([right[plan_ref[3, place]], right[plan_ref[3, place + 1]]], axis=0)
            term = lax.dot_general(
                pair, rights, (((1,), (0,)), ((), ())), preferred_element_type=jnp.float32
            )
            target = plan_ref[4, place]
            acc[target] = acc[target] + term
        return carry

    lax.fori_loop(0, target_turns, target_turn, 0)

    def dots(s, carry):
        t0 = trial[s, 0].astype(jnp.float32)
        t1 = trial[s, 1].astype(jnp.float32)
        a0 = acc[s, 0:128, :]
        a1 = acc[s, 128:256, :]
        p00, p01, p10, p11 = carry
        return p00 + fold(t0 * a0), p01 + fold(t0 * a1), p10 + fold(t1 * a0), p11 + fold(t1 * a1)

    zero = jnp.zeros((8, 128), jnp.float32)
    p00, p01, p10, p11 = [jnp.sum(x) for x in lax.fori_loop(0, n, dots, (zero,) * 4)]
    own = matrix_of({(0, 0): p00, (0, 1): p01, (1, 0): p10, (1, 1): p11})
    own_ref[...] = own
    me = lax.axis_index("op")

    def pack(j, carry):
        mine = jnp.bitwise_xor(me, 2 * j)
        keep_ref[j] = acc[mine]
        send_ref[pl.ds(pl.multiple_of(j * 256, 256), 256), :] = acc[jnp.bitwise_xor(mine, 1)].astype(jnp.bfloat16)
        return carry

    lax.fori_loop(0, n // 2, pack, 0)
    send_ref[n // 2 * 256 :, :] = split3(own)


def run_tasks(n, plan, left_ops, blocks):
    slots = left_ops.shape[0]
    places = plan.shape[1]
    terms_per = blocks[0][0].shape[0] // 2 - TRIALS
    kinds = tuple(block[1:] for block in blocks)
    hbm = pl.BlockSpec(memory_space=pltpu.HBM)
    return pl.pallas_call(
        functools.partial(tasks_kernel, n, terms_per, kinds),
        out_shape=(
            jax.ShapeDtypeStruct((n // 2 * 256 + TAIL, 128), jnp.bfloat16),
            jax.ShapeDtypeStruct((n // 2, 256, 128), jnp.float32),
            jax.ShapeDtypeStruct((8, 128), jnp.float32),
        ),
        in_specs=[pl.BlockSpec(memory_space=pltpu.SMEM), hbm] + [hbm] * len(blocks),
        scratch_shapes=[
            pltpu.VMEM((n, TRIALS, 128, 128), jnp.bfloat16),
            pltpu.VMEM((n * terms_per + 1, 128, 128), jnp.bfloat16),
            pltpu.VMEM((n + 1, 256, 128), jnp.float32),
            pltpu.VMEM((AHEAD, CHUNK, 128, 128), jnp.bfloat16),
            pltpu.VMEM((places, 2, 128, 128), jnp.bfloat16),
            pltpu.SemaphoreType.DMA((len(blocks), 4)),
            pltpu.SemaphoreType.DMA((AHEAD,)),
        ],
        compiler_params=pltpu.CompilerParams(vmem_limit_bytes=(53 if n <= 16 else 57) * MIB),
        cost_estimate=pl.CostEstimate(
            flops=slots * 8 * 128**3, bytes_accessed=slots * 32768 + n * 450000, transcendentals=0
        ),
    )(plan, left_ops, *[block[0] for block in blocks])


def corr_kernel(spans, *refs):
    blocks, corr_ref = refs[:-1], refs[-1]
    total = [jnp.zeros((8, 128), jnp.float32)] * 3
    for ref, span in zip(blocks, spans):
        for start in (0, span):
            t0, t1 = ref[start].astype(jnp.float32), ref[start + 1].astype(jnp.float32)
            total = [total[0] + fold(t0 * t0), total[1] + fold(t0 * t1), total[2] + fold(t1 * t1)]
    c00, c01, c11 = [jnp.sum(x) for x in total]
    corr_ref[...] = matrix_of({(0, 0): c00, (0, 1): c01, (1, 0): c01, (1, 1): c11})[0:2, 0:2]


def correlate(blocks):
    return pl.pallas_call(
        functools.partial(corr_kernel, [block.shape[0] // 2 for block in blocks]),
        out_shape=jax.ShapeDtypeStruct((2, 2), jnp.float32),
        compiler_params=pltpu.CompilerParams(vmem_limit_bytes=16 * MIB),
    )(*blocks)


def chip_kernel(chips, keep_ref, own_ref, received_ref, mine_ref, total_ref, *sends):
    total = own_ref[...] + join3(received_ref[chips * 256 :, :])
    total_ref[...] = total
    tail = split3(total)
    for j in range(chips):
        value = keep_ref[j] + received_ref[j * 256 : (j + 1) * 256, :].astype(jnp.float32)
        if j == 0:
            mine_ref[...] = value
        else:
            sends[j - 1][0:256, :] = value.astype(jnp.bfloat16)
            sends[j - 1][256:, :] = tail


def add_chip(keep, own, received):
    chips = keep.shape[0]
    return pl.pallas_call(
        functools.partial(chip_kernel, chips),
        out_shape=(jax.ShapeDtypeStruct((256, 128), jnp.float32), jax.ShapeDtypeStruct((8, 128), jnp.float32))
        + (jax.ShapeDtypeStruct((256 + TAIL, 128), jnp.bfloat16),) * (chips - 1),
        compiler_params=pltpu.CompilerParams(vmem_limit_bytes=16 * MIB),
    )(keep, own, received)


def last_kernel(mine_ref, total_ref, *refs):
    received, (product_ref, projected_ref) = refs[:-2], refs[-2:]
    value, total = mine_ref[...], total_ref[...]
    for ref in received:
        value = value + ref[0:256, :].astype(jnp.float32)
        total = total + join3(ref[256:, :])
    product_ref[0, 0] = value[0:128]
    product_ref[0, 1] = value[128:256]
    projected_ref[...] = total[0:2, 0:2]


def add_all(mine, total, received):
    return pl.pallas_call(
        last_kernel,
        out_shape=(
            jax.ShapeDtypeStruct((1, 2, 128, 128), jnp.float32),
            jax.ShapeDtypeStruct((2, 2), jnp.float32),
        ),
        compiler_params=pltpu.CompilerParams(vmem_limit_bytes=16 * MIB),
    )(mine, total, *received)


def body(n, trial, left_ops, right_ops, task_list):
    steps = n // 4
    own = (trial[0], right_ops.swapaxes(1, 2))
    other = [exchange(value, n, 1) for value in own]
    block = jnp.concatenate([*own, *other], axis=0)
    plan = make_plan(task_list.T, n, n * right_ops.shape[0])
    blocks = [(block, 0, False)]
    for step in range(1, steps + 1):
        block = ring_step(block, n)
        blocks.append((block, step, False))
        if step < steps:
            blocks.append((exchange(block, n, 1), step, True))
    send, keep, own = run_tasks(n, plan, left_ops, blocks)
    send, arrays = lax.optimization_barrier((send, [block[0] for block in blocks]))
    correlation = correlate(arrays)
    mine, total, *sends = add_chip(keep, own, exchange(send, n, 1))
    received = [exchange(value, n, 2 * (j + 1)) for j, value in enumerate(sends)]
    product, projected = add_all(mine, total, received)
    return product, correlation, projected


def solution(mesh):
    return jax.shard_map(
        functools.partial(body, mesh.shape["op"]),
        mesh=mesh,
        in_specs=(
            P(("groups", "op"), None, None, None),
            P(("groups", "op"), None, None),
            P(("groups", "op"), None, None),
            P(("groups", "op"), None),
        ),
        out_specs=(P(("groups", "op"), None, None, None), P("groups", None), P("groups", None)),
        check_vma=False,
    )
```

```python
import functools

import jax
import jax.numpy as jnp
from jax import lax
from jax.experimental import pallas as pl
from jax.experimental.pallas import tpu as pltpu
from jax.sharding import PartitionSpec as P

MIB = 1024 * 1024
AHEAD = 3
TAIL = 32
TRIALS = 2
CHUNK = 32
PAIRS = 16


def exchange(value, n, mask):
    return lax.ppermute(value, "op", [(i, i ^ mask) for i in range(n)])


def chip_at(place, chips):
    return 2 * place if place < chips // 2 else 2 * (chips - place) - 1


def ring_step(value, n):
    chips = n // 2
    order = [chip_at(place, chips) for place in range(chips)]
    pairs = []
    for place, chip in enumerate(order):
        pairs.append((2 * chip, 2 * order[(place + 1) % chips]))
        pairs.append((2 * chip + 1, 2 * order[(place - 1) % chips] + 1))
    return lax.ppermute(value, "op", pairs)


def owner_of(step, swapped, half, n):
    chips = n // 2
    me = lax.axis_index("op")
    chip, core = me // 2, lax.rem(me, 2)
    odd = lax.rem(chip, 2)
    mine = jnp.where(odd == 0, chip // 2, chips - 1 - chip // 2)
    line = 1 - core if swapped else core
    place = lax.rem(mine + (2 * line - 1) * step + 2 * chips, chips)
    there = jnp.where(place < chips // 2, 2 * place, 2 * (chips - place) - 1)
    return 2 * there + (line if half == 0 else 1 - line)


def split3(value):
    high = value.astype(jnp.bfloat16)
    rest = value - high.astype(jnp.float32)
    middle = rest.astype(jnp.bfloat16)
    low = (rest - middle.astype(jnp.float32)).astype(jnp.bfloat16)
    zero = jnp.zeros_like(value)
    return jnp.concatenate(
        [high.astype(jnp.float32), middle.astype(jnp.float32), low.astype(jnp.float32), zero], axis=0
    ).astype(jnp.bfloat16)


def join3(tail):
    wide = tail.astype(jnp.float32)
    return wide[0:8] + wide[8:16] + wide[16:24]


def matrix_of(values):
    rows = lax.broadcasted_iota(jnp.int32, (8, 128), 0)
    lanes = lax.broadcasted_iota(jnp.int32, (8, 128), 1)
    total = jnp.zeros((8, 128), jnp.float32)
    for (i, j), value in values.items():
        total = total + jnp.where((rows == i) & (lanes == j), value, 0.0)
    return total


def fold(value):
    return value.reshape(16, 8, 128).sum(axis=0)


def fits(n):
    return n <= 16


def run_of(slots, n):
    return 4 if slots >= 8 * n else 2


def plan_kernel(n, terms, tasks_ref, *refs):
    plan_ref = refs[-1]
    slots = tasks_ref.shape[1]
    places = plan_ref.shape[1]
    rows = tasks_ref[...].astype(jnp.float32)
    source, target, term, live = rows[0:1], rows[1:2], rows[2:3], rows[3:4]
    lane = lax.broadcasted_iota(jnp.int32, (1, slots), 1).astype(jnp.float32)
    number = lax.broadcasted_iota(jnp.int32, (1, places), 1).astype(jnp.float32)
    at = lax.broadcasted_iota(jnp.int32, (slots, places), 1).astype(jnp.float32)
    index = lax.broadcasted_iota(jnp.int32, (n, slots), 0).astype(jnp.float32)

    def column(*values):
        pad = [jnp.zeros((8 - len(values), slots), jnp.float32)]
        return jnp.transpose(jnp.concatenate(list(values) + pad, axis=0))

    def sort(sector, unit):
        key = jnp.where(live > 0, sector, float(n))
        columns = column(key, lane)
        earlier = jnp.where((columns[:, 0:1] == key) & (columns[:, 1:2] < lane), 1.0, 0.0)
        count = jnp.sum(jnp.where(index == key, 1.0, 0.0), axis=1, keepdims=True)
        padded = jnp.ceil(count / unit) * unit
        before = jnp.sum(jnp.where(index < key, padded, 0.0), axis=0, keepdims=True)
        place = before + jnp.sum(earlier, axis=0, keepdims=True)
        return jnp.where(live > 0, place, -1.0), jnp.sum(padded, axis=0, keepdims=True)

    by_source, source_places = sort(source, float(run_of(slots, n)))
    by_target, target_places = sort(target, 2.0)
    columns = column(by_source, by_target, lane, source, term, target)

    def picker(places_column):
        hit = places_column == at

        def pick(values, other):
            found = jnp.sum(jnp.where(hit, values - other, 0.0), axis=0, keepdims=True)
            return (found + other).astype(jnp.int32)

        return pick

    pick = picker(columns[:, 0:1])
    plan_ref[0:1] = pick(columns[:, 2:3], 0.0)
    plan_ref[1:2] = pick(columns[:, 3:4], 0.0)
    pick = picker(columns[:, 1:2])
    plan_ref[2:3] = pick(columns[:, 0:1], 0.0)
    plan_ref[3:4] = pick(columns[:, 4:5], float(terms))
    plan_ref[4:5] = pick(columns[:, 5:6], float(n))
    turns = jnp.where(
        number == 0, jnp.ceil(source_places / CHUNK), jnp.ceil(target_places / (2 * PAIRS))
    )
    plan_ref[5:6] = turns.astype(jnp.int32)
    plan_ref[6:8] = jnp.zeros((2, places), jnp.int32)


def source_places(slots, n):
    most = slots + min(slots, n) * (run_of(slots, n) - 1)
    return -(-most // CHUNK) * CHUNK


def make_plan(tasks, left_ops, n, terms):
    most = source_places(tasks.shape[1], n) + 2 * PAIRS
    given = [tasks, left_ops] if fits(n) else [tasks]
    return pl.pallas_call(
        functools.partial(plan_kernel, n, terms),
        in_specs=[pl.BlockSpec(memory_space=pltpu.VMEM)] * len(given),
        out_shape=jax.ShapeDtypeStruct((8, -(-most // 128) * 128), jnp.int32),
        compiler_params=pltpu.CompilerParams(vmem_limit_bytes=16 * MIB),
    )(*given)


def tasks_kernel(n, terms_per, kinds, plan_ref, left_ref, *refs):
    blocks, refs = refs[: len(kinds)], refs[len(kinds) :]
    send_ref, keep_ref, own_ref, trial, right, acc, halves, block_sem, *refs = refs
    run = run_of(left_ref.shape[0], n)
    source_turns, target_turns = plan_ref[5, 0], plan_ref[5, 1]

    def block_copy(b, which):
        owner = owner_of(*kinds[b], n)
        if which == 0:
            source, to = blocks[b].at[pl.ds(0, TRIALS)], trial.at[owner]
        else:
            source = blocks[b].at[pl.ds(TRIALS, terms_per)]
            to = right.at[pl.ds(owner * terms_per, terms_per)]
        return pltpu.make_async_copy(source, to, block_sem.at[b, which])

    def fetch(turn):
        left, left_sem = refs
        at = lax.rem(turn, AHEAD)
        for u in range(CHUNK):
            slot = plan_ref[0, turn * CHUNK + u]
            pltpu.make_async_copy(left_ref.at[slot], left.at[at, u], left_sem.at[at]).start()

    for b in range(len(kinds)):
        block_copy(b, 0).start()
    for turn in range(AHEAD - 1) if refs else ():

        @pl.when(turn < source_turns)
        def _():
            fetch(turn)

    for b in range(len(kinds)):
        block_copy(b, 1).start()
    right[n * terms_per] = jnp.zeros((128, 128), jnp.bfloat16)

    def clear(s, carry):
        acc[s] = jnp.zeros((256, 128), jnp.float32)
        return carry

    lax.fori_loop(0, n, clear, 0)
    for b in range(len(kinds)):
        block_copy(b, 0).wait()

    def source_turn(turn, carry):
        first = turn * CHUNK
        if refs:
            left, left_sem = refs

            @pl.when(turn + AHEAD - 1 < source_turns)
            def _():
                fetch(turn + AHEAD - 1)

            at = lax.rem(turn, AHEAD)
            pltpu.make_async_copy(left_ref.at[pl.ds(0, CHUNK)], left.at[at], left_sem.at[at]).wait()
        for r in range(0, CHUNK, run):
            source = plan_ref[1, first + r]
            vectors = jnp.concatenate([trial[source, 0], trial[source, 1]], axis=1)
            if refs:
                rows = left[at, r : r + run].reshape(run * 128, 128)
            else:
                rows = jnp.concatenate([left_ref[plan_ref[0, first + r + u]] for u in range(run)], axis=0)
            half = jnp.dot(rows, vectors, preferred_element_type=jnp.float32).astype(jnp.bfloat16)
            for u in range(run):
                halves[first + r + u, 0] = half[u * 128 : (u + 1) * 128, :128]
                halves[first + r + u, 1] = half[u * 128 : (u + 1) * 128, 128:]
        return carry

    lax.fori_loop(0, source_turns, source_turn, 0)
    for b in range(len(kinds)):
        block_copy(b, 1).wait()

    def target_turn(turn, carry):
        first = turn * 2 * PAIRS
        for u in range(0, 2 * PAIRS, 2):
            place = first + u
            one, two = plan_ref[2, place], plan_ref[2, place + 1]
            pair = jnp.concatenate(
                [
                    jnp.concatenate([halves[one, 0], halves[two, 0]], axis=1),
                    jnp.concatenate([halves[one, 1], halves[two, 1]], axis=1),
                ],
                axis=0,
            )
            rights = jnp.concatenate([right[plan_ref[3, place]], right[plan_ref[3, place + 1]]], axis=0)
            term = lax.dot_general(
                pair, rights, (((1,), (0,)), ((), ())), preferred_element_type=jnp.float32
            )
            target = plan_ref[4, place]
            acc[target] = acc[target] + term
        return carry

    lax.fori_loop(0, target_turns, target_turn, 0)

    def dots(s, carry):
        t0 = trial[s, 0].astype(jnp.float32)
        t1 = trial[s, 1].astype(jnp.float32)
        a0 = acc[s, 0:128, :]
        a1 = acc[s, 128:256, :]
        p00, p01, p10, p11 = carry
        return p00 + fold(t0 * a0), p01 + fold(t0 * a1), p10 + fold(t1 * a0), p11 + fold(t1 * a1)

    zero = jnp.zeros((8, 128), jnp.float32)
    p00, p01, p10, p11 = [jnp.sum(x) for x in lax.fori_loop(0, n, dots, (zero,) * 4)]
    own = matrix_of({(0, 0): p00, (0, 1): p01, (1, 0): p10, (1, 1): p11})
    own_ref[...] = own
    me = lax.axis_index("op")

    def pack(j, carry):
        mine = jnp.bitwise_xor(me, 2 * j)
        keep_ref[j] = acc[mine]
        send_ref[pl.ds(pl.multiple_of(j * 256, 256), 256), :] = acc[jnp.bitwise_xor(mine, 1)].astype(jnp.bfloat16)
        return carry

    lax.fori_loop(0, n // 2, pack, 0)
    send_ref[n // 2 * 256 :, :] = split3(own)


def run_tasks(n, plan, left_ops, blocks):
    slots = left_ops.shape[0]
    terms_per = blocks[0][0].shape[0] - TRIALS
    kinds = tuple(block[1:] for block in blocks)
    small = fits(n)
    given = pl.BlockSpec(memory_space=pltpu.VMEM if small else pltpu.HBM)
    fetched = [] if small else [
        pltpu.VMEM((AHEAD, CHUNK, 128, 128), jnp.bfloat16),
        pltpu.SemaphoreType.DMA((AHEAD,)),
    ]
    return pl.pallas_call(
        functools.partial(tasks_kernel, n, terms_per, kinds),
        out_shape=(
            jax.ShapeDtypeStruct((n // 2 * 256 + TAIL, 128), jnp.bfloat16),
            jax.ShapeDtypeStruct((n // 2, 256, 128), jnp.float32),
            jax.ShapeDtypeStruct((8, 128), jnp.float32),
        ),
        in_specs=[pl.BlockSpec(memory_space=pltpu.SMEM)] + [given] * (1 + len(blocks)),
        scratch_shapes=[
            pltpu.VMEM((n, TRIALS, 128, 128), jnp.bfloat16),
            pltpu.VMEM((n * terms_per + 1, 128, 128), jnp.bfloat16),
            pltpu.VMEM((n + 1, 256, 128), jnp.float32),
            pltpu.VMEM((source_places(slots, n), 2, 128, 128), jnp.bfloat16),
            pltpu.SemaphoreType.DMA((len(blocks), 2)),
        ]
        + fetched,
        compiler_params=pltpu.CompilerParams(vmem_limit_bytes=(34 if small else 58) * MIB),
        cost_estimate=pl.CostEstimate(
            flops=slots * 8 * 128**3, bytes_accessed=slots * 32768 + n * 450000, transcendentals=0
        ),
    )(plan, left_ops, *[block[0] for block in blocks])


def corr_kernel(*refs):
    blocks, corr_ref = refs[:-1], refs[-1]
    total = [jnp.zeros((8, 128), jnp.float32)] * 3
    for ref in blocks:
        t0, t1 = ref[0].astype(jnp.float32), ref[1].astype(jnp.float32)
        total = [total[0] + fold(t0 * t0), total[1] + fold(t0 * t1), total[2] + fold(t1 * t1)]
    c00, c01, c11 = [jnp.sum(x) for x in total]
    corr_ref[...] = matrix_of({(0, 0): c00, (0, 1): c01, (1, 0): c01, (1, 1): c11})[0:2, 0:2]


def correlate(blocks):
    return pl.pallas_call(
        corr_kernel,
        out_shape=jax.ShapeDtypeStruct((2, 2), jnp.float32),
        compiler_params=pltpu.CompilerParams(vmem_limit_bytes=16 * MIB),
    )(*blocks)


def chip_kernel(chips, keep_ref, own_ref, received_ref, mine_ref, total_ref, *sends):
    total = own_ref[...] + join3(received_ref[chips * 256 :, :])
    total_ref[...] = total
    tail = split3(total)
    for j in range(chips):
        value = keep_ref[j] + received_ref[j * 256 : (j + 1) * 256, :].astype(jnp.float32)
        if j == 0:
            mine_ref[...] = value
        else:
            sends[j - 1][0:256, :] = value.astype(jnp.bfloat16)
            sends[j - 1][256:, :] = tail


def add_chip(keep, own, received):
    chips = keep.shape[0]
    return pl.pallas_call(
        functools.partial(chip_kernel, chips),
        out_shape=(jax.ShapeDtypeStruct((256, 128), jnp.float32), jax.ShapeDtypeStruct((8, 128), jnp.float32))
        + (jax.ShapeDtypeStruct((256 + TAIL, 128), jnp.bfloat16),) * (chips - 1),
        compiler_params=pltpu.CompilerParams(vmem_limit_bytes=16 * MIB),
    )(keep, own, received)


def last_kernel(mine_ref, total_ref, *refs):
    received, (product_ref, projected_ref) = refs[:-2], refs[-2:]
    value, total = mine_ref[...], total_ref[...]
    for ref in received:
        value = value + ref[0:256, :].astype(jnp.float32)
        total = total + join3(ref[256:, :])
    product_ref[0, 0] = value[0:128]
    product_ref[0, 1] = value[128:256]
    projected_ref[...] = total[0:2, 0:2]


def add_all(mine, total, received):
    return pl.pallas_call(
        last_kernel,
        out_shape=(
            jax.ShapeDtypeStruct((1, 2, 128, 128), jnp.float32),
            jax.ShapeDtypeStruct((2, 2), jnp.float32),
        ),
        compiler_params=pltpu.CompilerParams(vmem_limit_bytes=16 * MIB),
    )(mine, total, *received)


def gather(own, n):
    steps = n // 4
    lines = [own, exchange(own, n, 1)]
    blocks = [(value, 0, False, half) for half, value in enumerate(lines)]
    for step in range(1, steps + 1):
        for half in range(2):
            lines[half] = ring_step(lines[half], n)
            blocks.append((lines[half], step, False, half))
        if step < steps:
            blocks += [(exchange(value, n, 1), step, True, half) for half, value in enumerate(lines)]
    return blocks


def body(n, trial, left_ops, right_ops, task_list):
    blocks = gather(jnp.concatenate([trial[0], right_ops.swapaxes(1, 2)], axis=0), n)
    plan = make_plan(task_list.T, left_ops, n, n * right_ops.shape[0])
    send, keep, own = run_tasks(n, plan, left_ops, blocks)
    send, arrays = lax.optimization_barrier((send, [block[0] for block in blocks]))
    correlation = correlate(arrays)
    mine, total, *sends = add_chip(keep, own, exchange(send, n, 1))
    received = [exchange(sends[j - 1], n, 2 * j) for j in reversed(range(1, n // 2))]
    product, projected = add_all(mine, total, received)
    return product, correlation, projected


def solution(mesh):
    return jax.shard_map(
        functools.partial(body, mesh.shape["op"]),
        mesh=mesh,
        in_specs=(
            P(("groups", "op"), None, None, None),
            P(("groups", "op"), None, None),
            P(("groups", "op"), None, None),
            P(("groups", "op"), None),
        ),
        out_specs=(P(("groups", "op"), None, None, None), P("groups", None), P("groups", None)),
        check_vma=False,
    )
```

```python
import functools

import jax
import jax.numpy as jnp
from jax import lax
from jax.experimental import pallas as pl
from jax.experimental.pallas import tpu as pltpu
from jax.sharding import PartitionSpec as P

MIB = 1024 * 1024
TAIL = 16
TRIALS = 2
CHUNK = 16
PAIRS = 8
AHEAD = 3


def exchange(value, n, mask):
    return lax.ppermute(value, "op", [(i, i ^ mask) for i in range(n)])


def chip_at(place, chips):
    return 2 * place if place < chips // 2 else 2 * (chips - place) - 1


def ring_step(value, n):
    chips = n // 2
    order = [chip_at(place, chips) for place in range(chips)]
    pairs = []
    for place, chip in enumerate(order):
        pairs.append((2 * chip, 2 * order[(place + 1) % chips]))
        pairs.append((2 * chip + 1, 2 * order[(place - 1) % chips] + 1))
    return lax.ppermute(value, "op", pairs)


def owner_of(step, swapped, half, n):
    chips = n // 2
    me = lax.axis_index("op")
    chip, core = me // 2, lax.rem(me, 2)
    odd = lax.rem(chip, 2)
    mine = jnp.where(odd == 0, chip // 2, chips - 1 - chip // 2)
    line = 1 - core if swapped else core
    place = lax.rem(mine + (2 * line - 1) * step + 2 * chips, chips)
    there = jnp.where(place < chips // 2, 2 * place, 2 * (chips - place) - 1)
    return 2 * there + (line if half == 0 else 1 - line)


def split3(value):
    lanes = lax.broadcasted_iota(jnp.int32, (8, 128), 1)
    high = value.astype(jnp.bfloat16).astype(jnp.float32)
    middle = (value - high).astype(jnp.bfloat16).astype(jnp.float32)
    low = (value - high - middle).astype(jnp.bfloat16).astype(jnp.float32)
    return jnp.where(lanes < 2, high, jnp.where(lanes < 4, middle, low))


def tail_of(first, second):
    return jnp.concatenate([first, second], axis=0).astype(jnp.bfloat16)


def matrix_of(values, repeats=1):
    rows = lax.broadcasted_iota(jnp.int32, (8, 128), 0)
    lanes = lax.broadcasted_iota(jnp.int32, (8, 128), 1)
    total = jnp.zeros((8, 128), jnp.float32)
    for (i, j), value in values.items():
        for repeat in range(repeats):
            total = total + jnp.where((rows == i) & (lanes == j + 2 * repeat), value, 0.0)
    return total


def fold(value):
    return value.reshape(16, 8, 128).sum(axis=0)


def fits(n):
    return n <= 16


def phases_of(n):
    return 1


def run_of(slots, n):
    return 4 if slots >= 8 * n else 2


def source_places(slots, n):
    most = slots + min(slots, n) * (run_of(slots, n) - 1) + phases_of(n) * CHUNK
    return -(-most // CHUNK) * CHUNK


def place_of(chip, chips):
    half = jnp.floor(chip * 0.5)
    return jnp.where(chip == 2.0 * half, half, chips - 1.0 - half)


def plan_kernel(n, terms, tasks_ref, plan_ref):
    slots = tasks_ref.shape[1]
    places = plan_ref.shape[1]
    chips = n // 2
    phases = phases_of(n)
    rows = tasks_ref[...].astype(jnp.float32)
    source, target, term, live = rows[0:1], rows[1:2], rows[2:3], rows[3:4]
    lane = lax.broadcasted_iota(jnp.int32, (1, slots), 1).astype(jnp.float32)
    number = lax.broadcasted_iota(jnp.int32, (1, places), 1).astype(jnp.float32)
    at = lax.broadcasted_iota(jnp.int32, (slots, places), 1).astype(jnp.float32)
    me = lax.axis_index("op")
    mine = place_of((jnp.zeros((1, slots), jnp.int32) + me // 2).astype(jnp.float32), float(chips))
    gap = place_of(jnp.floor(source * 0.5), float(chips)) - mine
    up = jnp.where(gap < 0, gap + chips, gap)
    far = jnp.minimum(up, chips - up)
    phase = jnp.clip(far - 1.0, 0.0, phases - 1.0)

    def column(*values):
        pad = [jnp.zeros((8 - len(values), slots), jnp.float32)]
        return jnp.transpose(jnp.concatenate(list(values) + pad, axis=0))

    def sort(sector, parts, unit, whole):
        keys = parts * n
        index = lax.broadcasted_iota(jnp.int32, (keys, slots), 0).astype(jnp.float32)
        part = phase if parts > 1 else jnp.zeros_like(phase)
        key = jnp.where(live > 0, part * n + sector, float(keys))
        columns = column(key, lane)
        earlier = jnp.where((columns[:, 0:1] == key) & (columns[:, 1:2] < lane), 1.0, 0.0)
        count = jnp.sum(jnp.where(index == key, 1.0, 0.0), axis=1, keepdims=True)
        padded = jnp.ceil(count / unit) * unit
        place = jnp.sum(earlier, axis=0, keepdims=True)
        start = jnp.zeros((1, 1), jnp.float32)
        starts = [start]
        for p in range(parts):
            lengths = padded[p * n : (p + 1) * n]
            before = jnp.where(index[p * n : (p + 1) * n] < key, lengths, 0.0)
            place = place + jnp.where(part == p, start * whole + jnp.sum(before, axis=0, keepdims=True), 0.0)
            start = start + jnp.ceil(jnp.sum(lengths, axis=0, keepdims=True) / whole)
            starts.append(start)
        return jnp.where(live > 0, place, -1.0), starts

    by_source, source_starts = sort(source, phases, float(run_of(slots, n)), float(CHUNK))
    by_target, target_starts = sort(target, 1, 2.0, 2.0 * PAIRS)
    columns = column(by_source, by_target, lane, source, term, target)

    def picker(places_column):
        hit = places_column == at

        def pick(values, other):
            found = jnp.sum(jnp.where(hit, values - other, 0.0), axis=0, keepdims=True)
            return (found + other).astype(jnp.int32)

        return pick

    own = (jnp.zeros((1, 1), jnp.int32) + me).astype(jnp.float32)
    pick = picker(columns[:, 0:1])
    plan_ref[0:1] = pick(columns[:, 2:3], 0.0)
    plan_ref[1:2] = pick(columns[:, 3:4], own)
    pick = picker(columns[:, 1:2])
    plan_ref[2:3] = pick(columns[:, 0:1], -1.0)
    plan_ref[3:4] = pick(columns[:, 4:5], float(terms))
    plan_ref[4:5] = pick(columns[:, 5:6], float(n))
    turns = jnp.zeros((1, places), jnp.float32)
    for p, start in enumerate(source_starts + [target_starts[1]]):
        turns = turns + jnp.where(number == p, start, 0.0)
    plan_ref[5:6] = turns.astype(jnp.int32)
    plan_ref[6:8] = jnp.zeros((2, places), jnp.int32)


def make_plan(tasks, n, terms):
    most = source_places(tasks.shape[1], n) + 2 * PAIRS
    return pl.pallas_call(
        functools.partial(plan_kernel, n, terms),
        out_shape=jax.ShapeDtypeStruct((8, -(-most // 128) * 128), jnp.int32),
        compiler_params=pltpu.CompilerParams(vmem_limit_bytes=16 * MIB),
    )(tasks)


def block_copies(n, kinds, blocks, trial, right, sem, which):
    copies = []
    for b, kind in enumerate(kinds):
        owner = owner_of(*kind, n)
        per = blocks[b].shape[0] - TRIALS
        if which == 0:
            source, to = blocks[b].at[pl.ds(0, TRIALS)], trial.at[owner]
        else:
            source, to = blocks[b].at[pl.ds(TRIALS, per)], right.at[pl.ds(owner * per, per)]
        copies.append(pltpu.make_async_copy(source, to, sem.at[b, which]))
    return copies


def half_steps(n, phase, plan_ref, left_ref, trial, halves, left, left_sem):
    first, last = plan_ref[5, phase], plan_ref[5, phase + 1]
    run = run_of(left_ref.shape[0], n)

    def fetch(turn):
        at = lax.rem(turn, AHEAD)
        for u in range(CHUNK):
            slot = plan_ref[0, turn * CHUNK + u]
            pltpu.make_async_copy(left_ref.at[slot], left.at[at, u], left_sem.at[at]).start()

    def start():
        for ahead in range(AHEAD - 1):

            @pl.when(first + ahead < last)
            def _():
                fetch(first + ahead)

    def turn_of(turn, carry):
        @pl.when(turn + AHEAD - 1 < last)
        def _():
            fetch(turn + AHEAD - 1)

        at = lax.rem(turn, AHEAD)
        pltpu.make_async_copy(left_ref.at[pl.ds(0, CHUNK)], left.at[at], left_sem.at[at]).wait()
        place = turn * CHUNK
        for r in range(0, CHUNK, run):
            source = plan_ref[1, place + r]
            vectors = jnp.concatenate([trial[source, 0], trial[source, 1]], axis=1)
            rows = left[at, r : r + run].reshape(run * 128, 128)
            half = jnp.dot(rows, vectors, preferred_element_type=jnp.float32).astype(jnp.bfloat16)
            for u in range(run):
                halves[place + r + u, 0] = half[u * 128 : (u + 1) * 128, :128]
                halves[place + r + u, 1] = half[u * 128 : (u + 1) * 128, 128:]
        return carry

    return start, lambda: lax.fori_loop(first, last, turn_of, 0)


def tasks_kernel(n, kinds, plan_ref, left_ref, *refs):
    blocks, refs = refs[: len(kinds)], refs[len(kinds) :]
    send_ref, keep_ref, own_ref, halves, trial, right, acc, left, block_sem, left_sem = refs
    phase = phases_of(n) - 1
    start, products = half_steps(n, phase, plan_ref, left_ref, trial, halves, left, left_sem)
    moves = [block_copies(n, kinds, blocks, trial, right, block_sem, which) for which in range(2)]
    for copy in moves[0]:
        copy.start()
    start()
    for copy in moves[1]:
        copy.start()
    right[right.shape[0] - 1] = jnp.zeros((128, 128), jnp.bfloat16)

    def clear(s, carry):
        acc[s] = jnp.zeros((256, 128), jnp.float32)
        return carry

    lax.fori_loop(0, n, clear, 0)
    for copy in moves[0]:
        copy.wait()
    products()
    for copy in moves[1]:
        copy.wait()

    def target_turn(turn, carry):
        first = turn * 2 * PAIRS
        for u in range(0, 2 * PAIRS, 2):
            place = first + u
            one = plan_ref[2, place]
            two = plan_ref[2, place + 1]
            one, two = jnp.maximum(one, 0), jnp.where(two < 0, jnp.maximum(one, 0), two)
            pair = jnp.concatenate(
                [
                    jnp.concatenate([halves[one, 0], halves[two, 0]], axis=1),
                    jnp.concatenate([halves[one, 1], halves[two, 1]], axis=1),
                ],
                axis=0,
            )
            rights = jnp.concatenate([right[plan_ref[3, place]], right[plan_ref[3, place + 1]]], axis=0)
            term = jnp.dot(pair, rights, preferred_element_type=jnp.float32)
            target = plan_ref[4, place]
            acc[target] = acc[target] + term
        return carry

    lax.fori_loop(0, plan_ref[5, phase + 2], target_turn, 0)
    me = lax.axis_index("op")

    def pack(j, carry):
        mine = jnp.bitwise_xor(me, 2 * j)
        p00, p01, p10, p11 = carry
        for other, s in enumerate((mine, jnp.bitwise_xor(mine, 1))):
            t0 = trial[s, 0].astype(jnp.float32)
            t1 = trial[s, 1].astype(jnp.float32)
            a0 = acc[s, 0:128, :]
            a1 = acc[s, 128:256, :]
            p00, p01 = p00 + fold(t0 * a0), p01 + fold(t0 * a1)
            p10, p11 = p10 + fold(t1 * a0), p11 + fold(t1 * a1)
            if other:
                rows = pl.multiple_of(j * 256, 256)
                send_ref[pl.ds(rows, 128), :] = a0.astype(jnp.bfloat16)
                send_ref[pl.ds(rows + 128, 128), :] = a1.astype(jnp.bfloat16)
            else:
                keep_ref[j, 0:128, :] = a0
                keep_ref[j, 128:256, :] = a1
        return p00, p01, p10, p11

    zero = jnp.zeros((8, 128), jnp.float32)
    sums = lax.fori_loop(0, n // 2, pack, (zero,) * 4, unroll=2)
    p00, p01, p10, p11 = [jnp.sum(x) for x in sums]
    own = split3(matrix_of({(0, 0): p00, (0, 1): p01, (1, 0): p10, (1, 1): p11}, 3))
    own_ref[...] = own
    send_ref[n // 2 * 256 :, :] = tail_of(own, jnp.zeros_like(own))


def run_tasks(n, plan, left_ops, blocks):
    slots = left_ops.shape[0]
    terms_per = blocks[0][0].shape[0] - TRIALS
    kinds = tuple(block[1:] for block in blocks)
    vmem, hbm = pl.BlockSpec(memory_space=pltpu.VMEM), pl.BlockSpec(memory_space=pltpu.HBM)
    return pl.pallas_call(
        functools.partial(tasks_kernel, n, kinds),
        out_shape=(
            jax.ShapeDtypeStruct((n // 2 * 256 + TAIL, 128), jnp.bfloat16),
            jax.ShapeDtypeStruct((n // 2, 256, 128), jnp.float32),
            jax.ShapeDtypeStruct((8, 128), jnp.float32),
        ),
        in_specs=[pl.BlockSpec(memory_space=pltpu.SMEM), hbm] + [vmem if fits(n) else hbm] * len(blocks),
        out_specs=(vmem,) * 3,
        scratch_shapes=[
            pltpu.VMEM((source_places(slots, n), 2, 128, 128), jnp.bfloat16),
            pltpu.VMEM((n, TRIALS, 128, 128), jnp.bfloat16),
            pltpu.VMEM((n * terms_per + 1, 128, 128), jnp.bfloat16),
            pltpu.VMEM((n + 1, 256, 128), jnp.float32),
            pltpu.VMEM((AHEAD, CHUNK, 128, 128), jnp.bfloat16),
            pltpu.SemaphoreType.DMA((len(blocks), 2)),
            pltpu.SemaphoreType.DMA((AHEAD,)),
        ],
        compiler_params=pltpu.CompilerParams(vmem_limit_bytes=(48 if fits(n) else 58) * MIB),
        cost_estimate=pl.CostEstimate(
            flops=slots * 8 * 128**3, bytes_accessed=slots * 32768 + n * 450000, transcendentals=0
        ),
    )(plan, left_ops, *[block[0] for block in blocks])


def join_kernel(trial_ref, right_ref, block_ref):
    block_ref[0:TRIALS] = trial_ref[0]
    for k in range(right_ref.shape[0]):
        block_ref[TRIALS + k] = jnp.transpose(right_ref[k])


def join(trial, right_ops):
    return pl.pallas_call(
        join_kernel,
        out_shape=jax.ShapeDtypeStruct((TRIALS + right_ops.shape[0], 128, 128), jnp.bfloat16),
        compiler_params=pltpu.CompilerParams(vmem_limit_bytes=16 * MIB),
    )(trial, right_ops)


def corr_kernel(*refs):
    blocks, corr_ref = refs[:-1], refs[-1]
    total = [jnp.zeros((8, 128), jnp.float32)] * 3
    for ref in blocks:
        t0, t1 = ref[0].astype(jnp.float32), ref[1].astype(jnp.float32)
        total = [total[0] + fold(t0 * t0), total[1] + fold(t0 * t1), total[2] + fold(t1 * t1)]
    c00, c01, c11 = [jnp.sum(x) for x in total]
    corr_ref[...] = matrix_of({(0, 0): c00, (0, 1): c01, (1, 0): c01, (1, 1): c11})[0:2, 0:2]


def correlate(blocks):
    return pl.pallas_call(
        corr_kernel,
        out_shape=jax.ShapeDtypeStruct((2, 2), jnp.float32),
        compiler_params=pltpu.CompilerParams(vmem_limit_bytes=16 * MIB),
    )(*blocks)


def chip_kernel(chips, keep_ref, own_ref, received_ref, mine_ref, total_ref, *sends):
    total = jnp.concatenate([own_ref[...], received_ref[chips * 256 :, :].astype(jnp.float32)[0:8]], axis=0)
    total_ref[...] = total
    tail = total.astype(jnp.bfloat16)
    for j in range(chips):
        value = keep_ref[j] + received_ref[j * 256 : (j + 1) * 256, :].astype(jnp.float32)
        if j == 0:
            mine_ref[...] = value
        else:
            sends[j - 1][0:256, :] = value.astype(jnp.bfloat16)
            sends[j - 1][256:, :] = tail


def add_chip(keep, own, received):
    chips = keep.shape[0]
    return pl.pallas_call(
        functools.partial(chip_kernel, chips),
        out_shape=(jax.ShapeDtypeStruct((256, 128), jnp.float32), jax.ShapeDtypeStruct((16, 128), jnp.float32))
        + (jax.ShapeDtypeStruct((256 + TAIL, 128), jnp.bfloat16),) * (chips - 1),
        compiler_params=pltpu.CompilerParams(vmem_limit_bytes=16 * MIB),
    )(keep, own, received)


def last_kernel(mine_ref, total_ref, *refs):
    received, (product_ref, projected_ref) = refs[:-2], refs[-2:]
    value, total = mine_ref[...], total_ref[...]
    for ref in received:
        value = value + ref[0:256, :].astype(jnp.float32)
        total = total + ref[256:, :].astype(jnp.float32)
    product_ref[0, 0] = value[0:128]
    product_ref[0, 1] = value[128:256]
    total = total[0:8] + total[8:16]
    projected_ref[...] = total[0:2, 0:2] + total[0:2, 2:4] + total[0:2, 4:6]


def add_all(mine, total, received):
    return pl.pallas_call(
        last_kernel,
        out_shape=(
            jax.ShapeDtypeStruct((1, 2, 128, 128), jnp.float32),
            jax.ShapeDtypeStruct((2, 2), jnp.float32),
        ),
        compiler_params=pltpu.CompilerParams(vmem_limit_bytes=16 * MIB),
    )(mine, total, *received)


def body(n, trial, left_ops, right_ops, task_list):
    steps = n // 4
    own = join(trial, right_ops)
    plan = make_plan(task_list.T, n, n * right_ops.shape[0])
    lines = [own, exchange(own, n, 1)]
    blocks = [(value, 0, False, half) for half, value in enumerate(lines)]
    for step in range(1, steps + 1):
        if step == steps // 2 + 1:
            lines, plan = lax.optimization_barrier((lines, plan))
        for half in range(2):
            lines[half] = ring_step(lines[half], n)
            blocks.append((lines[half], step, False, half))
        if step < steps:
            blocks += [(exchange(value, n, 1), step, True, half) for half, value in enumerate(lines)]
    send, keep, own = run_tasks(n, plan, left_ops, blocks)
    send, arrays = lax.optimization_barrier((send, [block[0] for block in blocks]))
    correlation = correlate(arrays)
    mine, total, *sends = add_chip(keep, own, exchange(send, n, 1))
    received = [exchange(sends[j - 1], n, 2 * j) for j in reversed(range(1, n // 2))]
    product, projected = add_all(mine, total, received)
    return product, correlation, projected


def solution(mesh):
    return jax.shard_map(
        functools.partial(body, mesh.shape["op"]),
        mesh=mesh,
        in_specs=(
            P(("groups", "op"), None, None, None),
            P(("groups", "op"), None, None),
            P(("groups", "op"), None, None),
            P(("groups", "op"), None),
        ),
        out_specs=(P(("groups", "op"), None, None, None), P("groups", None), P("groups", None)),
        check_vma=False,
    )
```

```python
import functools

import jax
import jax.numpy as jnp
from jax import lax
from jax.experimental import pallas as pl
from jax.experimental.pallas import tpu as pltpu
from jax.sharding import PartitionSpec as P

MIB = 1024 * 1024
TAIL = 16
TRIALS = 2
CHUNK = 48
PAIRS = 24
AHEAD = 3


def exchange(value, n, mask):
    return lax.ppermute(value, "op", [(i, i ^ mask) for i in range(n)])


def chip_at(place, chips):
    return 2 * place if place < chips // 2 else 2 * (chips - place) - 1


def ring_step(value, n):
    chips = n // 2
    order = [chip_at(place, chips) for place in range(chips)]
    pairs = []
    for place, chip in enumerate(order):
        pairs.append((2 * chip, 2 * order[(place + 1) % chips]))
        pairs.append((2 * chip + 1, 2 * order[(place - 1) % chips] + 1))
    return lax.ppermute(value, "op", pairs)


def owner_of(step, swapped, half, n):
    chips = n // 2
    me = lax.axis_index("op")
    chip, core = me // 2, lax.rem(me, 2)
    odd = lax.rem(chip, 2)
    mine = jnp.where(odd == 0, chip // 2, chips - 1 - chip // 2)
    line = 1 - core if swapped else core
    place = lax.rem(mine + (2 * line - 1) * step + 2 * chips, chips)
    there = jnp.where(place < chips // 2, 2 * place, 2 * (chips - place) - 1)
    return 2 * there + (line if half == 0 else 1 - line)


def split3(value):
    lanes = lax.broadcasted_iota(jnp.int32, (8, 128), 1)
    high = value.astype(jnp.bfloat16).astype(jnp.float32)
    middle = (value - high).astype(jnp.bfloat16).astype(jnp.float32)
    low = (value - high - middle).astype(jnp.bfloat16).astype(jnp.float32)
    return jnp.where(lanes < 2, high, jnp.where(lanes < 4, middle, low))


def tail_of(first, second):
    return jnp.concatenate([first, second], axis=0).astype(jnp.bfloat16)


def matrix_of(values, repeats=1):
    rows = lax.broadcasted_iota(jnp.int32, (8, 128), 0)
    lanes = lax.broadcasted_iota(jnp.int32, (8, 128), 1)
    total = jnp.zeros((8, 128), jnp.float32)
    for (i, j), value in values.items():
        for repeat in range(repeats):
            total = total + jnp.where((rows == i) & (lanes == j + 2 * repeat), value, 0.0)
    return total


def fold(value):
    return value.reshape(16, 8, 128).sum(axis=0)


def fits(n):
    return n <= 16


def phases_of(n):
    return 1


def run_of(slots, n):
    return 4 if slots >= 8 * n else 2


def source_places(slots, n):
    most = slots + min(slots, n) * (run_of(slots, n) - 1) + phases_of(n) * CHUNK
    return -(-most // CHUNK) * CHUNK


def place_of(chip, chips):
    half = jnp.floor(chip * 0.5)
    return jnp.where(chip == 2.0 * half, half, chips - 1.0 - half)


def stage_kernel(n, terms, tasks_ref, left_ref, plan_ref, held_ref, sem):
    copy = pltpu.make_async_copy(left_ref, held_ref, sem)
    copy.start()
    plan_kernel(n, terms, tasks_ref, plan_ref)
    copy.wait()


def plan_kernel(n, terms, tasks_ref, plan_ref):
    slots = tasks_ref.shape[1]
    places = plan_ref.shape[1]
    chips = n // 2
    phases = phases_of(n)
    rows = tasks_ref[...].astype(jnp.float32)
    source, target, term, live = rows[0:1], rows[1:2], rows[2:3], rows[3:4]
    lane = lax.broadcasted_iota(jnp.int32, (1, slots), 1).astype(jnp.float32)
    number = lax.broadcasted_iota(jnp.int32, (1, places), 1).astype(jnp.float32)
    at = lax.broadcasted_iota(jnp.int32, (slots, places), 1).astype(jnp.float32)
    me = lax.axis_index("op")
    mine = place_of((jnp.zeros((1, slots), jnp.int32) + me // 2).astype(jnp.float32), float(chips))
    gap = place_of(jnp.floor(source * 0.5), float(chips)) - mine
    up = jnp.where(gap < 0, gap + chips, gap)
    far = jnp.minimum(up, chips - up)
    phase = jnp.clip(far - 1.0, 0.0, phases - 1.0)

    def column(*values):
        pad = [jnp.zeros((8 - len(values), slots), jnp.float32)]
        return jnp.transpose(jnp.concatenate(list(values) + pad, axis=0))

    def sort(sector, parts, unit, whole):
        keys = parts * n
        index = lax.broadcasted_iota(jnp.int32, (keys, slots), 0).astype(jnp.float32)
        part = phase if parts > 1 else jnp.zeros_like(phase)
        key = jnp.where(live > 0, part * n + sector, float(keys))
        columns = column(key, lane)
        earlier = jnp.where((columns[:, 0:1] == key) & (columns[:, 1:2] < lane), 1.0, 0.0)
        count = jnp.sum(jnp.where(index == key, 1.0, 0.0), axis=1, keepdims=True)
        padded = jnp.ceil(count / unit) * unit
        place = jnp.sum(earlier, axis=0, keepdims=True)
        start = jnp.zeros((1, 1), jnp.float32)
        starts = [start]
        for p in range(parts):
            lengths = padded[p * n : (p + 1) * n]
            before = jnp.where(index[p * n : (p + 1) * n] < key, lengths, 0.0)
            place = place + jnp.where(part == p, start * whole + jnp.sum(before, axis=0, keepdims=True), 0.0)
            start = start + jnp.ceil(jnp.sum(lengths, axis=0, keepdims=True) / whole)
            starts.append(start)
        return jnp.where(live > 0, place, -1.0), starts

    by_source, source_starts = sort(source, phases, float(run_of(slots, n)), float(CHUNK))
    by_target, target_starts = sort(target, 1, 2.0, 2.0 * PAIRS)
    columns = column(by_source, by_target, lane, source, term, target)

    def picker(places_column):
        hit = places_column == at

        def pick(values, other):
            found = jnp.sum(jnp.where(hit, values - other, 0.0), axis=0, keepdims=True)
            return (found + other).astype(jnp.int32)

        return pick

    own = (jnp.zeros((1, 1), jnp.int32) + me).astype(jnp.float32)
    pick = picker(columns[:, 0:1])
    plan_ref[0:1] = pick(columns[:, 2:3], 0.0)
    plan_ref[1:2] = pick(columns[:, 3:4], own)
    pick = picker(columns[:, 1:2])
    plan_ref[2:3] = pick(columns[:, 0:1], -1.0)
    plan_ref[3:4] = pick(columns[:, 4:5], float(terms))
    plan_ref[4:5] = pick(columns[:, 5:6], float(n))
    turns = jnp.zeros((1, places), jnp.float32)
    for p, start in enumerate(source_starts + [target_starts[1]]):
        turns = turns + jnp.where(number == p, start, 0.0)
    plan_ref[5:6] = turns.astype(jnp.int32)
    plan_ref[6:8] = jnp.zeros((2, places), jnp.int32)


def make_plan(tasks, left_ops, n, terms):
    most = source_places(tasks.shape[1], n) + 2 * PAIRS
    plan = jax.ShapeDtypeStruct((8, -(-most // 128) * 128), jnp.int32)
    vmem = pl.BlockSpec(memory_space=pltpu.VMEM)
    if fits(n):
        return pl.pallas_call(
            functools.partial(stage_kernel, n, terms),
            in_specs=[vmem, pl.BlockSpec(memory_space=pltpu.HBM)],
            out_specs=(vmem, vmem),
            out_shape=(plan, jax.ShapeDtypeStruct(left_ops.shape, left_ops.dtype)),
            scratch_shapes=[pltpu.SemaphoreType.DMA],
            compiler_params=pltpu.CompilerParams(vmem_limit_bytes=42 * MIB),
        )(tasks, left_ops)
    return (
        pl.pallas_call(
            functools.partial(plan_kernel, n, terms),
            out_shape=plan,
            compiler_params=pltpu.CompilerParams(vmem_limit_bytes=16 * MIB),
        )(tasks),
        left_ops,
    )


def block_copies(n, kinds, blocks, trial, right, sem, which):
    copies = []
    for b, kind in enumerate(kinds):
        owner = owner_of(*kind, n)
        per = blocks[b].shape[0] - TRIALS
        if which == 0:
            source, to = blocks[b].at[pl.ds(0, TRIALS)], trial.at[owner]
        else:
            source, to = blocks[b].at[pl.ds(TRIALS, per)], right.at[pl.ds(owner * per, per)]
        copies.append(pltpu.make_async_copy(source, to, sem.at[b, which]))
    return copies


def make_halves(n, plan_ref, left_ref, trial, halves, fetched):
    turns = plan_ref[5, 1]
    run = run_of(left_ref.shape[0], n)

    def fetch(turn):
        left, left_sem = fetched
        at = lax.rem(turn, AHEAD)
        for u in range(CHUNK):
            slot = plan_ref[0, turn * CHUNK + u]
            pltpu.make_async_copy(left_ref.at[slot], left.at[at, u], left_sem.at[at]).start()

    def start():
        for turn in range(AHEAD - 1) if fetched else ():

            @pl.when(turn < turns)
            def _():
                fetch(turn)

    def turn_of(turn, carry):
        if fetched:
            left, left_sem = fetched

            @pl.when(turn + AHEAD - 1 < turns)
            def _():
                fetch(turn + AHEAD - 1)

            at = lax.rem(turn, AHEAD)
            pltpu.make_async_copy(left_ref.at[pl.ds(0, CHUNK)], left.at[at], left_sem.at[at]).wait()
        place = turn * CHUNK
        for r in range(0, CHUNK, run):
            source = plan_ref[1, place + r]
            vectors = jnp.concatenate([trial[source, 0], trial[source, 1]], axis=1)
            if fetched:
                rows = left[at, r : r + run].reshape(run * 128, 128)
            else:
                rows = jnp.concatenate([left_ref[plan_ref[0, place + r + u]] for u in range(run)], axis=0)
            half = jnp.dot(rows, vectors, preferred_element_type=jnp.float32).astype(jnp.bfloat16)
            for u in range(run):
                halves[place + r + u, 0] = half[u * 128 : (u + 1) * 128, :128]
                halves[place + r + u, 1] = half[u * 128 : (u + 1) * 128, 128:]
        return carry

    return start, lambda: lax.fori_loop(0, turns, turn_of, 0)


def tasks_kernel(n, kinds, plan_ref, left_ref, *refs):
    blocks, refs = refs[: len(kinds)], refs[len(kinds) :]
    send_ref, keep_ref, own_ref, halves, trial, right, acc, block_sem, *fetched = refs
    start, products = make_halves(n, plan_ref, left_ref, trial, halves, fetched)
    right[right.shape[0] - 1] = jnp.zeros((128, 128), jnp.bfloat16)
    start()
    if fits(n):
        moves = ([], [])
        for b, kind in enumerate(kinds):
            owner = owner_of(*kind, n)
            per = blocks[b].shape[0] - TRIALS
            trial[owner] = blocks[b][0:TRIALS]
            right[pl.ds(owner * per, per)] = blocks[b][TRIALS:]
    else:
        moves = [block_copies(n, kinds, blocks, trial, right, block_sem, which) for which in range(2)]
        for copy in moves[0] + moves[1]:
            copy.start()

    def clear(s, carry):
        acc[s] = jnp.zeros((256, 128), jnp.float32)
        return carry

    lax.fori_loop(0, n, clear, 0)
    for copy in moves[0]:
        copy.wait()
    products()
    for copy in moves[1]:
        copy.wait()

    def target_turn(turn, carry):
        first = turn * 2 * PAIRS
        for u in range(0, 2 * PAIRS, 2):
            place = first + u
            one = plan_ref[2, place]
            two = plan_ref[2, place + 1]
            one, two = jnp.maximum(one, 0), jnp.where(two < 0, jnp.maximum(one, 0), two)
            pair = jnp.concatenate(
                [
                    jnp.concatenate([halves[one, 0], halves[two, 0]], axis=1),
                    jnp.concatenate([halves[one, 1], halves[two, 1]], axis=1),
                ],
                axis=0,
            )
            rights = jnp.concatenate([right[plan_ref[3, place]], right[plan_ref[3, place + 1]]], axis=0)
            term = jnp.dot(pair, rights, preferred_element_type=jnp.float32)
            target = plan_ref[4, place]
            acc[target] = acc[target] + term
        return carry

    lax.fori_loop(0, plan_ref[5, 2], target_turn, 0)
    me = lax.axis_index("op")

    def dots(s, carry):
        t0 = trial[s, 0].astype(jnp.float32)
        t1 = trial[s, 1].astype(jnp.float32)
        a0 = acc[s, 0:128, :]
        a1 = acc[s, 128:256, :]
        p00, p01, p10, p11 = carry
        return p00 + fold(t0 * a0), p01 + fold(t0 * a1), p10 + fold(t1 * a0), p11 + fold(t1 * a1)

    zero = jnp.zeros((8, 128), jnp.float32)
    sums = lax.fori_loop(0, n, dots, (zero,) * 4)
    p00, p01, p10, p11 = [jnp.sum(x) for x in sums]

    def pack(j, carry):
        mine = jnp.bitwise_xor(me, 2 * j)
        keep_ref[j] = acc[mine]
        send_ref[pl.ds(pl.multiple_of(j * 256, 256), 256), :] = acc[jnp.bitwise_xor(mine, 1)].astype(jnp.bfloat16)
        return carry

    lax.fori_loop(0, n // 2, pack, 0)
    own = split3(matrix_of({(0, 0): p00, (0, 1): p01, (1, 0): p10, (1, 1): p11}, 3))
    own_ref[...] = own
    send_ref[n // 2 * 256 :, :] = tail_of(own, jnp.zeros_like(own))


def run_tasks(n, plan, left_ops, blocks):
    slots = left_ops.shape[0]
    terms_per = blocks[0][0].shape[0] - TRIALS
    kinds = tuple(block[1:] for block in blocks)
    vmem, hbm = pl.BlockSpec(memory_space=pltpu.VMEM), pl.BlockSpec(memory_space=pltpu.HBM)
    given = vmem if fits(n) else hbm
    fetched = [] if fits(n) else [
        pltpu.VMEM((AHEAD, CHUNK, 128, 128), jnp.bfloat16),
        pltpu.SemaphoreType.DMA((AHEAD,)),
    ]
    return pl.pallas_call(
        functools.partial(tasks_kernel, n, kinds),
        out_shape=(
            jax.ShapeDtypeStruct((n // 2 * 256 + TAIL, 128), jnp.bfloat16),
            jax.ShapeDtypeStruct((n // 2, 256, 128), jnp.float32),
            jax.ShapeDtypeStruct((8, 128), jnp.float32),
        ),
        in_specs=[pl.BlockSpec(memory_space=pltpu.SMEM)] + [given] * (1 + len(blocks)),
        out_specs=(vmem,) * 3,
        scratch_shapes=[
            pltpu.VMEM((source_places(slots, n), 2, 128, 128), jnp.bfloat16),
            pltpu.VMEM((n, TRIALS, 128, 128), jnp.bfloat16),
            pltpu.VMEM((n * terms_per + 1, 128, 128), jnp.bfloat16),
            pltpu.VMEM((n + 1, 256, 128), jnp.float32),
            pltpu.SemaphoreType.DMA((len(blocks), 2)),
        ]
        + fetched,
        compiler_params=pltpu.CompilerParams(vmem_limit_bytes=(30 if fits(n) else 58) * MIB),
        cost_estimate=pl.CostEstimate(
            flops=slots * 8 * 128**3, bytes_accessed=slots * 32768 + n * 450000, transcendentals=0
        ),
    )(plan, left_ops, *[block[0] for block in blocks])


def join_kernel(trial_ref, right_ref, block_ref):
    block_ref[0:TRIALS] = trial_ref[0]
    for k in range(right_ref.shape[0]):
        block_ref[TRIALS + k] = jnp.transpose(right_ref[k])


def join(trial, right_ops):
    return pl.pallas_call(
        join_kernel,
        out_shape=jax.ShapeDtypeStruct((TRIALS + right_ops.shape[0], 128, 128), jnp.bfloat16),
        compiler_params=pltpu.CompilerParams(vmem_limit_bytes=16 * MIB),
    )(trial, right_ops)


def corr_kernel(*refs):
    blocks, corr_ref = refs[:-1], refs[-1]
    total = [jnp.zeros((8, 128), jnp.float32)] * 3
    for ref in blocks:
        t0, t1 = ref[0].astype(jnp.float32), ref[1].astype(jnp.float32)
        total = [total[0] + fold(t0 * t0), total[1] + fold(t0 * t1), total[2] + fold(t1 * t1)]
    c00, c01, c11 = [jnp.sum(x) for x in total]
    corr_ref[...] = matrix_of({(0, 0): c00, (0, 1): c01, (1, 0): c01, (1, 1): c11})[0:2, 0:2]


def correlate(blocks):
    return pl.pallas_call(
        corr_kernel,
        out_shape=jax.ShapeDtypeStruct((2, 2), jnp.float32),
        compiler_params=pltpu.CompilerParams(vmem_limit_bytes=16 * MIB),
    )(*blocks)


def chip_kernel(chips, keep_ref, own_ref, received_ref, mine_ref, total_ref, *sends):
    total = jnp.concatenate([own_ref[...], received_ref[chips * 256 :, :].astype(jnp.float32)[0:8]], axis=0)
    total_ref[...] = total
    tail = total.astype(jnp.bfloat16)
    for j in range(chips):
        value = keep_ref[j] + received_ref[j * 256 : (j + 1) * 256, :].astype(jnp.float32)
        if j == 0:
            mine_ref[...] = value
        else:
            sends[j - 1][0:256, :] = value.astype(jnp.bfloat16)
            sends[j - 1][256:, :] = tail


def add_chip(keep, own, received):
    chips = keep.shape[0]
    return pl.pallas_call(
        functools.partial(chip_kernel, chips),
        out_shape=(jax.ShapeDtypeStruct((256, 128), jnp.float32), jax.ShapeDtypeStruct((16, 128), jnp.float32))
        + (jax.ShapeDtypeStruct((256 + TAIL, 128), jnp.bfloat16),) * (chips - 1),
        compiler_params=pltpu.CompilerParams(vmem_limit_bytes=16 * MIB),
    )(keep, own, received)


def last_kernel(mine_ref, total_ref, *refs):
    received, (product_ref, projected_ref) = refs[:-2], refs[-2:]
    value, total = mine_ref[...], total_ref[...]
    for ref in received:
        value = value + ref[0:256, :].astype(jnp.float32)
        total = total + ref[256:, :].astype(jnp.float32)
    product_ref[0, 0] = value[0:128]
    product_ref[0, 1] = value[128:256]
    total = total[0:8] + total[8:16]
    projected_ref[...] = total[0:2, 0:2] + total[0:2, 2:4] + total[0:2, 4:6]


def add_all(mine, total, received):
    return pl.pallas_call(
        last_kernel,
        out_shape=(
            jax.ShapeDtypeStruct((1, 2, 128, 128), jnp.float32),
            jax.ShapeDtypeStruct((2, 2), jnp.float32),
        ),
        compiler_params=pltpu.CompilerParams(vmem_limit_bytes=16 * MIB),
    )(mine, total, *received)


def body(n, trial, left_ops, right_ops, task_list):
    steps = n // 4
    own = join(trial, right_ops)
    plan, left_ops = make_plan(task_list.T, left_ops, n, n * right_ops.shape[0])
    lines = [own, exchange(own, n, 1)]
    blocks = [(value, 0, False, half) for half, value in enumerate(lines)]
    for step in range(1, steps + 1):
        if step == steps // 2 + 1:
            lines, plan, left_ops = lax.optimization_barrier((lines, plan, left_ops))
        for half in range(2):
            lines[half] = ring_step(lines[half], n)
            blocks.append((lines[half], step, False, half))
        if step < steps:
            blocks += [(exchange(value, n, 1), step, True, half) for half, value in enumerate(lines)]
    send, keep, own = run_tasks(n, plan, left_ops, blocks)
    send, arrays = lax.optimization_barrier((send, [block[0] for block in blocks]))
    correlation = correlate(arrays)
    mine, total, *sends = add_chip(keep, own, exchange(send, n, 1))
    received = [exchange(sends[j - 1], n, 2 * j) for j in reversed(range(1, n // 2))]
    product, projected = add_all(mine, total, received)
    return product, correlation, projected


def solution(mesh):
    return jax.shard_map(
        functools.partial(body, mesh.shape["op"]),
        mesh=mesh,
        in_specs=(
            P(("groups", "op"), None, None, None),
            P(("groups", "op"), None, None),
            P(("groups", "op"), None, None),
            P(("groups", "op"), None),
        ),
        out_specs=(P(("groups", "op"), None, None, None), P("groups", None), P("groups", None)),
        check_vma=False,
    )
```

```python
import functools

import jax
import jax.numpy as jnp
from jax import lax
from jax.experimental import pallas as pl
from jax.experimental.pallas import tpu as pltpu
from jax.sharding import PartitionSpec as P

MIB = 1024 * 1024
TAIL = 16
TRIALS = 2
CHUNK = 48
PAIRS = 24
AHEAD = 3


def exchange(value, n, mask):
    return lax.ppermute(value, "op", [(i, i ^ mask) for i in range(n)])


def chip_at(place, chips):
    return 2 * place if place < chips // 2 else 2 * (chips - place) - 1


def ring_step(value, n):
    chips = n // 2
    order = [chip_at(place, chips) for place in range(chips)]
    pairs = []
    for place, chip in enumerate(order):
        pairs.append((2 * chip, 2 * order[(place + 1) % chips]))
        pairs.append((2 * chip + 1, 2 * order[(place - 1) % chips] + 1))
    return lax.ppermute(value, "op", pairs)


def owner_of(step, swapped, half, n):
    chips = n // 2
    me = lax.axis_index("op")
    chip, core = me // 2, lax.rem(me, 2)
    odd = lax.rem(chip, 2)
    mine = jnp.where(odd == 0, chip // 2, chips - 1 - chip // 2)
    line = 1 - core if swapped else core
    place = lax.rem(mine + (2 * line - 1) * step + 2 * chips, chips)
    there = jnp.where(place < chips // 2, 2 * place, 2 * (chips - place) - 1)
    return 2 * there + (line if half == 0 else 1 - line)


def split3(value):
    lanes = lax.broadcasted_iota(jnp.int32, (8, 128), 1)
    high = value.astype(jnp.bfloat16).astype(jnp.float32)
    middle = (value - high).astype(jnp.bfloat16).astype(jnp.float32)
    low = (value - high - middle).astype(jnp.bfloat16).astype(jnp.float32)
    return jnp.where(lanes < 2, high, jnp.where(lanes < 4, middle, low))


def tail_of(first, second):
    return jnp.concatenate([first, second], axis=0).astype(jnp.bfloat16)


def matrix_of(values, repeats=1):
    rows = lax.broadcasted_iota(jnp.int32, (8, 128), 0)
    lanes = lax.broadcasted_iota(jnp.int32, (8, 128), 1)
    total = jnp.zeros((8, 128), jnp.float32)
    for (i, j), value in values.items():
        for repeat in range(repeats):
            total = total + jnp.where((rows == i) & (lanes == j + 2 * repeat), value, 0.0)
    return total


def fold(value):
    return value.reshape(16, 8, 128).sum(axis=0)


def fits(n):
    return n <= 16


def phases_of(n):
    return 1


def run_of(slots, n):
    return 4 if slots >= 8 * n else 2


def source_places(slots, n):
    most = slots + min(slots, n) * (run_of(slots, n) - 1) + phases_of(n) * CHUNK
    return -(-most // CHUNK) * CHUNK


def place_of(chip, chips):
    half = jnp.floor(chip * 0.5)
    return jnp.where(chip == 2.0 * half, half, chips - 1.0 - half)


def plan_kernel(n, terms, tasks_ref, plan_ref):
    slots = tasks_ref.shape[1]
    places = plan_ref.shape[1]
    chips = n // 2
    phases = phases_of(n)
    rows = tasks_ref[...].astype(jnp.float32)
    source, target, term, live = rows[0:1], rows[1:2], rows[2:3], rows[3:4]
    lane = lax.broadcasted_iota(jnp.int32, (1, slots), 1).astype(jnp.float32)
    number = lax.broadcasted_iota(jnp.int32, (1, places), 1).astype(jnp.float32)
    at = lax.broadcasted_iota(jnp.int32, (slots, places), 1).astype(jnp.float32)
    me = lax.axis_index("op")
    mine = place_of((jnp.zeros((1, slots), jnp.int32) + me // 2).astype(jnp.float32), float(chips))
    gap = place_of(jnp.floor(source * 0.5), float(chips)) - mine
    up = jnp.where(gap < 0, gap + chips, gap)
    far = jnp.minimum(up, chips - up)
    phase = jnp.clip(far - 1.0, 0.0, phases - 1.0)

    def column(*values):
        pad = [jnp.zeros((8 - len(values), slots), jnp.float32)]
        return jnp.transpose(jnp.concatenate(list(values) + pad, axis=0))

    def sort(sector, parts, unit, whole):
        keys = parts * n
        index = lax.broadcasted_iota(jnp.int32, (keys, slots), 0).astype(jnp.float32)
        part = phase if parts > 1 else jnp.zeros_like(phase)
        key = jnp.where(live > 0, part * n + sector, float(keys))
        columns = column(key, lane)
        earlier = jnp.where((columns[:, 0:1] == key) & (columns[:, 1:2] < lane), 1.0, 0.0)
        count = jnp.sum(jnp.where(index == key, 1.0, 0.0), axis=1, keepdims=True)
        padded = jnp.ceil(count / unit) * unit
        place = jnp.sum(earlier, axis=0, keepdims=True)
        start = jnp.zeros((1, 1), jnp.float32)
        starts = [start]
        for p in range(parts):
            lengths = padded[p * n : (p + 1) * n]
            before = jnp.where(index[p * n : (p + 1) * n] < key, lengths, 0.0)
            place = place + jnp.where(part == p, start * whole + jnp.sum(before, axis=0, keepdims=True), 0.0)
            start = start + jnp.ceil(jnp.sum(lengths, axis=0, keepdims=True) / whole)
            starts.append(start)
        return jnp.where(live > 0, place, -1.0), starts

    by_source, source_starts = sort(source, phases, float(run_of(slots, n)), float(CHUNK))
    by_target, target_starts = sort(target, 1, 2.0, 2.0 * PAIRS)
    columns = column(by_source, by_target, lane, source, term, target)

    def picker(places_column):
        hit = places_column == at

        def pick(values, other):
            found = jnp.sum(jnp.where(hit, values - other, 0.0), axis=0, keepdims=True)
            return (found + other).astype(jnp.int32)

        return pick

    own = (jnp.zeros((1, 1), jnp.int32) + me).astype(jnp.float32)
    pick = picker(columns[:, 0:1])
    plan_ref[0:1] = pick(columns[:, 2:3], 0.0)
    plan_ref[1:2] = pick(columns[:, 3:4], own)
    pick = picker(columns[:, 1:2])
    plan_ref[2:3] = pick(columns[:, 0:1], -1.0)
    plan_ref[3:4] = pick(columns[:, 4:5], float(terms))
    plan_ref[4:5] = pick(columns[:, 5:6], float(n))
    turns = jnp.zeros((1, places), jnp.float32)
    for p, start in enumerate(source_starts + [target_starts[1]]):
        turns = turns + jnp.where(number == p, start, 0.0)
    plan_ref[5:6] = turns.astype(jnp.int32)
    plan_ref[6:8] = jnp.zeros((2, places), jnp.int32)


def make_plan(tasks, n, terms):
    most = source_places(tasks.shape[1], n) + 2 * PAIRS
    return pl.pallas_call(
        functools.partial(plan_kernel, n, terms),
        out_shape=jax.ShapeDtypeStruct((8, -(-most // 128) * 128), jnp.int32),
        compiler_params=pltpu.CompilerParams(vmem_limit_bytes=16 * MIB),
    )(tasks)


def stage_kernel(left_ref, held_ref, sem):
    copy = pltpu.make_async_copy(left_ref, held_ref, sem)
    copy.start()
    copy.wait()


def stage(left_ops, n):
    if not fits(n):
        return left_ops
    return pl.pallas_call(
        stage_kernel,
        in_specs=[pl.BlockSpec(memory_space=pltpu.HBM)],
        out_specs=pl.BlockSpec(memory_space=pltpu.VMEM),
        out_shape=jax.ShapeDtypeStruct(left_ops.shape, left_ops.dtype),
        scratch_shapes=[pltpu.SemaphoreType.DMA],
        compiler_params=pltpu.CompilerParams(vmem_limit_bytes=42 * MIB),
    )(left_ops)


def block_copies(n, kinds, blocks, trial, right, sem, which):
    copies = []
    for b, kind in enumerate(kinds):
        owner = owner_of(*kind, n)
        per = blocks[b].shape[0] - TRIALS
        if which == 0:
            source, to = blocks[b].at[pl.ds(0, TRIALS)], trial.at[owner]
        else:
            source, to = blocks[b].at[pl.ds(TRIALS, per)], right.at[pl.ds(owner * per, per)]
        copies.append(pltpu.make_async_copy(source, to, sem.at[b, which]))
    return copies


def make_halves(n, plan_ref, left_ref, trial, halves, fetched):
    turns = plan_ref[5, 1]
    run = run_of(left_ref.shape[0], n)

    def fetch(turn):
        left, left_sem = fetched
        at = lax.rem(turn, AHEAD)
        for u in range(CHUNK):
            slot = plan_ref[0, turn * CHUNK + u]
            pltpu.make_async_copy(left_ref.at[slot], left.at[at, u], left_sem.at[at]).start()

    def start():
        for turn in range(AHEAD - 1) if fetched else ():

            @pl.when(turn < turns)
            def _():
                fetch(turn)

    def turn_of(turn, carry):
        if fetched:
            left, left_sem = fetched

            @pl.when(turn + AHEAD - 1 < turns)
            def _():
                fetch(turn + AHEAD - 1)

            at = lax.rem(turn, AHEAD)
            pltpu.make_async_copy(left_ref.at[pl.ds(0, CHUNK)], left.at[at], left_sem.at[at]).wait()
        place = turn * CHUNK
        for r in range(0, CHUNK, run):
            source = plan_ref[1, place + r]
            vectors = jnp.concatenate([trial[source, 0], trial[source, 1]], axis=1)
            if fetched:
                rows = left[at, r : r + run].reshape(run * 128, 128)
            else:
                rows = jnp.concatenate([left_ref[plan_ref[0, place + r + u]] for u in range(run)], axis=0)
            half = jnp.dot(rows, vectors, preferred_element_type=jnp.float32).astype(jnp.bfloat16)
            for u in range(run):
                halves[place + r + u, 0] = half[u * 128 : (u + 1) * 128, :128]
                halves[place + r + u, 1] = half[u * 128 : (u + 1) * 128, 128:]
        return carry

    return start, lambda: lax.fori_loop(0, turns, turn_of, 0)


def tasks_kernel(n, kinds, plan_ref, left_ref, *refs):
    blocks, refs = refs[: len(kinds)], refs[len(kinds) :]
    send_ref, keep_ref, own_ref, halves, trial, right, acc, block_sem, *fetched = refs
    start, products = make_halves(n, plan_ref, left_ref, trial, halves, fetched)
    right[right.shape[0] - 1] = jnp.zeros((128, 128), jnp.bfloat16)
    start()
    if fits(n):
        moves = ([], [])
        for b, kind in enumerate(kinds):
            owner = owner_of(*kind, n)
            per = blocks[b].shape[0] - TRIALS
            trial[owner] = blocks[b][0:TRIALS]
            right[pl.ds(owner * per, per)] = blocks[b][TRIALS:]
    else:
        moves = [block_copies(n, kinds, blocks, trial, right, block_sem, which) for which in range(2)]
        for copy in moves[0] + moves[1]:
            copy.start()

    def clear(s, carry):
        acc[s] = jnp.zeros((256, 128), jnp.float32)
        return carry

    lax.fori_loop(0, n, clear, 0)
    for copy in moves[0]:
        copy.wait()
    products()
    for copy in moves[1]:
        copy.wait()

    def target_turn(turn, carry):
        first = turn * 2 * PAIRS
        for u in range(0, 2 * PAIRS, 2):
            place = first + u
            one = plan_ref[2, place]
            two = plan_ref[2, place + 1]
            one, two = jnp.maximum(one, 0), jnp.where(two < 0, jnp.maximum(one, 0), two)
            pair = jnp.concatenate(
                [
                    jnp.concatenate([halves[one, 0], halves[two, 0]], axis=1),
                    jnp.concatenate([halves[one, 1], halves[two, 1]], axis=1),
                ],
                axis=0,
            )
            rights = jnp.concatenate([right[plan_ref[3, place]], right[plan_ref[3, place + 1]]], axis=0)
            term = jnp.dot(pair, rights, preferred_element_type=jnp.float32)
            target = plan_ref[4, place]
            acc[target] = acc[target] + term
        return carry

    lax.fori_loop(0, plan_ref[5, 2], target_turn, 0)
    me = lax.axis_index("op")

    def dots(s, carry):
        t0 = trial[s, 0].astype(jnp.float32)
        t1 = trial[s, 1].astype(jnp.float32)
        a0 = acc[s, 0:128, :]
        a1 = acc[s, 128:256, :]
        p00, p01, p10, p11 = carry
        return p00 + fold(t0 * a0), p01 + fold(t0 * a1), p10 + fold(t1 * a0), p11 + fold(t1 * a1)

    zero = jnp.zeros((8, 128), jnp.float32)
    sums = lax.fori_loop(0, n, dots, (zero,) * 4)
    p00, p01, p10, p11 = [jnp.sum(x) for x in sums]

    def pack(j, carry):
        mine = jnp.bitwise_xor(me, 2 * j)
        keep_ref[j] = acc[mine]
        send_ref[pl.ds(pl.multiple_of(j * 256, 256), 256), :] = acc[jnp.bitwise_xor(mine, 1)].astype(jnp.bfloat16)
        return carry

    lax.fori_loop(0, n // 2, pack, 0)
    own = split3(matrix_of({(0, 0): p00, (0, 1): p01, (1, 0): p10, (1, 1): p11}, 3))
    own_ref[...] = own
    send_ref[n // 2 * 256 :, :] = tail_of(own, jnp.zeros_like(own))


def run_tasks(n, plan, left_ops, blocks):
    slots = left_ops.shape[0]
    terms_per = blocks[0][0].shape[0] - TRIALS
    kinds = tuple(block[1:] for block in blocks)
    vmem, hbm = pl.BlockSpec(memory_space=pltpu.VMEM), pl.BlockSpec(memory_space=pltpu.HBM)
    given = vmem if fits(n) else hbm
    fetched = [] if fits(n) else [
        pltpu.VMEM((AHEAD, CHUNK, 128, 128), jnp.bfloat16),
        pltpu.SemaphoreType.DMA((AHEAD,)),
    ]
    return pl.pallas_call(
        functools.partial(tasks_kernel, n, kinds),
        out_shape=(
            jax.ShapeDtypeStruct((n // 2 * 256 + TAIL, 128), jnp.bfloat16),
            jax.ShapeDtypeStruct((n // 2, 256, 128), jnp.float32),
            jax.ShapeDtypeStruct((8, 128), jnp.float32),
        ),
        in_specs=[pl.BlockSpec(memory_space=pltpu.SMEM)] + [given] * (1 + len(blocks)),
        out_specs=(vmem,) * 3,
        scratch_shapes=[
            pltpu.VMEM((source_places(slots, n), 2, 128, 128), jnp.bfloat16),
            pltpu.VMEM((n, TRIALS, 128, 128), jnp.bfloat16),
            pltpu.VMEM((n * terms_per + 1, 128, 128), jnp.bfloat16),
            pltpu.VMEM((n + 1, 256, 128), jnp.float32),
            pltpu.SemaphoreType.DMA((len(blocks), 2)),
        ]
        + fetched,
        compiler_params=pltpu.CompilerParams(vmem_limit_bytes=(30 if fits(n) else 58) * MIB),
        cost_estimate=pl.CostEstimate(
            flops=slots * 8 * 128**3, bytes_accessed=slots * 32768 + n * 450000, transcendentals=0
        ),
    )(plan, left_ops, *[block[0] for block in blocks])


def join_kernel(trial_ref, right_ref, block_ref, right, sem):
    copies = [
        pltpu.make_async_copy(right_ref, right, sem.at[0]),
        pltpu.make_async_copy(trial_ref.at[0], block_ref.at[pl.ds(0, TRIALS)], sem.at[1]),
    ]
    for copy in copies:
        copy.start()
    copies[0].wait()
    for k in range(right.shape[0]):
        block_ref[TRIALS + k] = jnp.transpose(right[k])
    copies[1].wait()


def join(trial, right_ops):
    hbm = pl.BlockSpec(memory_space=pltpu.HBM)
    return pl.pallas_call(
        join_kernel,
        out_shape=jax.ShapeDtypeStruct((TRIALS + right_ops.shape[0], 128, 128), jnp.bfloat16),
        in_specs=[hbm, hbm],
        out_specs=pl.BlockSpec(memory_space=pltpu.VMEM),
        scratch_shapes=[pltpu.VMEM(right_ops.shape, jnp.bfloat16), pltpu.SemaphoreType.DMA((2,))],
        compiler_params=pltpu.CompilerParams(vmem_limit_bytes=59 * MIB),
    )(trial, right_ops)


def corr_kernel(*refs):
    blocks, corr_ref = refs[:-1], refs[-1]
    total = [jnp.zeros((8, 128), jnp.float32)] * 3
    for ref in blocks:
        t0, t1 = ref[0].astype(jnp.float32), ref[1].astype(jnp.float32)
        total = [total[0] + fold(t0 * t0), total[1] + fold(t0 * t1), total[2] + fold(t1 * t1)]
    c00, c01, c11 = [jnp.sum(x) for x in total]
    corr_ref[...] = matrix_of({(0, 0): c00, (0, 1): c01, (1, 0): c01, (1, 1): c11})[0:2, 0:2]


def correlate(blocks):
    return pl.pallas_call(
        corr_kernel,
        out_shape=jax.ShapeDtypeStruct((2, 2), jnp.float32),
        compiler_params=pltpu.CompilerParams(vmem_limit_bytes=16 * MIB),
    )(*blocks)


def chip_kernel(chips, keep_ref, own_ref, received_ref, mine_ref, total_ref, *sends):
    total = jnp.concatenate([own_ref[...], received_ref[chips * 256 :, :].astype(jnp.float32)[0:8]], axis=0)
    total_ref[...] = total
    tail = total.astype(jnp.bfloat16)
    for j in range(chips):
        value = keep_ref[j] + received_ref[j * 256 : (j + 1) * 256, :].astype(jnp.float32)
        if j == 0:
            mine_ref[...] = value
        else:
            sends[j - 1][0:256, :] = value.astype(jnp.bfloat16)
            sends[j - 1][256:, :] = tail


def add_chip(keep, own, received):
    chips = keep.shape[0]
    return pl.pallas_call(
        functools.partial(chip_kernel, chips),
        out_shape=(jax.ShapeDtypeStruct((256, 128), jnp.float32), jax.ShapeDtypeStruct((16, 128), jnp.float32))
        + (jax.ShapeDtypeStruct((256 + TAIL, 128), jnp.bfloat16),) * (chips - 1),
        compiler_params=pltpu.CompilerParams(vmem_limit_bytes=16 * MIB),
    )(keep, own, received)


def last_kernel(mine_ref, total_ref, *refs):
    received, (product_ref, projected_ref) = refs[:-2], refs[-2:]
    value, total = mine_ref[...], total_ref[...]
    for ref in received:
        value = value + ref[0:256, :].astype(jnp.float32)
        total = total + ref[256:, :].astype(jnp.float32)
    product_ref[0, 0] = value[0:128]
    product_ref[0, 1] = value[128:256]
    total = total[0:8] + total[8:16]
    projected_ref[...] = total[0:2, 0:2] + total[0:2, 2:4] + total[0:2, 4:6]


def add_all(mine, total, received):
    return pl.pallas_call(
        last_kernel,
        out_shape=(
            jax.ShapeDtypeStruct((1, 2, 128, 128), jnp.float32),
            jax.ShapeDtypeStruct((2, 2), jnp.float32),
        ),
        compiler_params=pltpu.CompilerParams(vmem_limit_bytes=16 * MIB),
    )(mine, total, *received)


def body(n, trial, left_ops, right_ops, task_list):
    steps = n // 4
    own = join(trial, right_ops)
    plan = make_plan(task_list.T, n, n * right_ops.shape[0])
    left_ops = stage(left_ops, n)
    lines = [own, exchange(own, n, 1)]
    blocks = [(value, 0, False, half) for half, value in enumerate(lines)]
    for step in range(1, steps + 1):
        if step == 2:
            lines[0], plan = lax.optimization_barrier((lines[0], plan))
        for half in range(2):
            lines[half] = ring_step(lines[half], n)
            blocks.append((lines[half], step, False, half))
        if step < steps:
            blocks += [(exchange(value, n, 1), step, True, half) for half, value in enumerate(lines)]
    send, keep, own = run_tasks(n, plan, left_ops, blocks)
    send, arrays = lax.optimization_barrier((send, [block[0] for block in blocks]))
    correlation = correlate(arrays)
    mine, total, *sends = add_chip(keep, own, exchange(send, n, 1))
    received = [exchange(sends[j - 1], n, 2 * j) for j in reversed(range(1, n // 2))]
    product, projected = add_all(mine, total, received)
    return product, correlation, projected


def solution(mesh):
    return jax.shard_map(
        functools.partial(body, mesh.shape["op"]),
        mesh=mesh,
        in_specs=(
            P(("groups", "op"), None, None, None),
            P(("groups", "op"), None, None),
            P(("groups", "op"), None, None),
            P(("groups", "op"), None),
        ),
        out_specs=(P(("groups", "op"), None, None, None), P("groups", None), P("groups", None)),
        check_vma=False,
    )
```

```python
import functools

import jax
import jax.numpy as jnp
from jax import lax
from jax.experimental import pallas as pl
from jax.experimental.pallas import tpu as pltpu
from jax.sharding import PartitionSpec as P

MIB = 1024 * 1024
TAIL = 16
TRIALS = 2
CHUNK = 48
PAIRS = 24
AHEAD = 3


def exchange(value, n, mask):
    return lax.ppermute(value, "op", [(i, i ^ mask) for i in range(n)])


def chip_at(place, chips):
    return 2 * place if place < chips // 2 else 2 * (chips - place) - 1


def ring_step(value, n):
    chips = n // 2
    order = [chip_at(place, chips) for place in range(chips)]
    pairs = []
    for place, chip in enumerate(order):
        pairs.append((2 * chip, 2 * order[(place + 1) % chips]))
        pairs.append((2 * chip + 1, 2 * order[(place - 1) % chips] + 1))
    return lax.ppermute(value, "op", pairs)


def owner_of(step, swapped, half, n):
    chips = n // 2
    me = lax.axis_index("op")
    chip, core = me // 2, lax.rem(me, 2)
    odd = lax.rem(chip, 2)
    mine = jnp.where(odd == 0, chip // 2, chips - 1 - chip // 2)
    line = 1 - core if swapped else core
    place = lax.rem(mine + (2 * line - 1) * step + 2 * chips, chips)
    there = jnp.where(place < chips // 2, 2 * place, 2 * (chips - place) - 1)
    return 2 * there + (line if half == 0 else 1 - line)


def split3(value):
    lanes = lax.broadcasted_iota(jnp.int32, (8, 128), 1)
    high = value.astype(jnp.bfloat16).astype(jnp.float32)
    middle = (value - high).astype(jnp.bfloat16).astype(jnp.float32)
    low = (value - high - middle).astype(jnp.bfloat16).astype(jnp.float32)
    return jnp.where(lanes < 2, high, jnp.where(lanes < 4, middle, low))


def tail_of(first, second):
    return jnp.concatenate([first, second], axis=0).astype(jnp.bfloat16)


def matrix_of(values, repeats=1):
    rows = lax.broadcasted_iota(jnp.int32, (8, 128), 0)
    lanes = lax.broadcasted_iota(jnp.int32, (8, 128), 1)
    total = jnp.zeros((8, 128), jnp.float32)
    for (i, j), value in values.items():
        for repeat in range(repeats):
            total = total + jnp.where((rows == i) & (lanes == j + 2 * repeat), value, 0.0)
    return total


def fold(value):
    return value.reshape(16, 8, 128).sum(axis=0)


def fits(n):
    return n <= 16


def phases_of(n):
    return 1


def run_of(slots, n):
    return 4 if slots >= 8 * n else 2


def source_places(slots, n):
    most = slots + min(slots, n) * (run_of(slots, n) - 1) + phases_of(n) * CHUNK
    return -(-most // CHUNK) * CHUNK


def place_of(chip, chips):
    half = jnp.floor(chip * 0.5)
    return jnp.where(chip == 2.0 * half, half, chips - 1.0 - half)


def plan_kernel(n, terms, tasks_ref, plan_ref):
    slots = tasks_ref.shape[1]
    places = plan_ref.shape[1]
    chips = n // 2
    phases = phases_of(n)
    rows = tasks_ref[...].astype(jnp.float32)
    source, target, term, live = rows[0:1], rows[1:2], rows[2:3], rows[3:4]
    lane = lax.broadcasted_iota(jnp.int32, (1, slots), 1).astype(jnp.float32)
    number = lax.broadcasted_iota(jnp.int32, (1, places), 1).astype(jnp.float32)
    at = lax.broadcasted_iota(jnp.int32, (slots, places), 1).astype(jnp.float32)
    me = lax.axis_index("op")
    mine = place_of((jnp.zeros((1, slots), jnp.int32) + me // 2).astype(jnp.float32), float(chips))
    gap = place_of(jnp.floor(source * 0.5), float(chips)) - mine
    up = jnp.where(gap < 0, gap + chips, gap)
    far = jnp.minimum(up, chips - up)
    phase = jnp.clip(far - 1.0, 0.0, phases - 1.0)

    def column(*values):
        pad = [jnp.zeros((8 - len(values), slots), jnp.float32)]
        return jnp.transpose(jnp.concatenate(list(values) + pad, axis=0))

    def sort(sector, parts, unit, whole):
        keys = parts * n
        index = lax.broadcasted_iota(jnp.int32, (keys, slots), 0).astype(jnp.float32)
        part = phase if parts > 1 else jnp.zeros_like(phase)
        key = jnp.where(live > 0, part * n + sector, float(keys))
        columns = column(key, lane)
        earlier = jnp.where((columns[:, 0:1] == key) & (columns[:, 1:2] < lane), 1.0, 0.0)
        count = jnp.sum(jnp.where(index == key, 1.0, 0.0), axis=1, keepdims=True)
        padded = jnp.ceil(count / unit) * unit
        place = jnp.sum(earlier, axis=0, keepdims=True)
        start = jnp.zeros((1, 1), jnp.float32)
        starts = [start]
        for p in range(parts):
            lengths = padded[p * n : (p + 1) * n]
            before = jnp.where(index[p * n : (p + 1) * n] < key, lengths, 0.0)
            place = place + jnp.where(part == p, start * whole + jnp.sum(before, axis=0, keepdims=True), 0.0)
            start = start + jnp.ceil(jnp.sum(lengths, axis=0, keepdims=True) / whole)
            starts.append(start)
        return jnp.where(live > 0, place, -1.0), starts

    by_source, source_starts = sort(source, phases, float(run_of(slots, n)), float(CHUNK))
    by_target, target_starts = sort(target, 1, 2.0, 2.0 * PAIRS)
    columns = column(by_source, by_target, lane, source, term, target)

    def picker(places_column):
        hit = places_column == at

        def pick(values, other):
            found = jnp.sum(jnp.where(hit, values - other, 0.0), axis=0, keepdims=True)
            return (found + other).astype(jnp.int32)

        return pick

    own = (jnp.zeros((1, 1), jnp.int32) + me).astype(jnp.float32)
    pick = picker(columns[:, 0:1])
    plan_ref[0:1] = pick(columns[:, 2:3], 0.0)
    plan_ref[1:2] = pick(columns[:, 3:4], own)
    pick = picker(columns[:, 1:2])
    plan_ref[2:3] = pick(columns[:, 0:1], -1.0)
    plan_ref[3:4] = pick(columns[:, 4:5], float(terms))
    plan_ref[4:5] = pick(columns[:, 5:6], float(n))
    turns = jnp.zeros((1, places), jnp.float32)
    for p, start in enumerate(source_starts + [target_starts[1]]):
        turns = turns + jnp.where(number == p, start, 0.0)
    plan_ref[5:6] = turns.astype(jnp.int32)
    plan_ref[6:8] = jnp.zeros((2, places), jnp.int32)


def make_plan(tasks, n, terms):
    most = source_places(tasks.shape[1], n) + 2 * PAIRS
    return pl.pallas_call(
        functools.partial(plan_kernel, n, terms),
        out_shape=jax.ShapeDtypeStruct((8, -(-most // 128) * 128), jnp.int32),
        compiler_params=pltpu.CompilerParams(vmem_limit_bytes=16 * MIB),
    )(tasks)


def stage_kernel(left_ref, held_ref, sem):
    copy = pltpu.make_async_copy(left_ref, held_ref, sem)
    copy.start()
    copy.wait()


def stage(left_ops, n):
    if not fits(n):
        return left_ops
    return pl.pallas_call(
        stage_kernel,
        in_specs=[pl.BlockSpec(memory_space=pltpu.HBM)],
        out_specs=pl.BlockSpec(memory_space=pltpu.VMEM),
        out_shape=jax.ShapeDtypeStruct(left_ops.shape, left_ops.dtype),
        scratch_shapes=[pltpu.SemaphoreType.DMA],
        compiler_params=pltpu.CompilerParams(vmem_limit_bytes=42 * MIB),
    )(left_ops)


def block_copies(n, kinds, trials, rights, trial, right, sem):
    copies = ([], [])
    for b, kind in enumerate(kinds):
        owner = owner_of(*kind, n)
        per = rights[b].shape[0]
        copies[0].append(pltpu.make_async_copy(trials[b], trial.at[owner], sem.at[b, 0]))
        copies[1].append(pltpu.make_async_copy(rights[b], right.at[pl.ds(owner * per, per)], sem.at[b, 1]))
    return copies


def make_halves(n, plan_ref, left_ref, trial, halves, fetched):
    turns = plan_ref[5, 1]
    run = run_of(left_ref.shape[0], n)

    def fetch(turn):
        left, left_sem = fetched
        at = lax.rem(turn, AHEAD)
        for u in range(CHUNK):
            slot = plan_ref[0, turn * CHUNK + u]
            pltpu.make_async_copy(left_ref.at[slot], left.at[at, u], left_sem.at[at]).start()

    def start():
        for turn in range(AHEAD - 1) if fetched else ():

            @pl.when(turn < turns)
            def _():
                fetch(turn)

    def turn_of(turn, carry):
        if fetched:
            left, left_sem = fetched

            @pl.when(turn + AHEAD - 1 < turns)
            def _():
                fetch(turn + AHEAD - 1)

            at = lax.rem(turn, AHEAD)
            pltpu.make_async_copy(left_ref.at[pl.ds(0, CHUNK)], left.at[at], left_sem.at[at]).wait()
        place = turn * CHUNK
        for r in range(0, CHUNK, run):
            source = plan_ref[1, place + r]
            vectors = jnp.concatenate([trial[source, 0], trial[source, 1]], axis=1)
            if fetched:
                rows = left[at, r : r + run].reshape(run * 128, 128)
            else:
                rows = jnp.concatenate([left_ref[plan_ref[0, place + r + u]] for u in range(run)], axis=0)
            half = jnp.dot(rows, vectors, preferred_element_type=jnp.float32).astype(jnp.bfloat16)
            for u in range(run):
                halves[place + r + u, 0] = half[u * 128 : (u + 1) * 128, :128]
                halves[place + r + u, 1] = half[u * 128 : (u + 1) * 128, 128:]
        return carry

    return start, lambda: lax.fori_loop(0, turns, turn_of, 0)


def tasks_kernel(n, kinds, plan_ref, left_ref, *refs):
    count = len(kinds)
    trials, rights, refs = refs[:count], refs[count : 2 * count], refs[2 * count :]
    send_ref, keep_ref, own_ref, halves, trial, right, acc, block_sem, *fetched = refs
    start, products = make_halves(n, plan_ref, left_ref, trial, halves, fetched)
    right[right.shape[0] - 1] = jnp.zeros((128, 128), jnp.bfloat16)
    start()
    if fits(n):
        moves = ([], [])
        for b, kind in enumerate(kinds):
            owner = owner_of(*kind, n)
            per = rights[b].shape[0]
            trial[owner] = trials[b][...]
            right[pl.ds(owner * per, per)] = rights[b][...]
    else:
        moves = block_copies(n, kinds, trials, rights, trial, right, block_sem)
        for copy in moves[0] + moves[1]:
            copy.start()

    def clear(s, carry):
        acc[s] = jnp.zeros((256, 128), jnp.float32)
        return carry

    lax.fori_loop(0, n, clear, 0)
    for copy in moves[0]:
        copy.wait()
    products()
    for copy in moves[1]:
        copy.wait()

    def target_turn(turn, carry):
        first = turn * 2 * PAIRS
        for u in range(0, 2 * PAIRS, 2):
            place = first + u
            one = plan_ref[2, place]
            two = plan_ref[2, place + 1]
            one, two = jnp.maximum(one, 0), jnp.where(two < 0, jnp.maximum(one, 0), two)
            pair = jnp.concatenate(
                [
                    jnp.concatenate([halves[one, 0], halves[two, 0]], axis=1),
                    jnp.concatenate([halves[one, 1], halves[two, 1]], axis=1),
                ],
                axis=0,
            )
            rights = jnp.concatenate([right[plan_ref[3, place]], right[plan_ref[3, place + 1]]], axis=0)
            term = jnp.dot(pair, rights, preferred_element_type=jnp.float32)
            target = plan_ref[4, place]
            acc[target] = acc[target] + term
        return carry

    lax.fori_loop(0, plan_ref[5, 2], target_turn, 0)
    me = lax.axis_index("op")

    def dots(s, carry):
        t0 = trial[s, 0].astype(jnp.float32)
        t1 = trial[s, 1].astype(jnp.float32)
        a0 = acc[s, 0:128, :]
        a1 = acc[s, 128:256, :]
        p00, p01, p10, p11 = carry
        return p00 + fold(t0 * a0), p01 + fold(t0 * a1), p10 + fold(t1 * a0), p11 + fold(t1 * a1)

    zero = jnp.zeros((8, 128), jnp.float32)
    sums = lax.fori_loop(0, n, dots, (zero,) * 4, unroll=4)
    p00, p01, p10, p11 = [jnp.sum(x) for x in sums]

    def pack(j, carry):
        mine = jnp.bitwise_xor(me, 2 * j)
        keep_ref[j] = acc[mine]
        send_ref[pl.ds(pl.multiple_of(j * 256, 256), 256), :] = acc[jnp.bitwise_xor(mine, 1)].astype(jnp.bfloat16)
        return carry

    lax.fori_loop(0, n // 2, pack, 0, unroll=2)
    own = split3(matrix_of({(0, 0): p00, (0, 1): p01, (1, 0): p10, (1, 1): p11}, 3))
    own_ref[...] = own
    send_ref[n // 2 * 256 :, :] = tail_of(own, jnp.zeros_like(own))


def run_tasks(n, plan, left_ops, blocks):
    slots = left_ops.shape[0]
    terms_per = blocks[0][1].shape[0]
    kinds = tuple(block[2:] for block in blocks)
    vmem, hbm = pl.BlockSpec(memory_space=pltpu.VMEM), pl.BlockSpec(memory_space=pltpu.HBM)
    given = vmem if fits(n) else hbm
    fetched = [] if fits(n) else [
        pltpu.VMEM((AHEAD, CHUNK, 128, 128), jnp.bfloat16),
        pltpu.SemaphoreType.DMA((AHEAD,)),
    ]
    return pl.pallas_call(
        functools.partial(tasks_kernel, n, kinds),
        out_shape=(
            jax.ShapeDtypeStruct((n // 2 * 256 + TAIL, 128), jnp.bfloat16),
            jax.ShapeDtypeStruct((n // 2, 256, 128), jnp.float32),
            jax.ShapeDtypeStruct((8, 128), jnp.float32),
        ),
        in_specs=[pl.BlockSpec(memory_space=pltpu.SMEM)] + [given] * (1 + 2 * len(blocks)),
        out_specs=(vmem,) * 3,
        scratch_shapes=[
            pltpu.VMEM((source_places(slots, n), 2, 128, 128), jnp.bfloat16),
            pltpu.VMEM((n, TRIALS, 128, 128), jnp.bfloat16),
            pltpu.VMEM((n * terms_per + 1, 128, 128), jnp.bfloat16),
            pltpu.VMEM((n + 1, 256, 128), jnp.float32),
            pltpu.SemaphoreType.DMA((len(blocks), 2)),
        ]
        + fetched,
        compiler_params=pltpu.CompilerParams(vmem_limit_bytes=(30 if fits(n) else 58) * MIB),
        cost_estimate=pl.CostEstimate(
            flops=slots * 8 * 128**3, bytes_accessed=slots * 32768 + n * 450000, transcendentals=0
        ),
    )(plan, left_ops, *[block[0] for block in blocks], *[block[1] for block in blocks])


def transpose_kernel(right_ref, result_ref):
    for k in range(right_ref.shape[0]):
        result_ref[k] = jnp.transpose(right_ref[k])


def transposed(right_ops):
    return pl.pallas_call(
        transpose_kernel,
        out_shape=jax.ShapeDtypeStruct(right_ops.shape, right_ops.dtype),
        compiler_params=pltpu.CompilerParams(vmem_limit_bytes=16 * MIB),
    )(right_ops)


def corr_kernel(*refs):
    blocks, corr_ref = refs[:-1], refs[-1]
    total = [jnp.zeros((8, 128), jnp.float32)] * 3
    for ref in blocks:
        t0, t1 = ref[0].astype(jnp.float32), ref[1].astype(jnp.float32)
        total = [total[0] + fold(t0 * t0), total[1] + fold(t0 * t1), total[2] + fold(t1 * t1)]
    c00, c01, c11 = [jnp.sum(x) for x in total]
    corr_ref[...] = matrix_of({(0, 0): c00, (0, 1): c01, (1, 0): c01, (1, 1): c11})[0:2, 0:2]


def correlate(blocks):
    return pl.pallas_call(
        corr_kernel,
        out_shape=jax.ShapeDtypeStruct((2, 2), jnp.float32),
        compiler_params=pltpu.CompilerParams(vmem_limit_bytes=16 * MIB),
    )(*blocks)


def chip_kernel(chips, keep_ref, own_ref, received_ref, mine_ref, total_ref, *sends):
    total = jnp.concatenate([own_ref[...], received_ref[chips * 256 :, :].astype(jnp.float32)[0:8]], axis=0)
    total_ref[...] = total
    tail = total.astype(jnp.bfloat16)
    for j in range(chips):
        value = keep_ref[j] + received_ref[j * 256 : (j + 1) * 256, :].astype(jnp.float32)
        if j == 0:
            mine_ref[...] = value
        else:
            sends[j - 1][0:256, :] = value.astype(jnp.bfloat16)
            sends[j - 1][256:, :] = tail


def add_chip(keep, own, received):
    chips = keep.shape[0]
    return pl.pallas_call(
        functools.partial(chip_kernel, chips),
        out_shape=(jax.ShapeDtypeStruct((256, 128), jnp.float32), jax.ShapeDtypeStruct((16, 128), jnp.float32))
        + (jax.ShapeDtypeStruct((256 + TAIL, 128), jnp.bfloat16),) * (chips - 1),
        compiler_params=pltpu.CompilerParams(vmem_limit_bytes=16 * MIB),
    )(keep, own, received)


def last_kernel(mine_ref, total_ref, *refs):
    received, (product_ref, projected_ref) = refs[:-2], refs[-2:]
    value, total = mine_ref[...], total_ref[...]
    for ref in received:
        value = value + ref[0:256, :].astype(jnp.float32)
        total = total + ref[256:, :].astype(jnp.float32)
    product_ref[0, 0] = value[0:128]
    product_ref[0, 1] = value[128:256]
    total = total[0:8] + total[8:16]
    projected_ref[...] = total[0:2, 0:2] + total[0:2, 2:4] + total[0:2, 4:6]


def add_all(mine, total, received):
    return pl.pallas_call(
        last_kernel,
        out_shape=(
            jax.ShapeDtypeStruct((1, 2, 128, 128), jnp.float32),
            jax.ShapeDtypeStruct((2, 2), jnp.float32),
        ),
        compiler_params=pltpu.CompilerParams(vmem_limit_bytes=16 * MIB),
    )(mine, total, *received)


def body(n, trial, left_ops, right_ops, task_list):
    steps = n // 4
    plan = make_plan(task_list.T, n, n * right_ops.shape[0])
    left_ops = stage(left_ops, n)
    own = [trial[0], transposed(right_ops)]
    lines = [own, [exchange(value, n, 1) for value in own]]
    blocks = [(*values, 0, False, half) for half, values in enumerate(lines)]
    for step in range(1, steps + 1):
        if step == 2:
            lines[0][0], plan = lax.optimization_barrier((lines[0][0], plan))
        lines = [[ring_step(value, n) for value in values] for values in lines]
        blocks += [(*values, step, False, half) for half, values in enumerate(lines)]
        if step < steps:
            for half, values in enumerate(lines):
                blocks.append((*[exchange(value, n, 1) for value in values], step, True, half))
    send, keep, own = run_tasks(n, plan, left_ops, blocks)
    send, arrays = lax.optimization_barrier((send, [block[0] for block in blocks]))
    correlation = correlate(arrays)
    mine, total, *sends = add_chip(keep, own, exchange(send, n, 1))
    received = [exchange(sends[j - 1], n, 2 * j) for j in reversed(range(1, n // 2))]
    product, projected = add_all(mine, total, received)
    return product, correlation, projected


def solution(mesh):
    return jax.shard_map(
        functools.partial(body, mesh.shape["op"]),
        mesh=mesh,
        in_specs=(
            P(("groups", "op"), None, None, None),
            P(("groups", "op"), None, None),
            P(("groups", "op"), None, None),
            P(("groups", "op"), None),
        ),
        out_specs=(P(("groups", "op"), None, None, None), P("groups", None), P("groups", None)),
        check_vma=False,
    )
```

```python
import functools

import jax
import jax.numpy as jnp
from jax import lax
from jax.experimental import pallas as pl
from jax.experimental.pallas import tpu as pltpu
from jax.sharding import PartitionSpec as P

MIB = 1024 * 1024
TAIL = 16
TRIALS = 2
CHUNK = 48
PAIRS = 24
AHEAD = 3


def exchange(value, n, mask):
    return lax.ppermute(value, "op", [(i, i ^ mask) for i in range(n)])


def chip_at(place, chips):
    return 2 * place if place < chips // 2 else 2 * (chips - place) - 1


def ring_step(value, n):
    chips = n // 2
    order = [chip_at(place, chips) for place in range(chips)]
    pairs = []
    for place, chip in enumerate(order):
        pairs.append((2 * chip, 2 * order[(place + 1) % chips]))
        pairs.append((2 * chip + 1, 2 * order[(place - 1) % chips] + 1))
    return lax.ppermute(value, "op", pairs)


def owner_of(step, swapped, half, n):
    chips = n // 2
    me = lax.axis_index("op")
    chip, core = me // 2, lax.rem(me, 2)
    odd = lax.rem(chip, 2)
    mine = jnp.where(odd == 0, chip // 2, chips - 1 - chip // 2)
    line = 1 - core if swapped else core
    place = lax.rem(mine + (2 * line - 1) * step + 2 * chips, chips)
    there = jnp.where(place < chips // 2, 2 * place, 2 * (chips - place) - 1)
    return 2 * there + (line if half == 0 else 1 - line)


def split3(value):
    lanes = lax.broadcasted_iota(jnp.int32, (8, 128), 1)
    high = value.astype(jnp.bfloat16).astype(jnp.float32)
    middle = (value - high).astype(jnp.bfloat16).astype(jnp.float32)
    low = (value - high - middle).astype(jnp.bfloat16).astype(jnp.float32)
    return jnp.where(lanes < 2, high, jnp.where(lanes < 4, middle, low))


def tail_of(first, second):
    return jnp.concatenate([first, second], axis=0).astype(jnp.bfloat16)


def matrix_of(values, repeats=1):
    rows = lax.broadcasted_iota(jnp.int32, (8, 128), 0)
    lanes = lax.broadcasted_iota(jnp.int32, (8, 128), 1)
    total = jnp.zeros((8, 128), jnp.float32)
    for (i, j), value in values.items():
        for repeat in range(repeats):
            total = total + jnp.where((rows == i) & (lanes == j + 2 * repeat), value, 0.0)
    return total


def fold(value):
    return value.reshape(16, 8, 128).sum(axis=0)


def fits(n):
    return n <= 16


def phases_of(n):
    return 1


def run_of(slots, n):
    return 4 if slots >= 8 * n else 2


def source_places(slots, n):
    most = slots + min(slots, n) * (run_of(slots, n) - 1) + phases_of(n) * CHUNK
    return -(-most // CHUNK) * CHUNK


def place_of(chip, chips):
    half = jnp.floor(chip * 0.5)
    return jnp.where(chip == 2.0 * half, half, chips - 1.0 - half)


def plan_kernel(n, terms, tasks_ref, plan_ref):
    slots = tasks_ref.shape[1]
    places = plan_ref.shape[1]
    chips = n // 2
    phases = phases_of(n)
    rows = tasks_ref[...].astype(jnp.float32)
    source, target, term, live = rows[0:1], rows[1:2], rows[2:3], rows[3:4]
    lane = lax.broadcasted_iota(jnp.int32, (1, slots), 1).astype(jnp.float32)
    number = lax.broadcasted_iota(jnp.int32, (1, places), 1).astype(jnp.float32)
    at = lax.broadcasted_iota(jnp.int32, (slots, places), 1).astype(jnp.float32)
    me = lax.axis_index("op")
    mine = place_of((jnp.zeros((1, slots), jnp.int32) + me // 2).astype(jnp.float32), float(chips))
    gap = place_of(jnp.floor(source * 0.5), float(chips)) - mine
    up = jnp.where(gap < 0, gap + chips, gap)
    far = jnp.minimum(up, chips - up)
    phase = jnp.clip(far - 1.0, 0.0, phases - 1.0)

    def column(*values):
        pad = [jnp.zeros((8 - len(values), slots), jnp.float32)]
        return jnp.transpose(jnp.concatenate(list(values) + pad, axis=0))

    def sort(sector, parts, unit, whole):
        keys = parts * n
        index = lax.broadcasted_iota(jnp.int32, (keys, slots), 0).astype(jnp.float32)
        part = phase if parts > 1 else jnp.zeros_like(phase)
        key = jnp.where(live > 0, part * n + sector, float(keys))
        columns = column(key, lane)
        earlier = jnp.where((columns[:, 0:1] == key) & (columns[:, 1:2] < lane), 1.0, 0.0)
        count = jnp.sum(jnp.where(index == key, 1.0, 0.0), axis=1, keepdims=True)
        padded = jnp.ceil(count / unit) * unit
        place = jnp.sum(earlier, axis=0, keepdims=True)
        start = jnp.zeros((1, 1), jnp.float32)
        starts = [start]
        for p in range(parts):
            lengths = padded[p * n : (p + 1) * n]
            before = jnp.where(index[p * n : (p + 1) * n] < key, lengths, 0.0)
            place = place + jnp.where(part == p, start * whole + jnp.sum(before, axis=0, keepdims=True), 0.0)
            start = start + jnp.ceil(jnp.sum(lengths, axis=0, keepdims=True) / whole)
            starts.append(start)
        return jnp.where(live > 0, place, -1.0), starts

    by_source, source_starts = sort(source, phases, float(run_of(slots, n)), float(CHUNK))
    by_target, target_starts = sort(target, 1, 2.0, 2.0 * PAIRS)
    columns = column(by_source, by_target, lane, source, term, target)

    def picker(places_column):
        hit = places_column == at

        def pick(values, other):
            found = jnp.sum(jnp.where(hit, values - other, 0.0), axis=0, keepdims=True)
            return (found + other).astype(jnp.int32)

        return pick

    own = (jnp.zeros((1, 1), jnp.int32) + me).astype(jnp.float32)
    pick = picker(columns[:, 0:1])
    plan_ref[0:1] = pick(columns[:, 2:3], 0.0)
    plan_ref[1:2] = pick(columns[:, 3:4], own)
    pick = picker(columns[:, 1:2])
    plan_ref[2:3] = pick(columns[:, 0:1], -1.0)
    plan_ref[3:4] = pick(columns[:, 4:5], float(terms))
    plan_ref[4:5] = pick(columns[:, 5:6], float(n))
    turns = jnp.zeros((1, places), jnp.float32)
    for p, start in enumerate(source_starts + [target_starts[1]]):
        turns = turns + jnp.where(number == p, start, 0.0)
    plan_ref[5:6] = turns.astype(jnp.int32)
    plan_ref[6:8] = jnp.zeros((2, places), jnp.int32)


def make_plan(tasks, n, terms):
    most = source_places(tasks.shape[1], n) + 2 * PAIRS
    return pl.pallas_call(
        functools.partial(plan_kernel, n, terms),
        out_shape=jax.ShapeDtypeStruct((8, -(-most // 128) * 128), jnp.int32),
        compiler_params=pltpu.CompilerParams(vmem_limit_bytes=16 * MIB),
    )(tasks)


def stage_kernel(left_ref, held_ref, sem):
    copy = pltpu.make_async_copy(left_ref, held_ref, sem)
    copy.start()
    copy.wait()


def stage(left_ops, n):
    if not fits(n):
        return left_ops
    return pl.pallas_call(
        stage_kernel,
        in_specs=[pl.BlockSpec(memory_space=pltpu.HBM)],
        out_specs=pl.BlockSpec(memory_space=pltpu.VMEM),
        out_shape=jax.ShapeDtypeStruct(left_ops.shape, left_ops.dtype),
        scratch_shapes=[pltpu.SemaphoreType.DMA],
        compiler_params=pltpu.CompilerParams(vmem_limit_bytes=42 * MIB),
    )(left_ops)


def block_copies(n, kinds, blocks, trial, right, sem, which):
    copies = []
    for b, kind in enumerate(kinds):
        owner = owner_of(*kind, n)
        per = blocks[b].shape[0] - TRIALS
        if which == 0:
            source, to = blocks[b].at[pl.ds(0, TRIALS)], trial.at[owner]
        else:
            source, to = blocks[b].at[pl.ds(TRIALS, per)], right.at[pl.ds(owner * per, per)]
        copies.append(pltpu.make_async_copy(source, to, sem.at[b, which]))
    return copies


def make_halves(n, plan_ref, left_ref, trial, halves, fetched):
    turns = plan_ref[5, 1]
    run = run_of(left_ref.shape[0], n)

    def fetch(turn):
        left, left_sem = fetched
        at = lax.rem(turn, AHEAD)
        for u in range(CHUNK):
            slot = plan_ref[0, turn * CHUNK + u]
            pltpu.make_async_copy(left_ref.at[slot], left.at[at, u], left_sem.at[at]).start()

    def start():
        for turn in range(AHEAD - 1) if fetched else ():

            @pl.when(turn < turns)
            def _():
                fetch(turn)

    def turn_of(turn, carry):
        if fetched:
            left, left_sem = fetched

            @pl.when(turn + AHEAD - 1 < turns)
            def _():
                fetch(turn + AHEAD - 1)

            at = lax.rem(turn, AHEAD)
            pltpu.make_async_copy(left_ref.at[pl.ds(0, CHUNK)], left.at[at], left_sem.at[at]).wait()
        place = turn * CHUNK
        for r in range(0, CHUNK, run):
            source = plan_ref[1, place + r]
            vectors = jnp.concatenate([trial[source, 0], trial[source, 1]], axis=1)
            if fetched:
                rows = left[at, r : r + run].reshape(run * 128, 128)
            else:
                rows = jnp.concatenate([left_ref[plan_ref[0, place + r + u]] for u in range(run)], axis=0)
            half = jnp.dot(rows, vectors, preferred_element_type=jnp.float32).astype(jnp.bfloat16)
            for u in range(run):
                halves[place + r + u, 0] = half[u * 128 : (u + 1) * 128, :128]
                halves[place + r + u, 1] = half[u * 128 : (u + 1) * 128, 128:]
        return carry

    return start, lambda: lax.fori_loop(0, turns, turn_of, 0)


def tasks_kernel(n, kinds, plan_ref, left_ref, *refs):
    blocks, refs = refs[: len(kinds)], refs[len(kinds) :]
    send_ref, acc, own_ref, halves, trial, right, block_sem, *fetched = refs
    start, products = make_halves(n, plan_ref, left_ref, trial, halves, fetched)
    right[right.shape[0] - 1] = jnp.zeros((128, 128), jnp.bfloat16)
    start()
    if fits(n):
        moves = ([], [])
        for b, kind in enumerate(kinds):
            owner = owner_of(*kind, n)
            per = blocks[b].shape[0] - TRIALS
            trial[owner] = blocks[b][0:TRIALS]
            right[pl.ds(owner * per, per)] = blocks[b][TRIALS:]
    else:
        moves = [block_copies(n, kinds, blocks, trial, right, block_sem, which) for which in range(2)]
        for copy in moves[0] + moves[1]:
            copy.start()

    def clear(s, carry):
        acc[s] = jnp.zeros((256, 128), jnp.float32)
        return carry

    lax.fori_loop(0, n, clear, 0)
    for copy in moves[0]:
        copy.wait()
    products()
    for copy in moves[1]:
        copy.wait()

    def target_turn(turn, carry):
        first = turn * 2 * PAIRS
        for u in range(0, 2 * PAIRS, 2):
            place = first + u
            one = plan_ref[2, place]
            two = plan_ref[2, place + 1]
            one, two = jnp.maximum(one, 0), jnp.where(two < 0, jnp.maximum(one, 0), two)
            pair = jnp.concatenate(
                [
                    jnp.concatenate([halves[one, 0], halves[two, 0]], axis=1),
                    jnp.concatenate([halves[one, 1], halves[two, 1]], axis=1),
                ],
                axis=0,
            )
            rights = jnp.concatenate([right[plan_ref[3, place]], right[plan_ref[3, place + 1]]], axis=1)
            term = lax.dot_general(
                pair, rights, (((1,), (1,)), ((), ())), preferred_element_type=jnp.float32
            )
            target = plan_ref[4, place]
            acc[target] = acc[target] + term
        return carry

    lax.fori_loop(0, plan_ref[5, 2], target_turn, 0)
    me = lax.axis_index("op")

    def dots(s, carry):
        t0 = trial[s, 0].astype(jnp.float32)
        t1 = trial[s, 1].astype(jnp.float32)
        a0 = acc[s, 0:128, :]
        a1 = acc[s, 128:256, :]
        p00, p01, p10, p11 = carry
        return p00 + fold(t0 * a0), p01 + fold(t0 * a1), p10 + fold(t1 * a0), p11 + fold(t1 * a1)

    zero = jnp.zeros((8, 128), jnp.float32)
    sums = lax.fori_loop(0, n, dots, (zero,) * 4, unroll=4)
    p00, p01, p10, p11 = [jnp.sum(x) for x in sums]

    def pack(j, carry):
        mine = jnp.bitwise_xor(me, 2 * j)
        send_ref[pl.ds(pl.multiple_of(j * 256, 256), 256), :] = acc[jnp.bitwise_xor(mine, 1)].astype(jnp.bfloat16)
        return carry

    lax.fori_loop(0, n // 2, pack, 0, unroll=2)
    own = split3(matrix_of({(0, 0): p00, (0, 1): p01, (1, 0): p10, (1, 1): p11}, 3))
    own_ref[...] = own
    send_ref[n // 2 * 256 :, :] = tail_of(own, jnp.zeros_like(own))


def run_tasks(n, plan, left_ops, blocks):
    slots = left_ops.shape[0]
    terms_per = blocks[0][0].shape[0] - TRIALS
    kinds = tuple(block[1:] for block in blocks)
    vmem, hbm = pl.BlockSpec(memory_space=pltpu.VMEM), pl.BlockSpec(memory_space=pltpu.HBM)
    given = vmem if fits(n) else hbm
    fetched = [] if fits(n) else [
        pltpu.VMEM((AHEAD, CHUNK, 128, 128), jnp.bfloat16),
        pltpu.SemaphoreType.DMA((AHEAD,)),
    ]
    return pl.pallas_call(
        functools.partial(tasks_kernel, n, kinds),
        out_shape=(
            jax.ShapeDtypeStruct((n // 2 * 256 + TAIL, 128), jnp.bfloat16),
            jax.ShapeDtypeStruct((n + 1, 256, 128), jnp.float32),
            jax.ShapeDtypeStruct((8, 128), jnp.float32),
        ),
        in_specs=[pl.BlockSpec(memory_space=pltpu.SMEM)] + [given] * (1 + len(blocks)),
        out_specs=(vmem,) * 3,
        scratch_shapes=[
            pltpu.VMEM((source_places(slots, n), 2, 128, 128), jnp.bfloat16),
            pltpu.VMEM((n, TRIALS, 128, 128), jnp.bfloat16),
            pltpu.VMEM((n * terms_per + 1, 128, 128), jnp.bfloat16),
            pltpu.SemaphoreType.DMA((len(blocks), 2)),
        ]
        + fetched,
        compiler_params=pltpu.CompilerParams(vmem_limit_bytes=(30 if fits(n) else 58) * MIB),
        cost_estimate=pl.CostEstimate(
            flops=slots * 8 * 128**3, bytes_accessed=slots * 32768 + n * 450000, transcendentals=0
        ),
    )(plan, left_ops, *[block[0] for block in blocks])


def corr_kernel(*refs):
    blocks, corr_ref = refs[:-1], refs[-1]
    total = [jnp.zeros((8, 128), jnp.float32)] * 3
    for ref in blocks:
        t0, t1 = ref[0].astype(jnp.float32), ref[1].astype(jnp.float32)
        total = [total[0] + fold(t0 * t0), total[1] + fold(t0 * t1), total[2] + fold(t1 * t1)]
    c00, c01, c11 = [jnp.sum(x) for x in total]
    corr_ref[...] = matrix_of({(0, 0): c00, (0, 1): c01, (1, 0): c01, (1, 1): c11})[0:2, 0:2]


def correlate(blocks):
    return pl.pallas_call(
        corr_kernel,
        out_shape=jax.ShapeDtypeStruct((2, 2), jnp.float32),
        compiler_params=pltpu.CompilerParams(vmem_limit_bytes=16 * MIB),
    )(*blocks)


def chip_kernel(chips, keep_ref, own_ref, received_ref, mine_ref, total_ref, *sends):
    total = jnp.concatenate([own_ref[...], received_ref[chips * 256 :, :].astype(jnp.float32)[0:8]], axis=0)
    total_ref[...] = total
    tail = total.astype(jnp.bfloat16)
    me = lax.axis_index("op")
    for j in range(chips):
        value = keep_ref[jnp.bitwise_xor(me, 2 * j)] + received_ref[j * 256 : (j + 1) * 256, :].astype(jnp.float32)
        if j == 0:
            mine_ref[...] = value
        else:
            sends[j - 1][0:256, :] = value.astype(jnp.bfloat16)
            sends[j - 1][256:, :] = tail


def add_chip(keep, own, received):
    chips = keep.shape[0] // 2
    return pl.pallas_call(
        functools.partial(chip_kernel, chips),
        out_shape=(jax.ShapeDtypeStruct((256, 128), jnp.float32), jax.ShapeDtypeStruct((16, 128), jnp.float32))
        + (jax.ShapeDtypeStruct((256 + TAIL, 128), jnp.bfloat16),) * (chips - 1),
        compiler_params=pltpu.CompilerParams(vmem_limit_bytes=16 * MIB),
    )(keep, own, received)


def last_kernel(mine_ref, total_ref, *refs):
    received, (product_ref, projected_ref) = refs[:-2], refs[-2:]
    value, total = mine_ref[...], total_ref[...]
    for ref in received:
        value = value + ref[0:256, :].astype(jnp.float32)
        total = total + ref[256:, :].astype(jnp.float32)
    product_ref[0, 0] = value[0:128]
    product_ref[0, 1] = value[128:256]
    total = total[0:8] + total[8:16]
    projected_ref[...] = total[0:2, 0:2] + total[0:2, 2:4] + total[0:2, 4:6]


def add_all(mine, total, received):
    return pl.pallas_call(
        last_kernel,
        out_shape=(
            jax.ShapeDtypeStruct((1, 2, 128, 128), jnp.float32),
            jax.ShapeDtypeStruct((2, 2), jnp.float32),
        ),
        compiler_params=pltpu.CompilerParams(vmem_limit_bytes=16 * MIB),
    )(mine, total, *received)


def body(n, trial, left_ops, right_ops, task_list):
    steps = n // 4
    own = jnp.concatenate([trial[0], right_ops], axis=0)
    plan = make_plan(task_list.T, n, n * right_ops.shape[0])
    left_ops = stage(left_ops, n)
    lines = [own, exchange(own, n, 1)]
    blocks = [(value, 0, False, half) for half, value in enumerate(lines)]
    for step in range(1, steps + 1):
        if step == 2:
            lines[0], plan = lax.optimization_barrier((lines[0], plan))
        for half in range(2):
            lines[half] = ring_step(lines[half], n)
            blocks.append((lines[half], step, False, half))
        if step < steps:
            blocks += [(exchange(value, n, 1), step, True, half) for half, value in enumerate(lines)]
    send, keep, own = run_tasks(n, plan, left_ops, blocks)
    send, arrays = lax.optimization_barrier((send, [block[0] for block in blocks]))
    correlation = correlate(arrays)
    mine, total, *sends = add_chip(keep, own, exchange(send, n, 1))
    received = [exchange(sends[j - 1], n, 2 * j) for j in reversed(range(1, n // 2))]
    product, projected = add_all(mine, total, received)
    return product, correlation, projected


def solution(mesh):
    return jax.shard_map(
        functools.partial(body, mesh.shape["op"]),
        mesh=mesh,
        in_specs=(
            P(("groups", "op"), None, None, None),
            P(("groups", "op"), None, None),
            P(("groups", "op"), None, None),
            P(("groups", "op"), None),
        ),
        out_specs=(P(("groups", "op"), None, None, None), P("groups", None), P("groups", None)),
        check_vma=False,
    )
```

```python
import functools

import jax
import jax.numpy as jnp
from jax import lax
from jax.experimental import pallas as pl
from jax.experimental.pallas import tpu as pltpu
from jax.sharding import PartitionSpec as P

MIB = 1024 * 1024
TAIL = 16
TRIALS = 2
AHEAD = 3


def exchange(value, n, mask):
    return lax.ppermute(value, "op", [(i, i ^ mask) for i in range(n)])


def chip_at(place, chips):
    return 2 * place if place < chips // 2 else 2 * (chips - place) - 1


def ring_step(value, n):
    chips = n // 2
    order = [chip_at(place, chips) for place in range(chips)]
    pairs = []
    for place, chip in enumerate(order):
        pairs.append((2 * chip, 2 * order[(place + 1) % chips]))
        pairs.append((2 * chip + 1, 2 * order[(place - 1) % chips] + 1))
    return lax.ppermute(value, "op", pairs)


def owner_of(step, swapped, half, n):
    chips = n // 2
    me = lax.axis_index("op")
    chip, core = me // 2, lax.rem(me, 2)
    odd = lax.rem(chip, 2)
    mine = jnp.where(odd == 0, chip // 2, chips - 1 - chip // 2)
    line = 1 - core if swapped else core
    place = lax.rem(mine + (2 * line - 1) * step + 2 * chips, chips)
    there = jnp.where(place < chips // 2, 2 * place, 2 * (chips - place) - 1)
    return 2 * there + (line if half == 0 else 1 - line)


def split3(value):
    lanes = lax.broadcasted_iota(jnp.int32, (8, 128), 1)
    high = value.astype(jnp.bfloat16).astype(jnp.float32)
    middle = (value - high).astype(jnp.bfloat16).astype(jnp.float32)
    low = (value - high - middle).astype(jnp.bfloat16).astype(jnp.float32)
    return jnp.where(lanes < 2, high, jnp.where(lanes < 4, middle, low))


def tail_of(first, second):
    return jnp.concatenate([first, second], axis=0).astype(jnp.bfloat16)


def matrix_of(values, repeats=1):
    rows = lax.broadcasted_iota(jnp.int32, (8, 128), 0)
    lanes = lax.broadcasted_iota(jnp.int32, (8, 128), 1)
    total = jnp.zeros((8, 128), jnp.float32)
    for (i, j), value in values.items():
        for repeat in range(repeats):
            total = total + jnp.where((rows == i) & (lanes == j + 2 * repeat), value, 0.0)
    return total


def fold(value):
    return value.reshape(16, 8, 128).sum(axis=0)


def fits(n):
    return n <= 16


def phases_of(n):
    return 1


def chunk_of(n):
    return 96 if fits(n) else 48


def run_of(slots, n):
    return 4 if slots >= 8 * n else 2


def source_places(slots, n):
    chunk = chunk_of(n)
    most = slots + min(slots, n) * (run_of(slots, n) - 1)
    return -(-most // chunk) * chunk


def place_of(chip, chips):
    half = jnp.floor(chip * 0.5)
    return jnp.where(chip == 2.0 * half, half, chips - 1.0 - half)


def plan_kernel(n, terms, tasks_ref, plan_ref):
    slots = tasks_ref.shape[1]
    places = plan_ref.shape[1]
    chips = n // 2
    phases = phases_of(n)
    rows = tasks_ref[...].astype(jnp.float32)
    source, target, term, live = rows[0:1], rows[1:2], rows[2:3], rows[3:4]
    lane = lax.broadcasted_iota(jnp.int32, (1, slots), 1).astype(jnp.float32)
    number = lax.broadcasted_iota(jnp.int32, (1, places), 1).astype(jnp.float32)
    at = lax.broadcasted_iota(jnp.int32, (slots, places), 1).astype(jnp.float32)
    me = lax.axis_index("op")
    mine = place_of((jnp.zeros((1, slots), jnp.int32) + me // 2).astype(jnp.float32), float(chips))
    gap = place_of(jnp.floor(source * 0.5), float(chips)) - mine
    up = jnp.where(gap < 0, gap + chips, gap)
    far = jnp.minimum(up, chips - up)
    phase = jnp.clip(far - 1.0, 0.0, phases - 1.0)

    def column(*values):
        pad = [jnp.zeros((8 - len(values), slots), jnp.float32)]
        return jnp.transpose(jnp.concatenate(list(values) + pad, axis=0))

    def sort(sector, parts, unit, whole):
        keys = parts * n
        index = lax.broadcasted_iota(jnp.int32, (keys, slots), 0).astype(jnp.float32)
        part = phase if parts > 1 else jnp.zeros_like(phase)
        key = jnp.where(live > 0, part * n + sector, float(keys))
        columns = column(key, lane)
        earlier = jnp.where((columns[:, 0:1] == key) & (columns[:, 1:2] < lane), 1.0, 0.0)
        count = jnp.sum(jnp.where(index == key, 1.0, 0.0), axis=1, keepdims=True)
        padded = jnp.ceil(count / unit) * unit
        place = jnp.sum(earlier, axis=0, keepdims=True)
        start = jnp.zeros((1, 1), jnp.float32)
        starts = [start]
        for p in range(parts):
            lengths = padded[p * n : (p + 1) * n]
            before = jnp.where(index[p * n : (p + 1) * n] < key, lengths, 0.0)
            place = place + jnp.where(part == p, start * whole + jnp.sum(before, axis=0, keepdims=True), 0.0)
            start = start + jnp.ceil(jnp.sum(lengths, axis=0, keepdims=True) / whole)
            starts.append(start)
        return jnp.where(live > 0, place, -1.0), starts

    by_source, source_starts = sort(source, phases, float(run_of(slots, n)), float(chunk_of(n)))
    by_target, target_starts = sort(target, 1, 2.0, float(chunk_of(n)))
    columns = column(by_source, by_target, lane, source, term, target)

    def picker(places_column):
        hit = places_column == at

        def pick(values, other):
            found = jnp.sum(jnp.where(hit, values - other, 0.0), axis=0, keepdims=True)
            return (found + other).astype(jnp.int32)

        return pick

    own = (jnp.zeros((1, 1), jnp.int32) + me).astype(jnp.float32)
    pick = picker(columns[:, 0:1])
    plan_ref[0:1] = pick(columns[:, 2:3], 0.0)
    plan_ref[1:2] = pick(columns[:, 3:4], own)
    pick = picker(columns[:, 1:2])
    plan_ref[2:3] = pick(columns[:, 0:1], -1.0)
    plan_ref[3:4] = pick(columns[:, 4:5], float(terms))
    plan_ref[4:5] = pick(columns[:, 5:6], float(n))
    turns = jnp.zeros((1, places), jnp.float32)
    for p, start in enumerate(source_starts + [target_starts[1]]):
        turns = turns + jnp.where(number == p, start, 0.0)
    plan_ref[5:6] = turns.astype(jnp.int32)
    plan_ref[6:8] = jnp.zeros((2, places), jnp.int32)


def make_plan(tasks, n, terms):
    most = source_places(tasks.shape[1], n) + chunk_of(n)
    return pl.pallas_call(
        functools.partial(plan_kernel, n, terms),
        out_shape=jax.ShapeDtypeStruct((8, -(-most // 128) * 128), jnp.int32),
        compiler_params=pltpu.CompilerParams(vmem_limit_bytes=16 * MIB),
    )(tasks)


def stage_kernel(left_ref, held_ref, sem):
    copy = pltpu.make_async_copy(left_ref, held_ref, sem)
    copy.start()
    copy.wait()


def stage(left_ops, n):
    if not fits(n):
        return left_ops
    return pl.pallas_call(
        stage_kernel,
        in_specs=[pl.BlockSpec(memory_space=pltpu.HBM)],
        out_specs=pl.BlockSpec(memory_space=pltpu.VMEM),
        out_shape=jax.ShapeDtypeStruct(left_ops.shape, left_ops.dtype),
        scratch_shapes=[pltpu.SemaphoreType.DMA],
        compiler_params=pltpu.CompilerParams(vmem_limit_bytes=42 * MIB),
    )(left_ops)


def block_parts(n, kinds, blocks, trial, right):
    parts = []
    for b, kind in enumerate(kinds):
        first, second, rest = blocks[3 * b : 3 * b + 3]
        some = first.shape[0] - TRIALS
        others = rest.shape[0] // 2
        for half, ref in enumerate((first, second)):
            owner = owner_of(*kind, half, n)
            base = owner * (some + others)
            parts.append((ref.at[pl.ds(0, TRIALS)], trial.at[owner]))
            parts.append((ref.at[pl.ds(TRIALS, some)], right.at[pl.ds(base, some)]))
            parts.append((rest.at[pl.ds(half * others, others)], right.at[pl.ds(base + some, others)]))
    return parts


def make_halves(n, plan_ref, left_ref, trial, halves, fetched):
    turns = plan_ref[5, 1]
    run = run_of(left_ref.shape[0], n)
    chunk = chunk_of(n)

    def fetch(turn):
        left, left_sem = fetched
        at = lax.rem(turn, AHEAD)
        for u in range(chunk):
            slot = plan_ref[0, turn * chunk + u]
            pltpu.make_async_copy(left_ref.at[slot], left.at[at, u], left_sem.at[at]).start()

    def start():
        for turn in range(AHEAD - 1) if fetched else ():

            @pl.when(turn < turns)
            def _():
                fetch(turn)

    def turn_of(turn, carry):
        if fetched:
            left, left_sem = fetched

            @pl.when(turn + AHEAD - 1 < turns)
            def _():
                fetch(turn + AHEAD - 1)

            at = lax.rem(turn, AHEAD)
            pltpu.make_async_copy(left_ref.at[pl.ds(0, chunk)], left.at[at], left_sem.at[at]).wait()
        place = turn * chunk
        for r in range(0, chunk, run):
            source = plan_ref[1, place + r]
            vectors = jnp.concatenate([trial[source, 0], trial[source, 1]], axis=1)
            if fetched:
                rows = left[at, r : r + run].reshape(run * 128, 128)
            else:
                rows = jnp.concatenate([left_ref[plan_ref[0, place + r + u]] for u in range(run)], axis=0)
            half = jnp.dot(rows, vectors, preferred_element_type=jnp.float32).astype(jnp.bfloat16)
            for u in range(run):
                halves[place + r + u, 0] = half[u * 128 : (u + 1) * 128, :128]
                halves[place + r + u, 1] = half[u * 128 : (u + 1) * 128, 128:]
        return carry

    return start, lambda: lax.fori_loop(0, turns, turn_of, 0)


def tasks_kernel(n, kinds, plan_ref, left_ref, *refs):
    blocks, refs = refs[: 3 * len(kinds)], refs[3 * len(kinds) :]
    send_ref, acc, own_ref, halves, trial, right, block_sem, *fetched = refs
    start, products = make_halves(n, plan_ref, left_ref, trial, halves, fetched)
    right[right.shape[0] - 1] = jnp.zeros((128, 128), jnp.bfloat16)
    start()
    parts = block_parts(n, kinds, blocks, trial, right)
    copies = []
    for index, (source, to) in enumerate(parts):
        if fits(n):
            to[...] = source[...]
        else:
            copies.append(pltpu.make_async_copy(source, to, block_sem.at[index]))
            copies[-1].start()

    def clear(s, carry):
        acc[s] = jnp.zeros((256, 128), jnp.float32)
        return carry

    lax.fori_loop(0, n, clear, 0)
    for copy in copies:
        copy.wait()
    products()

    def target_turn(turn, carry):
        first = turn * chunk_of(n)
        for u in range(0, chunk_of(n), 2):
            place = first + u
            one = plan_ref[2, place]
            two = plan_ref[2, place + 1]
            one, two = jnp.maximum(one, 0), jnp.where(two < 0, jnp.maximum(one, 0), two)
            pair = jnp.concatenate(
                [
                    jnp.concatenate([halves[one, 0], halves[two, 0]], axis=1),
                    jnp.concatenate([halves[one, 1], halves[two, 1]], axis=1),
                ],
                axis=0,
            )
            rights = jnp.concatenate([right[plan_ref[3, place]], right[plan_ref[3, place + 1]]], axis=1)
            term = lax.dot_general(
                pair, rights, (((1,), (1,)), ((), ())), preferred_element_type=jnp.float32
            )
            target = plan_ref[4, place]
            acc[target] = acc[target] + term
        return carry

    lax.fori_loop(0, plan_ref[5, 2], target_turn, 0)
    me = lax.axis_index("op")

    def dots(s, carry):
        t0 = trial[s, 0].astype(jnp.float32)
        t1 = trial[s, 1].astype(jnp.float32)
        a0 = acc[s, 0:128, :]
        a1 = acc[s, 128:256, :]
        p00, p01, p10, p11 = carry
        return p00 + fold(t0 * a0), p01 + fold(t0 * a1), p10 + fold(t1 * a0), p11 + fold(t1 * a1)

    zero = jnp.zeros((8, 128), jnp.float32)
    sums = lax.fori_loop(0, n, dots, (zero,) * 4, unroll=4)
    p00, p01, p10, p11 = [jnp.sum(x) for x in sums]

    def pack(j, carry):
        mine = jnp.bitwise_xor(me, 2 * j)
        send_ref[pl.ds(pl.multiple_of(j * 256, 256), 256), :] = acc[jnp.bitwise_xor(mine, 1)].astype(jnp.bfloat16)
        return carry

    lax.fori_loop(0, n // 2, pack, 0, unroll=2)
    own = split3(matrix_of({(0, 0): p00, (0, 1): p01, (1, 0): p10, (1, 1): p11}, 3))
    own_ref[...] = own
    send_ref[n // 2 * 256 :, :] = tail_of(own, jnp.zeros_like(own))


def run_tasks(n, plan, left_ops, blocks):
    slots = left_ops.shape[0]
    first, unused, rest = blocks[0][0]
    terms_per = first.shape[0] - TRIALS + rest.shape[0] // 2
    kinds = tuple(block[1:] for block in blocks)
    vmem, hbm = pl.BlockSpec(memory_space=pltpu.VMEM), pl.BlockSpec(memory_space=pltpu.HBM)
    given = vmem if fits(n) else hbm
    fetched = [] if fits(n) else [
        pltpu.VMEM((AHEAD, chunk_of(n), 128, 128), jnp.bfloat16),
        pltpu.SemaphoreType.DMA((AHEAD,)),
    ]
    return pl.pallas_call(
        functools.partial(tasks_kernel, n, kinds),
        out_shape=(
            jax.ShapeDtypeStruct((n // 2 * 256 + TAIL, 128), jnp.bfloat16),
            jax.ShapeDtypeStruct((n + 1, 256, 128), jnp.float32),
            jax.ShapeDtypeStruct((8, 128), jnp.float32),
        ),
        in_specs=[pl.BlockSpec(memory_space=pltpu.SMEM)] + [given] * (1 + 3 * len(blocks)),
        out_specs=(vmem,) * 3,
        scratch_shapes=[
            pltpu.VMEM((source_places(slots, n), 2, 128, 128), jnp.bfloat16),
            pltpu.VMEM((n, TRIALS, 128, 128), jnp.bfloat16),
            pltpu.VMEM((n * terms_per + 1, 128, 128), jnp.bfloat16),
            pltpu.SemaphoreType.DMA((6 * len(blocks),)),
        ]
        + fetched,
        compiler_params=pltpu.CompilerParams(vmem_limit_bytes=(30 if fits(n) else 58) * MIB),
        cost_estimate=pl.CostEstimate(
            flops=slots * 8 * 128**3, bytes_accessed=slots * 32768 + n * 450000, transcendentals=0
        ),
    )(plan, left_ops, *[value for block in blocks for value in block[0]])


def corr_kernel(*refs):
    blocks, corr_ref = refs[:-1], refs[-1]
    total = [jnp.zeros((8, 128), jnp.float32)] * 3
    for ref in blocks:
        t0, t1 = ref[0].astype(jnp.float32), ref[1].astype(jnp.float32)
        total = [total[0] + fold(t0 * t0), total[1] + fold(t0 * t1), total[2] + fold(t1 * t1)]
    c00, c01, c11 = [jnp.sum(x) for x in total]
    corr_ref[...] = matrix_of({(0, 0): c00, (0, 1): c01, (1, 0): c01, (1, 1): c11})[0:2, 0:2]


def correlate(blocks):
    return pl.pallas_call(
        corr_kernel,
        out_shape=jax.ShapeDtypeStruct((2, 2), jnp.float32),
        compiler_params=pltpu.CompilerParams(vmem_limit_bytes=16 * MIB),
    )(*blocks)


def chip_kernel(chips, keep_ref, own_ref, received_ref, mine_ref, total_ref, *sends):
    total = jnp.concatenate([own_ref[...], received_ref[chips * 256 :, :].astype(jnp.float32)[0:8]], axis=0)
    total_ref[...] = total
    tail = total.astype(jnp.bfloat16)
    me = lax.axis_index("op")
    for j in range(chips):
        value = keep_ref[jnp.bitwise_xor(me, 2 * j)] + received_ref[j * 256 : (j + 1) * 256, :].astype(jnp.float32)
        if j == 0:
            mine_ref[...] = value
        else:
            sends[j - 1][0:256, :] = value.astype(jnp.bfloat16)
            sends[j - 1][256:, :] = tail


def add_chip(keep, own, received):
    chips = keep.shape[0] // 2
    return pl.pallas_call(
        functools.partial(chip_kernel, chips),
        out_shape=(jax.ShapeDtypeStruct((256, 128), jnp.float32), jax.ShapeDtypeStruct((16, 128), jnp.float32))
        + (jax.ShapeDtypeStruct((256 + TAIL, 128), jnp.bfloat16),) * (chips - 1),
        compiler_params=pltpu.CompilerParams(vmem_limit_bytes=16 * MIB),
    )(keep, own, received)


def last_kernel(mine_ref, total_ref, *refs):
    received, (product_ref, projected_ref) = refs[:-2], refs[-2:]
    value, total = mine_ref[...], total_ref[...]
    for ref in received:
        value = value + ref[0:256, :].astype(jnp.float32)
        total = total + ref[256:, :].astype(jnp.float32)
    product_ref[0, 0] = value[0:128]
    product_ref[0, 1] = value[128:256]
    total = total[0:8] + total[8:16]
    projected_ref[...] = total[0:2, 0:2] + total[0:2, 2:4] + total[0:2, 4:6]


def add_all(mine, total, received):
    return pl.pallas_call(
        last_kernel,
        out_shape=(
            jax.ShapeDtypeStruct((1, 2, 128, 128), jnp.float32),
            jax.ShapeDtypeStruct((2, 2), jnp.float32),
        ),
        compiler_params=pltpu.CompilerParams(vmem_limit_bytes=16 * MIB),
    )(mine, total, *received)


def body(n, trial, left_ops, right_ops, task_list):
    steps = n // 4
    left_ops = stage(left_ops, n)
    some = right_ops.shape[0] // 2
    own = jnp.concatenate([trial[0], right_ops[:some]], axis=0)
    rest = jnp.concatenate([right_ops[some:], exchange(right_ops[some:], n, 1)], axis=0)
    line = [own, exchange(own, n, 1), rest]
    blocks = [(line, 0, False)]
    for step in range(1, steps + 1):
        if step == 2:
            tasks, first = lax.optimization_barrier((task_list.T, line[0]))
            line = [first, *line[1:]]
            plan = make_plan(tasks, n, n * right_ops.shape[0])
        if step == 3:
            last, plan = lax.optimization_barrier((line[2], plan))
            line = [*line[:2], last]
        line = [ring_step(value, n) for value in line]
        blocks.append((line, step, False))
        if step < steps:
            blocks.append(([exchange(value, n, 1) for value in line], step, True))
    send, keep, own = run_tasks(n, plan, left_ops, blocks)
    send, arrays = lax.optimization_barrier((send, [value for block in blocks for value in block[0][:2]]))
    correlation = correlate(arrays)
    mine, total, *sends = add_chip(keep, own, exchange(send, n, 1))
    received = [exchange(sends[j - 1], n, 2 * j) for j in reversed(range(1, n // 2))]
    product, projected = add_all(mine, total, received)
    return product, correlation, projected


def solution(mesh):
    return jax.shard_map(
        functools.partial(body, mesh.shape["op"]),
        mesh=mesh,
        in_specs=(
            P(("groups", "op"), None, None, None),
            P(("groups", "op"), None, None),
            P(("groups", "op"), None, None),
            P(("groups", "op"), None),
        ),
        out_specs=(P(("groups", "op"), None, None, None), P("groups", None), P("groups", None)),
        check_vma=False,
    )
```

```python
import functools

import jax
import jax.numpy as jnp
from jax import lax
from jax.experimental import pallas as pl
from jax.experimental.pallas import tpu as pltpu
from jax.sharding import PartitionSpec as P

MIB = 1024 * 1024
TAIL = 16
TRIALS = 2
AHEAD = 3


def exchange(value, n, mask):
    return lax.ppermute(value, "op", [(i, i ^ mask) for i in range(n)])


def chip_at(place, chips):
    return 2 * place if place < chips // 2 else 2 * (chips - place) - 1


def ring_step(value, n):
    chips = n // 2
    order = [chip_at(place, chips) for place in range(chips)]
    pairs = []
    for place, chip in enumerate(order):
        pairs.append((2 * chip, 2 * order[(place + 1) % chips]))
        pairs.append((2 * chip + 1, 2 * order[(place - 1) % chips] + 1))
    return lax.ppermute(value, "op", pairs)


def owner_of(step, swapped, half, n):
    chips = n // 2
    me = lax.axis_index("op")
    chip, core = me // 2, lax.rem(me, 2)
    odd = lax.rem(chip, 2)
    mine = jnp.where(odd == 0, chip // 2, chips - 1 - chip // 2)
    line = 1 - core if swapped else core
    place = lax.rem(mine + (2 * line - 1) * step + 2 * chips, chips)
    there = jnp.where(place < chips // 2, 2 * place, 2 * (chips - place) - 1)
    return 2 * there + (line if half == 0 else 1 - line)


def split3(value):
    lanes = lax.broadcasted_iota(jnp.int32, (8, 128), 1)
    high = value.astype(jnp.bfloat16).astype(jnp.float32)
    middle = (value - high).astype(jnp.bfloat16).astype(jnp.float32)
    low = (value - high - middle).astype(jnp.bfloat16).astype(jnp.float32)
    return jnp.where(lanes < 2, high, jnp.where(lanes < 4, middle, low))


def tail_of(first, second):
    return jnp.concatenate([first, second], axis=0).astype(jnp.bfloat16)


def matrix_of(values, repeats=1):
    rows = lax.broadcasted_iota(jnp.int32, (8, 128), 0)
    lanes = lax.broadcasted_iota(jnp.int32, (8, 128), 1)
    total = jnp.zeros((8, 128), jnp.float32)
    for (i, j), value in values.items():
        for repeat in range(repeats):
            total = total + jnp.where((rows == i) & (lanes == j + 2 * repeat), value, 0.0)
    return total


def fold(value):
    return value.reshape(16, 8, 128).sum(axis=0)


def fits(n):
    return n <= 16


def phases_of(n):
    return 1


def chunk_of(n):
    return 96 if fits(n) else 48


def run_of(slots, n):
    return 4 if slots >= 8 * n else 2


def source_places(slots, n):
    chunk = chunk_of(n)
    most = slots + min(slots, n) * (run_of(slots, n) - 1)
    return -(-most // chunk) * chunk


def place_of(chip, chips):
    half = jnp.floor(chip * 0.5)
    return jnp.where(chip == 2.0 * half, half, chips - 1.0 - half)


def plan_kernel(n, terms, tasks_ref, plan_ref):
    slots = tasks_ref.shape[1]
    places = plan_ref.shape[1]
    chips = n // 2
    phases = phases_of(n)
    rows = tasks_ref[...].astype(jnp.float32)
    source, target, term, live = rows[0:1], rows[1:2], rows[2:3], rows[3:4]
    lane = lax.broadcasted_iota(jnp.int32, (1, slots), 1).astype(jnp.float32)
    number = lax.broadcasted_iota(jnp.int32, (1, places), 1).astype(jnp.float32)
    at = lax.broadcasted_iota(jnp.int32, (slots, places), 1).astype(jnp.float32)
    me = lax.axis_index("op")
    mine = place_of((jnp.zeros((1, slots), jnp.int32) + me // 2).astype(jnp.float32), float(chips))
    gap = place_of(jnp.floor(source * 0.5), float(chips)) - mine
    up = jnp.where(gap < 0, gap + chips, gap)
    far = jnp.minimum(up, chips - up)
    phase = jnp.clip(far - 1.0, 0.0, phases - 1.0)

    def column(*values):
        pad = [jnp.zeros((8 - len(values), slots), jnp.float32)]
        return jnp.transpose(jnp.concatenate(list(values) + pad, axis=0))

    def sort(sector, parts, unit, whole):
        keys = parts * n
        index = lax.broadcasted_iota(jnp.int32, (keys, slots), 0).astype(jnp.float32)
        part = phase if parts > 1 else jnp.zeros_like(phase)
        key = jnp.where(live > 0, part * n + sector, float(keys))
        columns = column(key, lane)
        earlier = jnp.where((columns[:, 0:1] == key) & (columns[:, 1:2] < lane), 1.0, 0.0)
        count = jnp.sum(jnp.where(index == key, 1.0, 0.0), axis=1, keepdims=True)
        padded = jnp.ceil(count / unit) * unit
        place = jnp.sum(earlier, axis=0, keepdims=True)
        start = jnp.zeros((1, 1), jnp.float32)
        starts = [start]
        for p in range(parts):
            lengths = padded[p * n : (p + 1) * n]
            before = jnp.where(index[p * n : (p + 1) * n] < key, lengths, 0.0)
            place = place + jnp.where(part == p, start * whole + jnp.sum(before, axis=0, keepdims=True), 0.0)
            start = start + jnp.ceil(jnp.sum(lengths, axis=0, keepdims=True) / whole)
            starts.append(start)
        return jnp.where(live > 0, place, -1.0), starts

    by_source, source_starts = sort(source, phases, float(run_of(slots, n)), float(chunk_of(n)))
    by_target, target_starts = sort(target, 1, 2.0, float(chunk_of(n)))
    columns = column(by_source, by_target, lane, source, term, target)

    def picker(places_column):
        hit = places_column == at

        def pick(values, other):
            found = jnp.sum(jnp.where(hit, values - other, 0.0), axis=0, keepdims=True)
            return (found + other).astype(jnp.int32)

        return pick

    own = (jnp.zeros((1, 1), jnp.int32) + me).astype(jnp.float32)
    pick = picker(columns[:, 0:1])
    plan_ref[0:1] = pick(columns[:, 2:3], 0.0)
    plan_ref[1:2] = pick(columns[:, 3:4], own)
    pick = picker(columns[:, 1:2])
    plan_ref[2:3] = pick(columns[:, 0:1], -1.0)
    plan_ref[3:4] = pick(columns[:, 4:5], float(terms))
    plan_ref[4:5] = pick(columns[:, 5:6], float(n))
    turns = jnp.zeros((1, places), jnp.float32)
    for p, start in enumerate(source_starts + [target_starts[1]]):
        turns = turns + jnp.where(number == p, start, 0.0)
    plan_ref[5:6] = turns.astype(jnp.int32)
    plan_ref[6:8] = jnp.zeros((2, places), jnp.int32)


def stage_kernel(n, terms, tasks_ref, left_ref, plan_ref, held_ref, tasks, sem):
    copies = [
        pltpu.make_async_copy(tasks_ref, tasks, sem.at[0]),
        pltpu.make_async_copy(left_ref, held_ref, sem.at[1]),
    ]
    for copy in copies:
        copy.start()
    copies[0].wait()
    plan_kernel(n, terms, tasks, plan_ref)
    copies[1].wait()


def make_plan(tasks, left_ops, n, terms):
    most = source_places(tasks.shape[1], n) + chunk_of(n)
    plan = jax.ShapeDtypeStruct((8, -(-most // 128) * 128), jnp.int32)
    vmem, hbm = pl.BlockSpec(memory_space=pltpu.VMEM), pl.BlockSpec(memory_space=pltpu.HBM)
    if fits(n):
        return pl.pallas_call(
            functools.partial(stage_kernel, n, terms),
            in_specs=[hbm, hbm],
            out_specs=(vmem, vmem),
            out_shape=(plan, jax.ShapeDtypeStruct(left_ops.shape, left_ops.dtype)),
            scratch_shapes=[pltpu.VMEM(tasks.shape, jnp.int32), pltpu.SemaphoreType.DMA((2,))],
            compiler_params=pltpu.CompilerParams(vmem_limit_bytes=42 * MIB),
        )(tasks, left_ops)
    return (
        pl.pallas_call(
            functools.partial(plan_kernel, n, terms),
            out_shape=plan,
            compiler_params=pltpu.CompilerParams(vmem_limit_bytes=16 * MIB),
        )(tasks),
        left_ops,
    )


def block_parts(n, kinds, blocks, trial, right):
    parts = []
    for b, kind in enumerate(kinds):
        vectors, *terms = blocks[3 * b : 3 * b + 3]
        for half, ref in enumerate(terms):
            owner = owner_of(*kind, half, n)
            per = ref.shape[0]
            parts.append((vectors.at[pl.ds(half * TRIALS, TRIALS)], trial.at[owner]))
            parts.append((ref, right.at[pl.ds(owner * per, per)]))
    return parts


def make_halves(n, plan_ref, left_ref, trial, halves, fetched):
    turns = plan_ref[5, 1]
    run = run_of(left_ref.shape[0], n)
    chunk = chunk_of(n)

    def fetch(turn):
        left, left_sem = fetched
        at = lax.rem(turn, AHEAD)
        for u in range(chunk):
            slot = plan_ref[0, turn * chunk + u]
            pltpu.make_async_copy(left_ref.at[slot], left.at[at, u], left_sem.at[at]).start()

    def start():
        for turn in range(AHEAD - 1) if fetched else ():

            @pl.when(turn < turns)
            def _():
                fetch(turn)

    def turn_of(turn, carry):
        if fetched:
            left, left_sem = fetched

            @pl.when(turn + AHEAD - 1 < turns)
            def _():
                fetch(turn + AHEAD - 1)

            at = lax.rem(turn, AHEAD)
            pltpu.make_async_copy(left_ref.at[pl.ds(0, chunk)], left.at[at], left_sem.at[at]).wait()
        place = turn * chunk
        for r in range(0, chunk, run):
            source = plan_ref[1, place + r]
            vectors = jnp.concatenate([trial[source, 0], trial[source, 1]], axis=1)
            if fetched:
                rows = left[at, r : r + run].reshape(run * 128, 128)
            else:
                rows = jnp.concatenate([left_ref[plan_ref[0, place + r + u]] for u in range(run)], axis=0)
            half = jnp.dot(rows, vectors, preferred_element_type=jnp.float32).astype(jnp.bfloat16)
            for u in range(run):
                halves[place + r + u, 0] = half[u * 128 : (u + 1) * 128, :128]
                halves[place + r + u, 1] = half[u * 128 : (u + 1) * 128, 128:]
        return carry

    return start, lambda: lax.fori_loop(0, turns, turn_of, 0)


def tasks_kernel(n, kinds, plan_ref, left_ref, *refs):
    blocks, refs = refs[: 3 * len(kinds)], refs[3 * len(kinds) :]
    send_ref, acc, own_ref, halves, trial, right, block_sem, *fetched = refs
    start, products = make_halves(n, plan_ref, left_ref, trial, halves, fetched)
    right[right.shape[0] - 1] = jnp.zeros((128, 128), jnp.bfloat16)
    start()
    parts = block_parts(n, kinds, blocks, trial, right)
    copies = []
    for index, (source, to) in enumerate(parts):
        if fits(n):
            to[...] = source[...]
        else:
            copies.append(pltpu.make_async_copy(source, to, block_sem.at[index]))
            copies[-1].start()

    def clear(s, carry):
        acc[s] = jnp.zeros((256, 128), jnp.float32)
        return carry

    lax.fori_loop(0, n, clear, 0)
    for copy in copies:
        copy.wait()
    products()

    def target_turn(turn, carry):
        first = turn * chunk_of(n)
        for u in range(0, chunk_of(n), 2):
            place = first + u
            one = plan_ref[2, place]
            two = plan_ref[2, place + 1]
            one, two = jnp.maximum(one, 0), jnp.where(two < 0, jnp.maximum(one, 0), two)
            pair = jnp.concatenate(
                [
                    jnp.concatenate([halves[one, 0], halves[two, 0]], axis=1),
                    jnp.concatenate([halves[one, 1], halves[two, 1]], axis=1),
                ],
                axis=0,
            )
            rights = jnp.concatenate([right[plan_ref[3, place]], right[plan_ref[3, place + 1]]], axis=1)
            term = lax.dot_general(
                pair, rights, (((1,), (1,)), ((), ())), preferred_element_type=jnp.float32
            )
            target = plan_ref[4, place]
            acc[target] = acc[target] + term
        return carry

    lax.fori_loop(0, plan_ref[5, 2], target_turn, 0)
    me = lax.axis_index("op")

    def dots(s, carry):
        t0 = trial[s, 0].astype(jnp.float32)
        t1 = trial[s, 1].astype(jnp.float32)
        a0 = acc[s, 0:128, :]
        a1 = acc[s, 128:256, :]
        p00, p01, p10, p11 = carry
        return p00 + fold(t0 * a0), p01 + fold(t0 * a1), p10 + fold(t1 * a0), p11 + fold(t1 * a1)

    zero = jnp.zeros((8, 128), jnp.float32)
    sums = lax.fori_loop(0, n, dots, (zero,) * 4, unroll=4)
    p00, p01, p10, p11 = [jnp.sum(x) for x in sums]

    def pack(j, carry):
        mine = jnp.bitwise_xor(me, 2 * j)
        send_ref[pl.ds(pl.multiple_of(j * 256, 256), 256), :] = acc[jnp.bitwise_xor(mine, 1)].astype(jnp.bfloat16)
        return carry

    lax.fori_loop(0, n // 2, pack, 0, unroll=2)
    own = split3(matrix_of({(0, 0): p00, (0, 1): p01, (1, 0): p10, (1, 1): p11}, 3))
    own_ref[...] = own
    send_ref[n // 2 * 256 :, :] = tail_of(own, jnp.zeros_like(own))


def run_tasks(n, plan, left_ops, blocks):
    slots = left_ops.shape[0]
    terms_per = blocks[0][0][1].shape[0]
    kinds = tuple(block[1:] for block in blocks)
    vmem, hbm = pl.BlockSpec(memory_space=pltpu.VMEM), pl.BlockSpec(memory_space=pltpu.HBM)
    given = vmem if fits(n) else hbm
    fetched = [] if fits(n) else [
        pltpu.VMEM((AHEAD, chunk_of(n), 128, 128), jnp.bfloat16),
        pltpu.SemaphoreType.DMA((AHEAD,)),
    ]
    return pl.pallas_call(
        functools.partial(tasks_kernel, n, kinds),
        out_shape=(
            jax.ShapeDtypeStruct((n // 2 * 256 + TAIL, 128), jnp.bfloat16),
            jax.ShapeDtypeStruct((n + 1, 256, 128), jnp.float32),
            jax.ShapeDtypeStruct((8, 128), jnp.float32),
        ),
        in_specs=[pl.BlockSpec(memory_space=pltpu.SMEM)] + [given] * (1 + 3 * len(blocks)),
        out_specs=(vmem,) * 3,
        scratch_shapes=[
            pltpu.VMEM((source_places(slots, n), 2, 128, 128), jnp.bfloat16),
            pltpu.VMEM((n, TRIALS, 128, 128), jnp.bfloat16),
            pltpu.VMEM((n * terms_per + 1, 128, 128), jnp.bfloat16),
            pltpu.SemaphoreType.DMA((4 * len(blocks),)),
        ]
        + fetched,
        compiler_params=pltpu.CompilerParams(vmem_limit_bytes=(30 if fits(n) else 58) * MIB),
        cost_estimate=pl.CostEstimate(
            flops=slots * 8 * 128**3, bytes_accessed=slots * 32768 + n * 450000, transcendentals=0
        ),
    )(plan, left_ops, *[value for block in blocks for value in block[0]])


def corr_kernel(*refs):
    blocks, corr_ref = refs[:-1], refs[-1]
    total = [jnp.zeros((8, 128), jnp.float32)] * 3
    for ref in blocks:
        for start in range(0, ref.shape[0], TRIALS):
            t0, t1 = ref[start].astype(jnp.float32), ref[start + 1].astype(jnp.float32)
            total = [total[0] + fold(t0 * t0), total[1] + fold(t0 * t1), total[2] + fold(t1 * t1)]
    c00, c01, c11 = [jnp.sum(x) for x in total]
    corr_ref[...] = matrix_of({(0, 0): c00, (0, 1): c01, (1, 0): c01, (1, 1): c11})[0:2, 0:2]


def correlate(blocks):
    return pl.pallas_call(
        corr_kernel,
        out_shape=jax.ShapeDtypeStruct((2, 2), jnp.float32),
        compiler_params=pltpu.CompilerParams(vmem_limit_bytes=16 * MIB),
    )(*blocks)


def chip_kernel(chips, keep_ref, own_ref, received_ref, mine_ref, total_ref, *sends):
    total = jnp.concatenate([own_ref[...], received_ref[chips * 256 :, :].astype(jnp.float32)[0:8]], axis=0)
    total_ref[...] = total
    tail = total.astype(jnp.bfloat16)
    me = lax.axis_index("op")
    for j in range(chips):
        value = keep_ref[jnp.bitwise_xor(me, 2 * j)] + received_ref[j * 256 : (j + 1) * 256, :].astype(jnp.float32)
        if j == 0:
            mine_ref[...] = value
        else:
            sends[j - 1][0:256, :] = value.astype(jnp.bfloat16)
            sends[j - 1][256:, :] = tail


def add_chip(keep, own, received):
    chips = keep.shape[0] // 2
    return pl.pallas_call(
        functools.partial(chip_kernel, chips),
        out_shape=(jax.ShapeDtypeStruct((256, 128), jnp.float32), jax.ShapeDtypeStruct((16, 128), jnp.float32))
        + (jax.ShapeDtypeStruct((256 + TAIL, 128), jnp.bfloat16),) * (chips - 1),
        compiler_params=pltpu.CompilerParams(vmem_limit_bytes=16 * MIB),
    )(keep, own, received)


def last_kernel(mine_ref, total_ref, *refs):
    received, (product_ref, projected_ref) = refs[:-2], refs[-2:]
    value, total = mine_ref[...], total_ref[...]
    for ref in received:
        value = value + ref[0:256, :].astype(jnp.float32)
        total = total + ref[256:, :].astype(jnp.float32)
    product_ref[0, 0] = value[0:128]
    product_ref[0, 1] = value[128:256]
    total = total[0:8] + total[8:16]
    projected_ref[...] = total[0:2, 0:2] + total[0:2, 2:4] + total[0:2, 4:6]


def add_all(mine, total, received):
    return pl.pallas_call(
        last_kernel,
        out_shape=(
            jax.ShapeDtypeStruct((1, 2, 128, 128), jnp.float32),
            jax.ShapeDtypeStruct((2, 2), jnp.float32),
        ),
        compiler_params=pltpu.CompilerParams(vmem_limit_bytes=16 * MIB),
    )(mine, total, *received)


def body(n, trial, left_ops, right_ops, task_list):
    steps = n // 4
    plan, left_ops = make_plan(task_list.T, left_ops, n, n * right_ops.shape[0])
    vectors = jnp.concatenate([trial[0], exchange(trial[0], n, 1)], axis=0)
    line = [vectors, right_ops, exchange(right_ops, n, 1)]
    blocks = [(line, 0, False)]
    for step in range(1, steps + 1):
        line = [ring_step(value, n) for value in line]
        blocks.append((line, step, False))
        if step < steps:
            blocks.append(([exchange(value, n, 1) for value in line], step, True))
    send, keep, own = run_tasks(n, plan, left_ops, blocks)
    send, arrays = lax.optimization_barrier((send, [block[0][0] for block in blocks]))
    correlation = correlate(arrays)
    mine, total, *sends = add_chip(keep, own, exchange(send, n, 1))
    received = [exchange(sends[j - 1], n, 2 * j) for j in reversed(range(1, n // 2))]
    product, projected = add_all(mine, total, received)
    return product, correlation, projected


def solution(mesh):
    return jax.shard_map(
        functools.partial(body, mesh.shape["op"]),
        mesh=mesh,
        in_specs=(
            P(("groups", "op"), None, None, None),
            P(("groups", "op"), None, None),
            P(("groups", "op"), None, None),
            P(("groups", "op"), None),
        ),
        out_specs=(P(("groups", "op"), None, None, None), P("groups", None), P("groups", None)),
        check_vma=False,
    )
```

```python
import functools

import jax
import jax.numpy as jnp
from jax import lax
from jax.experimental import pallas as pl
from jax.experimental.pallas import tpu as pltpu
from jax.sharding import PartitionSpec as P

MIB = 1024 * 1024
TAIL = 16
TRIALS = 2
AHEAD = 3
STAGED = 8


def exchange(value, n, mask):
    return lax.ppermute(value, "op", [(i, i ^ mask) for i in range(n)])


def chip_at(place, chips):
    return 2 * place if place < chips // 2 else 2 * (chips - place) - 1


def ring_step(value, n):
    chips = n // 2
    order = [chip_at(place, chips) for place in range(chips)]
    pairs = []
    for place, chip in enumerate(order):
        pairs.append((2 * chip, 2 * order[(place + 1) % chips]))
        pairs.append((2 * chip + 1, 2 * order[(place - 1) % chips] + 1))
    return lax.ppermute(value, "op", pairs)


def owner_of(step, swapped, half, n):
    chips = n // 2
    me = lax.axis_index("op")
    chip, core = me // 2, lax.rem(me, 2)
    odd = lax.rem(chip, 2)
    mine = jnp.where(odd == 0, chip // 2, chips - 1 - chip // 2)
    line = 1 - core if swapped else core
    place = lax.rem(mine + (2 * line - 1) * step + 2 * chips, chips)
    there = jnp.where(place < chips // 2, 2 * place, 2 * (chips - place) - 1)
    return 2 * there + (line if half == 0 else 1 - line)


def split3(value):
    lanes = lax.broadcasted_iota(jnp.int32, (8, 128), 1)
    high = value.astype(jnp.bfloat16).astype(jnp.float32)
    middle = (value - high).astype(jnp.bfloat16).astype(jnp.float32)
    low = (value - high - middle).astype(jnp.bfloat16).astype(jnp.float32)
    return jnp.where(lanes < 2, high, jnp.where(lanes < 4, middle, low))


def tail_of(first, second):
    return jnp.concatenate([first, second], axis=0).astype(jnp.bfloat16)


def matrix_of(values, repeats=1):
    rows = lax.broadcasted_iota(jnp.int32, (8, 128), 0)
    lanes = lax.broadcasted_iota(jnp.int32, (8, 128), 1)
    total = jnp.zeros((8, 128), jnp.float32)
    for (i, j), value in values.items():
        for repeat in range(repeats):
            total = total + jnp.where((rows == i) & (lanes == j + 2 * repeat), value, 0.0)
    return total


def fold(value):
    return value.reshape(16, 8, 128).sum(axis=0)


def across(left, right):
    return lax.dot_general(left, right, (((1,), (1,)), ((), ())), preferred_element_type=jnp.float32)


def fits(n):
    return n <= 16


def phases_of(n):
    return 1


def chunk_of(n):
    return 96 if fits(n) else 48


def run_of(slots, n):
    return 4 if slots >= 8 * n else 2


def source_places(slots, n):
    chunk = chunk_of(n)
    most = slots + min(slots, n) * (run_of(slots, n) - 1)
    return -(-most // chunk) * chunk


def place_of(chip, chips):
    half = jnp.floor(chip * 0.5)
    return jnp.where(chip == 2.0 * half, half, chips - 1.0 - half)


def plan_kernel(n, terms, tasks_ref, plan_ref):
    slots = tasks_ref.shape[1]
    places = plan_ref.shape[1]
    chips = n // 2
    phases = phases_of(n)
    rows = tasks_ref[...].astype(jnp.float32)
    source, target, term, live = rows[0:1], rows[1:2], rows[2:3], rows[3:4]
    lane = lax.broadcasted_iota(jnp.int32, (1, slots), 1).astype(jnp.float32)
    number = lax.broadcasted_iota(jnp.int32, (1, places), 1).astype(jnp.float32)
    at = lax.broadcasted_iota(jnp.int32, (slots, places), 1).astype(jnp.float32)
    me = lax.axis_index("op")
    mine = place_of((jnp.zeros((1, slots), jnp.int32) + me // 2).astype(jnp.float32), float(chips))
    gap = place_of(jnp.floor(source * 0.5), float(chips)) - mine
    up = jnp.where(gap < 0, gap + chips, gap)
    far = jnp.minimum(up, chips - up)
    phase = jnp.clip(far - 1.0, 0.0, phases - 1.0)

    def column(*values):
        pad = [jnp.zeros((8 - len(values), slots), jnp.float32)]
        return jnp.transpose(jnp.concatenate(list(values) + pad, axis=0))

    def sort(sector, parts, unit, whole):
        keys = parts * n
        index = lax.broadcasted_iota(jnp.int32, (keys, slots), 0).astype(jnp.float32)
        part = phase if parts > 1 else jnp.zeros_like(phase)
        key = jnp.where(live > 0, part * n + sector, float(keys))
        columns = column(key, lane)
        earlier = jnp.where((columns[:, 0:1] == key) & (columns[:, 1:2] < lane), 1.0, 0.0)
        count = jnp.sum(jnp.where(index == key, 1.0, 0.0), axis=1, keepdims=True)
        padded = jnp.ceil(count / unit) * unit
        place = jnp.sum(earlier, axis=0, keepdims=True)
        start = jnp.zeros((1, 1), jnp.float32)
        starts = [start]
        for p in range(parts):
            lengths = padded[p * n : (p + 1) * n]
            before = jnp.where(index[p * n : (p + 1) * n] < key, lengths, 0.0)
            place = place + jnp.where(part == p, start * whole + jnp.sum(before, axis=0, keepdims=True), 0.0)
            start = start + jnp.ceil(jnp.sum(lengths, axis=0, keepdims=True) / whole)
            starts.append(start)
        return jnp.where(live > 0, place, -1.0), starts

    by_source, source_starts = sort(source, phases, float(run_of(slots, n)), float(chunk_of(n)))
    by_target, target_starts = sort(target, 1, 2.0, float(chunk_of(n)))
    columns = column(by_source, by_target, lane, source, term, target)

    def picker(places_column):
        hit = places_column == at

        def pick(values, other):
            found = jnp.sum(jnp.where(hit, values - other, 0.0), axis=0, keepdims=True)
            return (found + other).astype(jnp.int32)

        return pick

    own = (jnp.zeros((1, 1), jnp.int32) + me).astype(jnp.float32)
    pick = picker(columns[:, 0:1])
    plan_ref[0:1] = pick(columns[:, 2:3], 0.0)
    plan_ref[1:2] = pick(columns[:, 3:4], own)
    pick = picker(columns[:, 1:2])
    plan_ref[2:3] = pick(columns[:, 0:1], -1.0)
    plan_ref[3:4] = pick(columns[:, 4:5], float(terms))
    plan_ref[4:5] = pick(columns[:, 5:6], float(n))
    turns = jnp.zeros((1, places), jnp.float32)
    for p, start in enumerate(source_starts + [target_starts[1]]):
        turns = turns + jnp.where(number == p, start, 0.0)
    plan_ref[5:6] = turns.astype(jnp.int32)
    plan_ref[6:8] = jnp.zeros((2, places), jnp.int32)


def stage_kernel(n, terms, tasks_ref, left_ref, plan_ref, held_ref, tasks, sem):
    copies = [pltpu.make_async_copy(tasks_ref, tasks, sem.at[0])]
    share = left_ref.shape[0] // STAGED
    for part in range(STAGED):
        rows = pl.ds(part * share, share)
        copies.append(pltpu.make_async_copy(left_ref.at[rows], held_ref.at[rows], sem.at[1 + part]))
    for copy in copies:
        copy.start()
    copies[0].wait()
    plan_kernel(n, terms, tasks, plan_ref)
    for copy in copies[1:]:
        copy.wait()


def make_plan(tasks, left_ops, n, terms):
    most = source_places(tasks.shape[1], n) + chunk_of(n)
    plan = jax.ShapeDtypeStruct((8, -(-most // 128) * 128), jnp.int32)
    vmem, hbm = pl.BlockSpec(memory_space=pltpu.VMEM), pl.BlockSpec(memory_space=pltpu.HBM)
    if fits(n):
        return pl.pallas_call(
            functools.partial(stage_kernel, n, terms),
            in_specs=[hbm, hbm],
            out_specs=(vmem, vmem),
            out_shape=(plan, jax.ShapeDtypeStruct(left_ops.shape, left_ops.dtype)),
            scratch_shapes=[pltpu.VMEM(tasks.shape, jnp.int32), pltpu.SemaphoreType.DMA((1 + STAGED,))],
            compiler_params=pltpu.CompilerParams(vmem_limit_bytes=42 * MIB),
        )(tasks, left_ops)
    return (
        pl.pallas_call(
            functools.partial(plan_kernel, n, terms),
            out_shape=plan,
            compiler_params=pltpu.CompilerParams(vmem_limit_bytes=16 * MIB),
        )(tasks),
        left_ops,
    )


def block_parts(n, kinds, blocks, trial, right):
    parts = []
    for b, kind in enumerate(kinds):
        vectors, *terms = blocks[3 * b : 3 * b + 3]
        for half, ref in enumerate(terms):
            owner = owner_of(*kind, half, n)
            per = ref.shape[0]
            parts.append((vectors.at[pl.ds(half * TRIALS, TRIALS)], trial.at[owner]))
            parts.append((ref, right.at[pl.ds(owner * per, per)]))
    return parts


def make_halves(n, plan_ref, left_ref, trial, halves, fetched):
    turns = plan_ref[5, 1]
    run = run_of(left_ref.shape[0], n)
    chunk = chunk_of(n)

    def fetch(turn):
        left, left_sem = fetched
        at = lax.rem(turn, AHEAD)
        for u in range(chunk):
            slot = plan_ref[0, turn * chunk + u]
            pltpu.make_async_copy(left_ref.at[slot], left.at[at, u], left_sem.at[at]).start()

    def start():
        for turn in range(AHEAD - 1) if fetched else ():

            @pl.when(turn < turns)
            def _():
                fetch(turn)

    def turn_of(turn, carry):
        if fetched:
            left, left_sem = fetched

            @pl.when(turn + AHEAD - 1 < turns)
            def _():
                fetch(turn + AHEAD - 1)

            at = lax.rem(turn, AHEAD)
            pltpu.make_async_copy(left_ref.at[pl.ds(0, chunk)], left.at[at], left_sem.at[at]).wait()
        place = turn * chunk
        for r in range(0, chunk, run):
            source = plan_ref[1, place + r]
            vectors = jnp.concatenate([trial[source, 0], trial[source, 1]], axis=0)
            if fetched:
                rows = left[at, r : r + run].reshape(run * 128, 128)
            else:
                rows = jnp.concatenate([left_ref[plan_ref[0, place + r + u]] for u in range(run)], axis=0)
            half = across(rows, vectors).astype(jnp.bfloat16)
            for u in range(run):
                halves[place + r + u, 0] = half[u * 128 : (u + 1) * 128, :128]
                halves[place + r + u, 1] = half[u * 128 : (u + 1) * 128, 128:]
        return carry

    return start, lambda: lax.fori_loop(0, turns, turn_of, 0)


def tasks_kernel(n, kinds, plan_ref, left_ref, *refs):
    blocks, refs = refs[: 3 * len(kinds)], refs[3 * len(kinds) :]
    send_ref, acc, own_ref, halves, trial, right, block_sem, *fetched = refs
    start, products = make_halves(n, plan_ref, left_ref, trial, halves, fetched)
    right[right.shape[0] - 1] = jnp.zeros((128, 128), jnp.bfloat16)
    start()
    parts = block_parts(n, kinds, blocks, trial, right)
    copies = []
    for index, (source, to) in enumerate(parts):
        if fits(n):
            to[...] = source[...]
        else:
            copies.append(pltpu.make_async_copy(source, to, block_sem.at[index]))
            copies[-1].start()

    def clear(s, carry):
        acc[s] = jnp.zeros((256, 128), jnp.float32)
        return carry

    lax.fori_loop(0, n, clear, 0)
    for copy in copies:
        copy.wait()
    products()

    def target_turn(turn, carry):
        first = turn * chunk_of(n)
        for u in range(0, chunk_of(n), 2):
            place = first + u
            one = plan_ref[2, place]
            two = plan_ref[2, place + 1]
            one, two = jnp.maximum(one, 0), jnp.where(two < 0, jnp.maximum(one, 0), two)
            pair = jnp.concatenate(
                [
                    jnp.concatenate([halves[one, 0], halves[two, 0]], axis=1),
                    jnp.concatenate([halves[one, 1], halves[two, 1]], axis=1),
                ],
                axis=0,
            )
            rights = jnp.concatenate([right[plan_ref[3, place]], right[plan_ref[3, place + 1]]], axis=1)
            term = across(rights, pair)
            target = plan_ref[4, place]
            acc[target, 0:128] = acc[target, 0:128] + term[:, :128]
            acc[target, 128:256] = acc[target, 128:256] + term[:, 128:]
        return carry

    lax.fori_loop(0, plan_ref[5, 2], target_turn, 0)
    me = lax.axis_index("op")

    def dots(s, carry):
        t0 = trial[s, 0].astype(jnp.float32)
        t1 = trial[s, 1].astype(jnp.float32)
        a0 = acc[s, 0:128, :]
        a1 = acc[s, 128:256, :]
        p00, p01, p10, p11 = carry
        return p00 + fold(t0 * a0), p01 + fold(t0 * a1), p10 + fold(t1 * a0), p11 + fold(t1 * a1)

    zero = jnp.zeros((8, 128), jnp.float32)
    sums = lax.fori_loop(0, n, dots, (zero,) * 4, unroll=4)
    p00, p01, p10, p11 = [jnp.sum(x) for x in sums]

    def pack(j, carry):
        mine = jnp.bitwise_xor(me, 2 * j)
        send_ref[pl.ds(pl.multiple_of(j * 256, 256), 256), :] = acc[jnp.bitwise_xor(mine, 1)].astype(jnp.bfloat16)
        return carry

    lax.fori_loop(0, n // 2, pack, 0, unroll=2)
    own = split3(matrix_of({(0, 0): p00, (0, 1): p01, (1, 0): p10, (1, 1): p11}, 3))
    own_ref[...] = own
    send_ref[n // 2 * 256 :, :] = tail_of(own, jnp.zeros_like(own))


def run_tasks(n, plan, left_ops, blocks):
    slots = left_ops.shape[0]
    terms_per = blocks[0][0][1].shape[0]
    kinds = tuple(block[1:] for block in blocks)
    vmem, hbm = pl.BlockSpec(memory_space=pltpu.VMEM), pl.BlockSpec(memory_space=pltpu.HBM)
    given = vmem if fits(n) else hbm
    fetched = [] if fits(n) else [
        pltpu.VMEM((AHEAD, chunk_of(n), 128, 128), jnp.bfloat16),
        pltpu.SemaphoreType.DMA((AHEAD,)),
    ]
    return pl.pallas_call(
        functools.partial(tasks_kernel, n, kinds),
        out_shape=(
            jax.ShapeDtypeStruct((n // 2 * 256 + TAIL, 128), jnp.bfloat16),
            jax.ShapeDtypeStruct((n + 1, 256, 128), jnp.float32),
            jax.ShapeDtypeStruct((8, 128), jnp.float32),
        ),
        in_specs=[pl.BlockSpec(memory_space=pltpu.SMEM)] + [given] * (1 + 3 * len(blocks)),
        out_specs=(vmem,) * 3,
        scratch_shapes=[
            pltpu.VMEM((source_places(slots, n), 2, 128, 128), jnp.bfloat16),
            pltpu.VMEM((n, TRIALS, 128, 128), jnp.bfloat16),
            pltpu.VMEM((n * terms_per + 1, 128, 128), jnp.bfloat16),
            pltpu.SemaphoreType.DMA((4 * len(blocks),)),
        ]
        + fetched,
        compiler_params=pltpu.CompilerParams(vmem_limit_bytes=(30 if fits(n) else 58) * MIB),
        cost_estimate=pl.CostEstimate(
            flops=slots * 8 * 128**3, bytes_accessed=slots * 32768 + n * 450000, transcendentals=0
        ),
    )(plan, left_ops, *[value for block in blocks for value in block[0]])


def join_kernel(own_ref, other_ref, both_ref):
    for i, ref in enumerate((own_ref, other_ref)):
        for v in range(TRIALS):
            both_ref[i * TRIALS + v] = jnp.transpose(ref[v])


def join(own, other):
    return pl.pallas_call(
        join_kernel,
        out_shape=jax.ShapeDtypeStruct((2 * TRIALS, 128, 128), jnp.bfloat16),
        compiler_params=pltpu.CompilerParams(vmem_limit_bytes=16 * MIB),
    )(own, other)


def corr_kernel(*refs):
    blocks, corr_ref = refs[:-1], refs[-1]
    total = [jnp.zeros((8, 128), jnp.float32)] * 3
    for ref in blocks:
        for start in range(0, ref.shape[0], TRIALS):
            t0, t1 = ref[start].astype(jnp.float32), ref[start + 1].astype(jnp.float32)
            total = [total[0] + fold(t0 * t0), total[1] + fold(t0 * t1), total[2] + fold(t1 * t1)]
    c00, c01, c11 = [jnp.sum(x) for x in total]
    corr_ref[...] = matrix_of({(0, 0): c00, (0, 1): c01, (1, 0): c01, (1, 1): c11})[0:2, 0:2]


def correlate(blocks):
    return pl.pallas_call(
        corr_kernel,
        out_shape=jax.ShapeDtypeStruct((2, 2), jnp.float32),
        compiler_params=pltpu.CompilerParams(vmem_limit_bytes=16 * MIB),
    )(*blocks)


def chip_kernel(chips, keep_ref, own_ref, received_ref, mine_ref, total_ref, *sends):
    total = jnp.concatenate([own_ref[...], received_ref[chips * 256 :, :].astype(jnp.float32)[0:8]], axis=0)
    total_ref[...] = total
    tail = total.astype(jnp.bfloat16)
    me = lax.axis_index("op")
    for j in range(chips):
        value = keep_ref[jnp.bitwise_xor(me, 2 * j)] + received_ref[j * 256 : (j + 1) * 256, :].astype(jnp.float32)
        if j == 0:
            mine_ref[...] = value
        else:
            sends[j - 1][0:256, :] = value.astype(jnp.bfloat16)
            sends[j - 1][256:, :] = tail


def add_chip(keep, own, received):
    chips = keep.shape[0] // 2
    return pl.pallas_call(
        functools.partial(chip_kernel, chips),
        out_shape=(jax.ShapeDtypeStruct((256, 128), jnp.float32), jax.ShapeDtypeStruct((16, 128), jnp.float32))
        + (jax.ShapeDtypeStruct((256 + TAIL, 128), jnp.bfloat16),) * (chips - 1),
        compiler_params=pltpu.CompilerParams(vmem_limit_bytes=16 * MIB),
    )(keep, own, received)


def last_kernel(mine_ref, total_ref, *refs):
    received, (product_ref, projected_ref) = refs[:-2], refs[-2:]
    value, total = mine_ref[...], total_ref[...]
    for ref in received:
        value = value + ref[0:256, :].astype(jnp.float32)
        total = total + ref[256:, :].astype(jnp.float32)
    product_ref[0, 0] = jnp.transpose(value[0:128])
    product_ref[0, 1] = jnp.transpose(value[128:256])
    total = total[0:8] + total[8:16]
    projected_ref[...] = total[0:2, 0:2] + total[0:2, 2:4] + total[0:2, 4:6]


def add_all(mine, total, received):
    return pl.pallas_call(
        last_kernel,
        out_shape=(
            jax.ShapeDtypeStruct((1, 2, 128, 128), jnp.float32),
            jax.ShapeDtypeStruct((2, 2), jnp.float32),
        ),
        compiler_params=pltpu.CompilerParams(vmem_limit_bytes=16 * MIB),
    )(mine, total, *received)


def body(n, trial, left_ops, right_ops, task_list):
    steps = n // 4
    plan, left_ops = make_plan(task_list.T, left_ops, n, n * right_ops.shape[0])
    vectors = join(trial[0], exchange(trial[0], n, 1))
    line = [vectors, right_ops, exchange(right_ops, n, 1)]
    blocks = [(line, 0, False)]
    for step in range(1, steps + 1):
        line = [ring_step(value, n) for value in line]
        blocks.append((line, step, False))
        if step < steps:
            blocks.append(([exchange(value, n, 1) for value in line], step, True))
    send, keep, own = run_tasks(n, plan, left_ops, blocks)
    send, arrays = lax.optimization_barrier((send, [block[0][0] for block in blocks]))
    correlation = correlate(arrays)
    mine, total, *sends = add_chip(keep, own, exchange(send, n, 1))
    received = [exchange(sends[j - 1], n, 2 * j) for j in reversed(range(1, n // 2))]
    product, projected = add_all(mine, total, received)
    return product, correlation, projected


def solution(mesh):
    return jax.shard_map(
        functools.partial(body, mesh.shape["op"]),
        mesh=mesh,
        in_specs=(
            P(("groups", "op"), None, None, None),
            P(("groups", "op"), None, None),
            P(("groups", "op"), None, None),
            P(("groups", "op"), None),
        ),
        out_specs=(P(("groups", "op"), None, None, None), P("groups", None), P("groups", None)),
        check_vma=False,
    )
```

```python
import functools

import jax
import jax.numpy as jnp
from jax import lax
from jax.experimental import pallas as pl
from jax.experimental.pallas import tpu as pltpu
from jax.sharding import PartitionSpec as P

MIB = 1024 * 1024
TAIL = 16
TRIALS = 2
AHEAD = 3


def exchange(value, n, mask):
    return lax.ppermute(value, "op", [(i, i ^ mask) for i in range(n)])


def chip_at(place, chips):
    return 2 * place if place < chips // 2 else 2 * (chips - place) - 1


def ring_step(value, n):
    chips = n // 2
    order = [chip_at(place, chips) for place in range(chips)]
    pairs = []
    for place, chip in enumerate(order):
        pairs.append((2 * chip, 2 * order[(place + 1) % chips]))
        pairs.append((2 * chip + 1, 2 * order[(place - 1) % chips] + 1))
    return lax.ppermute(value, "op", pairs)


def owner_of(step, swapped, half, n):
    chips = n // 2
    me = lax.axis_index("op")
    chip, core = me // 2, lax.rem(me, 2)
    odd = lax.rem(chip, 2)
    mine = jnp.where(odd == 0, chip // 2, chips - 1 - chip // 2)
    line = 1 - core if swapped else core
    place = lax.rem(mine + (2 * line - 1) * step + 2 * chips, chips)
    there = jnp.where(place < chips // 2, 2 * place, 2 * (chips - place) - 1)
    return 2 * there + (line if half == 0 else 1 - line)


def split3(value):
    lanes = lax.broadcasted_iota(jnp.int32, (8, 128), 1)
    high = value.astype(jnp.bfloat16).astype(jnp.float32)
    middle = (value - high).astype(jnp.bfloat16).astype(jnp.float32)
    low = (value - high - middle).astype(jnp.bfloat16).astype(jnp.float32)
    return jnp.where(lanes < 2, high, jnp.where(lanes < 4, middle, low))


def tail_of(first, second):
    return jnp.concatenate([first, second], axis=0).astype(jnp.bfloat16)


def matrix_of(values, repeats=1):
    rows = lax.broadcasted_iota(jnp.int32, (8, 128), 0)
    lanes = lax.broadcasted_iota(jnp.int32, (8, 128), 1)
    total = jnp.zeros((8, 128), jnp.float32)
    for (i, j), value in values.items():
        for repeat in range(repeats):
            total = total + jnp.where((rows == i) & (lanes == j + 2 * repeat), value, 0.0)
    return total


def fold(value):
    return value.reshape(16, 8, 128).sum(axis=0)


def fits(n):
    return n <= 16


def near_chips(n):
    return n // 4


def phases_of(n):
    return 1


def chunk_of(n):
    return 96 if fits(n) else 48


def pairs_of(n):
    return 46 if fits(n) else 24


def run_of(slots, n):
    return 4 if slots >= 8 * n else 2


def source_places(slots, n):
    chunk = chunk_of(n)
    most = slots + min(slots, n) * (run_of(slots, n) - 1)
    return -(-most // chunk) * chunk


def place_of(chip, chips):
    half = jnp.floor(chip * 0.5)
    return jnp.where(chip == 2.0 * half, half, chips - 1.0 - half)


def plan_kernel(n, terms, tasks_ref, plan_ref):
    slots = tasks_ref.shape[1]
    places = plan_ref.shape[1]
    chips = n // 2
    phases = phases_of(n)
    rows = tasks_ref[...].astype(jnp.float32)
    source, target, term, live = rows[0:1], rows[1:2], rows[2:3], rows[3:4]
    lane = lax.broadcasted_iota(jnp.int32, (1, slots), 1).astype(jnp.float32)
    number = lax.broadcasted_iota(jnp.int32, (1, places), 1).astype(jnp.float32)
    at = lax.broadcasted_iota(jnp.int32, (slots, places), 1).astype(jnp.float32)
    me = lax.axis_index("op")
    mine = place_of((jnp.zeros((1, slots), jnp.int32) + me // 2).astype(jnp.float32), float(chips))
    gap = place_of(jnp.floor(source * 0.5), float(chips)) - mine
    up = jnp.where(gap < 0, gap + chips, gap)
    far = jnp.minimum(up, chips - up)
    phase = jnp.clip(far - 1.0, 0.0, phases - 1.0)

    def column(*values):
        pad = [jnp.zeros((8 - len(values), slots), jnp.float32)]
        return jnp.transpose(jnp.concatenate(list(values) + pad, axis=0))

    def sort(sector, parts, unit, whole):
        keys = parts * n
        index = lax.broadcasted_iota(jnp.int32, (keys, slots), 0).astype(jnp.float32)
        part = phase if parts > 1 else jnp.zeros_like(phase)
        key = jnp.where(live > 0, part * n + sector, float(keys))
        columns = column(key, lane)
        earlier = jnp.where((columns[:, 0:1] == key) & (columns[:, 1:2] < lane), 1.0, 0.0)
        count = jnp.sum(jnp.where(index == key, 1.0, 0.0), axis=1, keepdims=True)
        padded = jnp.ceil(count / unit) * unit
        place = jnp.sum(earlier, axis=0, keepdims=True)
        start = jnp.zeros((1, 1), jnp.float32)
        starts = [start]
        for p in range(parts):
            lengths = padded[p * n : (p + 1) * n]
            before = jnp.where(index[p * n : (p + 1) * n] < key, lengths, 0.0)
            place = place + jnp.where(part == p, start * whole + jnp.sum(before, axis=0, keepdims=True), 0.0)
            start = start + jnp.ceil(jnp.sum(lengths, axis=0, keepdims=True) / whole)
            starts.append(start)
        return jnp.where(live > 0, place, -1.0), starts

    by_source, source_starts = sort(source, phases, float(run_of(slots, n)), float(chunk_of(n)))
    by_target, target_starts = sort(target, 1, 2.0, 2.0 * pairs_of(n))
    columns = column(by_source, by_target, lane, source, term, target)

    def picker(places_column):
        hit = places_column == at

        def pick(values, other):
            found = jnp.sum(jnp.where(hit, values - other, 0.0), axis=0, keepdims=True)
            return (found + other).astype(jnp.int32)

        return pick

    own = (jnp.zeros((1, 1), jnp.int32) + me).astype(jnp.float32)
    pick = picker(columns[:, 0:1])
    plan_ref[0:1] = pick(columns[:, 2:3], 0.0)
    plan_ref[1:2] = pick(columns[:, 3:4], own)
    pick = picker(columns[:, 1:2])
    plan_ref[2:3] = pick(columns[:, 0:1], -1.0)
    plan_ref[3:4] = pick(columns[:, 4:5], float(terms))
    plan_ref[4:5] = pick(columns[:, 5:6], float(n))
    turns = jnp.zeros((1, places), jnp.float32)
    for p, start in enumerate(source_starts + [target_starts[1]]):
        turns = turns + jnp.where(number == p, start, 0.0)
    plan_ref[5:6] = turns.astype(jnp.int32)


def stage_kernel(n, terms, tasks_ref, left_ref, plan_ref, held_ref, tasks, sem):
    copies = [
        pltpu.make_async_copy(tasks_ref, tasks, sem.at[0]),
        pltpu.make_async_copy(left_ref, held_ref, sem.at[1]),
    ]
    for copy in copies:
        copy.start()
    copies[0].wait()
    plan_kernel(n, terms, tasks, plan_ref)
    copies[1].wait()


def make_plan(tasks, left_ops, n, terms):
    most = source_places(tasks.shape[1], n)
    plan = jax.ShapeDtypeStruct((6, -(-most // 128) * 128), jnp.int32)
    vmem, hbm = pl.BlockSpec(memory_space=pltpu.VMEM), pl.BlockSpec(memory_space=pltpu.HBM)
    if fits(n):
        return pl.pallas_call(
            functools.partial(stage_kernel, n, terms),
            in_specs=[hbm, hbm],
            out_specs=(vmem, vmem),
            out_shape=(plan, jax.ShapeDtypeStruct(left_ops.shape, left_ops.dtype)),
            scratch_shapes=[pltpu.VMEM(tasks.shape, jnp.int32), pltpu.SemaphoreType.DMA((2,))],
            compiler_params=pltpu.CompilerParams(vmem_limit_bytes=42 * MIB),
        )(tasks, left_ops)
    return (
        pl.pallas_call(
            functools.partial(plan_kernel, n, terms),
            out_shape=plan,
            compiler_params=pltpu.CompilerParams(vmem_limit_bytes=16 * MIB),
        )(tasks),
        left_ops,
    )


def block_parts(n, kinds, blocks, trial, right):
    parts = []
    for b, kind in enumerate(kinds):
        vectors, *terms = blocks[3 * b : 3 * b + 3]
        for half, ref in enumerate(terms):
            owner = owner_of(*kind, half, n)
            per = ref.shape[0]
            parts.append((vectors.at[pl.ds(half * TRIALS, TRIALS)], trial.at[owner]))
            parts.append((ref, right.at[pl.ds(owner * per, per)]))
    return parts


def make_halves(n, plan_ref, left_ref, trial, halves, fetched):
    turns = plan_ref[5, 1]
    run = run_of(left_ref.shape[0], n)
    chunk = chunk_of(n)

    def fetch(turn):
        left, left_sem = fetched
        at = lax.rem(turn, AHEAD)
        for u in range(chunk):
            slot = plan_ref[0, turn * chunk + u]
            pltpu.make_async_copy(left_ref.at[slot], left.at[at, u], left_sem.at[at]).start()

    def start():
        for turn in range(AHEAD - 1) if fetched else ():

            @pl.when(turn < turns)
            def _():
                fetch(turn)

    def turn_of(turn, carry):
        if fetched:
            left, left_sem = fetched

            @pl.when(turn + AHEAD - 1 < turns)
            def _():
                fetch(turn + AHEAD - 1)

            at = lax.rem(turn, AHEAD)
            pltpu.make_async_copy(left_ref.at[pl.ds(0, chunk)], left.at[at], left_sem.at[at]).wait()
        place = turn * chunk
        for r in range(0, chunk, run):
            source = plan_ref[1, place + r]
            vectors = jnp.concatenate([trial[source, 0], trial[source, 1]], axis=1)
            if fetched:
                rows = left[at, r : r + run].reshape(run * 128, 128)
            else:
                rows = jnp.concatenate([left_ref[plan_ref[0, place + r + u]] for u in range(run)], axis=0)
            half = jnp.dot(rows, vectors, preferred_element_type=jnp.float32).astype(jnp.bfloat16)
            for u in range(run):
                halves[place + r + u, 0] = half[u * 128 : (u + 1) * 128, :128]
                halves[place + r + u, 1] = half[u * 128 : (u + 1) * 128, 128:]
        return carry

    return start, lambda: lax.fori_loop(0, turns, turn_of, 0)


def tasks_kernel(n, kinds, plan_ref, left_ref, *refs):
    blocks, refs = refs[: 3 * len(kinds)], refs[3 * len(kinds) :]
    far_ref, near_ref, acc, own_ref, halves, trial, right, block_sem, *fetched = refs
    start, products = make_halves(n, plan_ref, left_ref, trial, halves, fetched)
    right[right.shape[0] - 1] = jnp.zeros((128, 128), jnp.bfloat16)
    start()
    parts = block_parts(n, kinds, blocks, trial, right)
    copies = []
    for index, (source, to) in enumerate(parts):
        if fits(n):
            to[...] = source[...]
        else:
            copies.append(pltpu.make_async_copy(source, to, block_sem.at[index]))
            copies[-1].start()

    def clear(s, carry):
        acc[s] = jnp.zeros((256, 128), jnp.float32)
        return carry

    lax.fori_loop(0, n, clear, 0)
    for copy in copies:
        copy.wait()
    products()

    def target_turn(turn, carry):
        first = turn * 2 * pairs_of(n)
        for u in range(0, 2 * pairs_of(n), 2):
            place = first + u
            one = plan_ref[2, place]
            two = plan_ref[2, place + 1]
            one, two = jnp.maximum(one, 0), jnp.where(two < 0, jnp.maximum(one, 0), two)
            pair = jnp.concatenate(
                [
                    jnp.concatenate([halves[one, 0], halves[two, 0]], axis=1),
                    jnp.concatenate([halves[one, 1], halves[two, 1]], axis=1),
                ],
                axis=0,
            )
            rights = jnp.concatenate([right[plan_ref[3, place]], right[plan_ref[3, place + 1]]], axis=1)
            term = lax.dot_general(
                pair, rights, (((1,), (1,)), ((), ())), preferred_element_type=jnp.float32
            )
            target = plan_ref[4, place]
            acc[target] = acc[target] + term
        return carry

    lax.fori_loop(0, plan_ref[5, 2], target_turn, 0)
    me = lax.axis_index("op")

    def dots(s, carry):
        t0 = trial[s, 0].astype(jnp.float32)
        t1 = trial[s, 1].astype(jnp.float32)
        a0 = acc[s, 0:128, :]
        a1 = acc[s, 128:256, :]
        p00, p01, p10, p11 = carry
        return p00 + fold(t0 * a0), p01 + fold(t0 * a1), p10 + fold(t1 * a0), p11 + fold(t1 * a1)

    zero = jnp.zeros((8, 128), jnp.float32)
    sums = lax.fori_loop(0, n, dots, (zero,) * 4, unroll=4)
    p00, p01, p10, p11 = [jnp.sum(x) for x in sums]

    chips = n // 2
    near = near_chips(n)

    def pack(j, carry):
        value = acc[jnp.bitwise_xor(me, 2 * j + 1)].astype(jnp.bfloat16)

        @pl.when(j < near)
        def _():
            near_ref[pl.ds(pl.multiple_of(j * 256, 256), 256), :] = value

        @pl.when(j >= near)
        def _():
            far_ref[pl.ds(pl.multiple_of((j - near) * 256, 256), 256), :] = value

        return carry

    lax.fori_loop(0, chips, pack, 0, unroll=2)
    own = split3(matrix_of({(0, 0): p00, (0, 1): p01, (1, 0): p10, (1, 1): p11}, 3))
    own_ref[...] = own
    far_ref[(chips - near) * 256 :, :] = tail_of(own, jnp.zeros_like(own))


def run_tasks(n, plan, left_ops, blocks):
    slots = left_ops.shape[0]
    terms_per = blocks[0][0][1].shape[0]
    kinds = tuple(block[1:] for block in blocks)
    vmem, hbm = pl.BlockSpec(memory_space=pltpu.VMEM), pl.BlockSpec(memory_space=pltpu.HBM)
    given = vmem if fits(n) else hbm
    fetched = [] if fits(n) else [
        pltpu.VMEM((AHEAD, chunk_of(n), 128, 128), jnp.bfloat16),
        pltpu.SemaphoreType.DMA((AHEAD,)),
    ]
    return pl.pallas_call(
        functools.partial(tasks_kernel, n, kinds),
        out_shape=(
            jax.ShapeDtypeStruct(((n // 2 - near_chips(n)) * 256 + TAIL, 128), jnp.bfloat16),
            jax.ShapeDtypeStruct((near_chips(n) * 256, 128), jnp.bfloat16),
            jax.ShapeDtypeStruct((n + 1, 256, 128), jnp.float32),
            jax.ShapeDtypeStruct((8, 128), jnp.float32),
        ),
        in_specs=[pl.BlockSpec(memory_space=pltpu.SMEM)] + [given] * (1 + 3 * len(blocks)),
        out_specs=(vmem,) * 4,
        scratch_shapes=[
            pltpu.VMEM((source_places(slots, n), 2, 128, 128), jnp.bfloat16),
            pltpu.VMEM((n, TRIALS, 128, 128), jnp.bfloat16),
            pltpu.VMEM((n * terms_per + 1, 128, 128), jnp.bfloat16),
            pltpu.SemaphoreType.DMA((4 * len(blocks),)),
        ]
        + fetched,
        compiler_params=pltpu.CompilerParams(vmem_limit_bytes=(30 if fits(n) else 58) * MIB),
        cost_estimate=pl.CostEstimate(
            flops=slots * 8 * 128**3, bytes_accessed=slots * 32768 + n * 450000, transcendentals=0
        ),
    )(plan, left_ops, *[value for block in blocks for value in block[0]])


def corr_kernel(*refs):
    blocks, corr_ref = refs[:-1], refs[-1]
    total = [jnp.zeros((8, 128), jnp.float32)] * 3
    for ref in blocks:
        for start in range(0, ref.shape[0], TRIALS):
            t0, t1 = ref[start].astype(jnp.float32), ref[start + 1].astype(jnp.float32)
            total = [total[0] + fold(t0 * t0), total[1] + fold(t0 * t1), total[2] + fold(t1 * t1)]
    c00, c01, c11 = [jnp.sum(x) for x in total]
    corr_ref[...] = matrix_of({(0, 0): c00, (0, 1): c01, (1, 0): c01, (1, 1): c11})[0:2, 0:2]


def correlate(blocks):
    return pl.pallas_call(
        corr_kernel,
        out_shape=jax.ShapeDtypeStruct((2, 2), jnp.float32),
        compiler_params=pltpu.CompilerParams(vmem_limit_bytes=16 * MIB),
    )(*blocks)


def far_kernel(n, acc_ref, own_ref, received_ref, total_ref, *sends):
    far, near = n // 2 - near_chips(n), near_chips(n)
    total = jnp.concatenate([own_ref[...], received_ref[far * 256 :, :].astype(jnp.float32)[0:8]], axis=0)
    total_ref[...] = total
    me = lax.axis_index("op")
    for j in range(far):
        value = acc_ref[jnp.bitwise_xor(me, 2 * (near + j))] + received_ref[j * 256 : (j + 1) * 256, :].astype(
            jnp.float32
        )
        sends[j][0:256, :] = value.astype(jnp.bfloat16)
        sends[j][256:, :] = total.astype(jnp.bfloat16)


def add_far(n, acc, own, received):
    return pl.pallas_call(
        functools.partial(far_kernel, n),
        out_shape=(jax.ShapeDtypeStruct((16, 128), jnp.float32),)
        + (jax.ShapeDtypeStruct((256 + TAIL, 128), jnp.bfloat16),) * (n // 2 - near_chips(n)),
        compiler_params=pltpu.CompilerParams(vmem_limit_bytes=16 * MIB),
    )(acc, own, received)


def near_kernel(n, acc_ref, total_ref, received_ref, mine_ref, *sends):
    me = lax.axis_index("op")
    for j in range(near_chips(n)):
        value = acc_ref[jnp.bitwise_xor(me, 2 * j)] + received_ref[j * 256 : (j + 1) * 256, :].astype(jnp.float32)
        if j == 0:
            mine_ref[...] = value
        else:
            sends[j - 1][0:256, :] = value.astype(jnp.bfloat16)
            sends[j - 1][256:, :] = total_ref[...].astype(jnp.bfloat16)


def add_near(n, acc, total, received):
    return pl.pallas_call(
        functools.partial(near_kernel, n),
        out_shape=(jax.ShapeDtypeStruct((256, 128), jnp.float32),)
        + (jax.ShapeDtypeStruct((256 + TAIL, 128), jnp.bfloat16),) * (near_chips(n) - 1),
        compiler_params=pltpu.CompilerParams(vmem_limit_bytes=16 * MIB),
    )(acc, total, received)


def last_kernel(mine_ref, total_ref, *refs):
    received, (product_ref, projected_ref) = refs[:-2], refs[-2:]
    value, total = mine_ref[...], total_ref[...]
    for ref in received:
        value = value + ref[0:256, :].astype(jnp.float32)
        total = total + ref[256:, :].astype(jnp.float32)
    product_ref[0, 0] = value[0:128]
    product_ref[0, 1] = value[128:256]
    total = total[0:8] + total[8:16]
    projected_ref[...] = total[0:2, 0:2] + total[0:2, 2:4] + total[0:2, 4:6]


def add_all(mine, total, received):
    return pl.pallas_call(
        last_kernel,
        out_shape=(
            jax.ShapeDtypeStruct((1, 2, 128, 128), jnp.float32),
            jax.ShapeDtypeStruct((2, 2), jnp.float32),
        ),
        compiler_params=pltpu.CompilerParams(vmem_limit_bytes=16 * MIB),
    )(mine, total, *received)


def body(n, trial, left_ops, right_ops, task_list):
    steps = n // 4
    plan, left_ops = make_plan(task_list.T, left_ops, n, n * right_ops.shape[0])
    vectors = jnp.concatenate([trial[0], exchange(trial[0], n, 1)], axis=0)
    line = [vectors, right_ops, exchange(right_ops, n, 1)]
    blocks = [(line, 0, False)]
    for step in range(1, steps + 1):
        line = [ring_step(value, n) for value in line]
        blocks.append((line, step, False))
        if step < steps:
            blocks.append(([exchange(value, n, 1) for value in line], step, True))
    far, near, acc, own = run_tasks(n, plan, left_ops, blocks)
    far, arrays = lax.optimization_barrier((far, [block[0][0] for block in blocks]))
    correlation = correlate(arrays)
    far, near = exchange(far, n, 1), exchange(near, n, 1)
    total, *messages = add_far(n, acc, own, far)
    first = near_chips(n)
    received = [exchange(messages[j], n, 2 * (first + j)) for j in reversed(range(len(messages)))]
    mine, *messages = add_near(n, acc, total, near)
    received += [exchange(messages[j - 1], n, 2 * j) for j in reversed(range(1, first))]
    product, projected = add_all(mine, total, received)
    return product, correlation, projected


def solution(mesh):
    return jax.shard_map(
        functools.partial(body, mesh.shape["op"]),
        mesh=mesh,
        in_specs=(
            P(("groups", "op"), None, None, None),
            P(("groups", "op"), None, None),
            P(("groups", "op"), None, None),
            P(("groups", "op"), None),
        ),
        out_specs=(P(("groups", "op"), None, None, None), P("groups", None), P("groups", None)),
        check_vma=False,
    )
```

```python
import functools

import jax
import jax.numpy as jnp
from jax import lax
from jax.experimental import pallas as pl
from jax.experimental.pallas import tpu as pltpu
from jax.sharding import PartitionSpec as P

MIB = 1024 * 1024
TAIL = 16
TRIALS = 2
AHEAD = 3


def exchange(value, n, mask):
    return lax.ppermute(value, "op", [(i, i ^ mask) for i in range(n)])


def chip_at(place, chips):
    return 2 * place if place < chips // 2 else 2 * (chips - place) - 1


def ring_step(value, n):
    chips = n // 2
    order = [chip_at(place, chips) for place in range(chips)]
    pairs = []
    for place, chip in enumerate(order):
        pairs.append((2 * chip, 2 * order[(place + 1) % chips]))
        pairs.append((2 * chip + 1, 2 * order[(place - 1) % chips] + 1))
    return lax.ppermute(value, "op", pairs)


def owner_of(step, swapped, half, n):
    chips = n // 2
    me = lax.axis_index("op")
    chip, core = me // 2, lax.rem(me, 2)
    odd = lax.rem(chip, 2)
    mine = jnp.where(odd == 0, chip // 2, chips - 1 - chip // 2)
    line = 1 - core if swapped else core
    place = lax.rem(mine + (2 * line - 1) * step + 2 * chips, chips)
    there = jnp.where(place < chips // 2, 2 * place, 2 * (chips - place) - 1)
    return 2 * there + (line if half == 0 else 1 - line)


def split3(value):
    lanes = lax.broadcasted_iota(jnp.int32, (8, 128), 1)
    high = value.astype(jnp.bfloat16).astype(jnp.float32)
    middle = (value - high).astype(jnp.bfloat16).astype(jnp.float32)
    low = (value - high - middle).astype(jnp.bfloat16).astype(jnp.float32)
    return jnp.where(lanes < 2, high, jnp.where(lanes < 4, middle, low))


def tail_of(first, second):
    return jnp.concatenate([first, second], axis=0).astype(jnp.bfloat16)


def matrix_of(values, repeats=1):
    rows = lax.broadcasted_iota(jnp.int32, (8, 128), 0)
    lanes = lax.broadcasted_iota(jnp.int32, (8, 128), 1)
    total = jnp.zeros((8, 128), jnp.float32)
    for (i, j), value in values.items():
        for repeat in range(repeats):
            total = total + jnp.where((rows == i) & (lanes == j + 2 * repeat), value, 0.0)
    return total


def fold(value):
    return value.reshape(16, 8, 128).sum(axis=0)


def fits(n):
    return n <= 16


def near_chips(n):
    return n // 4


def phases_of(n):
    return 1


def chunk_of(n):
    return 144 if fits(n) else 48


def pairs_of(n):
    return 69 if fits(n) else 24


def run_of(slots, n):
    return 4 if slots >= 8 * n else 2


def source_places(slots, n):
    chunk = chunk_of(n)
    most = slots + min(slots, n) * (run_of(slots, n) - 1)
    return -(-most // chunk) * chunk


def place_of(chip, chips):
    half = jnp.floor(chip * 0.5)
    return jnp.where(chip == 2.0 * half, half, chips - 1.0 - half)


def plan_kernel(n, terms, tasks_ref, plan_ref):
    slots = tasks_ref.shape[1]
    places = plan_ref.shape[1]
    chips = n // 2
    phases = phases_of(n)
    rows = tasks_ref[...].astype(jnp.float32)
    source, target, term, live = rows[0:1], rows[1:2], rows[2:3], rows[3:4]
    lane = lax.broadcasted_iota(jnp.int32, (1, slots), 1).astype(jnp.float32)
    number = lax.broadcasted_iota(jnp.int32, (1, places), 1).astype(jnp.float32)
    at = lax.broadcasted_iota(jnp.int32, (slots, places), 1).astype(jnp.float32)
    me = lax.axis_index("op")
    mine = place_of((jnp.zeros((1, slots), jnp.int32) + me // 2).astype(jnp.float32), float(chips))
    gap = place_of(jnp.floor(source * 0.5), float(chips)) - mine
    up = jnp.where(gap < 0, gap + chips, gap)
    far = jnp.minimum(up, chips - up)
    phase = jnp.clip(far - 1.0, 0.0, phases - 1.0)

    def column(*values):
        pad = [jnp.zeros((8 - len(values), slots), jnp.float32)]
        return jnp.transpose(jnp.concatenate(list(values) + pad, axis=0))

    def sort(sector, parts, unit, whole):
        keys = parts * n
        index = lax.broadcasted_iota(jnp.int32, (keys, slots), 0).astype(jnp.float32)
        part = phase if parts > 1 else jnp.zeros_like(phase)
        key = jnp.where(live > 0, part * n + sector, float(keys))
        columns = column(key, lane)
        earlier = jnp.where((columns[:, 0:1] == key) & (columns[:, 1:2] < lane), 1.0, 0.0)
        count = jnp.sum(jnp.where(index == key, 1.0, 0.0), axis=1, keepdims=True)
        padded = jnp.ceil(count / unit) * unit
        place = jnp.sum(earlier, axis=0, keepdims=True)
        start = jnp.zeros((1, 1), jnp.float32)
        starts = [start]
        for p in range(parts):
            lengths = padded[p * n : (p + 1) * n]
            before = jnp.where(index[p * n : (p + 1) * n] < key, lengths, 0.0)
            place = place + jnp.where(part == p, start * whole + jnp.sum(before, axis=0, keepdims=True), 0.0)
            start = start + jnp.ceil(jnp.sum(lengths, axis=0, keepdims=True) / whole)
            starts.append(start)
        return jnp.where(live > 0, place, -1.0), starts

    by_source, source_starts = sort(source, phases, float(run_of(slots, n)), float(chunk_of(n)))
    by_target, target_starts = sort(target, 1, 2.0, 2.0 * pairs_of(n))
    columns = column(by_source, by_target, lane, source, term, target)

    def picker(places_column):
        hit = places_column == at

        def pick(values, other):
            found = jnp.sum(jnp.where(hit, values - other, 0.0), axis=0, keepdims=True)
            return (found + other).astype(jnp.int32)

        return pick

    own = (jnp.zeros((1, 1), jnp.int32) + me).astype(jnp.float32)
    pick = picker(columns[:, 0:1])
    plan_ref[0:1] = pick(columns[:, 2:3], 0.0)
    plan_ref[1:2] = pick(columns[:, 3:4], own)
    pick = picker(columns[:, 1:2])
    plan_ref[2:3] = pick(columns[:, 0:1], -1.0)
    plan_ref[3:4] = pick(columns[:, 4:5], float(terms))
    plan_ref[4:5] = pick(columns[:, 5:6], float(n))
    turns = jnp.zeros((1, places), jnp.float32)
    for p, start in enumerate(source_starts + [target_starts[1]]):
        turns = turns + jnp.where(number == p, start, 0.0)
    plan_ref[5:6] = turns.astype(jnp.int32)


def stage_kernel(n, terms, tasks_ref, left_ref, plan_ref, held_ref, tasks, sem):
    copies = [
        pltpu.make_async_copy(tasks_ref, tasks, sem.at[0]),
        pltpu.make_async_copy(left_ref, held_ref, sem.at[1]),
    ]
    for copy in copies:
        copy.start()
    copies[0].wait()
    plan_kernel(n, terms, tasks, plan_ref)
    copies[1].wait()


def make_plan(tasks, left_ops, n, terms):
    most = source_places(tasks.shape[1], n)
    plan = jax.ShapeDtypeStruct((6, -(-most // 128) * 128), jnp.int32)
    vmem, hbm = pl.BlockSpec(memory_space=pltpu.VMEM), pl.BlockSpec(memory_space=pltpu.HBM)
    if fits(n):
        return pl.pallas_call(
            functools.partial(stage_kernel, n, terms),
            in_specs=[hbm, hbm],
            out_specs=(vmem, vmem),
            out_shape=(plan, jax.ShapeDtypeStruct(left_ops.shape, left_ops.dtype)),
            scratch_shapes=[pltpu.VMEM(tasks.shape, jnp.int32), pltpu.SemaphoreType.DMA((2,))],
            compiler_params=pltpu.CompilerParams(vmem_limit_bytes=42 * MIB),
        )(tasks, left_ops)
    return (
        pl.pallas_call(
            functools.partial(plan_kernel, n, terms),
            out_shape=plan,
            compiler_params=pltpu.CompilerParams(vmem_limit_bytes=16 * MIB),
        )(tasks),
        left_ops,
    )


def block_parts(n, kinds, blocks, trial, right):
    parts = []
    for b, kind in enumerate(kinds):
        vectors, *terms = blocks[3 * b : 3 * b + 3]
        for half, ref in enumerate(terms):
            owner = owner_of(*kind, half, n)
            per = ref.shape[0]
            parts.append((vectors.at[pl.ds(half * TRIALS, TRIALS)], trial.at[owner]))
            parts.append((ref, right.at[pl.ds(owner * per, per)]))
    return parts


def make_halves(n, plan_ref, left_ref, trial, halves, fetched):
    turns = plan_ref[5, 1]
    run = run_of(left_ref.shape[0], n)
    chunk = chunk_of(n)

    def fetch(turn):
        left, left_sem = fetched
        at = lax.rem(turn, AHEAD)
        for u in range(chunk):
            slot = plan_ref[0, turn * chunk + u]
            pltpu.make_async_copy(left_ref.at[slot], left.at[at, u], left_sem.at[at]).start()

    def start():
        for turn in range(AHEAD - 1) if fetched else ():

            @pl.when(turn < turns)
            def _():
                fetch(turn)

    def turn_of(turn, carry):
        if fetched:
            left, left_sem = fetched

            @pl.when(turn + AHEAD - 1 < turns)
            def _():
                fetch(turn + AHEAD - 1)

            at = lax.rem(turn, AHEAD)
            pltpu.make_async_copy(left_ref.at[pl.ds(0, chunk)], left.at[at], left_sem.at[at]).wait()
        place = turn * chunk
        for r in range(0, chunk, run):
            source = plan_ref[1, place + r]
            vectors = jnp.concatenate([trial[source, 0], trial[source, 1]], axis=1)
            if fetched:
                rows = left[at, r : r + run].reshape(run * 128, 128)
            else:
                rows = jnp.concatenate([left_ref[plan_ref[0, place + r + u]] for u in range(run)], axis=0)
            half = jnp.dot(rows, vectors, preferred_element_type=jnp.float32).astype(jnp.bfloat16)
            for u in range(run):
                halves[place + r + u, 0] = half[u * 128 : (u + 1) * 128, :128]
                halves[place + r + u, 1] = half[u * 128 : (u + 1) * 128, 128:]
        return carry

    return start, lambda: lax.fori_loop(0, turns, turn_of, 0)


def tasks_kernel(n, kinds, plan_ref, left_ref, *refs):
    blocks, refs = refs[: 3 * len(kinds)], refs[3 * len(kinds) :]
    far_ref, near_ref, acc, own_ref, halves, trial, right, block_sem, *fetched = refs
    start, products = make_halves(n, plan_ref, left_ref, trial, halves, fetched)
    right[right.shape[0] - 1] = jnp.zeros((128, 128), jnp.bfloat16)
    start()
    parts = block_parts(n, kinds, blocks, trial, right)
    copies = []
    for index, (source, to) in enumerate(parts):
        if fits(n):
            to[...] = source[...]
        else:
            copies.append(pltpu.make_async_copy(source, to, block_sem.at[index]))
            copies[-1].start()

    def clear(s, carry):
        acc[s] = jnp.zeros((256, 128), jnp.float32)
        return carry

    lax.fori_loop(0, n, clear, 0)
    for copy in copies:
        copy.wait()
    products()

    def target_turn(turn, carry):
        first = turn * 2 * pairs_of(n)
        for u in range(0, 2 * pairs_of(n), 2):
            place = first + u
            one = plan_ref[2, place]
            two = plan_ref[2, place + 1]
            one, two = jnp.maximum(one, 0), jnp.where(two < 0, jnp.maximum(one, 0), two)
            pair = jnp.concatenate(
                [
                    jnp.concatenate([halves[one, 0], halves[two, 0]], axis=1),
                    jnp.concatenate([halves[one, 1], halves[two, 1]], axis=1),
                ],
                axis=0,
            )
            rights = jnp.concatenate([right[plan_ref[3, place]], right[plan_ref[3, place + 1]]], axis=1)
            term = lax.dot_general(
                pair, rights, (((1,), (1,)), ((), ())), preferred_element_type=jnp.float32
            )
            target = plan_ref[4, place]
            acc[target] = acc[target] + term
        return carry

    lax.fori_loop(0, plan_ref[5, 2], target_turn, 0)
    me = lax.axis_index("op")

    def dots(s, carry):
        t0 = trial[s, 0].astype(jnp.float32)
        t1 = trial[s, 1].astype(jnp.float32)
        a0 = acc[s, 0:128, :]
        a1 = acc[s, 128:256, :]
        p00, p01, p10, p11 = carry
        return p00 + fold(t0 * a0), p01 + fold(t0 * a1), p10 + fold(t1 * a0), p11 + fold(t1 * a1)

    zero = jnp.zeros((8, 128), jnp.float32)
    sums = lax.fori_loop(0, n, dots, (zero,) * 4, unroll=8)
    p00, p01, p10, p11 = [jnp.sum(x) for x in sums]

    chips = n // 2
    near = near_chips(n)

    def pack(j, carry):
        value = acc[jnp.bitwise_xor(me, 2 * j + 1)].astype(jnp.bfloat16)

        @pl.when(j < near)
        def _():
            near_ref[pl.ds(pl.multiple_of(j * 256, 256), 256), :] = value

        @pl.when(j >= near)
        def _():
            far_ref[pl.ds(pl.multiple_of((j - near) * 256, 256), 256), :] = value

        return carry

    lax.fori_loop(0, chips, pack, 0, unroll=2)
    own = split3(matrix_of({(0, 0): p00, (0, 1): p01, (1, 0): p10, (1, 1): p11}, 3))
    own_ref[...] = own
    far_ref[(chips - near) * 256 :, :] = tail_of(own, jnp.zeros_like(own))


def run_tasks(n, plan, left_ops, blocks):
    slots = left_ops.shape[0]
    terms_per = blocks[0][0][1].shape[0]
    kinds = tuple(block[1:] for block in blocks)
    vmem, hbm = pl.BlockSpec(memory_space=pltpu.VMEM), pl.BlockSpec(memory_space=pltpu.HBM)
    given = vmem if fits(n) else hbm
    fetched = [] if fits(n) else [
        pltpu.VMEM((AHEAD, chunk_of(n), 128, 128), jnp.bfloat16),
        pltpu.SemaphoreType.DMA((AHEAD,)),
    ]
    return pl.pallas_call(
        functools.partial(tasks_kernel, n, kinds),
        out_shape=(
            jax.ShapeDtypeStruct(((n // 2 - near_chips(n)) * 256 + TAIL, 128), jnp.bfloat16),
            jax.ShapeDtypeStruct((near_chips(n) * 256, 128), jnp.bfloat16),
            jax.ShapeDtypeStruct((n + 1, 256, 128), jnp.float32),
            jax.ShapeDtypeStruct((8, 128), jnp.float32),
        ),
        in_specs=[pl.BlockSpec(memory_space=pltpu.SMEM)] + [given] * (1 + 3 * len(blocks)),
        out_specs=(vmem,) * 4,
        scratch_shapes=[
            pltpu.VMEM((source_places(slots, n), 2, 128, 128), jnp.bfloat16),
            pltpu.VMEM((n, TRIALS, 128, 128), jnp.bfloat16),
            pltpu.VMEM((n * terms_per + 1, 128, 128), jnp.bfloat16),
            pltpu.SemaphoreType.DMA((4 * len(blocks),)),
        ]
        + fetched,
        compiler_params=pltpu.CompilerParams(vmem_limit_bytes=(33 if fits(n) else 58) * MIB),
        cost_estimate=pl.CostEstimate(
            flops=slots * 8 * 128**3, bytes_accessed=slots * 32768 + n * 450000, transcendentals=0
        ),
    )(plan, left_ops, *[value for block in blocks for value in block[0]])


def corr_kernel(*refs):
    blocks, corr_ref = refs[:-1], refs[-1]
    total = [jnp.zeros((8, 128), jnp.float32)] * 3
    for ref in blocks:
        for start in range(0, ref.shape[0], TRIALS):
            t0, t1 = ref[start].astype(jnp.float32), ref[start + 1].astype(jnp.float32)
            total = [total[0] + fold(t0 * t0), total[1] + fold(t0 * t1), total[2] + fold(t1 * t1)]
    c00, c01, c11 = [jnp.sum(x) for x in total]
    corr_ref[...] = matrix_of({(0, 0): c00, (0, 1): c01, (1, 0): c01, (1, 1): c11})[0:2, 0:2]


def correlate(blocks):
    return pl.pallas_call(
        corr_kernel,
        out_shape=jax.ShapeDtypeStruct((2, 2), jnp.float32),
        compiler_params=pltpu.CompilerParams(vmem_limit_bytes=16 * MIB),
    )(*blocks)


def far_kernel(n, acc_ref, own_ref, received_ref, total_ref, *sends):
    far, near = n // 2 - near_chips(n), near_chips(n)
    total = jnp.concatenate([own_ref[...], received_ref[far * 256 :, :].astype(jnp.float32)[0:8]], axis=0)
    total_ref[...] = total
    me = lax.axis_index("op")
    for j in range(far):
        value = acc_ref[jnp.bitwise_xor(me, 2 * (near + j))] + received_ref[j * 256 : (j + 1) * 256, :].astype(
            jnp.float32
        )
        sends[j][0:256, :] = value.astype(jnp.bfloat16)
        sends[j][256:, :] = total.astype(jnp.bfloat16)


def add_far(n, acc, own, received):
    return pl.pallas_call(
        functools.partial(far_kernel, n),
        out_shape=(jax.ShapeDtypeStruct((16, 128), jnp.float32),)
        + (jax.ShapeDtypeStruct((256 + TAIL, 128), jnp.bfloat16),) * (n // 2 - near_chips(n)),
        compiler_params=pltpu.CompilerParams(vmem_limit_bytes=16 * MIB),
    )(acc, own, received)


def near_kernel(n, acc_ref, total_ref, received_ref, mine_ref, *sends):
    me = lax.axis_index("op")
    for j in range(near_chips(n)):
        value = acc_ref[jnp.bitwise_xor(me, 2 * j)] + received_ref[j * 256 : (j + 1) * 256, :].astype(jnp.float32)
        if j == 0:
            mine_ref[...] = value
        else:
            sends[j - 1][0:256, :] = value.astype(jnp.bfloat16)
            sends[j - 1][256:, :] = total_ref[...].astype(jnp.bfloat16)


def add_near(n, acc, total, received):
    return pl.pallas_call(
        functools.partial(near_kernel, n),
        out_shape=(jax.ShapeDtypeStruct((256, 128), jnp.float32),)
        + (jax.ShapeDtypeStruct((256 + TAIL, 128), jnp.bfloat16),) * (near_chips(n) - 1),
        compiler_params=pltpu.CompilerParams(vmem_limit_bytes=16 * MIB),
    )(acc, total, received)


def last_kernel(mine_ref, total_ref, *refs):
    received, (product_ref, projected_ref) = refs[:-2], refs[-2:]
    value, total = mine_ref[...], total_ref[...]
    for ref in received:
        value = value + ref[0:256, :].astype(jnp.float32)
        total = total + ref[256:, :].astype(jnp.float32)
    product_ref[0, 0] = value[0:128]
    product_ref[0, 1] = value[128:256]
    total = total[0:8] + total[8:16]
    projected_ref[...] = total[0:2, 0:2] + total[0:2, 2:4] + total[0:2, 4:6]


def add_all(mine, total, received):
    return pl.pallas_call(
        last_kernel,
        out_shape=(
            jax.ShapeDtypeStruct((1, 2, 128, 128), jnp.float32),
            jax.ShapeDtypeStruct((2, 2), jnp.float32),
        ),
        compiler_params=pltpu.CompilerParams(vmem_limit_bytes=16 * MIB),
    )(mine, total, *received)


def body(n, trial, left_ops, right_ops, task_list):
    steps = n // 4
    plan, left_ops = make_plan(task_list.T, left_ops, n, n * right_ops.shape[0])
    vectors = jnp.concatenate([trial[0], exchange(trial[0], n, 1)], axis=0)
    line = [vectors, right_ops, exchange(right_ops, n, 1)]
    blocks = [(line, 0, False)]
    for step in range(1, steps + 1):
        line = [ring_step(value, n) for value in line]
        blocks.append((line, step, False))
        if step < steps:
            blocks.append(([exchange(value, n, 1) for value in line], step, True))
    far, near, acc, own = run_tasks(n, plan, left_ops, blocks)
    far, arrays = lax.optimization_barrier((far, [block[0][0] for block in blocks]))
    correlation = correlate(arrays)
    far, near = exchange(far, n, 1), exchange(near, n, 1)
    total, *messages = add_far(n, acc, own, far)
    first = near_chips(n)
    received = [exchange(messages[j], n, 2 * (first + j)) for j in reversed(range(len(messages)))]
    mine, *messages = add_near(n, acc, total, near)
    received += [exchange(messages[j - 1], n, 2 * j) for j in reversed(range(1, first))]
    product, projected = add_all(mine, total, received)
    return product, correlation, projected


def solution(mesh):
    return jax.shard_map(
        functools.partial(body, mesh.shape["op"]),
        mesh=mesh,
        in_specs=(
            P(("groups", "op"), None, None, None),
            P(("groups", "op"), None, None),
            P(("groups", "op"), None, None),
            P(("groups", "op"), None),
        ),
        out_specs=(P(("groups", "op"), None, None, None), P("groups", None), P("groups", None)),
        check_vma=False,
    )
```

```python
import functools

import jax
import jax.numpy as jnp
from jax import lax
from jax.experimental import pallas as pl
from jax.experimental.pallas import tpu as pltpu
from jax.sharding import PartitionSpec as P

MIB = 1024 * 1024
TAIL = 16
TRIALS = 2
AHEAD = 3


def exchange(value, n, mask):
    return lax.ppermute(value, "op", [(i, i ^ mask) for i in range(n)])


def chip_at(place, chips):
    return 2 * place if place < chips // 2 else 2 * (chips - place) - 1


def ring_step(value, n):
    chips = n // 2
    order = [chip_at(place, chips) for place in range(chips)]
    pairs = []
    for place, chip in enumerate(order):
        pairs.append((2 * chip, 2 * order[(place + 1) % chips]))
        pairs.append((2 * chip + 1, 2 * order[(place - 1) % chips] + 1))
    return lax.ppermute(value, "op", pairs)


def owner_of(step, swapped, half, n):
    chips = n // 2
    me = lax.axis_index("op")
    chip, core = me // 2, lax.rem(me, 2)
    odd = lax.rem(chip, 2)
    mine = jnp.where(odd == 0, chip // 2, chips - 1 - chip // 2)
    line = 1 - core if swapped else core
    place = lax.rem(mine + (2 * line - 1) * step + 2 * chips, chips)
    there = jnp.where(place < chips // 2, 2 * place, 2 * (chips - place) - 1)
    return 2 * there + (line if half == 0 else 1 - line)


def split3(value):
    lanes = lax.broadcasted_iota(jnp.int32, (8, 128), 1)
    high = value.astype(jnp.bfloat16).astype(jnp.float32)
    middle = (value - high).astype(jnp.bfloat16).astype(jnp.float32)
    low = (value - high - middle).astype(jnp.bfloat16).astype(jnp.float32)
    return jnp.where(lanes < 2, high, jnp.where(lanes < 4, middle, low))


def tail_of(first, second):
    return jnp.concatenate([first, second], axis=0).astype(jnp.bfloat16)


def matrix_of(values, repeats=1):
    rows = lax.broadcasted_iota(jnp.int32, (8, 128), 0)
    lanes = lax.broadcasted_iota(jnp.int32, (8, 128), 1)
    total = jnp.zeros((8, 128), jnp.float32)
    for (i, j), value in values.items():
        for repeat in range(repeats):
            total = total + jnp.where((rows == i) & (lanes == j + 2 * repeat), value, 0.0)
    return total


def fold(value):
    return value.reshape(16, 8, 128).sum(axis=0)


def fits(n):
    return n <= 16


def near_chips(n):
    return n // 4


def phases_of(n):
    return 1


def chunk_of(n):
    return 144 if fits(n) else 48


def pairs_of(n):
    return 69 if fits(n) else 24


def run_of(slots, n):
    return 4 if slots >= 8 * n else 2


def source_places(slots, n):
    chunk = chunk_of(n)
    most = slots + min(slots, n) * (run_of(slots, n) - 1)
    return -(-most // chunk) * chunk


def place_of(chip, chips):
    half = jnp.floor(chip * 0.5)
    return jnp.where(chip == 2.0 * half, half, chips - 1.0 - half)


def plan_kernel(n, terms, tasks_ref, plan_ref):
    slots = tasks_ref.shape[1]
    places = plan_ref.shape[1]
    chips = n // 2
    phases = phases_of(n)
    rows = tasks_ref[...].astype(jnp.float32)
    source, target, term, live = rows[0:1], rows[1:2], rows[2:3], rows[3:4]
    lane = lax.broadcasted_iota(jnp.int32, (1, slots), 1).astype(jnp.float32)
    number = lax.broadcasted_iota(jnp.int32, (1, places), 1).astype(jnp.float32)
    at = lax.broadcasted_iota(jnp.int32, (slots, places), 1).astype(jnp.float32)
    me = lax.axis_index("op")
    mine = place_of((jnp.zeros((1, slots), jnp.int32) + me // 2).astype(jnp.float32), float(chips))
    gap = place_of(jnp.floor(source * 0.5), float(chips)) - mine
    up = jnp.where(gap < 0, gap + chips, gap)
    far = jnp.minimum(up, chips - up)
    phase = jnp.clip(far - 1.0, 0.0, phases - 1.0)

    def column(*values):
        pad = [jnp.zeros((8 - len(values), slots), jnp.float32)]
        return jnp.transpose(jnp.concatenate(list(values) + pad, axis=0))

    def sort(sector, parts, unit, whole):
        keys = parts * n
        index = lax.broadcasted_iota(jnp.int32, (keys, slots), 0).astype(jnp.float32)
        part = phase if parts > 1 else jnp.zeros_like(phase)
        key = jnp.where(live > 0, part * n + sector, float(keys))
        columns = column(key, lane)
        earlier = jnp.where((columns[:, 0:1] == key) & (columns[:, 1:2] < lane), 1.0, 0.0)
        count = jnp.sum(jnp.where(index == key, 1.0, 0.0), axis=1, keepdims=True)
        padded = jnp.ceil(count / unit) * unit
        place = jnp.sum(earlier, axis=0, keepdims=True)
        start = jnp.zeros((1, 1), jnp.float32)
        starts = [start]
        for p in range(parts):
            lengths = padded[p * n : (p + 1) * n]
            before = jnp.where(index[p * n : (p + 1) * n] < key, lengths, 0.0)
            place = place + jnp.where(part == p, start * whole + jnp.sum(before, axis=0, keepdims=True), 0.0)
            start = start + jnp.ceil(jnp.sum(lengths, axis=0, keepdims=True) / whole)
            starts.append(start)
        return jnp.where(live > 0, place, -1.0), starts

    by_source, source_starts = sort(source, phases, float(run_of(slots, n)), float(chunk_of(n)))
    by_target, target_starts = sort(target, 1, 2.0, 2.0 * pairs_of(n))
    columns = column(by_source, by_target, lane, source, term, target)

    def picker(places_column):
        hit = places_column == at

        def pick(values, other):
            found = jnp.sum(jnp.where(hit, values - other, 0.0), axis=0, keepdims=True)
            return (found + other).astype(jnp.int32)

        return pick

    own = (jnp.zeros((1, 1), jnp.int32) + me).astype(jnp.float32)
    pick = picker(columns[:, 0:1])
    plan_ref[0:1] = pick(columns[:, 2:3], 0.0)
    plan_ref[1:2] = pick(columns[:, 3:4], own)
    pick = picker(columns[:, 1:2])
    plan_ref[2:3] = pick(columns[:, 0:1], -1.0)
    plan_ref[3:4] = pick(columns[:, 4:5], float(terms))
    plan_ref[4:5] = pick(columns[:, 5:6], float(n))
    turns = jnp.zeros((1, places), jnp.float32)
    for p, start in enumerate(source_starts + [target_starts[1]]):
        turns = turns + jnp.where(number == p, start, 0.0)
    plan_ref[5:6] = turns.astype(jnp.int32)


def stage_kernel(n, terms, tasks_ref, left_ref, plan_ref, held_ref, tasks, sem):
    copies = [
        pltpu.make_async_copy(tasks_ref, tasks, sem.at[0]),
        pltpu.make_async_copy(left_ref, held_ref, sem.at[1]),
    ]
    for copy in copies:
        copy.start()
    copies[0].wait()
    plan_kernel(n, terms, tasks, plan_ref)
    copies[1].wait()


def make_plan(tasks, left_ops, n, terms):
    most = source_places(tasks.shape[1], n)
    plan = jax.ShapeDtypeStruct((6, -(-most // 128) * 128), jnp.int32)
    vmem, hbm = pl.BlockSpec(memory_space=pltpu.VMEM), pl.BlockSpec(memory_space=pltpu.HBM)
    if fits(n):
        return pl.pallas_call(
            functools.partial(stage_kernel, n, terms),
            in_specs=[hbm, hbm],
            out_specs=(vmem, vmem),
            out_shape=(plan, jax.ShapeDtypeStruct(left_ops.shape, left_ops.dtype)),
            scratch_shapes=[pltpu.VMEM(tasks.shape, jnp.int32), pltpu.SemaphoreType.DMA((2,))],
            compiler_params=pltpu.CompilerParams(vmem_limit_bytes=42 * MIB),
        )(tasks, left_ops)
    return (
        pl.pallas_call(
            functools.partial(plan_kernel, n, terms),
            out_shape=plan,
            compiler_params=pltpu.CompilerParams(vmem_limit_bytes=16 * MIB),
        )(tasks),
        left_ops,
    )


def block_parts(n, kinds, blocks, trial, right):
    parts = []
    for b, kind in enumerate(kinds):
        vectors, *terms = blocks[3 * b : 3 * b + 3]
        for half, ref in enumerate(terms):
            owner = owner_of(*kind, half, n)
            per = ref.shape[0]
            parts.append((vectors.at[pl.ds(half * TRIALS, TRIALS)], trial.at[owner]))
            parts.append((ref, right.at[pl.ds(owner * per, per)]))
    return parts


def make_halves(n, plan_ref, left_ref, trial, halves, fetched):
    turns = plan_ref[5, 1]
    run = run_of(left_ref.shape[0], n)
    chunk = chunk_of(n)

    def fetch(turn):
        left, left_sem = fetched
        at = lax.rem(turn, AHEAD)
        for u in range(chunk):
            slot = plan_ref[0, turn * chunk + u]
            pltpu.make_async_copy(left_ref.at[slot], left.at[at, u], left_sem.at[at]).start()

    def start():
        for turn in range(AHEAD - 1) if fetched else ():

            @pl.when(turn < turns)
            def _():
                fetch(turn)

    def turn_of(turn, carry):
        if fetched:
            left, left_sem = fetched

            @pl.when(turn + AHEAD - 1 < turns)
            def _():
                fetch(turn + AHEAD - 1)

            at = lax.rem(turn, AHEAD)
            pltpu.make_async_copy(left_ref.at[pl.ds(0, chunk)], left.at[at], left_sem.at[at]).wait()
        place = turn * chunk
        for r in range(0, chunk, run):
            source = plan_ref[1, place + r]
            vectors = jnp.concatenate([trial[source, 0], trial[source, 1]], axis=1)
            if fetched:
                rows = left[at, r : r + run].reshape(run * 128, 128)
            else:
                rows = jnp.concatenate([left_ref[plan_ref[0, place + r + u]] for u in range(run)], axis=0)
            half = jnp.dot(rows, vectors, preferred_element_type=jnp.float32).astype(jnp.bfloat16)
            for u in range(run):
                halves[place + r + u, 0] = half[u * 128 : (u + 1) * 128, :128]
                halves[place + r + u, 1] = half[u * 128 : (u + 1) * 128, 128:]
        return carry

    return start, lambda: lax.fori_loop(0, turns, turn_of, 0)


def tasks_kernel(n, kinds, plan_ref, left_ref, *refs):
    blocks, refs = refs[: 3 * len(kinds)], refs[3 * len(kinds) :]
    far_ref, near_ref, acc, own_ref, halves, trial, right, block_sem, *fetched = refs
    start, products = make_halves(n, plan_ref, left_ref, trial, halves, fetched)
    right[right.shape[0] - 1] = jnp.zeros((128, 128), jnp.bfloat16)
    start()
    parts = block_parts(n, kinds, blocks, trial, right)
    copies = []
    for index, (source, to) in enumerate(parts):
        if fits(n):
            to[...] = source[...]
        else:
            copies.append(pltpu.make_async_copy(source, to, block_sem.at[index]))
            copies[-1].start()

    def clear(s, carry):
        acc[s] = jnp.zeros((256, 128), jnp.float32)
        return carry

    lax.fori_loop(0, n, clear, 0)
    for copy in copies:
        copy.wait()
    products()

    def target_turn(turn, carry):
        first = turn * 2 * pairs_of(n)
        for u in range(0, 2 * pairs_of(n), 2):
            place = first + u
            one = plan_ref[2, place]
            two = plan_ref[2, place + 1]
            one, two = jnp.maximum(one, 0), jnp.where(two < 0, jnp.maximum(one, 0), two)
            pair = jnp.concatenate(
                [
                    jnp.concatenate([halves[one, 0], halves[two, 0]], axis=1),
                    jnp.concatenate([halves[one, 1], halves[two, 1]], axis=1),
                ],
                axis=0,
            )
            rights = jnp.concatenate([right[plan_ref[3, place]], right[plan_ref[3, place + 1]]], axis=1)
            term = lax.dot_general(
                pair, rights, (((1,), (1,)), ((), ())), preferred_element_type=jnp.float32
            )
            target = plan_ref[4, place]
            acc[target] = acc[target] + term
        return carry

    lax.fori_loop(0, plan_ref[5, 2], target_turn, 0)
    me = lax.axis_index("op")

    def dots(s, carry):
        t0 = trial[s, 0].astype(jnp.float32)
        t1 = trial[s, 1].astype(jnp.float32)
        a0 = acc[s, 0:128, :]
        a1 = acc[s, 128:256, :]
        p00, p01, p10, p11 = carry
        return p00 + fold(t0 * a0), p01 + fold(t0 * a1), p10 + fold(t1 * a0), p11 + fold(t1 * a1)

    zero = jnp.zeros((8, 128), jnp.float32)
    sums = lax.fori_loop(0, n, dots, (zero,) * 4, unroll=8)
    p00, p01, p10, p11 = [jnp.sum(x) for x in sums]

    chips = n // 2
    near = near_chips(n)

    def pack(j, carry):
        value = acc[jnp.bitwise_xor(me, 2 * j + 1)].astype(jnp.bfloat16)

        @pl.when(j < near)
        def _():
            near_ref[pl.ds(pl.multiple_of(j * 256, 256), 256), :] = value

        @pl.when(j >= near)
        def _():
            far_ref[pl.ds(pl.multiple_of((j - near) * 256, 256), 256), :] = value

        return carry

    lax.fori_loop(0, chips, pack, 0, unroll=2)
    own = split3(matrix_of({(0, 0): p00, (0, 1): p01, (1, 0): p10, (1, 1): p11}, 3))
    own_ref[...] = own
    far_ref[(chips - near) * 256 :, :] = tail_of(own, jnp.zeros_like(own))


def run_tasks(n, plan, left_ops, blocks):
    slots = left_ops.shape[0]
    terms_per = blocks[0][0][1].shape[0]
    kinds = tuple(block[1:] for block in blocks)
    vmem, hbm = pl.BlockSpec(memory_space=pltpu.VMEM), pl.BlockSpec(memory_space=pltpu.HBM)
    given = vmem if fits(n) else hbm
    fetched = [] if fits(n) else [
        pltpu.VMEM((AHEAD, chunk_of(n), 128, 128), jnp.bfloat16),
        pltpu.SemaphoreType.DMA((AHEAD,)),
    ]
    return pl.pallas_call(
        functools.partial(tasks_kernel, n, kinds),
        out_shape=(
            jax.ShapeDtypeStruct(((n // 2 - near_chips(n)) * 256 + TAIL, 128), jnp.bfloat16),
            jax.ShapeDtypeStruct((near_chips(n) * 256, 128), jnp.bfloat16),
            jax.ShapeDtypeStruct((n + 1, 256, 128), jnp.float32),
            jax.ShapeDtypeStruct((8, 128), jnp.float32),
        ),
        in_specs=[pl.BlockSpec(memory_space=pltpu.SMEM)] + [given] * (1 + 3 * len(blocks)),
        out_specs=(vmem,) * 4,
        scratch_shapes=[
            pltpu.VMEM((source_places(slots, n), 2, 128, 128), jnp.bfloat16),
            pltpu.VMEM((n, TRIALS, 128, 128), jnp.bfloat16),
            pltpu.VMEM((n * terms_per + 1, 128, 128), jnp.bfloat16),
            pltpu.SemaphoreType.DMA((4 * len(blocks),)),
        ]
        + fetched,
        compiler_params=pltpu.CompilerParams(vmem_limit_bytes=(33 if fits(n) else 58) * MIB),
        cost_estimate=pl.CostEstimate(
            flops=slots * 8 * 128**3, bytes_accessed=slots * 32768 + n * 450000, transcendentals=0
        ),
    )(plan, left_ops, *[value for block in blocks for value in block[0]])


def corr_kernel(*refs):
    blocks, corr_ref = refs[:-1], refs[-1]
    total = [jnp.zeros((8, 128), jnp.float32)] * 3
    for ref in blocks:
        for start in range(0, ref.shape[0], TRIALS):
            t0, t1 = ref[start].astype(jnp.float32), ref[start + 1].astype(jnp.float32)
            total = [total[0] + fold(t0 * t0), total[1] + fold(t0 * t1), total[2] + fold(t1 * t1)]
    c00, c01, c11 = [jnp.sum(x) for x in total]
    corr_ref[...] = matrix_of({(0, 0): c00, (0, 1): c01, (1, 0): c01, (1, 1): c11})[0:2, 0:2]


def correlate(blocks):
    return pl.pallas_call(
        corr_kernel,
        out_shape=jax.ShapeDtypeStruct((2, 2), jnp.float32),
        compiler_params=pltpu.CompilerParams(vmem_limit_bytes=16 * MIB),
    )(*blocks)


def sum_part(n, acc_ref, received_ref, chip, row):
    part = acc_ref[jnp.bitwise_xor(lax.axis_index("op"), 2 * chip)]
    return part + received_ref[row * 256 : (row + 1) * 256, :].astype(jnp.float32)


def far_kernel(n, acc_ref, own_ref, received_ref, total_ref, *sends):
    far, near = n // 2 - near_chips(n), near_chips(n)
    total = jnp.concatenate([own_ref[...], received_ref[far * 256 :, :].astype(jnp.float32)[0:8]], axis=0)
    total_ref[...] = total
    for row, ref in zip(range(far - len(sends), far), sends):
        ref[0:256, :] = sum_part(n, acc_ref, received_ref, near + row, row).astype(jnp.bfloat16)
        ref[256:, :] = total.astype(jnp.bfloat16)


def add_far(n, acc, own, received):
    return pl.pallas_call(
        functools.partial(far_kernel, n),
        out_shape=(jax.ShapeDtypeStruct((16, 128), jnp.float32),)
        + (jax.ShapeDtypeStruct((256 + TAIL, 128), jnp.bfloat16),) * (near_chips(n) // 2),
        compiler_params=pltpu.CompilerParams(vmem_limit_bytes=16 * MIB),
    )(acc, own, received)


def near_kernel(n, acc_ref, total_ref, far_ref, near_ref, mine_ref, *sends):
    near = near_chips(n)
    mine_ref[...] = sum_part(n, acc_ref, near_ref, 0, 0)
    for index, ref in enumerate(sends):
        if index < near - 1:
            value = sum_part(n, acc_ref, near_ref, index + 1, index + 1)
        else:
            value = sum_part(n, acc_ref, far_ref, index + 1, index + 1 - near)
        ref[0:256, :] = value.astype(jnp.bfloat16)
        ref[256:, :] = total_ref[...].astype(jnp.bfloat16)


def add_near(n, acc, total, far, near):
    messages = near_chips(n) - 1 + near_chips(n) // 2
    return pl.pallas_call(
        functools.partial(near_kernel, n),
        out_shape=(jax.ShapeDtypeStruct((256, 128), jnp.float32),)
        + (jax.ShapeDtypeStruct((256 + TAIL, 128), jnp.bfloat16),) * messages,
        compiler_params=pltpu.CompilerParams(vmem_limit_bytes=16 * MIB),
    )(acc, total, far, near)


def last_kernel(mine_ref, total_ref, *refs):
    received, (product_ref, projected_ref) = refs[:-2], refs[-2:]
    value, total = mine_ref[...], total_ref[...]
    for ref in received:
        value = value + ref[0:256, :].astype(jnp.float32)
        total = total + ref[256:, :].astype(jnp.float32)
    product_ref[0, 0] = value[0:128]
    product_ref[0, 1] = value[128:256]
    total = total[0:8] + total[8:16]
    projected_ref[...] = total[0:2, 0:2] + total[0:2, 2:4] + total[0:2, 4:6]


def add_all(mine, total, received):
    return pl.pallas_call(
        last_kernel,
        out_shape=(
            jax.ShapeDtypeStruct((1, 2, 128, 128), jnp.float32),
            jax.ShapeDtypeStruct((2, 2), jnp.float32),
        ),
        compiler_params=pltpu.CompilerParams(vmem_limit_bytes=16 * MIB),
    )(mine, total, *received)


def body(n, trial, left_ops, right_ops, task_list):
    steps = n // 4
    plan, left_ops = make_plan(task_list.T, left_ops, n, n * right_ops.shape[0])
    vectors = jnp.concatenate([trial[0], exchange(trial[0], n, 1)], axis=0)
    line = [vectors, right_ops, exchange(right_ops, n, 1)]
    blocks = [(line, 0, False)]
    for step in range(1, steps + 1):
        line = [ring_step(value, n) for value in line]
        blocks.append((line, step, False))
        if step < steps:
            blocks.append(([exchange(value, n, 1) for value in line], step, True))
    far, near, acc, own = run_tasks(n, plan, left_ops, blocks)
    far, arrays = lax.optimization_barrier((far, [block[0][0] for block in blocks]))
    correlation = correlate(arrays)
    far, near = exchange(far, n, 1), exchange(near, n, 1)
    total, *messages = add_far(n, acc, own, far)
    last = n // 2 - len(messages)
    received = [exchange(value, n, 2 * j) for j, value in reversed(list(enumerate(messages, last)))]
    mine, *messages = add_near(n, acc, total, far, near)
    received += [exchange(value, n, 2 * j) for j, value in enumerate(messages, 1)]
    product, projected = add_all(mine, total, received)
    return product, correlation, projected


def solution(mesh):
    return jax.shard_map(
        functools.partial(body, mesh.shape["op"]),
        mesh=mesh,
        in_specs=(
            P(("groups", "op"), None, None, None),
            P(("groups", "op"), None, None),
            P(("groups", "op"), None, None),
            P(("groups", "op"), None),
        ),
        out_specs=(P(("groups", "op"), None, None, None), P("groups", None), P("groups", None)),
        check_vma=False,
    )
```

```python
import functools

import jax
import jax.numpy as jnp
from jax import lax
from jax.experimental import pallas as pl
from jax.experimental.pallas import tpu as pltpu
from jax.sharding import PartitionSpec as P

MIB = 1024 * 1024
TAIL = 16
TRIALS = 2
AHEAD = 3


def exchange(value, n, mask):
    return lax.ppermute(value, "op", [(i, i ^ mask) for i in range(n)])


def chip_at(place, chips):
    return 2 * place if place < chips // 2 else 2 * (chips - place) - 1


def ring_step(value, n):
    chips = n // 2
    order = [chip_at(place, chips) for place in range(chips)]
    pairs = []
    for place, chip in enumerate(order):
        pairs.append((2 * chip, 2 * order[(place + 1) % chips]))
        pairs.append((2 * chip + 1, 2 * order[(place - 1) % chips] + 1))
    return lax.ppermute(value, "op", pairs)


def owner_of(step, swapped, half, n):
    chips = n // 2
    me = lax.axis_index("op")
    chip, core = me // 2, lax.rem(me, 2)
    odd = lax.rem(chip, 2)
    mine = jnp.where(odd == 0, chip // 2, chips - 1 - chip // 2)
    line = 1 - core if swapped else core
    place = lax.rem(mine + (2 * line - 1) * step + 2 * chips, chips)
    there = jnp.where(place < chips // 2, 2 * place, 2 * (chips - place) - 1)
    return 2 * there + (line if half == 0 else 1 - line)


def split3(value):
    lanes = lax.broadcasted_iota(jnp.int32, (8, 128), 1)
    high = value.astype(jnp.bfloat16).astype(jnp.float32)
    middle = (value - high).astype(jnp.bfloat16).astype(jnp.float32)
    low = (value - high - middle).astype(jnp.bfloat16).astype(jnp.float32)
    return jnp.where(lanes < 2, high, jnp.where(lanes < 4, middle, low))


def tail_of(first, second):
    return jnp.concatenate([first, second], axis=0).astype(jnp.bfloat16)


def matrix_of(values, repeats=1):
    rows = lax.broadcasted_iota(jnp.int32, (8, 128), 0)
    lanes = lax.broadcasted_iota(jnp.int32, (8, 128), 1)
    total = jnp.zeros((8, 128), jnp.float32)
    for (i, j), value in values.items():
        for repeat in range(repeats):
            total = total + jnp.where((rows == i) & (lanes == j + 2 * repeat), value, 0.0)
    return total


def fold(value):
    return value.reshape(16, 8, 128).sum(axis=0)


def fits(n):
    return n <= 16


def near_chips(n):
    return n // 4


def phases_of(n):
    return 1


def chunk_of(n):
    return 144 if fits(n) else 48


def pairs_of(n):
    return 69 if fits(n) else 24


def run_of(slots, n):
    return 4 if slots >= 8 * n else 2


def source_places(slots, n):
    chunk = chunk_of(n)
    most = slots + min(slots, n) * (run_of(slots, n) - 1)
    return -(-most // chunk) * chunk


def place_of(chip, chips):
    half = jnp.floor(chip * 0.5)
    return jnp.where(chip == 2.0 * half, half, chips - 1.0 - half)


def plan_kernel(n, terms, tasks_ref, plan_ref):
    slots = tasks_ref.shape[1]
    places = plan_ref.shape[1]
    chips = n // 2
    phases = phases_of(n)
    rows = tasks_ref[...].astype(jnp.float32)
    source, target, term, live = rows[0:1], rows[1:2], rows[2:3], rows[3:4]
    lane = lax.broadcasted_iota(jnp.int32, (1, slots), 1).astype(jnp.float32)
    number = lax.broadcasted_iota(jnp.int32, (1, places), 1).astype(jnp.float32)
    at = lax.broadcasted_iota(jnp.int32, (slots, places), 1).astype(jnp.float32)
    me = lax.axis_index("op")
    mine = place_of((jnp.zeros((1, slots), jnp.int32) + me // 2).astype(jnp.float32), float(chips))
    gap = place_of(jnp.floor(source * 0.5), float(chips)) - mine
    up = jnp.where(gap < 0, gap + chips, gap)
    far = jnp.minimum(up, chips - up)
    phase = jnp.clip(far - 1.0, 0.0, phases - 1.0)

    def column(*values):
        pad = [jnp.zeros((8 - len(values), slots), jnp.float32)]
        return jnp.transpose(jnp.concatenate(list(values) + pad, axis=0))

    def sort(sector, parts, unit, whole):
        keys = parts * n
        index = lax.broadcasted_iota(jnp.int32, (keys, slots), 0).astype(jnp.float32)
        part = phase if parts > 1 else jnp.zeros_like(phase)
        key = jnp.where(live > 0, part * n + sector, float(keys))
        columns = column(key, lane)
        earlier = jnp.where((columns[:, 0:1] == key) & (columns[:, 1:2] < lane), 1.0, 0.0)
        count = jnp.sum(jnp.where(index == key, 1.0, 0.0), axis=1, keepdims=True)
        padded = jnp.ceil(count / unit) * unit
        place = jnp.sum(earlier, axis=0, keepdims=True)
        start = jnp.zeros((1, 1), jnp.float32)
        starts = [start]
        for p in range(parts):
            lengths = padded[p * n : (p + 1) * n]
            before = jnp.where(index[p * n : (p + 1) * n] < key, lengths, 0.0)
            place = place + jnp.where(part == p, start * whole + jnp.sum(before, axis=0, keepdims=True), 0.0)
            start = start + jnp.ceil(jnp.sum(lengths, axis=0, keepdims=True) / whole)
            starts.append(start)
        return jnp.where(live > 0, place, -1.0), starts

    by_source, source_starts = sort(source, phases, float(run_of(slots, n)), float(chunk_of(n)))
    by_target, target_starts = sort(target, 1, 2.0, 2.0 * pairs_of(n))
    columns = column(by_source, by_target, lane, source, term, target)

    def picker(places_column):
        hit = places_column == at

        def pick(values, other):
            found = jnp.sum(jnp.where(hit, values - other, 0.0), axis=0, keepdims=True)
            return (found + other).astype(jnp.int32)

        return pick

    own = (jnp.zeros((1, 1), jnp.int32) + me).astype(jnp.float32)
    pick = picker(columns[:, 0:1])
    plan_ref[0:1] = pick(columns[:, 2:3], 0.0)
    plan_ref[1:2] = pick(columns[:, 3:4], own)
    pick = picker(columns[:, 1:2])
    plan_ref[2:3] = pick(columns[:, 0:1], -1.0)
    plan_ref[3:4] = pick(columns[:, 4:5], float(terms))
    plan_ref[4:5] = pick(columns[:, 5:6], float(n))
    turns = jnp.zeros((1, places), jnp.float32)
    for p, start in enumerate(source_starts + [target_starts[1]]):
        turns = turns + jnp.where(number == p, start, 0.0)
    plan_ref[5:6] = turns.astype(jnp.int32)


def stage_kernel(n, terms, tasks_ref, left_ref, plan_ref, held_ref, tasks, sem):
    copies = [
        pltpu.make_async_copy(tasks_ref, tasks, sem.at[0]),
        pltpu.make_async_copy(left_ref, held_ref, sem.at[1]),
    ]
    for copy in copies:
        copy.start()
    copies[0].wait()
    plan_kernel(n, terms, tasks, plan_ref)
    copies[1].wait()


def make_plan(tasks, left_ops, n, terms):
    most = source_places(tasks.shape[1], n)
    plan = jax.ShapeDtypeStruct((6, -(-most // 128) * 128), jnp.int32)
    vmem, hbm = pl.BlockSpec(memory_space=pltpu.VMEM), pl.BlockSpec(memory_space=pltpu.HBM)
    if fits(n):
        return pl.pallas_call(
            functools.partial(stage_kernel, n, terms),
            in_specs=[hbm, hbm],
            out_specs=(vmem, vmem),
            out_shape=(plan, jax.ShapeDtypeStruct(left_ops.shape, left_ops.dtype)),
            scratch_shapes=[pltpu.VMEM(tasks.shape, jnp.int32), pltpu.SemaphoreType.DMA((2,))],
            compiler_params=pltpu.CompilerParams(vmem_limit_bytes=42 * MIB),
        )(tasks, left_ops)
    return (
        pl.pallas_call(
            functools.partial(plan_kernel, n, terms),
            out_shape=plan,
            compiler_params=pltpu.CompilerParams(vmem_limit_bytes=16 * MIB),
        )(tasks),
        left_ops,
    )


def block_parts(n, kinds, blocks, trial, right):
    parts = []
    for b, kind in enumerate(kinds):
        vectors, *terms = blocks[3 * b : 3 * b + 3]
        for half, ref in enumerate(terms):
            owner = owner_of(*kind, half, n)
            per = ref.shape[0]
            parts.append((vectors.at[pl.ds(half * TRIALS, TRIALS)], trial.at[owner]))
            parts.append((ref, right.at[pl.ds(owner * per, per)]))
    return parts


def make_halves(n, plan_ref, left_ref, trial, halves, fetched):
    turns = plan_ref[5, 1]
    run = run_of(left_ref.shape[0], n)
    chunk = chunk_of(n)

    def fetch(turn):
        left, left_sem = fetched
        at = lax.rem(turn, AHEAD)
        for u in range(chunk):
            slot = plan_ref[0, turn * chunk + u]
            pltpu.make_async_copy(left_ref.at[slot], left.at[at, u], left_sem.at[at]).start()

    def start():
        for turn in range(AHEAD - 1) if fetched else ():

            @pl.when(turn < turns)
            def _():
                fetch(turn)

    def turn_of(turn, carry):
        if fetched:
            left, left_sem = fetched

            @pl.when(turn + AHEAD - 1 < turns)
            def _():
                fetch(turn + AHEAD - 1)

            at = lax.rem(turn, AHEAD)
            pltpu.make_async_copy(left_ref.at[pl.ds(0, chunk)], left.at[at], left_sem.at[at]).wait()
        place = turn * chunk
        for r in range(0, chunk, run):
            source = plan_ref[1, place + r]
            vectors = jnp.concatenate([trial[source, 0], trial[source, 1]], axis=1)
            if fetched:
                rows = left[at, r : r + run].reshape(run * 128, 128)
            else:
                rows = jnp.concatenate([left_ref[plan_ref[0, place + r + u]] for u in range(run)], axis=0)
            half = jnp.dot(rows, vectors, preferred_element_type=jnp.float32).astype(jnp.bfloat16)
            for u in range(run):
                halves[place + r + u, 0] = half[u * 128 : (u + 1) * 128, :128]
                halves[place + r + u, 1] = half[u * 128 : (u + 1) * 128, 128:]
        return carry

    return start, lambda: lax.fori_loop(0, turns, turn_of, 0)


def tasks_kernel(n, kinds, plan_ref, left_ref, *refs):
    blocks, refs = refs[: 3 * len(kinds)], refs[3 * len(kinds) :]
    far_ref, near_ref, acc, own_ref, halves, trial, right, block_sem, *fetched = refs
    start, products = make_halves(n, plan_ref, left_ref, trial, halves, fetched)
    right[right.shape[0] - 1] = jnp.zeros((128, 128), jnp.bfloat16)
    start()
    parts = block_parts(n, kinds, blocks, trial, right)
    copies = []
    for index, (source, to) in enumerate(parts):
        if fits(n):
            to[...] = source[...]
        else:
            copies.append(pltpu.make_async_copy(source, to, block_sem.at[index]))
            copies[-1].start()

    def clear(s, carry):
        acc[s] = jnp.zeros((256, 128), jnp.float32)
        return carry

    lax.fori_loop(0, n, clear, 0)
    for copy in copies:
        copy.wait()
    products()

    def target_turn(turn, carry):
        first = turn * 2 * pairs_of(n)
        for u in range(0, 2 * pairs_of(n), 2):
            place = first + u
            one = plan_ref[2, place]
            two = plan_ref[2, place + 1]
            one, two = jnp.maximum(one, 0), jnp.where(two < 0, jnp.maximum(one, 0), two)
            pair = jnp.concatenate(
                [
                    jnp.concatenate([halves[one, 0], halves[two, 0]], axis=1),
                    jnp.concatenate([halves[one, 1], halves[two, 1]], axis=1),
                ],
                axis=0,
            )
            rights = jnp.concatenate([right[plan_ref[3, place]], right[plan_ref[3, place + 1]]], axis=1)
            term = lax.dot_general(
                pair, rights, (((1,), (1,)), ((), ())), preferred_element_type=jnp.float32
            )
            target = plan_ref[4, place]
            acc[target] = acc[target] + term
        return carry

    lax.fori_loop(0, plan_ref[5, 2], target_turn, 0)
    me = lax.axis_index("op")

    def dots(s, carry):
        t0 = trial[s, 0].astype(jnp.float32)
        t1 = trial[s, 1].astype(jnp.float32)
        a0 = acc[s, 0:128, :]
        a1 = acc[s, 128:256, :]
        p00, p01, p10, p11 = carry
        return p00 + fold(t0 * a0), p01 + fold(t0 * a1), p10 + fold(t1 * a0), p11 + fold(t1 * a1)

    zero = jnp.zeros((8, 128), jnp.float32)
    sums = lax.fori_loop(0, n, dots, (zero,) * 4, unroll=8)
    p00, p01, p10, p11 = [jnp.sum(x) for x in sums]

    chips = n // 2
    near = near_chips(n)

    def pack(j, carry):
        value = acc[jnp.bitwise_xor(me, 2 * j + 1)].astype(jnp.bfloat16)

        @pl.when(j < near)
        def _():
            near_ref[pl.ds(pl.multiple_of(j * 256, 256), 256), :] = value

        @pl.when(j >= near)
        def _():
            far_ref[pl.ds(pl.multiple_of((j - near) * 256, 256), 256), :] = value

        return carry

    lax.fori_loop(0, chips, pack, 0, unroll=2)
    own = split3(matrix_of({(0, 0): p00, (0, 1): p01, (1, 0): p10, (1, 1): p11}, 3))
    own_ref[...] = own
    far_ref[(chips - near) * 256 :, :] = tail_of(own, jnp.zeros_like(own))


def run_tasks(n, plan, left_ops, blocks):
    slots = left_ops.shape[0]
    terms_per = blocks[0][0][1].shape[0]
    kinds = tuple(block[1:] for block in blocks)
    vmem, hbm = pl.BlockSpec(memory_space=pltpu.VMEM), pl.BlockSpec(memory_space=pltpu.HBM)
    given = vmem if fits(n) else hbm
    fetched = [] if fits(n) else [
        pltpu.VMEM((AHEAD, chunk_of(n), 128, 128), jnp.bfloat16),
        pltpu.SemaphoreType.DMA((AHEAD,)),
    ]
    return pl.pallas_call(
        functools.partial(tasks_kernel, n, kinds),
        out_shape=(
            jax.ShapeDtypeStruct(((n // 2 - near_chips(n)) * 256 + TAIL, 128), jnp.bfloat16),
            jax.ShapeDtypeStruct((near_chips(n) * 256, 128), jnp.bfloat16),
            jax.ShapeDtypeStruct((n + 1, 256, 128), jnp.float32),
            jax.ShapeDtypeStruct((8, 128), jnp.float32),
        ),
        in_specs=[pl.BlockSpec(memory_space=pltpu.SMEM)] + [given] * (1 + 3 * len(blocks)),
        out_specs=(vmem,) * 4,
        scratch_shapes=[
            pltpu.VMEM((source_places(slots, n), 2, 128, 128), jnp.bfloat16),
            pltpu.VMEM((n, TRIALS, 128, 128), jnp.bfloat16),
            pltpu.VMEM((n * terms_per + 1, 128, 128), jnp.bfloat16),
            pltpu.SemaphoreType.DMA((4 * len(blocks),)),
        ]
        + fetched,
        compiler_params=pltpu.CompilerParams(vmem_limit_bytes=(33 if fits(n) else 58) * MIB),
        cost_estimate=pl.CostEstimate(
            flops=slots * 8 * 128**3, bytes_accessed=slots * 32768 + n * 450000, transcendentals=0
        ),
    )(plan, left_ops, *[value for block in blocks for value in block[0]])


def corr_kernel(*refs):
    blocks, corr_ref = refs[:-1], refs[-1]
    total = [jnp.zeros((8, 128), jnp.float32)] * 3
    for ref in blocks:
        for start in range(0, ref.shape[0], TRIALS):
            t0, t1 = ref[start].astype(jnp.float32), ref[start + 1].astype(jnp.float32)
            total = [total[0] + fold(t0 * t0), total[1] + fold(t0 * t1), total[2] + fold(t1 * t1)]
    c00, c01, c11 = [jnp.sum(x) for x in total]
    corr_ref[...] = matrix_of({(0, 0): c00, (0, 1): c01, (1, 0): c01, (1, 1): c11})[0:2, 0:2]


def correlate(blocks):
    return pl.pallas_call(
        corr_kernel,
        out_shape=jax.ShapeDtypeStruct((2, 2), jnp.float32),
        compiler_params=pltpu.CompilerParams(vmem_limit_bytes=16 * MIB),
    )(*blocks)


def far_kernel(n, acc_ref, own_ref, received_ref, total_ref, *sends):
    far, near = n // 2 - near_chips(n), near_chips(n)
    total = jnp.concatenate([own_ref[...], received_ref[far * 256 :, :].astype(jnp.float32)[0:8]], axis=0)
    total_ref[...] = total
    me = lax.axis_index("op")
    for j in range(far):
        value = acc_ref[jnp.bitwise_xor(me, 2 * (near + j))] + received_ref[j * 256 : (j + 1) * 256, :].astype(
            jnp.float32
        )
        sends[j][0:256, :] = value.astype(jnp.bfloat16)
        sends[j][256:, :] = total.astype(jnp.bfloat16)


def add_far(n, acc, own, received):
    return pl.pallas_call(
        functools.partial(far_kernel, n),
        out_shape=(jax.ShapeDtypeStruct((16, 128), jnp.float32),)
        + (jax.ShapeDtypeStruct((256 + TAIL, 128), jnp.bfloat16),) * (n // 2 - near_chips(n)),
        compiler_params=pltpu.CompilerParams(vmem_limit_bytes=16 * MIB),
    )(acc, own, received)


def near_kernel(n, acc_ref, total_ref, received_ref, mine_ref, *sends):
    me = lax.axis_index("op")
    for j in range(near_chips(n)):
        value = acc_ref[jnp.bitwise_xor(me, 2 * j)] + received_ref[j * 256 : (j + 1) * 256, :].astype(jnp.float32)
        if j == 0:
            mine_ref[...] = value
        else:
            sends[j - 1][0:256, :] = value.astype(jnp.bfloat16)
            sends[j - 1][256:, :] = total_ref[...].astype(jnp.bfloat16)


def add_near(n, acc, total, received):
    return pl.pallas_call(
        functools.partial(near_kernel, n),
        out_shape=(jax.ShapeDtypeStruct((256, 128), jnp.float32),)
        + (jax.ShapeDtypeStruct((256 + TAIL, 128), jnp.bfloat16),) * (near_chips(n) - 1),
        compiler_params=pltpu.CompilerParams(vmem_limit_bytes=16 * MIB),
    )(acc, total, received)


def last_kernel(mine_ref, total_ref, *refs):
    received, (product_ref, projected_ref) = refs[:-2], refs[-2:]
    value, total = mine_ref[...], total_ref[...]
    for ref in received:
        value = value + ref[0:256, :].astype(jnp.float32)
        total = total + ref[256:, :].astype(jnp.float32)
    product_ref[0, 0] = value[0:128]
    product_ref[0, 1] = value[128:256]
    total = total[0:8] + total[8:16]
    projected_ref[...] = total[0:2, 0:2] + total[0:2, 2:4] + total[0:2, 4:6]


def add_all(mine, total, received):
    return pl.pallas_call(
        last_kernel,
        out_shape=(
            jax.ShapeDtypeStruct((1, 2, 128, 128), jnp.float32),
            jax.ShapeDtypeStruct((2, 2), jnp.float32),
        ),
        compiler_params=pltpu.CompilerParams(vmem_limit_bytes=16 * MIB),
    )(mine, total, *received)


def body(n, trial, left_ops, right_ops, task_list):
    steps = n // 4
    plan, left_ops = make_plan(task_list.T, left_ops, n, n * right_ops.shape[0])
    vectors = jnp.concatenate([trial[0], exchange(trial[0], n, 1)], axis=0)
    line = [vectors, right_ops, exchange(right_ops, n, 1)]
    blocks = [(line, 0, False)]
    for step in range(1, steps + 1):
        line = [ring_step(value, n) for value in line]
        blocks.append((line, step, False))
        if step < steps:
            blocks.append(([exchange(value, n, 1) for value in line], step, True))
    far, near, acc, own = run_tasks(n, plan, left_ops, blocks)
    far, arrays = lax.optimization_barrier((far, [block[0][0] for block in blocks]))
    correlation = correlate(arrays)
    far, near = exchange(far, n, 1), exchange(near, n, 1)
    total, *messages = add_far(n, acc, own, far)
    first = near_chips(n)
    received = [exchange(value, n, 2 * j) for j, value in enumerate(messages, first)]
    mine, *messages = add_near(n, acc, total, near)
    received += [exchange(messages[j - 1], n, 2 * j) for j in reversed(range(1, first))]
    product, projected = add_all(mine, total, received)
    return product, correlation, projected


def solution(mesh):
    return jax.shard_map(
        functools.partial(body, mesh.shape["op"]),
        mesh=mesh,
        in_specs=(
            P(("groups", "op"), None, None, None),
            P(("groups", "op"), None, None),
            P(("groups", "op"), None, None),
            P(("groups", "op"), None),
        ),
        out_specs=(P(("groups", "op"), None, None, None), P("groups", None), P("groups", None)),
        check_vma=False,
    )
```

```python
import functools

import jax
import jax.numpy as jnp
from jax import lax
from jax.experimental import pallas as pl
from jax.experimental.pallas import tpu as pltpu
from jax.sharding import PartitionSpec as P

MIB = 1024 * 1024
TAIL = 16
TRIALS = 2
AHEAD = 3


def exchange(value, n, mask):
    return lax.ppermute(value, "op", [(i, i ^ mask) for i in range(n)])


def chip_at(place, chips):
    return 2 * place if place < chips // 2 else 2 * (chips - place) - 1


def ring_step(value, n):
    chips = n // 2
    order = [chip_at(place, chips) for place in range(chips)]
    pairs = []
    for place, chip in enumerate(order):
        pairs.append((2 * chip, 2 * order[(place + 1) % chips]))
        pairs.append((2 * chip + 1, 2 * order[(place - 1) % chips] + 1))
    return lax.ppermute(value, "op", pairs)


def owner_of(step, swapped, half, n):
    chips = n // 2
    me = lax.axis_index("op")
    chip, core = me // 2, lax.rem(me, 2)
    odd = lax.rem(chip, 2)
    mine = jnp.where(odd == 0, chip // 2, chips - 1 - chip // 2)
    line = 1 - core if swapped else core
    place = lax.rem(mine + (2 * line - 1) * step + 2 * chips, chips)
    there = jnp.where(place < chips // 2, 2 * place, 2 * (chips - place) - 1)
    return 2 * there + (line if half == 0 else 1 - line)


def split3(value):
    lanes = lax.broadcasted_iota(jnp.int32, (8, 128), 1)
    high = value.astype(jnp.bfloat16).astype(jnp.float32)
    middle = (value - high).astype(jnp.bfloat16).astype(jnp.float32)
    low = (value - high - middle).astype(jnp.bfloat16).astype(jnp.float32)
    return jnp.where(lanes < 2, high, jnp.where(lanes < 4, middle, low))


def tail_of(first, second):
    return jnp.concatenate([first, second], axis=0).astype(jnp.bfloat16)


def matrix_of(values, repeats=1):
    rows = lax.broadcasted_iota(jnp.int32, (8, 128), 0)
    lanes = lax.broadcasted_iota(jnp.int32, (8, 128), 1)
    total = jnp.zeros((8, 128), jnp.float32)
    for (i, j), value in values.items():
        for repeat in range(repeats):
            total = total + jnp.where((rows == i) & (lanes == j + 2 * repeat), value, 0.0)
    return total


def fold(value):
    return value.reshape(16, 8, 128).sum(axis=0)


def fits(n):
    return n <= 16


def near_chips(n):
    return n // 4


def phases_of(n):
    return 1


def chunk_of(n):
    return 144 if fits(n) else 48


def pairs_of(n):
    return 69 if fits(n) else 24


def run_of(slots, n):
    return 4 if slots >= 8 * n else 2


def source_places(slots, n):
    chunk = chunk_of(n)
    most = slots + min(slots, n) * (run_of(slots, n) - 1)
    return -(-most // chunk) * chunk


def place_of(chip, chips):
    half = jnp.floor(chip * 0.5)
    return jnp.where(chip == 2.0 * half, half, chips - 1.0 - half)


def plan_kernel(n, terms, tasks_ref, plan_ref):
    slots = tasks_ref.shape[1]
    places = plan_ref.shape[1]
    chips = n // 2
    phases = phases_of(n)
    rows = tasks_ref[...].astype(jnp.float32)
    source, target, term, live = rows[0:1], rows[1:2], rows[2:3], rows[3:4]
    lane = lax.broadcasted_iota(jnp.int32, (1, slots), 1).astype(jnp.float32)
    number = lax.broadcasted_iota(jnp.int32, (1, places), 1).astype(jnp.float32)
    at = lax.broadcasted_iota(jnp.int32, (slots, places), 1).astype(jnp.float32)
    me = lax.axis_index("op")
    mine = place_of((jnp.zeros((1, slots), jnp.int32) + me // 2).astype(jnp.float32), float(chips))
    gap = place_of(jnp.floor(source * 0.5), float(chips)) - mine
    up = jnp.where(gap < 0, gap + chips, gap)
    far = jnp.minimum(up, chips - up)
    phase = jnp.clip(far - 1.0, 0.0, phases - 1.0)

    def column(*values):
        pad = [jnp.zeros((8 - len(values), slots), jnp.float32)]
        return jnp.transpose(jnp.concatenate(list(values) + pad, axis=0))

    def sort(sector, parts, unit, whole):
        keys = parts * n
        index = lax.broadcasted_iota(jnp.int32, (keys, slots), 0).astype(jnp.float32)
        part = phase if parts > 1 else jnp.zeros_like(phase)
        key = jnp.where(live > 0, part * n + sector, float(keys))
        columns = column(key, lane)
        earlier = jnp.where((columns[:, 0:1] == key) & (columns[:, 1:2] < lane), 1.0, 0.0)
        count = jnp.sum(jnp.where(index == key, 1.0, 0.0), axis=1, keepdims=True)
        padded = jnp.ceil(count / unit) * unit
        place = jnp.sum(earlier, axis=0, keepdims=True)
        start = jnp.zeros((1, 1), jnp.float32)
        starts = [start]
        for p in range(parts):
            lengths = padded[p * n : (p + 1) * n]
            before = jnp.where(index[p * n : (p + 1) * n] < key, lengths, 0.0)
            place = place + jnp.where(part == p, start * whole + jnp.sum(before, axis=0, keepdims=True), 0.0)
            start = start + jnp.ceil(jnp.sum(lengths, axis=0, keepdims=True) / whole)
            starts.append(start)
        return jnp.where(live > 0, place, -1.0), starts

    by_source, source_starts = sort(source, phases, float(run_of(slots, n)), float(chunk_of(n)))
    by_target, target_starts = sort(target, 1, 2.0, 2.0 * pairs_of(n))
    columns = column(by_source, by_target, lane, source, term, target)

    def picker(places_column):
        hit = places_column == at

        def pick(values, other):
            found = jnp.sum(jnp.where(hit, values - other, 0.0), axis=0, keepdims=True)
            return (found + other).astype(jnp.int32)

        return pick

    own = (jnp.zeros((1, 1), jnp.int32) + me).astype(jnp.float32)
    pick = picker(columns[:, 0:1])
    plan_ref[0:1] = pick(columns[:, 2:3], 0.0)
    plan_ref[1:2] = pick(columns[:, 3:4], own)
    pick = picker(columns[:, 1:2])
    plan_ref[2:3] = pick(columns[:, 0:1], -1.0)
    plan_ref[3:4] = pick(columns[:, 4:5], float(terms))
    plan_ref[4:5] = pick(columns[:, 5:6], float(n))
    turns = jnp.zeros((1, places), jnp.float32)
    for p, start in enumerate(source_starts + [target_starts[1]]):
        turns = turns + jnp.where(number == p, start, 0.0)
    plan_ref[5:6] = turns.astype(jnp.int32)


def stage_kernel(n, terms, tasks_ref, left_ref, plan_ref, held_ref, tasks, sem):
    copies = [
        pltpu.make_async_copy(tasks_ref, tasks, sem.at[0]),
        pltpu.make_async_copy(left_ref, held_ref, sem.at[1]),
    ]
    for copy in copies:
        copy.start()
    copies[0].wait()
    plan_kernel(n, terms, tasks, plan_ref)
    copies[1].wait()


def make_plan(tasks, left_ops, n, terms):
    most = source_places(tasks.shape[1], n)
    plan = jax.ShapeDtypeStruct((6, -(-most // 128) * 128), jnp.int32)
    vmem, hbm = pl.BlockSpec(memory_space=pltpu.VMEM), pl.BlockSpec(memory_space=pltpu.HBM)
    if fits(n):
        return pl.pallas_call(
            functools.partial(stage_kernel, n, terms),
            in_specs=[hbm, hbm],
            out_specs=(vmem, vmem),
            out_shape=(plan, jax.ShapeDtypeStruct(left_ops.shape, left_ops.dtype)),
            scratch_shapes=[pltpu.VMEM(tasks.shape, jnp.int32), pltpu.SemaphoreType.DMA((2,))],
            compiler_params=pltpu.CompilerParams(vmem_limit_bytes=42 * MIB),
        )(tasks, left_ops)
    return (
        pl.pallas_call(
            functools.partial(plan_kernel, n, terms),
            out_shape=plan,
            compiler_params=pltpu.CompilerParams(vmem_limit_bytes=16 * MIB),
        )(tasks),
        left_ops,
    )


def block_parts(n, kinds, blocks, trial, right):
    parts = []
    for b, kind in enumerate(kinds):
        vectors, *terms = blocks[3 * b : 3 * b + 3]
        for half, ref in enumerate(terms):
            owner = owner_of(*kind, half, n)
            per = ref.shape[0]
            parts.append((vectors.at[pl.ds(half * TRIALS, TRIALS)], trial.at[owner]))
            parts.append((ref, right.at[pl.ds(owner * per, per)]))
    return parts


def make_halves(n, plan_ref, left_ref, trial, halves, fetched):
    turns = plan_ref[5, 1]
    run = run_of(left_ref.shape[0], n)
    chunk = chunk_of(n)

    def fetch(turn):
        left, left_sem = fetched
        at = lax.rem(turn, AHEAD)
        for u in range(chunk):
            slot = plan_ref[0, turn * chunk + u]
            pltpu.make_async_copy(left_ref.at[slot], left.at[at, u], left_sem.at[at]).start()

    def start():
        for turn in range(AHEAD - 1) if fetched else ():

            @pl.when(turn < turns)
            def _():
                fetch(turn)

    def turn_of(turn, carry):
        if fetched:
            left, left_sem = fetched

            @pl.when(turn + AHEAD - 1 < turns)
            def _():
                fetch(turn + AHEAD - 1)

            at = lax.rem(turn, AHEAD)
            pltpu.make_async_copy(left_ref.at[pl.ds(0, chunk)], left.at[at], left_sem.at[at]).wait()
        place = turn * chunk
        for r in range(0, chunk, run):
            source = plan_ref[1, place + r]
            vectors = jnp.concatenate([trial[source, 0], trial[source, 1]], axis=1)
            if fetched:
                rows = left[at, r : r + run].reshape(run * 128, 128)
            else:
                rows = jnp.concatenate([left_ref[plan_ref[0, place + r + u]] for u in range(run)], axis=0)
            half = jnp.dot(rows, vectors, preferred_element_type=jnp.float32).astype(jnp.bfloat16)
            for u in range(run):
                halves[place + r + u, 0] = half[u * 128 : (u + 1) * 128, :128]
                halves[place + r + u, 1] = half[u * 128 : (u + 1) * 128, 128:]
        return carry

    return start, lambda: lax.fori_loop(0, turns, turn_of, 0)


def tasks_kernel(n, kinds, plan_ref, left_ref, *refs):
    blocks, refs = refs[: 3 * len(kinds)], refs[3 * len(kinds) :]
    far_ref, near_ref, acc, own_ref, halves, trial, right, block_sem, *fetched = refs
    start, products = make_halves(n, plan_ref, left_ref, trial, halves, fetched)
    right[right.shape[0] - 1] = jnp.zeros((128, 128), jnp.bfloat16)
    start()
    parts = block_parts(n, kinds, blocks, trial, right)
    copies = []
    for index, (source, to) in enumerate(parts):
        if fits(n):
            to[...] = source[...]
        else:
            copies.append(pltpu.make_async_copy(source, to, block_sem.at[index]))
            copies[-1].start()

    def clear(s, carry):
        acc[s] = jnp.zeros((256, 128), jnp.float32)
        return carry

    lax.fori_loop(0, n, clear, 0)
    for copy in copies:
        copy.wait()
    products()

    def target_turn(turn, carry):
        first = turn * 2 * pairs_of(n)
        for u in range(0, 2 * pairs_of(n), 2):
            place = first + u
            one = plan_ref[2, place]
            two = plan_ref[2, place + 1]
            one, two = jnp.maximum(one, 0), jnp.where(two < 0, jnp.maximum(one, 0), two)
            pair = jnp.concatenate(
                [
                    jnp.concatenate([halves[one, 0], halves[two, 0]], axis=1),
                    jnp.concatenate([halves[one, 1], halves[two, 1]], axis=1),
                ],
                axis=0,
            )
            rights = jnp.concatenate([right[plan_ref[3, place]], right[plan_ref[3, place + 1]]], axis=1)
            term = lax.dot_general(
                pair, rights, (((1,), (1,)), ((), ())), preferred_element_type=jnp.float32
            )
            target = plan_ref[4, place]
            acc[target] = acc[target] + term
        return carry

    lax.fori_loop(0, plan_ref[5, 2], target_turn, 0)
    me = lax.axis_index("op")

    def dots(s, carry):
        t0 = trial[s, 0].astype(jnp.float32)
        t1 = trial[s, 1].astype(jnp.float32)
        a0 = acc[s, 0:128, :]
        a1 = acc[s, 128:256, :]
        p00, p01, p10, p11 = carry
        return p00 + fold(t0 * a0), p01 + fold(t0 * a1), p10 + fold(t1 * a0), p11 + fold(t1 * a1)

    zero = jnp.zeros((8, 128), jnp.float32)
    sums = lax.fori_loop(0, n, dots, (zero,) * 4, unroll=8)
    p00, p01, p10, p11 = [jnp.sum(x) for x in sums]

    chips = n // 2
    near = near_chips(n)

    def pack(j, carry):
        value = acc[jnp.bitwise_xor(me, 2 * j + 1)].astype(jnp.bfloat16)

        @pl.when(j < near)
        def _():
            near_ref[pl.ds(pl.multiple_of(j * 256, 256), 256), :] = value

        @pl.when(j >= near)
        def _():
            far_ref[pl.ds(pl.multiple_of((j - near) * 256, 256), 256), :] = value

        return carry

    lax.fori_loop(0, chips, pack, 0, unroll=2)
    own = split3(matrix_of({(0, 0): p00, (0, 1): p01, (1, 0): p10, (1, 1): p11}, 3))
    own_ref[...] = own
    far_ref[(chips - near) * 256 :, :] = tail_of(own, jnp.zeros_like(own))


def run_tasks(n, plan, left_ops, blocks):
    slots = left_ops.shape[0]
    terms_per = blocks[0][0][1].shape[0]
    kinds = tuple(block[1:] for block in blocks)
    vmem, hbm = pl.BlockSpec(memory_space=pltpu.VMEM), pl.BlockSpec(memory_space=pltpu.HBM)
    given = vmem if fits(n) else hbm
    fetched = [] if fits(n) else [
        pltpu.VMEM((AHEAD, chunk_of(n), 128, 128), jnp.bfloat16),
        pltpu.SemaphoreType.DMA((AHEAD,)),
    ]
    return pl.pallas_call(
        functools.partial(tasks_kernel, n, kinds),
        out_shape=(
            jax.ShapeDtypeStruct(((n // 2 - near_chips(n)) * 256 + TAIL, 128), jnp.bfloat16),
            jax.ShapeDtypeStruct((near_chips(n) * 256, 128), jnp.bfloat16),
            jax.ShapeDtypeStruct((n + 1, 256, 128), jnp.float32),
            jax.ShapeDtypeStruct((8, 128), jnp.float32),
        ),
        in_specs=[pl.BlockSpec(memory_space=pltpu.SMEM)] + [given] * (1 + 3 * len(blocks)),
        out_specs=(vmem,) * 4,
        scratch_shapes=[
            pltpu.VMEM((source_places(slots, n), 2, 128, 128), jnp.bfloat16),
            pltpu.VMEM((n, TRIALS, 128, 128), jnp.bfloat16),
            pltpu.VMEM((n * terms_per + 1, 128, 128), jnp.bfloat16),
            pltpu.SemaphoreType.DMA((4 * len(blocks),)),
        ]
        + fetched,
        compiler_params=pltpu.CompilerParams(vmem_limit_bytes=(33 if fits(n) else 58) * MIB),
        cost_estimate=pl.CostEstimate(
            flops=slots * 8 * 128**3, bytes_accessed=slots * 32768 + n * 450000, transcendentals=0
        ),
    )(plan, left_ops, *[value for block in blocks for value in block[0]])


def corr_kernel(*refs):
    blocks, corr_ref = refs[:-1], refs[-1]
    total = [jnp.zeros((8, 128), jnp.float32)] * 3
    for ref in blocks:
        for start in range(0, ref.shape[0], TRIALS):
            t0, t1 = ref[start].astype(jnp.float32), ref[start + 1].astype(jnp.float32)
            total = [total[0] + fold(t0 * t0), total[1] + fold(t0 * t1), total[2] + fold(t1 * t1)]
    c00, c01, c11 = [jnp.sum(x) for x in total]
    corr_ref[...] = matrix_of({(0, 0): c00, (0, 1): c01, (1, 0): c01, (1, 1): c11})[0:2, 0:2]


def correlate(blocks):
    return pl.pallas_call(
        corr_kernel,
        out_shape=jax.ShapeDtypeStruct((2, 2), jnp.float32),
        compiler_params=pltpu.CompilerParams(vmem_limit_bytes=16 * MIB),
    )(*blocks)


def far_kernel(n, acc_ref, own_ref, received_ref, total_ref, *sends):
    far, near = n // 2 - near_chips(n), near_chips(n)
    total = jnp.concatenate([own_ref[...], received_ref[far * 256 :, :].astype(jnp.float32)[0:8]], axis=0)
    total_ref[...] = total
    me = lax.axis_index("op")
    for j in range(far):
        value = acc_ref[jnp.bitwise_xor(me, 2 * (near + j))] + received_ref[j * 256 : (j + 1) * 256, :].astype(
            jnp.float32
        )
        sends[j][0:256, :] = value.astype(jnp.bfloat16)
        sends[j][256:, :] = total.astype(jnp.bfloat16)


def add_far(n, acc, own, received):
    return pl.pallas_call(
        functools.partial(far_kernel, n),
        out_shape=(jax.ShapeDtypeStruct((16, 128), jnp.float32),)
        + (jax.ShapeDtypeStruct((256 + TAIL, 128), jnp.bfloat16),) * (n // 2 - near_chips(n)),
        compiler_params=pltpu.CompilerParams(vmem_limit_bytes=16 * MIB),
    )(acc, own, received)


def near_kernel(n, acc_ref, total_ref, received_ref, mine_ref, *sends):
    me = lax.axis_index("op")
    for j in range(near_chips(n)):
        value = acc_ref[jnp.bitwise_xor(me, 2 * j)] + received_ref[j * 256 : (j + 1) * 256, :].astype(jnp.float32)
        if j == 0:
            mine_ref[...] = value
        else:
            sends[j - 1][0:256, :] = value.astype(jnp.bfloat16)
            sends[j - 1][256:, :] = total_ref[...].astype(jnp.bfloat16)


def add_near(n, acc, total, received):
    return pl.pallas_call(
        functools.partial(near_kernel, n),
        out_shape=(jax.ShapeDtypeStruct((256, 128), jnp.float32),)
        + (jax.ShapeDtypeStruct((256 + TAIL, 128), jnp.bfloat16),) * (near_chips(n) - 1),
        compiler_params=pltpu.CompilerParams(vmem_limit_bytes=16 * MIB),
    )(acc, total, received)


def last_kernel(mine_ref, total_ref, *refs):
    received, (product_ref, projected_ref) = refs[:-2], refs[-2:]
    value, total = mine_ref[...], total_ref[...]
    for ref in received:
        value = value + ref[0:256, :].astype(jnp.float32)
        total = total + ref[256:, :].astype(jnp.float32)
    product_ref[0, 0] = value[0:128]
    product_ref[0, 1] = value[128:256]
    total = total[0:8] + total[8:16]
    projected_ref[...] = total[0:2, 0:2] + total[0:2, 2:4] + total[0:2, 4:6]


def add_all(mine, total, received):
    return pl.pallas_call(
        last_kernel,
        out_shape=(
            jax.ShapeDtypeStruct((1, 2, 128, 128), jnp.float32),
            jax.ShapeDtypeStruct((2, 2), jnp.float32),
        ),
        compiler_params=pltpu.CompilerParams(vmem_limit_bytes=16 * MIB),
    )(mine, total, *received)


def body(n, trial, left_ops, right_ops, task_list):
    steps = n // 4
    plan, left_ops = make_plan(pltpu.with_memory_space_constraint(task_list.T, pltpu.HBM), left_ops, n, n * right_ops.shape[0])
    vectors = jnp.concatenate([trial[0], exchange(trial[0], n, 1)], axis=0)
    line = [vectors, right_ops, exchange(right_ops, n, 1)]
    blocks = [(line, 0, False)]
    for step in range(1, steps + 1):
        line = [ring_step(value, n) for value in line]
        blocks.append((line, step, False))
        if step < steps:
            blocks.append(([exchange(value, n, 1) for value in line], step, True))
    far, near, acc, own = run_tasks(n, plan, left_ops, blocks)
    far, arrays = lax.optimization_barrier((far, [block[0][0] for block in blocks]))
    correlation = correlate(arrays)
    far, near = exchange(far, n, 1), exchange(near, n, 1)
    total, *messages = add_far(n, acc, own, far)
    first = near_chips(n)
    received = [exchange(messages[j], n, 2 * (first + j)) for j in reversed(range(len(messages)))]
    mine, *messages = add_near(n, acc, total, near)
    received += [exchange(messages[j - 1], n, 2 * j) for j in reversed(range(1, first))]
    product, projected = add_all(mine, total, received)
    return product, correlation, projected


def solution(mesh):
    return jax.shard_map(
        functools.partial(body, mesh.shape["op"]),
        mesh=mesh,
        in_specs=(
            P(("groups", "op"), None, None, None),
            P(("groups", "op"), None, None),
            P(("groups", "op"), None, None),
            P(("groups", "op"), None),
        ),
        out_specs=(P(("groups", "op"), None, None, None), P("groups", None), P("groups", None)),
        check_vma=False,
    )
```

```python
import functools

import jax
import jax.numpy as jnp
from jax import lax
from jax.experimental import pallas as pl
from jax.experimental.pallas import tpu as pltpu
from jax.sharding import PartitionSpec as P

MIB = 1024 * 1024
TAIL = 16
TRIALS = 2
AHEAD = 3


def exchange(value, n, mask):
    return lax.ppermute(value, "op", [(i, i ^ mask) for i in range(n)])


def chip_at(place, chips):
    return 2 * place if place < chips // 2 else 2 * (chips - place) - 1


def ring_step(value, n):
    chips = n // 2
    order = [chip_at(place, chips) for place in range(chips)]
    pairs = []
    for place, chip in enumerate(order):
        pairs.append((2 * chip, 2 * order[(place + 1) % chips]))
        pairs.append((2 * chip + 1, 2 * order[(place - 1) % chips] + 1))
    return lax.ppermute(value, "op", pairs)


def owner_of(step, swapped, half, n):
    chips = n // 2
    me = lax.axis_index("op")
    chip, core = me // 2, lax.rem(me, 2)
    odd = lax.rem(chip, 2)
    mine = jnp.where(odd == 0, chip // 2, chips - 1 - chip // 2)
    line = 1 - core if swapped else core
    place = lax.rem(mine + (2 * line - 1) * step + 2 * chips, chips)
    there = jnp.where(place < chips // 2, 2 * place, 2 * (chips - place) - 1)
    return 2 * there + (line if half == 0 else 1 - line)


def split3(value):
    lanes = lax.broadcasted_iota(jnp.int32, (8, 128), 1)
    high = value.astype(jnp.bfloat16).astype(jnp.float32)
    middle = (value - high).astype(jnp.bfloat16).astype(jnp.float32)
    low = (value - high - middle).astype(jnp.bfloat16).astype(jnp.float32)
    return jnp.where(lanes < 2, high, jnp.where(lanes < 4, middle, low))


def tail_of(first, second):
    return jnp.concatenate([first, second], axis=0).astype(jnp.bfloat16)


def matrix_of(values, repeats=1):
    rows = lax.broadcasted_iota(jnp.int32, (8, 128), 0)
    lanes = lax.broadcasted_iota(jnp.int32, (8, 128), 1)
    total = jnp.zeros((8, 128), jnp.float32)
    for (i, j), value in values.items():
        for repeat in range(repeats):
            total = total + jnp.where((rows == i) & (lanes == j + 2 * repeat), value, 0.0)
    return total


def fold(value):
    return value.reshape(16, 8, 128).sum(axis=0)


def fits(n):
    return n <= 16


def near_chips(n):
    return n // 4


def phases_of(n):
    return 1


def chunk_of(n):
    return 144 if fits(n) else 48


def pairs_of(n):
    return 68 if fits(n) else 24


def run_of(slots, n):
    return 4 if slots >= 8 * n else 2


def source_places(slots, n):
    chunk = chunk_of(n)
    most = slots + min(slots, n) * (run_of(slots, n) - 1)
    return -(-most // chunk) * chunk


def place_of(chip, chips):
    half = jnp.floor(chip * 0.5)
    return jnp.where(chip == 2.0 * half, half, chips - 1.0 - half)


def plan_kernel(n, terms, tasks_ref, plan_ref):
    slots = tasks_ref.shape[1]
    places = plan_ref.shape[1]
    chips = n // 2
    phases = phases_of(n)
    rows = tasks_ref[...].astype(jnp.float32)
    source, target, term, live = rows[0:1], rows[1:2], rows[2:3], rows[3:4]
    lane = lax.broadcasted_iota(jnp.int32, (1, slots), 1).astype(jnp.float32)
    number = lax.broadcasted_iota(jnp.int32, (1, places), 1).astype(jnp.float32)
    at = lax.broadcasted_iota(jnp.int32, (slots, places), 1).astype(jnp.float32)
    me = lax.axis_index("op")
    mine = place_of((jnp.zeros((1, slots), jnp.int32) + me // 2).astype(jnp.float32), float(chips))
    gap = place_of(jnp.floor(source * 0.5), float(chips)) - mine
    up = jnp.where(gap < 0, gap + chips, gap)
    far = jnp.minimum(up, chips - up)
    phase = jnp.clip(far - 1.0, 0.0, phases - 1.0)

    def column(*values):
        pad = [jnp.zeros((8 - len(values), slots), jnp.float32)]
        return jnp.transpose(jnp.concatenate(list(values) + pad, axis=0))

    def sort(sector, parts, unit, whole):
        keys = parts * n
        index = lax.broadcasted_iota(jnp.int32, (keys, slots), 0).astype(jnp.float32)
        part = phase if parts > 1 else jnp.zeros_like(phase)
        key = jnp.where(live > 0, part * n + sector, float(keys))
        columns = column(key, lane)
        earlier = jnp.where((columns[:, 0:1] == key) & (columns[:, 1:2] < lane), 1.0, 0.0)
        count = jnp.sum(jnp.where(index == key, 1.0, 0.0), axis=1, keepdims=True)
        padded = jnp.ceil(count / unit) * unit
        place = jnp.sum(earlier, axis=0, keepdims=True)
        start = jnp.zeros((1, 1), jnp.float32)
        starts = [start]
        for p in range(parts):
            lengths = padded[p * n : (p + 1) * n]
            before = jnp.where(index[p * n : (p + 1) * n] < key, lengths, 0.0)
            place = place + jnp.where(part == p, start * whole + jnp.sum(before, axis=0, keepdims=True), 0.0)
            start = start + jnp.ceil(jnp.sum(lengths, axis=0, keepdims=True) / whole)
            starts.append(start)
        return jnp.where(live > 0, place, -1.0), starts

    by_source, source_starts = sort(source, phases, float(run_of(slots, n)), float(chunk_of(n)))
    by_target, target_starts = sort(target, 1, 2.0, 2.0 * pairs_of(n))
    columns = column(by_source, by_target, lane, source, term, target)

    def picker(places_column):
        hit = places_column == at

        def pick(values, other):
            found = jnp.sum(jnp.where(hit, values - other, 0.0), axis=0, keepdims=True)
            return (found + other).astype(jnp.int32)

        return pick

    own = (jnp.zeros((1, 1), jnp.int32) + me).astype(jnp.float32)
    pick = picker(columns[:, 0:1])
    plan_ref[0:1] = pick(columns[:, 2:3], 0.0)
    plan_ref[1:2] = pick(columns[:, 3:4], own)
    pick = picker(columns[:, 1:2])
    plan_ref[2:3] = pick(columns[:, 0:1], -1.0)
    plan_ref[3:4] = pick(columns[:, 4:5], float(terms))
    plan_ref[4:5] = pick(columns[:, 5:6], float(n))
    turns = jnp.zeros((1, places), jnp.float32)
    for p, start in enumerate(source_starts + [target_starts[1]]):
        turns = turns + jnp.where(number == p, start, 0.0)
    plan_ref[5:6] = turns.astype(jnp.int32)


def stage_kernel(n, terms, tasks_ref, left_ref, plan_ref, held_ref, tasks, sem):
    copies = [
        pltpu.make_async_copy(tasks_ref, tasks, sem.at[0]),
        pltpu.make_async_copy(left_ref, held_ref, sem.at[1]),
    ]
    for copy in copies:
        copy.start()
    copies[0].wait()
    plan_kernel(n, terms, tasks, plan_ref)
    copies[1].wait()


def make_plan(tasks, left_ops, n, terms):
    most = source_places(tasks.shape[1], n)
    plan = jax.ShapeDtypeStruct((6, -(-most // 128) * 128), jnp.int32)
    vmem, hbm = pl.BlockSpec(memory_space=pltpu.VMEM), pl.BlockSpec(memory_space=pltpu.HBM)
    if fits(n):
        return pl.pallas_call(
            functools.partial(stage_kernel, n, terms),
            in_specs=[hbm, hbm],
            out_specs=(vmem, vmem),
            out_shape=(plan, jax.ShapeDtypeStruct(left_ops.shape, left_ops.dtype)),
            scratch_shapes=[pltpu.VMEM(tasks.shape, jnp.int32), pltpu.SemaphoreType.DMA((2,))],
            compiler_params=pltpu.CompilerParams(vmem_limit_bytes=42 * MIB),
        )(tasks, left_ops)
    return (
        pl.pallas_call(
            functools.partial(plan_kernel, n, terms),
            out_shape=plan,
            compiler_params=pltpu.CompilerParams(vmem_limit_bytes=16 * MIB),
        )(tasks),
        left_ops,
    )


def block_parts(n, kinds, blocks, trial, right):
    parts = []
    for b, kind in enumerate(kinds):
        vectors, *terms = blocks[3 * b : 3 * b + 3]
        for half, ref in enumerate(terms):
            owner = owner_of(*kind, half, n)
            per = ref.shape[0]
            parts.append((vectors.at[pl.ds(half * TRIALS, TRIALS)], trial.at[owner]))
            parts.append((ref, right.at[pl.ds(owner * per, per)]))
    return parts


def make_halves(n, plan_ref, left_ref, trial, halves, fetched, beside):
    turns = plan_ref[5, 1]
    run = run_of(left_ref.shape[0], n)
    chunk = chunk_of(n)

    def fetch(turn):
        left, left_sem = fetched
        at = lax.rem(turn, AHEAD)
        for u in range(chunk):
            slot = plan_ref[0, turn * chunk + u]
            pltpu.make_async_copy(left_ref.at[slot], left.at[at, u], left_sem.at[at]).start()

    def start():
        for turn in range(AHEAD - 1) if fetched else ():

            @pl.when(turn < turns)
            def _():
                fetch(turn)

    def turn_of(turn, carry):
        if fetched:
            left, left_sem = fetched

            @pl.when(turn + AHEAD - 1 < turns)
            def _():
                fetch(turn + AHEAD - 1)

            at = lax.rem(turn, AHEAD)
            pltpu.make_async_copy(left_ref.at[pl.ds(0, chunk)], left.at[at], left_sem.at[at]).wait()
        beside()
        place = turn * chunk
        for r in range(0, chunk, run):
            source = plan_ref[1, place + r]
            vectors = jnp.concatenate([trial[source, 0], trial[source, 1]], axis=1)
            if fetched:
                rows = left[at, r : r + run].reshape(run * 128, 128)
            else:
                rows = jnp.concatenate([left_ref[plan_ref[0, place + r + u]] for u in range(run)], axis=0)
            half = jnp.dot(rows, vectors, preferred_element_type=jnp.float32).astype(jnp.bfloat16)
            for u in range(run):
                halves[place + r + u, 0] = half[u * 128 : (u + 1) * 128, :128]
                halves[place + r + u, 1] = half[u * 128 : (u + 1) * 128, 128:]
        return carry

    return start, lambda: lax.fori_loop(0, turns, turn_of, 0)


def tasks_kernel(n, kinds, plan_ref, left_ref, *refs):
    blocks, refs = refs[: 3 * len(kinds)], refs[3 * len(kinds) :]
    far_ref, near_ref, acc, own_ref, halves, trial, right, block_sem, *fetched = refs
    parts = block_parts(n, kinds, blocks, trial, right)

    def clear():
        for s in range(n):
            acc[s] = jnp.zeros((256, 128), jnp.float32)

    def beside():
        if fits(n):
            clear()
            for source, to in parts[1::2]:
                to[...] = source[...]

    start, products = make_halves(n, plan_ref, left_ref, trial, halves, fetched, beside)
    right[right.shape[0] - 1] = jnp.zeros((128, 128), jnp.bfloat16)
    start()
    copies = []
    if fits(n):
        for source, to in parts[0::2]:
            to[...] = source[...]
        pl.when(plan_ref[5, 1] == 0)(clear)
    else:
        for index, (source, to) in enumerate(parts):
            copies.append(pltpu.make_async_copy(source, to, block_sem.at[index]))
            copies[-1].start()
        clear()
    for copy in copies:
        copy.wait()
    products()

    def target_turn(turn, carry):
        first = turn * 2 * pairs_of(n)
        for u in range(0, 2 * pairs_of(n), 2):
            place = first + u
            one = plan_ref[2, place]
            two = plan_ref[2, place + 1]
            one, two = jnp.maximum(one, 0), jnp.where(two < 0, jnp.maximum(one, 0), two)
            pair = jnp.concatenate(
                [
                    jnp.concatenate([halves[one, 0], halves[two, 0]], axis=1),
                    jnp.concatenate([halves[one, 1], halves[two, 1]], axis=1),
                ],
                axis=0,
            )
            rights = jnp.concatenate([right[plan_ref[3, place]], right[plan_ref[3, place + 1]]], axis=1)
            term = lax.dot_general(
                pair, rights, (((1,), (1,)), ((), ())), preferred_element_type=jnp.float32
            )
            target = plan_ref[4, place]
            acc[target] = acc[target] + term
        return carry

    lax.fori_loop(0, plan_ref[5, 2], target_turn, 0)
    me = lax.axis_index("op")

    def dots(s, carry):
        t0 = trial[s, 0].astype(jnp.float32)
        t1 = trial[s, 1].astype(jnp.float32)
        a0 = acc[s, 0:128, :]
        a1 = acc[s, 128:256, :]
        p00, p01, p10, p11 = carry
        return p00 + fold(t0 * a0), p01 + fold(t0 * a1), p10 + fold(t1 * a0), p11 + fold(t1 * a1)

    zero = jnp.zeros((8, 128), jnp.float32)
    sums = lax.fori_loop(0, n, dots, (zero,) * 4, unroll=8)
    p00, p01, p10, p11 = [jnp.sum(x) for x in sums]

    chips = n // 2
    near = near_chips(n)

    def pack(j, carry):
        value = acc[jnp.bitwise_xor(me, 2 * j + 1)].astype(jnp.bfloat16)

        @pl.when(j < near)
        def _():
            near_ref[pl.ds(pl.multiple_of(j * 256, 256), 256), :] = value

        @pl.when(j >= near)
        def _():
            far_ref[pl.ds(pl.multiple_of((j - near) * 256, 256), 256), :] = value

        return carry

    lax.fori_loop(0, chips, pack, 0, unroll=2)
    own = split3(matrix_of({(0, 0): p00, (0, 1): p01, (1, 0): p10, (1, 1): p11}, 3))
    own_ref[...] = own
    far_ref[(chips - near) * 256 :, :] = tail_of(own, jnp.zeros_like(own))


def run_tasks(n, plan, left_ops, blocks):
    slots = left_ops.shape[0]
    terms_per = blocks[0][0][1].shape[0]
    kinds = tuple(block[1:] for block in blocks)
    vmem, hbm = pl.BlockSpec(memory_space=pltpu.VMEM), pl.BlockSpec(memory_space=pltpu.HBM)
    given = vmem if fits(n) else hbm
    fetched = [] if fits(n) else [
        pltpu.VMEM((AHEAD, chunk_of(n), 128, 128), jnp.bfloat16),
        pltpu.SemaphoreType.DMA((AHEAD,)),
    ]
    return pl.pallas_call(
        functools.partial(tasks_kernel, n, kinds),
        out_shape=(
            jax.ShapeDtypeStruct(((n // 2 - near_chips(n)) * 256 + TAIL, 128), jnp.bfloat16),
            jax.ShapeDtypeStruct((near_chips(n) * 256, 128), jnp.bfloat16),
            jax.ShapeDtypeStruct((n + 1, 256, 128), jnp.float32),
            jax.ShapeDtypeStruct((8, 128), jnp.float32),
        ),
        in_specs=[pl.BlockSpec(memory_space=pltpu.SMEM)] + [given] * (1 + 3 * len(blocks)),
        out_specs=(vmem,) * 4,
        scratch_shapes=[
            pltpu.VMEM((source_places(slots, n), 2, 128, 128), jnp.bfloat16),
            pltpu.VMEM((n, TRIALS, 128, 128), jnp.bfloat16),
            pltpu.VMEM((n * terms_per + 1, 128, 128), jnp.bfloat16),
            pltpu.SemaphoreType.DMA((4 * len(blocks),)),
        ]
        + fetched,
        compiler_params=pltpu.CompilerParams(vmem_limit_bytes=(33 if fits(n) else 58) * MIB),
        cost_estimate=pl.CostEstimate(
            flops=slots * 8 * 128**3, bytes_accessed=slots * 32768 + n * 450000, transcendentals=0
        ),
    )(plan, left_ops, *[value for block in blocks for value in block[0]])


def corr_kernel(*refs):
    blocks, corr_ref = refs[:-1], refs[-1]
    total = [jnp.zeros((8, 128), jnp.float32)] * 3
    for ref in blocks:
        for start in range(0, ref.shape[0], TRIALS):
            t0, t1 = ref[start].astype(jnp.float32), ref[start + 1].astype(jnp.float32)
            total = [total[0] + fold(t0 * t0), total[1] + fold(t0 * t1), total[2] + fold(t1 * t1)]
    c00, c01, c11 = [jnp.sum(x) for x in total]
    corr_ref[...] = matrix_of({(0, 0): c00, (0, 1): c01, (1, 0): c01, (1, 1): c11})[0:2, 0:2]


def correlate(blocks):
    return pl.pallas_call(
        corr_kernel,
        out_shape=jax.ShapeDtypeStruct((2, 2), jnp.float32),
        compiler_params=pltpu.CompilerParams(vmem_limit_bytes=16 * MIB),
    )(*blocks)


def far_kernel(n, acc_ref, own_ref, received_ref, total_ref, *sends):
    far, near = n // 2 - near_chips(n), near_chips(n)
    total = jnp.concatenate([own_ref[...], received_ref[far * 256 :, :].astype(jnp.float32)[0:8]], axis=0)
    total_ref[...] = total
    me = lax.axis_index("op")
    for j in range(far):
        value = acc_ref[jnp.bitwise_xor(me, 2 * (near + j))] + received_ref[j * 256 : (j + 1) * 256, :].astype(
            jnp.float32
        )
        sends[j][0:256, :] = value.astype(jnp.bfloat16)
        sends[j][256:, :] = total.astype(jnp.bfloat16)


def add_far(n, acc, own, received):
    return pl.pallas_call(
        functools.partial(far_kernel, n),
        out_shape=(jax.ShapeDtypeStruct((16, 128), jnp.float32),)
        + (jax.ShapeDtypeStruct((256 + TAIL, 128), jnp.bfloat16),) * (n // 2 - near_chips(n)),
        compiler_params=pltpu.CompilerParams(vmem_limit_bytes=16 * MIB),
    )(acc, own, received)


def near_kernel(n, acc_ref, total_ref, received_ref, mine_ref, *sends):
    me = lax.axis_index("op")
    for j in range(near_chips(n)):
        value = acc_ref[jnp.bitwise_xor(me, 2 * j)] + received_ref[j * 256 : (j + 1) * 256, :].astype(jnp.float32)
        if j == 0:
            mine_ref[...] = value
        else:
            sends[j - 1][0:256, :] = value.astype(jnp.bfloat16)
            sends[j - 1][256:, :] = total_ref[...].astype(jnp.bfloat16)


def add_near(n, acc, total, received):
    return pl.pallas_call(
        functools.partial(near_kernel, n),
        out_shape=(jax.ShapeDtypeStruct((256, 128), jnp.float32),)
        + (jax.ShapeDtypeStruct((256 + TAIL, 128), jnp.bfloat16),) * (near_chips(n) - 1),
        compiler_params=pltpu.CompilerParams(vmem_limit_bytes=16 * MIB),
    )(acc, total, received)


def last_kernel(mine_ref, total_ref, *refs):
    received, (product_ref, projected_ref) = refs[:-2], refs[-2:]
    value, total = mine_ref[...], total_ref[...]
    for ref in received:
        value = value + ref[0:256, :].astype(jnp.float32)
        total = total + ref[256:, :].astype(jnp.float32)
    product_ref[0, 0] = value[0:128]
    product_ref[0, 1] = value[128:256]
    total = total[0:8] + total[8:16]
    projected_ref[...] = total[0:2, 0:2] + total[0:2, 2:4] + total[0:2, 4:6]


def add_all(mine, total, received):
    return pl.pallas_call(
        last_kernel,
        out_shape=(
            jax.ShapeDtypeStruct((1, 2, 128, 128), jnp.float32),
            jax.ShapeDtypeStruct((2, 2), jnp.float32),
        ),
        compiler_params=pltpu.CompilerParams(vmem_limit_bytes=16 * MIB),
    )(mine, total, *received)


def body(n, trial, left_ops, right_ops, task_list):
    steps = n // 4
    plan, left_ops = make_plan(pltpu.with_memory_space_constraint(task_list.T, pltpu.HBM), left_ops, n, n * right_ops.shape[0])
    vectors = jnp.concatenate([trial[0], exchange(trial[0], n, 1)], axis=0)
    line = [vectors, right_ops, exchange(right_ops, n, 1)]
    blocks = [(line, 0, False)]
    for step in range(1, steps + 1):
        line = [ring_step(value, n) for value in line]
        blocks.append((line, step, False))
        if step < steps:
            blocks.append(([exchange(value, n, 1) for value in line], step, True))
    far, near, acc, own = run_tasks(n, plan, left_ops, blocks)
    far, arrays = lax.optimization_barrier((far, [block[0][0] for block in blocks]))
    correlation = correlate(arrays)
    far, near = exchange(far, n, 1), exchange(near, n, 1)
    total, *messages = add_far(n, acc, own, far)
    first = near_chips(n)
    received = [exchange(messages[j], n, 2 * (first + j)) for j in reversed(range(len(messages)))]
    mine, *messages = add_near(n, acc, total, near)
    received += [exchange(messages[j - 1], n, 2 * j) for j in reversed(range(1, first))]
    product, projected = add_all(mine, total, received)
    return product, correlation, projected


def solution(mesh):
    return jax.shard_map(
        functools.partial(body, mesh.shape["op"]),
        mesh=mesh,
        in_specs=(
            P(("groups", "op"), None, None, None),
            P(("groups", "op"), None, None),
            P(("groups", "op"), None, None),
            P(("groups", "op"), None),
        ),
        out_specs=(P(("groups", "op"), None, None, None), P("groups", None), P("groups", None)),
        check_vma=False,
    )
```

```python
import functools

import jax
import jax.numpy as jnp
from jax import lax
from jax.experimental import pallas as pl
from jax.experimental.pallas import tpu as pltpu
from jax.sharding import PartitionSpec as P

MIB = 1024 * 1024
TAIL = 16
TRIALS = 2
AHEAD = 3


def exchange(value, n, mask):
    return lax.ppermute(value, "op", [(i, i ^ mask) for i in range(n)])


def chip_at(place, chips):
    return 2 * place if place < chips // 2 else 2 * (chips - place) - 1


def ring_step(value, n):
    chips = n // 2
    order = [chip_at(place, chips) for place in range(chips)]
    pairs = []
    for place, chip in enumerate(order):
        pairs.append((2 * chip, 2 * order[(place + 1) % chips]))
        pairs.append((2 * chip + 1, 2 * order[(place - 1) % chips] + 1))
    return lax.ppermute(value, "op", pairs)


def owner_of(step, swapped, half, n):
    chips = n // 2
    me = lax.axis_index("op")
    chip, core = me // 2, lax.rem(me, 2)
    odd = lax.rem(chip, 2)
    mine = jnp.where(odd == 0, chip // 2, chips - 1 - chip // 2)
    line = 1 - core if swapped else core
    place = lax.rem(mine + (2 * line - 1) * step + 2 * chips, chips)
    there = jnp.where(place < chips // 2, 2 * place, 2 * (chips - place) - 1)
    return 2 * there + (line if half == 0 else 1 - line)


def split3(value):
    lanes = lax.broadcasted_iota(jnp.int32, (8, 128), 1)
    high = value.astype(jnp.bfloat16).astype(jnp.float32)
    middle = (value - high).astype(jnp.bfloat16).astype(jnp.float32)
    low = (value - high - middle).astype(jnp.bfloat16).astype(jnp.float32)
    return jnp.where(lanes < 2, high, jnp.where(lanes < 4, middle, low))


def tail_of(first, second):
    return jnp.concatenate([first, second], axis=0).astype(jnp.bfloat16)


def matrix_of(values, repeats=1):
    rows = lax.broadcasted_iota(jnp.int32, (8, 128), 0)
    lanes = lax.broadcasted_iota(jnp.int32, (8, 128), 1)
    total = jnp.zeros((8, 128), jnp.float32)
    for (i, j), value in values.items():
        for repeat in range(repeats):
            total = total + jnp.where((rows == i) & (lanes == j + 2 * repeat), value, 0.0)
    return total


def fold(value):
    return value.reshape(16, 8, 128).sum(axis=0)


def fits(n):
    return n <= 16


def near_chips(n):
    return n // 4


def phases_of(n):
    return 1


def chunk_of(n):
    return 144 if fits(n) else 48


def pairs_of(n):
    return 68 if fits(n) else 24


def run_of(slots, n):
    return 4 if slots >= 8 * n else 2


def source_places(slots, n):
    chunk = chunk_of(n)
    most = slots + min(slots, n) * (run_of(slots, n) - 1)
    return -(-most // chunk) * chunk


def place_of(chip, chips):
    half = jnp.floor(chip * 0.5)
    return jnp.where(chip == 2.0 * half, half, chips - 1.0 - half)


def plan_kernel(n, terms, tasks_ref, plan_ref):
    slots = tasks_ref.shape[1]
    places = plan_ref.shape[1]
    chips = n // 2
    phases = phases_of(n)
    rows = tasks_ref[...].astype(jnp.float32)
    source, target, term, live = rows[0:1], rows[1:2], rows[2:3], rows[3:4]
    lane = lax.broadcasted_iota(jnp.int32, (1, slots), 1).astype(jnp.float32)
    number = lax.broadcasted_iota(jnp.int32, (1, places), 1).astype(jnp.float32)
    at = lax.broadcasted_iota(jnp.int32, (slots, places), 1).astype(jnp.float32)
    me = lax.axis_index("op")
    mine = place_of((jnp.zeros((1, slots), jnp.int32) + me // 2).astype(jnp.float32), float(chips))
    gap = place_of(jnp.floor(source * 0.5), float(chips)) - mine
    up = jnp.where(gap < 0, gap + chips, gap)
    far = jnp.minimum(up, chips - up)
    phase = jnp.clip(far - 1.0, 0.0, phases - 1.0)

    def column(*values):
        pad = [jnp.zeros((8 - len(values), slots), jnp.float32)]
        return jnp.transpose(jnp.concatenate(list(values) + pad, axis=0))

    def sort(sector, parts, unit, whole):
        keys = parts * n
        index = lax.broadcasted_iota(jnp.int32, (keys, slots), 0).astype(jnp.float32)
        part = phase if parts > 1 else jnp.zeros_like(phase)
        key = jnp.where(live > 0, part * n + sector, float(keys))
        columns = column(key, lane)
        earlier = jnp.where((columns[:, 0:1] == key) & (columns[:, 1:2] < lane), 1.0, 0.0)
        count = jnp.sum(jnp.where(index == key, 1.0, 0.0), axis=1, keepdims=True)
        padded = jnp.ceil(count / unit) * unit
        place = jnp.sum(earlier, axis=0, keepdims=True)
        start = jnp.zeros((1, 1), jnp.float32)
        starts = [start]
        for p in range(parts):
            lengths = padded[p * n : (p + 1) * n]
            before = jnp.where(index[p * n : (p + 1) * n] < key, lengths, 0.0)
            place = place + jnp.where(part == p, start * whole + jnp.sum(before, axis=0, keepdims=True), 0.0)
            start = start + jnp.ceil(jnp.sum(lengths, axis=0, keepdims=True) / whole)
            starts.append(start)
        return jnp.where(live > 0, place, -1.0), starts

    by_source, source_starts = sort(source, phases, float(run_of(slots, n)), float(chunk_of(n)))
    by_target, target_starts = sort(target, 1, 2.0, 2.0 * pairs_of(n))
    columns = column(by_source, by_target, lane, source, term, target)

    def picker(places_column):
        hit = places_column == at

        def pick(values, other):
            found = jnp.sum(jnp.where(hit, values - other, 0.0), axis=0, keepdims=True)
            return (found + other).astype(jnp.int32)

        return pick

    own = (jnp.zeros((1, 1), jnp.int32) + me).astype(jnp.float32)
    pick = picker(columns[:, 0:1])
    plan_ref[0:1] = pick(columns[:, 2:3], 0.0)
    plan_ref[1:2] = pick(columns[:, 3:4], own)
    pick = picker(columns[:, 1:2])
    plan_ref[2:3] = pick(columns[:, 0:1], -1.0)
    plan_ref[3:4] = pick(columns[:, 4:5], float(terms))
    plan_ref[4:5] = pick(columns[:, 5:6], float(n))
    turns = jnp.zeros((1, places), jnp.float32)
    for p, start in enumerate(source_starts + [target_starts[1]]):
        turns = turns + jnp.where(number == p, start, 0.0)
    plan_ref[5:6] = turns.astype(jnp.int32)


def stage_kernel(n, terms, tasks_ref, left_ref, plan_ref, held_ref, tasks, sem):
    copies = [
        pltpu.make_async_copy(tasks_ref, tasks, sem.at[0]),
        pltpu.make_async_copy(left_ref, held_ref, sem.at[1]),
    ]
    for copy in copies:
        copy.start()
    copies[0].wait()
    plan_kernel(n, terms, tasks, plan_ref)
    copies[1].wait()


def make_plan(tasks, left_ops, n, terms):
    most = source_places(tasks.shape[1], n)
    plan = jax.ShapeDtypeStruct((6, -(-most // 128) * 128), jnp.int32)
    vmem, hbm = pl.BlockSpec(memory_space=pltpu.VMEM), pl.BlockSpec(memory_space=pltpu.HBM)
    if fits(n):
        return pl.pallas_call(
            functools.partial(stage_kernel, n, terms),
            in_specs=[hbm, hbm],
            out_specs=(vmem, vmem),
            out_shape=(plan, jax.ShapeDtypeStruct(left_ops.shape, left_ops.dtype)),
            scratch_shapes=[pltpu.VMEM(tasks.shape, jnp.int32), pltpu.SemaphoreType.DMA((2,))],
            compiler_params=pltpu.CompilerParams(vmem_limit_bytes=42 * MIB),
        )(tasks, left_ops)
    return (
        pl.pallas_call(
            functools.partial(plan_kernel, n, terms),
            out_shape=plan,
            compiler_params=pltpu.CompilerParams(vmem_limit_bytes=16 * MIB),
        )(tasks),
        left_ops,
    )


def block_parts(n, kinds, blocks, trial, right):
    parts = []
    for b, kind in enumerate(kinds):
        vectors, *terms = blocks[3 * b : 3 * b + 3]
        for half, ref in enumerate(terms):
            owner = owner_of(*kind, half, n)
            per = ref.shape[0]
            parts.append((vectors.at[pl.ds(half * TRIALS, TRIALS)], trial.at[owner]))
            parts.append((ref, right.at[pl.ds(owner * per, per)]))
    return parts


def make_halves(n, plan_ref, left_ref, trial, halves, fetched, beside):
    turns = plan_ref[5, 1]
    run = run_of(left_ref.shape[0], n)
    chunk = chunk_of(n)

    def fetch(turn):
        left, left_sem = fetched
        at = lax.rem(turn, AHEAD)
        for u in range(chunk):
            slot = plan_ref[0, turn * chunk + u]
            pltpu.make_async_copy(left_ref.at[slot], left.at[at, u], left_sem.at[at]).start()

    def start():
        for turn in range(AHEAD - 1) if fetched else ():

            @pl.when(turn < turns)
            def _():
                fetch(turn)

    def turn_of(turn, carry):
        if fetched:
            left, left_sem = fetched

            @pl.when(turn + AHEAD - 1 < turns)
            def _():
                fetch(turn + AHEAD - 1)

            at = lax.rem(turn, AHEAD)
            pltpu.make_async_copy(left_ref.at[pl.ds(0, chunk)], left.at[at], left_sem.at[at]).wait()
        beside()
        place = turn * chunk
        for r in range(0, chunk, run):
            source = plan_ref[1, place + r]
            vectors = jnp.concatenate([trial[source, 0], trial[source, 1]], axis=1)
            if fetched:
                rows = left[at, r : r + run].reshape(run * 128, 128)
            else:
                rows = jnp.concatenate([left_ref[plan_ref[0, place + r + u]] for u in range(run)], axis=0)
            half = jnp.dot(rows, vectors, preferred_element_type=jnp.float32).astype(jnp.bfloat16)
            for u in range(run):
                halves[place + r + u, 0] = half[u * 128 : (u + 1) * 128, :128]
                halves[place + r + u, 1] = half[u * 128 : (u + 1) * 128, 128:]
        return carry

    return start, lambda: lax.fori_loop(0, turns, turn_of, 0)


def tasks_kernel(n, kinds, plan_ref, left_ref, *refs):
    blocks, refs = refs[: 3 * len(kinds)], refs[3 * len(kinds) :]
    far_ref, near_ref, acc, own_ref, halves, trial, right, block_sem, *fetched = refs
    parts = block_parts(n, kinds, blocks, trial, right)

    def clear():
        for s in range(n):
            acc[s] = jnp.zeros((256, 128), jnp.float32)

    def beside():
        if fits(n):
            clear()
            for source, to in parts[1::2]:
                to[...] = source[...]

    start, products = make_halves(n, plan_ref, left_ref, trial, halves, fetched, beside)
    right[right.shape[0] - 1] = jnp.zeros((128, 128), jnp.bfloat16)
    start()
    copies = []
    if fits(n):
        for source, to in parts[0::2]:
            to[...] = source[...]
        pl.when(plan_ref[5, 1] == 0)(clear)
    else:
        for index, (source, to) in enumerate(parts):
            copies.append(pltpu.make_async_copy(source, to, block_sem.at[index]))
            copies[-1].start()
        clear()
    for copy in copies:
        copy.wait()
    products()

    def target_turn(turn, carry):
        first = turn * 2 * pairs_of(n)
        for u in range(0, 2 * pairs_of(n), 2):
            place = first + u
            one = plan_ref[2, place]
            two = plan_ref[2, place + 1]
            one, two = jnp.maximum(one, 0), jnp.where(two < 0, jnp.maximum(one, 0), two)
            pair = jnp.concatenate(
                [
                    jnp.concatenate([halves[one, 0], halves[two, 0]], axis=1),
                    jnp.concatenate([halves[one, 1], halves[two, 1]], axis=1),
                ],
                axis=0,
            )
            rights = jnp.concatenate([right[plan_ref[3, place]], right[plan_ref[3, place + 1]]], axis=1)
            term = lax.dot_general(
                pair, rights, (((1,), (1,)), ((), ())), preferred_element_type=jnp.float32
            )
            target = plan_ref[4, place]
            acc[target] = acc[target] + term
        return carry

    lax.fori_loop(0, plan_ref[5, 2], target_turn, 0)
    me = lax.axis_index("op")

    def dots(s, carry):
        t0 = trial[s, 0].astype(jnp.float32)
        t1 = trial[s, 1].astype(jnp.float32)
        a0 = acc[s, 0:128, :]
        a1 = acc[s, 128:256, :]
        p00, p01, p10, p11 = carry
        return p00 + fold(t0 * a0), p01 + fold(t0 * a1), p10 + fold(t1 * a0), p11 + fold(t1 * a1)

    zero = jnp.zeros((8, 128), jnp.float32)
    sums = lax.fori_loop(0, n, dots, (zero,) * 4, unroll=16)
    p00, p01, p10, p11 = [jnp.sum(x) for x in sums]

    chips = n // 2
    near = near_chips(n)

    def pack(j, carry):
        value = acc[jnp.bitwise_xor(me, 2 * j + 1)].astype(jnp.bfloat16)

        @pl.when(j < near)
        def _():
            near_ref[pl.ds(pl.multiple_of(j * 256, 256), 256), :] = value

        @pl.when(j >= near)
        def _():
            far_ref[pl.ds(pl.multiple_of((j - near) * 256, 256), 256), :] = value

        return carry

    lax.fori_loop(0, chips, pack, 0, unroll=8)
    own = split3(matrix_of({(0, 0): p00, (0, 1): p01, (1, 0): p10, (1, 1): p11}, 3))
    own_ref[...] = own
    far_ref[(chips - near) * 256 :, :] = tail_of(own, jnp.zeros_like(own))


def run_tasks(n, plan, left_ops, blocks):
    slots = left_ops.shape[0]
    terms_per = blocks[0][0][1].shape[0]
    kinds = tuple(block[1:] for block in blocks)
    vmem, hbm = pl.BlockSpec(memory_space=pltpu.VMEM), pl.BlockSpec(memory_space=pltpu.HBM)
    given = vmem if fits(n) else hbm
    fetched = [] if fits(n) else [
        pltpu.VMEM((AHEAD, chunk_of(n), 128, 128), jnp.bfloat16),
        pltpu.SemaphoreType.DMA((AHEAD,)),
    ]
    return pl.pallas_call(
        functools.partial(tasks_kernel, n, kinds),
        out_shape=(
            jax.ShapeDtypeStruct(((n // 2 - near_chips(n)) * 256 + TAIL, 128), jnp.bfloat16),
            jax.ShapeDtypeStruct((near_chips(n) * 256, 128), jnp.bfloat16),
            jax.ShapeDtypeStruct((n + 1, 256, 128), jnp.float32),
            jax.ShapeDtypeStruct((8, 128), jnp.float32),
        ),
        in_specs=[pl.BlockSpec(memory_space=pltpu.SMEM)] + [given] * (1 + 3 * len(blocks)),
        out_specs=(vmem,) * 4,
        scratch_shapes=[
            pltpu.VMEM((source_places(slots, n), 2, 128, 128), jnp.bfloat16),
            pltpu.VMEM((n, TRIALS, 128, 128), jnp.bfloat16),
            pltpu.VMEM((n * terms_per + 1, 128, 128), jnp.bfloat16),
            pltpu.SemaphoreType.DMA((4 * len(blocks),)),
        ]
        + fetched,
        compiler_params=pltpu.CompilerParams(vmem_limit_bytes=(33 if fits(n) else 58) * MIB),
        cost_estimate=pl.CostEstimate(
            flops=slots * 8 * 128**3, bytes_accessed=slots * 32768 + n * 450000, transcendentals=0
        ),
    )(plan, left_ops, *[value for block in blocks for value in block[0]])


def corr_kernel(*refs):
    blocks, corr_ref = refs[:-1], refs[-1]
    total = [jnp.zeros((8, 128), jnp.float32)] * 3
    for ref in blocks:
        for start in range(0, ref.shape[0], TRIALS):
            t0, t1 = ref[start].astype(jnp.float32), ref[start + 1].astype(jnp.float32)
            total = [total[0] + fold(t0 * t0), total[1] + fold(t0 * t1), total[2] + fold(t1 * t1)]
    c00, c01, c11 = [jnp.sum(x) for x in total]
    corr_ref[...] = matrix_of({(0, 0): c00, (0, 1): c01, (1, 0): c01, (1, 1): c11})[0:2, 0:2]


def correlate(blocks):
    return pl.pallas_call(
        corr_kernel,
        out_shape=jax.ShapeDtypeStruct((2, 2), jnp.float32),
        compiler_params=pltpu.CompilerParams(vmem_limit_bytes=16 * MIB),
    )(*blocks)


def far_kernel(n, acc_ref, own_ref, received_ref, total_ref, *sends):
    far, near = n // 2 - near_chips(n), near_chips(n)
    total = jnp.concatenate([own_ref[...], received_ref[far * 256 :, :].astype(jnp.float32)[0:8]], axis=0)
    total_ref[...] = total
    me = lax.axis_index("op")
    for j in range(far):
        value = acc_ref[jnp.bitwise_xor(me, 2 * (near + j))] + received_ref[j * 256 : (j + 1) * 256, :].astype(
            jnp.float32
        )
        sends[j][0:256, :] = value.astype(jnp.bfloat16)
        sends[j][256:, :] = total.astype(jnp.bfloat16)


def add_far(n, acc, own, received):
    return pl.pallas_call(
        functools.partial(far_kernel, n),
        out_shape=(jax.ShapeDtypeStruct((16, 128), jnp.float32),)
        + (jax.ShapeDtypeStruct((256 + TAIL, 128), jnp.bfloat16),) * (n // 2 - near_chips(n)),
        compiler_params=pltpu.CompilerParams(vmem_limit_bytes=16 * MIB),
    )(acc, own, received)


def near_kernel(n, acc_ref, total_ref, received_ref, mine_ref, *sends):
    me = lax.axis_index("op")
    for j in range(near_chips(n)):
        value = acc_ref[jnp.bitwise_xor(me, 2 * j)] + received_ref[j * 256 : (j + 1) * 256, :].astype(jnp.float32)
        if j == 0:
            mine_ref[...] = value
        else:
            sends[j - 1][0:256, :] = value.astype(jnp.bfloat16)
            sends[j - 1][256:, :] = total_ref[...].astype(jnp.bfloat16)


def add_near(n, acc, total, received):
    return pl.pallas_call(
        functools.partial(near_kernel, n),
        out_shape=(jax.ShapeDtypeStruct((256, 128), jnp.float32),)
        + (jax.ShapeDtypeStruct((256 + TAIL, 128), jnp.bfloat16),) * (near_chips(n) - 1),
        compiler_params=pltpu.CompilerParams(vmem_limit_bytes=16 * MIB),
    )(acc, total, received)


def last_kernel(mine_ref, total_ref, *refs):
    received, (product_ref, projected_ref) = refs[:-2], refs[-2:]
    value, total = mine_ref[...], total_ref[...]
    for ref in received:
        value = value + ref[0:256, :].astype(jnp.float32)
        total = total + ref[256:, :].astype(jnp.float32)
    product_ref[0, 0] = value[0:128]
    product_ref[0, 1] = value[128:256]
    total = total[0:8] + total[8:16]
    projected_ref[...] = total[0:2, 0:2] + total[0:2, 2:4] + total[0:2, 4:6]


def add_all(mine, total, received):
    return pl.pallas_call(
        last_kernel,
        out_shape=(
            jax.ShapeDtypeStruct((1, 2, 128, 128), jnp.float32),
            jax.ShapeDtypeStruct((2, 2), jnp.float32),
        ),
        compiler_params=pltpu.CompilerParams(vmem_limit_bytes=16 * MIB),
    )(mine, total, *received)


def body(n, trial, left_ops, right_ops, task_list):
    steps = n // 4
    plan, left_ops = make_plan(pltpu.with_memory_space_constraint(task_list.T, pltpu.HBM), left_ops, n, n * right_ops.shape[0])
    vectors = jnp.concatenate([trial[0], exchange(trial[0], n, 1)], axis=0)
    line = [vectors, right_ops, exchange(right_ops, n, 1)]
    blocks = [(line, 0, False)]
    for step in range(1, steps + 1):
        line = [ring_step(value, n) for value in line]
        blocks.append((line, step, False))
        if step < steps:
            blocks.append(([exchange(value, n, 1) for value in line], step, True))
    far, near, acc, own = run_tasks(n, plan, left_ops, blocks)
    far, arrays = lax.optimization_barrier((far, [block[0][0] for block in blocks]))
    correlation = correlate(arrays)
    far, near = exchange(far, n, 1), exchange(near, n, 1)
    total, *messages = add_far(n, acc, own, far)
    first = near_chips(n)
    received = [exchange(messages[j], n, 2 * (first + j)) for j in reversed(range(len(messages)))]
    mine, *messages = add_near(n, acc, total, near)
    received += [exchange(messages[j - 1], n, 2 * j) for j in reversed(range(1, first))]
    product, projected = add_all(mine, total, received)
    return product, correlation, projected


def solution(mesh):
    return jax.shard_map(
        functools.partial(body, mesh.shape["op"]),
        mesh=mesh,
        in_specs=(
            P(("groups", "op"), None, None, None),
            P(("groups", "op"), None, None),
            P(("groups", "op"), None, None),
            P(("groups", "op"), None),
        ),
        out_specs=(P(("groups", "op"), None, None, None), P("groups", None), P("groups", None)),
        check_vma=False,
    )
```
